32 devices in a mesh: seq: 4 (over y, x), img: 8 (over z, core).
Axes of the slice: x: 2, y: 2, z: 4, core: 2. Of those that a mesh axis runs over, the one named last changes fastest.
Arguments:
- enc_input: bfloat16 [8, 2, 292, 768], P('img', None, 'seq'), may hold values from -6 to 6
- cotangent: bfloat16 [8, 2, 1176, 512], P('img', None, 'seq'), may hold values from -6 to 6
- enc_image: int32 [8, 2, 292], P('img'), may hold values from 0 to 2, as said below
- visible_rows: int32 [8, 2, 292], P('img'), may hold values from 0 to 1175, as said below
- enc_norms: float32 [768, 6], replicated, may hold values from -1.2 to 1.5
- enc_qkv: bfloat16 [768, 2304], replicated, may hold values from -0.21875 to 0.21875
- enc_proj: bfloat16 [768, 768], replicated, may hold values from -0.625 to 0.625
- enc_up: bfloat16 [768, 3072], replicated, may hold values from -0.21875 to 0.21875
- enc_down: bfloat16 [3072, 768], replicated, may hold values from -0.109375 to 0.109375
- embed: bfloat16 [768, 512], replicated, may hold values from -0.21875 to 0.21875
- dec_vecs: float32 [512, 5], replicated, may hold values from -3 to 3
- dec_qkv: bfloat16 [512, 1536], replicated, may hold values from -0.25 to 0.25
- dec_proj: bfloat16 [512, 512], replicated, may hold values from -1 to 1
- dec_up: bfloat16 [512, 2048], replicated, may hold values from -0.25 to 0.25
- dec_down: bfloat16 [2048, 512], replicated, may hold values from -0.125 to 0.125
Outputs:
- decoded: bfloat16 [8, 2, 1176, 512], P('img', None, 'seq')
- grad_input: float32 [8, 2, 292, 768], P('img', None, 'seq')
- grad_enc_norms: float32 [768, 6], P('img')
- grad_enc_qkv: float32 [768, 2304], P('img')
- grad_enc_proj: float32 [768, 768], P('img')
- grad_enc_up: float32 [768, 3072], P('img')
- grad_enc_down: float32 [3072, 768], P('img')
- grad_embed: float32 [768, 512], P('img')
- grad_dec_vecs: float32 [512, 5], P('img')
- grad_dec_qkv: float32 [512, 1536], P('img')
- grad_dec_proj: float32 [512, 512], P('img')
- grad_dec_up: float32 [512, 2048], P('img')
- grad_dec_down: float32 [2048, 512], P('img')
The draws below stay inside these ranges and needn't reach their ends.
Inputs may be any that keep to these rules, and one draw needn't show every extreme that they name: `enc_image`: A pack's visible tokens belong to its three images numbered 0, 1, 2 in order along the pack, each number one run. `visible_rows`: each visible token names a row of its own image; no row is named twice; within an image the order is random.
All inputs are finite; a program needn't handle non-finite values.
Results may differ from the reference program's by a relative error of at most 0.018.
Values may be sent and summed in bfloat16 or wider, within the bound.
A program may use at most 192 MiB of HBM per device.

```python
import math
import jax
import jax.numpy as jnp
from jax import lax

DE = 768
HE = 12
FE = 3072
DD = 512
HD = 16
FD = 2048
PATCHES = 784
PACKS = 2
DEC_LEN = 1176
ENC_LEN = 292
N_IMG = 8


def pack_one(pack_key):
    count_key, order_key = jax.random.split(pack_key, 2)
    small_rows = PATCHES // 4
    small_seen = PATCHES // 16
    reach = max(PATCHES // 64, 1)
    counts = jax.random.randint(count_key, (2,), small_seen - reach, small_seen + reach + 1).astype(jnp.int32)
    first_count = counts[0]
    third_start = ENC_LEN - counts[1]
    tokens = jnp.arange(ENC_LEN, dtype=jnp.int32)
    enc_groups = (tokens >= first_count).astype(jnp.int32) + (tokens >= third_start).astype(jnp.int32)
    starts = jnp.stack([jnp.zeros((), jnp.int32), first_count, third_start])
    local_index = tokens - starts[enc_groups]
    rows = jnp.arange(DEC_LEN, dtype=jnp.int32)
    dec_groups = (rows >= small_rows).astype(jnp.int32) + (rows >= small_rows + PATCHES).astype(jnp.int32)
    row_starts = jnp.array([0, small_rows, small_rows + PATCHES], jnp.int32)
    shuffle = jax.random.permutation(order_key, DEC_LEN).astype(jnp.int32)
    sorted_rows = jnp.argsort(dec_groups * DEC_LEN + shuffle).astype(jnp.int32)
    visible = sorted_rows[row_starts[enc_groups] + local_index]
    return (enc_groups, visible)


def pack_tables(key):
    pack_keys = jax.random.split(jax.random.fold_in(key, 17), N_IMG * PACKS)
    enc_groups, visible = jax.vmap(pack_one)(pack_keys)
    return (enc_groups.reshape(N_IMG, PACKS, ENC_LEN), visible.reshape(N_IMG, PACKS, ENC_LEN))


def draw_enc_image(key, part):
    return pack_tables(key)[0]


def draw_visible_rows(key, part):
    return pack_tables(key)[1]


def norm_columns(table_key, row_width, columns):
    first_key, second_key = jax.random.split(table_key)
    gain_part = 1.0 + jax.random.uniform(first_key, (row_width, columns), jnp.float32, -0.4, 0.4)
    shifts = 0.3 * jnp.clip(jax.random.normal(second_key, (row_width, columns), jnp.float32), -4.0, 4.0)
    is_even = (jnp.arange(columns) % 2 == 0)[None, :]
    return jnp.where(is_even, gain_part, shifts)


def draw_enc_norms(key, part):
    return norm_columns(jax.random.fold_in(key, 3), DE, 6)


def draw_dec_vecs(key, part):
    columns_table = norm_columns(jax.random.fold_in(key, 5), DD, 5)
    token_key = jax.random.fold_in(key, 9)
    mask_token = jnp.clip(jax.random.normal(token_key, (DD,), jnp.float32), -3.0, 3.0)
    return columns_table.at[:, 4].set(mask_token)


def block_scale(own_key, shape, shards, least, top_value):
    loudness, own = 1.0, jax.random.fold_in(own_key, 6)
    for dim, blocks in shards:
        steps = jnp.exp(jax.random.uniform(jax.random.fold_in(own, dim), (blocks,), jnp.float32, least / len(shards), top_value / len(shards)))
        loudness = loudness * jnp.repeat(steps, shape[dim] // blocks).reshape([-1 if axis == dim else 1 for axis in range(len(shape))])
    return loudness


def centred(rng, dims, width, limit, cuts=(), kind=jnp.bfloat16):
    factor_of = block_scale(rng, dims, cuts, -0.22, 0.18) if cuts else 1.0
    entries = jax.random.normal(rng, dims, jnp.float32) * width * factor_of
    return jnp.minimum(jnp.maximum(entries, -limit), limit).astype(kind)


def setup_inputs(seed: int = 0) -> dict:
    streams_of = jax.random.split(jax.random.key(seed), 16)
    return {
        "enc_input": centred(streams_of[0], (N_IMG, PACKS, ENC_LEN, DE), 1.0, 6.0, ((0, 8), (2, 4))),
        "cotangent": centred(streams_of[1], (N_IMG, PACKS, DEC_LEN, DD), 1.0, 6.0, ((0, 8), (2, 4))),
        "enc_image": draw_enc_image(jax.random.fold_in(streams_of[15], 71), 0),
        "visible_rows": draw_visible_rows(jax.random.fold_in(streams_of[15], 71), 0),
        "enc_norms": draw_enc_norms(jax.random.fold_in(streams_of[15], 71), 0),
        "enc_qkv": centred(streams_of[5], (DE, 3 * DE), DE ** -0.5, 0.21875),
        "enc_proj": centred(streams_of[6], (DE, DE), (DE // 8) ** -0.5, 0.625),
        "enc_up": centred(streams_of[7], (DE, FE), DE ** -0.5, 0.21875),
        "enc_down": centred(streams_of[8], (FE, DE), FE ** -0.5, 0.109375),
        "embed": centred(streams_of[9], (DE, DD), DE ** -0.5, 0.21875),
        "dec_vecs": draw_dec_vecs(jax.random.fold_in(streams_of[15], 71), 0),
        "dec_qkv": centred(streams_of[11], (DD, 3 * DD), DD ** -0.5, 0.25),
        "dec_proj": centred(streams_of[12], (DD, DD), (DD // 16) ** -0.5, 1.0),
        "dec_up": centred(streams_of[13], (DD, FD), DD ** -0.5, 0.25),
        "dec_down": centred(streams_of[14], (FD, DD), FD ** -0.5, 0.125),
    }


@jax.custom_vjp
def low(v):
    return lax.optimization_barrier(v.astype(jnp.bfloat16)).astype(jnp.float32)

@jax.custom_vjp
def low_back(v):
    return v

def low_keep(v):
    return (low(v), None)

def low_pass(kept, grad):
    return (grad,)

def back_keep(v):
    return (v, None)

def back_low(kept, grad):
    return (low(grad),)
low.defvjp(low_keep, low_pass)
low_back.defvjp(back_keep, back_low)
eps_norm = 1e-06
highest = lax.Precision.HIGHEST

def matmul(left_side, right_side):
    return jnp.dot(left_side, right_side, precision=highest, preferred_element_type=jnp.float32)

def layer_norm(values, norm_gain, norm_shift):
    average = lax.optimization_barrier(jnp.mean(values, axis=-1, keepdims=True))
    centered = values - average
    variance = lax.optimization_barrier(jnp.mean(centered * centered, axis=-1, keepdims=True))
    return centered * lax.rsqrt(variance + eps_norm) * norm_gain + norm_shift

def head_attend(head_items, segments, score_scale):
    queries, key_rows, value_rows = (head_items[0], head_items[1], head_items[2])
    scores = low_back(matmul(queries, key_rows.T) * score_scale)
    scores = jnp.where(segments[:, None] == segments[None, :], scores, -1e+30)
    probabilities = jax.nn.softmax(scores, axis=-1)
    return matmul(low(probabilities), value_rows)

def attention(mixed, segments, head_count):
    row_count = mixed.shape[0]
    model_width = mixed.shape[1] // 3
    head_size = model_width // head_count
    score_scale = 1.0 / math.sqrt(head_size)
    head_parts = mixed.reshape(row_count, 3, head_count, head_size).transpose(2, 1, 0, 3)

    def one_head(head_items):
        return head_attend(head_items, segments, score_scale)
    outputs = lax.map(jax.checkpoint(one_head), head_parts)
    return outputs.transpose(1, 0, 2).reshape(row_count, model_width)

def residual_block(rows_in, norms, w_qkv, w_proj, w_up, w_down, segments, head_count):
    attn_in = low(layer_norm(rows_in, norms[:, 0], norms[:, 1]))
    mixed = low(low_back(matmul(attn_in, w_qkv)))
    attended = low(low_back(attention(mixed, segments, head_count)))
    middle = rows_in + low_back(matmul(attended, w_proj))
    mlp_in = low(layer_norm(middle, norms[:, 2], norms[:, 3]))
    hidden = low_back(matmul(mlp_in, w_up))
    active = low(jax.nn.gelu(hidden, approximate=False))
    return middle + low_back(matmul(active, w_down))

def row_images():
    indices = jnp.arange(DEC_LEN, dtype=jnp.int32)
    small_rows = PATCHES // 4
    return (indices >= small_rows).astype(jnp.int32) + (indices >= small_rows + PATCHES).astype(jnp.int32)

def position_code(dec_groups, row_width):
    row_total = dec_groups.shape[0]
    indices = jnp.arange(row_total, dtype=jnp.int32)
    boundary = jnp.concatenate([jnp.ones((1,), jnp.bool_), dec_groups[1:] != dec_groups[:-1]])
    starts = lax.cummax(jnp.where(boundary, indices, 0), axis=0)
    offsets = indices - starts
    halfway = row_width // 2
    frequency = jnp.exp(jnp.arange(halfway, dtype=jnp.float32) * (-math.log(10000.0) / halfway))
    angles = offsets.astype(jnp.float32)[:, None] * frequency[None, :]
    return jnp.concatenate([jnp.sin(angles), jnp.cos(angles)], axis=1)

def pack_forward(params, inputs, enc_groups, dec_groups, visible):
    enc_norms, enc_qkv, enc_proj, enc_up, enc_down, embed, dec_vecs, dec_qkv, dec_proj, dec_up, dec_down = params
    enc_out = residual_block(inputs, enc_norms, enc_qkv, enc_proj, enc_up, enc_down, enc_groups, HE)
    enc_final = low(layer_norm(enc_out, enc_norms[:, 4], enc_norms[:, 5]))
    embedded = low(low_back(matmul(enc_final, embed)))
    source = jnp.full((DEC_LEN,), ENC_LEN, jnp.int32).at[visible].set(jnp.arange(ENC_LEN, dtype=jnp.int32))
    padded = jnp.concatenate([embedded, jnp.zeros((1, DD), embedded.dtype)], axis=0)
    shown = (source < ENC_LEN)[:, None]
    dec_input = jnp.where(shown, padded[source], dec_vecs[None, :, 4]) + position_code(dec_groups, DD)
    return residual_block(dec_input, dec_vecs, dec_qkv, dec_proj, dec_up, dec_down, dec_groups, HD)

def reference(enc_input, cotangent, enc_image, visible_rows, enc_norms, enc_qkv, enc_proj, enc_up, enc_down, embed, dec_vecs, dec_qkv, dec_proj, dec_up, dec_down):
    params = (enc_norms.astype(jnp.float32), enc_qkv.astype(jnp.float32), enc_proj.astype(jnp.float32), enc_up.astype(jnp.float32), enc_down.astype(jnp.float32), embed.astype(jnp.float32), dec_vecs.astype(jnp.float32), dec_qkv.astype(jnp.float32), dec_proj.astype(jnp.float32), dec_up.astype(jnp.float32), dec_down.astype(jnp.float32))
    inputs = enc_input.astype(jnp.float32)
    dec_groups = row_images()
    enc_flat = enc_image.reshape(N_IMG * PACKS, ENC_LEN)
    visible_flat = visible_rows.reshape(N_IMG * PACKS, ENC_LEN)

    def forward(weights_all, inputs_all):
        flat_inputs = inputs_all.reshape(N_IMG * PACKS, ENC_LEN, DE)

        def scan_step(scan_carry, packed):
            return (scan_carry, pack_forward(weights_all, packed[0], packed[1], dec_groups, packed[2]))
        _, outputs = lax.scan(scan_step, jnp.zeros((), jnp.float32), (flat_inputs, enc_flat, visible_flat))
        return outputs.reshape(N_IMG, PACKS, DEC_LEN, DD)
    outputs, pullback = jax.vjp(forward, params, inputs)
    gradients, grad_input = pullback(cotangent.astype(jnp.float32))
    return (outputs.astype(jnp.bfloat16), grad_input, gradients[0], gradients[1], gradients[2], gradients[3], gradients[4], gradients[5], gradients[6], gradients[7], gradients[8], gradients[9], gradients[10])
```

```python
import math

import jax
import jax.numpy as jnp
import numpy as np
from jax import lax
from jax.sharding import PartitionSpec as P

HE = 12
HD = 16
PATCHES = 784
SMALL = PATCHES // 4
HALF = PATCHES // 2
SMALL_PAD = 208
BIG_PAD = 400
DEC_PAD = SMALL_PAD + BIG_PAD
ENC_PAD = 160

eps_norm = 1e-06
masked_score = -1e30
bf16 = jnp.bfloat16
f32 = jnp.float32


def product(left_side, right_side):
    return jnp.dot(left_side, right_side, preferred_element_type=f32)


def inner_rows(left_side, right_side):
    return lax.dot_general(
        left_side, right_side, (((0,), (0,)), ((), ())), preferred_element_type=f32
    )


def inner_cols(left_side, right_side):
    return lax.dot_general(
        left_side, right_side, (((1,), (1,)), ((), ())), preferred_element_type=f32
    )


def exact_gelu(values):
    return jax.nn.gelu(values, approximate=False)


def gelu_grad(hidden, grad_active):
    _, pullback = jax.vjp(exact_gelu, hidden)
    return pullback(grad_active)[0]


def norm_forward(values, norm_gain, norm_shift):
    centered = values - jnp.mean(values, axis=-1, keepdims=True)
    inverse = lax.rsqrt(jnp.mean(centered * centered, axis=-1, keepdims=True) + eps_norm)
    normed = centered * inverse
    return ((normed * norm_gain + norm_shift).astype(bf16), normed, inverse)


def norm_backward(grad_out, normed, inverse, norm_gain):
    scaled = grad_out * norm_gain
    grad_values = inverse * (
        scaled
        - jnp.mean(scaled, axis=-1, keepdims=True)
        - normed * jnp.mean(scaled * normed, axis=-1, keepdims=True)
    )
    return (grad_values, jnp.sum(grad_out * normed, axis=0), jnp.sum(grad_out, axis=0))


def permute(array, where_to):
    seq_count = lax.axis_size("seq")
    img_count = lax.axis_size("img")
    pairs = []
    for seq in range(seq_count):
        for img in range(img_count):
            seq_to, img_to = where_to(seq, img)
            pairs.append((seq * img_count + img, seq_to * img_count + img_to))
    return lax.ppermute(array, ("seq", "img"), pairs)


def swap(array):
    return permute(array, lambda seq, img: (seq, img ^ 1))


def pack_move(turn):
    def where_to(seq, img):
        return (2 * (img & 1) + (turn ^ (seq & 1)), (img & ~1) | (seq >> 1))

    return where_to


def exchange_packs(blocks, odd):
    rounds = [
        permute(jnp.where(odd, blocks[1 - turn], blocks[turn]), pack_move(turn)) for turn in (0, 1)
    ]
    return (jnp.where(odd, rounds[1], rounds[0]), jnp.where(odd, rounds[0], rounds[1]))


def pick(array, index, axis):
    return lax.dynamic_index_in_dim(array, index, axis, keepdims=False)


def pad_rows(array, rows):
    return jnp.pad(array, ((0, rows - array.shape[0]),) + ((0, 0),) * (array.ndim - 1))


def split_heads(array, head_count):
    return array.reshape(array.shape[0], head_count, array.shape[1] // head_count).transpose(
        1, 0, 2
    )


def join_heads(array):
    return array.transpose(1, 0, 2).reshape(array.shape[1], array.shape[0] * array.shape[2])


def attend(queries, key_rows, value_rows, same, head_count):
    scale = 1.0 / math.sqrt(queries.shape[1] // head_count)
    q, k, v = (split_heads(a, head_count) for a in (queries, key_rows, value_rows))
    scores = jnp.einsum("hqd,hkd->hqk", q, k, preferred_element_type=f32) * scale
    scores = jnp.where(same[None], scores, masked_score)
    row_max = jnp.max(scores, axis=2, keepdims=True)
    weights = jnp.exp(scores - row_max)
    row_total = jnp.sum(weights, axis=2, keepdims=True)
    probs = (weights / row_total).astype(bf16)
    out = jnp.einsum("hqk,hkd->hqd", probs, v, preferred_element_type=f32)
    return join_heads(out).astype(bf16), row_max + jnp.log(row_total)


def attend_back(queries, key_rows, value_rows, same, head_count, logsum, grad_att, att):
    scale = 1.0 / math.sqrt(queries.shape[1] // head_count)
    q, k, v, g, o = (
        split_heads(a, head_count) for a in (queries, key_rows, value_rows, grad_att, att)
    )
    scores = jnp.einsum("hqd,hkd->hqk", q, k, preferred_element_type=f32) * scale
    scores = jnp.where(same[None], scores, masked_score)
    probs = jnp.exp(scores - logsum)
    delta = jnp.sum(g.astype(f32) * o.astype(f32), axis=2, keepdims=True)
    grad_probs = jnp.einsum("hqd,hkd->hqk", g, v, preferred_element_type=f32)
    grad_scores = (probs * (grad_probs - delta)).astype(bf16)
    grad_q = jnp.einsum("hqk,hkd->hqd", grad_scores, k, preferred_element_type=f32) * scale
    grad_k = jnp.einsum("hqk,hqd->hkd", grad_scores, q, preferred_element_type=f32) * scale
    grad_v = jnp.einsum("hqk,hqd->hkd", probs.astype(bf16), g, preferred_element_type=f32)
    return join_heads(grad_q), join_heads(grad_k), join_heads(grad_v)


def position_table(row_width):
    halfway = row_width // 2
    frequency = np.exp(np.arange(halfway, dtype=np.float64) * (-math.log(10000.0) / halfway))
    angles = np.arange(PATCHES, dtype=np.float64)[:, None] * frequency[None, :]
    return np.concatenate([np.sin(angles), np.cos(angles)], axis=1).astype(np.float32)


def reduce_pair(grad, core):
    images, rows, width = grad.shape
    both = grad.reshape(images // 2, 2, rows, width)
    arrived = swap(pick(both, 1 - core, 1))
    return (pick(both, core, 1).astype(f32) + arrived.astype(f32)).astype(bf16)


def reduce_rest(chunk, seq):
    chips, rows, width = chunk.shape
    high, low = seq // 2, seq % 2
    eighth = -(-rows // 8)
    chunk = jnp.pad(chunk, ((0, 0), (0, 8 * eighth - rows), (0, 0)))
    parts = chunk.reshape(chips, 2, 2, 2, eighth, width)

    def along_x(array):
        return permute(array, lambda s, i: (s ^ 1, i))

    def along_y(array):
        return permute(array, lambda s, i: (s ^ 2, i))

    def add(one, two):
        return (one.astype(f32) + two.astype(f32)).astype(bf16)

    one, two = parts[:, 0], parts[:, 1]
    one = add(pick(one, low, 2), along_x(pick(one, 1 - low, 2)))
    two = add(pick(two, high, 1), along_y(pick(two, 1 - high, 1)))
    one = add(pick(one, high, 1), along_y(pick(one, 1 - high, 1)))
    two = add(pick(two, low, 1), along_x(pick(two, 1 - low, 1)))
    mine = jnp.stack([one, two], axis=1)
    chip = lax.axis_index("img") // 2
    total = pick(mine, chip, 0).astype(f32)
    for step in range(1, chips):
        leaving = pick(mine, (chip + step) % chips, 0)
        arrived = permute(
            leaving,
            lambda s, i, step=step: (s, ((i // 2 + step) % chips) * 2 + (i & 1)),
        )
        total = total + arrived.astype(f32)
    own = total.astype(bf16)
    others = [permute(own, lambda s, i, step=step: (s ^ step, i)) for step in (1, 2, 3)]
    by_xor = jnp.stack([own] + others)
    ordered = jnp.stack([pick(by_xor, seq ^ place, 0) for place in range(4)], axis=1)
    return ordered.reshape(8 * eighth, width)[:rows].astype(f32)


def shards(
    enc_input,
    cotangent,
    enc_image,
    visible_rows,
    enc_norms,
    enc_qkv,
    enc_proj,
    enc_up,
    enc_down,
    embed,
    dec_vecs,
    dec_qkv,
    dec_proj,
    dec_up,
    dec_down,
):
    seq = lax.axis_index("seq")
    img = lax.axis_index("img")
    images = lax.axis_size("img")
    core = img % 2
    odd = seq % 2 == 1
    enc_width = enc_input.shape[3]
    dec_width = dec_vecs.shape[0]
    enc_half = 2 * enc_input.shape[2]
    dec_quarter = cotangent.shape[2]

    tables = jnp.stack([enc_image[0], visible_rows[0]])
    other_tables = swap(tables)
    tables = jnp.where(seq // 2 == core, tables, other_tables)
    tables = jnp.where(odd, tables[:, 1], tables[:, 0])
    halves = tables.reshape(2, 2, enc_half)
    halves = jnp.pad(halves, ((0, 0), (0, 0), (0, ENC_PAD - enc_half)), constant_values=-2)
    own = pick(halves, core, 1)
    ids = jnp.concatenate([own, pick(halves, 1 - core, 1)], axis=1)
    enc_same = own[0][:, None] == ids[0][None, :]

    inputs = jnp.concatenate(exchange_packs(enc_input[0], odd), axis=0)
    inputs = pad_rows(inputs, ENC_PAD).astype(f32)
    cot = jnp.concatenate(exchange_packs(cotangent[0], odd), axis=0)
    cot = jnp.concatenate(
        [
            pad_rows(lax.dynamic_slice_in_dim(cot, core * HALF, SMALL, 0), SMALL_PAD),
            pad_rows(lax.dynamic_slice_in_dim(cot, (1 - core) * SMALL, HALF, 0), BIG_PAD),
        ],
        axis=0,
    )

    enc_attn_in, enc_normed_one, enc_inverse_one = norm_forward(
        inputs, enc_norms[:, 0], enc_norms[:, 1]
    )
    enc_mixed = product(enc_attn_in, enc_qkv).astype(bf16)
    enc_other = swap(enc_mixed[:, enc_width:])
    enc_query = enc_mixed[:, :enc_width]
    enc_keys = jnp.concatenate([enc_mixed[:, enc_width : 2 * enc_width], enc_other[:, :enc_width]])
    enc_values = jnp.concatenate([enc_mixed[:, 2 * enc_width :], enc_other[:, enc_width:]])
    enc_att, enc_logsum = attend(enc_query, enc_keys, enc_values, enc_same, HE)
    enc_middle = inputs + product(enc_att, enc_proj)
    enc_mlp_in, enc_normed_two, enc_inverse_two = norm_forward(
        enc_middle, enc_norms[:, 2], enc_norms[:, 3]
    )
    enc_hidden = product(enc_mlp_in, enc_up)
    enc_active = exact_gelu(enc_hidden).astype(bf16)
    enc_out = enc_middle + product(enc_active, enc_down)
    enc_final, final_normed, final_inverse = norm_forward(enc_out, enc_norms[:, 4], enc_norms[:, 5])
    embedded = product(enc_final, embed).astype(bf16)
    every_embedded = jnp.concatenate([embedded, swap(embedded)], axis=0)

    small_index = jnp.arange(SMALL_PAD, dtype=jnp.int32)
    big_index = jnp.arange(BIG_PAD, dtype=jnp.int32)
    row_ids = jnp.concatenate(
        [
            jnp.where(small_index < SMALL, core * (SMALL + PATCHES) + small_index, -1),
            jnp.where(big_index < HALF, SMALL + core * HALF + big_index, -1),
        ]
    )
    chosen = row_ids[:, None] == ids[1][None, :]
    visible = jnp.any(chosen, axis=1)
    chosen = chosen.astype(bf16)
    table = jnp.asarray(position_table(dec_width))
    code = jnp.concatenate(
        [
            pad_rows(table[:SMALL], SMALL_PAD),
            pad_rows(lax.dynamic_slice_in_dim(table, core * HALF, HALF, 0), BIG_PAD),
        ]
    )
    dec_input = (
        jnp.where(visible[:, None], product(chosen, every_embedded), dec_vecs[None, :, 4]) + code
    )
    dec_attn_in, dec_normed_one, dec_inverse_one = norm_forward(
        dec_input, dec_vecs[:, 0], dec_vecs[:, 1]
    )
    dec_mixed = product(dec_attn_in, dec_qkv).astype(bf16)
    dec_other = swap(dec_mixed[SMALL_PAD:, dec_width:])
    dec_query, dec_key, dec_value = (
        dec_mixed[:, :dec_width],
        dec_mixed[:, dec_width : 2 * dec_width],
        dec_mixed[:, 2 * dec_width :],
    )
    small_same = jnp.broadcast_to((small_index < SMALL)[None, :], (SMALL_PAD, SMALL_PAD))
    big_valid = jnp.concatenate([big_index < HALF, big_index < HALF])
    big_same = jnp.broadcast_to(big_valid[None, :], (BIG_PAD, 2 * BIG_PAD))
    big_keys = jnp.concatenate([dec_key[SMALL_PAD:], dec_other[:, :dec_width]])
    big_values = jnp.concatenate([dec_value[SMALL_PAD:], dec_other[:, dec_width:]])
    small_items = (dec_query[:SMALL_PAD], dec_key[:SMALL_PAD], dec_value[:SMALL_PAD], small_same, HD)
    big_items = (dec_query[SMALL_PAD:], big_keys, big_values, big_same, HD)
    small_att, small_logsum = attend(*small_items)
    big_att, big_logsum = attend(*big_items)
    dec_att = jnp.concatenate([small_att, big_att])
    dec_middle = dec_input + product(dec_att, dec_proj)
    dec_mlp_in, dec_normed_two, dec_inverse_two = norm_forward(
        dec_middle, dec_vecs[:, 2], dec_vecs[:, 3]
    )
    dec_hidden = product(dec_mlp_in, dec_up)
    dec_active = exact_gelu(dec_hidden).astype(bf16)
    decoded = (dec_middle + product(dec_active, dec_down)).astype(bf16)

    def to_images(*grads):
        width = min(grad.shape[1] for grad in grads)
        pieces = []
        for grad in grads:
            low = grad.astype(bf16)
            for start in range(0, grad.shape[1], width):
                piece = low[:, start : start + width]
                pieces.append(piece.reshape(images, piece.shape[0] // images, width))
        return jnp.concatenate(pieces, axis=1)

    grad_dec_down = inner_rows(dec_active, cot)
    dec_grad_hidden = gelu_grad(dec_hidden, inner_cols(cot, dec_down)).astype(bf16)
    grad_dec_up = inner_rows(dec_mlp_in, dec_grad_hidden)
    grad_norm_in, dec_gain_two, dec_shift_two = norm_backward(
        inner_cols(dec_grad_hidden, dec_up), dec_normed_two, dec_inverse_two, dec_vecs[:, 2]
    )
    grad_dec_middle = cot.astype(f32) + grad_norm_in
    low_middle = grad_dec_middle.astype(bf16)
    dec_grad_att = inner_cols(low_middle, dec_proj).astype(bf16)
    grad_dec_proj = inner_rows(dec_att, low_middle)
    small_q, small_k, small_v = attend_back(
        *small_items, small_logsum, dec_grad_att[:SMALL_PAD], small_att
    )
    big_q, big_k, big_v = attend_back(*big_items, big_logsum, dec_grad_att[SMALL_PAD:], big_att)
    leaving = jnp.concatenate([big_k[BIG_PAD:], big_v[BIG_PAD:]], axis=1).astype(bf16)
    arrived = swap(leaving).astype(f32)
    big_k = big_k[:BIG_PAD] + arrived[:, :dec_width]
    big_v = big_v[:BIG_PAD] + arrived[:, dec_width:]
    dec_grad_mixed = jnp.concatenate(
        [
            jnp.concatenate([small_q, small_k, small_v], axis=1),
            jnp.concatenate([big_q, big_k, big_v], axis=1),
        ]
    ).astype(bf16)
    grad_dec_qkv = inner_rows(dec_attn_in, dec_grad_mixed)
    grad_norm_in, dec_gain_one, dec_shift_one = norm_backward(
        inner_cols(dec_grad_mixed, dec_qkv), dec_normed_one, dec_inverse_one, dec_vecs[:, 0]
    )
    grad_dec_input = grad_dec_middle + grad_norm_in
    grad_mask = jnp.sum(jnp.where(visible[:, None], 0.0, grad_dec_input), axis=0)
    grad_dec_vecs = jnp.stack(
        [dec_gain_one, dec_shift_one, dec_gain_two, dec_shift_two, grad_mask], axis=1
    )
    dec_chunk = to_images(grad_dec_down, grad_dec_up, grad_dec_proj, grad_dec_qkv)
    dec_share = reduce_rest(reduce_pair(dec_chunk, core), seq)

    spread = inner_rows(chosen, grad_dec_input.astype(bf16)).astype(bf16)
    grad_embedded = spread[:ENC_PAD] + swap(spread[ENC_PAD:])

    grad_embed = inner_rows(enc_final, grad_embedded)
    grad_enc_out, final_gain, final_shift = norm_backward(
        inner_cols(grad_embedded, embed), final_normed, final_inverse, enc_norms[:, 4]
    )
    low_out = grad_enc_out.astype(bf16)
    grad_enc_down = inner_rows(enc_active, low_out)
    enc_grad_hidden = gelu_grad(enc_hidden, inner_cols(low_out, enc_down)).astype(bf16)
    grad_enc_up = inner_rows(enc_mlp_in, enc_grad_hidden)
    grad_norm_in, enc_gain_two, enc_shift_two = norm_backward(
        inner_cols(enc_grad_hidden, enc_up), enc_normed_two, enc_inverse_two, enc_norms[:, 2]
    )
    grad_enc_middle = grad_enc_out + grad_norm_in
    embed_share = reduce_rest(reduce_pair(to_images(grad_embed), core), seq)
    mlp_share = reduce_rest(reduce_pair(to_images(grad_enc_down, grad_enc_up), core), seq)
    low_middle = grad_enc_middle.astype(bf16)
    enc_grad_att = inner_cols(low_middle, enc_proj).astype(bf16)
    grad_enc_proj = inner_rows(enc_att, low_middle)
    enc_q, enc_k, enc_v = attend_back(
        enc_query, enc_keys, enc_values, enc_same, HE, enc_logsum, enc_grad_att, enc_att
    )
    leaving = jnp.concatenate([enc_k[ENC_PAD:], enc_v[ENC_PAD:]], axis=1).astype(bf16)
    arrived = swap(leaving).astype(f32)
    enc_grad_mixed = jnp.concatenate(
        [enc_q, enc_k[:ENC_PAD] + arrived[:, :enc_width], enc_v[:ENC_PAD] + arrived[:, enc_width:]],
        axis=1,
    ).astype(bf16)
    grad_enc_qkv = inner_rows(enc_attn_in, enc_grad_mixed)
    grad_norm_in, enc_gain_one, enc_shift_one = norm_backward(
        inner_cols(enc_grad_mixed, enc_qkv), enc_normed_one, enc_inverse_one, enc_norms[:, 0]
    )
    grad_input = grad_enc_middle + grad_norm_in
    grad_enc_norms = jnp.stack(
        [enc_gain_one, enc_shift_one, enc_gain_two, enc_shift_two, final_gain, final_shift], axis=1
    )
    att_share = reduce_rest(reduce_pair(to_images(grad_enc_proj, grad_enc_qkv), core), seq)

    vectors = lax.psum(
        jnp.concatenate([grad_enc_norms.reshape(-1), grad_dec_vecs.reshape(-1)]), ("seq", "img")
    )
    norm_size = grad_enc_norms.size
    enc_norm_share = pick(vectors[:norm_size].reshape(images, -1, grad_enc_norms.shape[1]), img, 0)
    dec_vec_share = pick(vectors[norm_size:].reshape(images, -1, grad_dec_vecs.shape[1]), img, 0)

    def from_images(share, *shapes):
        width = share.shape[1]
        results, start = [], 0
        for rows, columns in shapes:
            count = rows // images
            pieces = []
            for _ in range(columns // width):
                pieces.append(share[start : start + count])
                start += count
            results.append(pieces[0] if len(pieces) == 1 else jnp.concatenate(pieces, axis=1))
        return results

    dec_down_share, dec_up_share, dec_proj_share, dec_qkv_share = from_images(
        dec_share, dec_down.shape, dec_up.shape, dec_proj.shape, dec_qkv.shape
    )
    enc_down_share, enc_up_share = from_images(mlp_share, enc_down.shape, enc_up.shape)
    enc_proj_share, enc_qkv_share = from_images(att_share, enc_proj.shape, enc_qkv.shape)

    start = jnp.concatenate([decoded[:SMALL], decoded[SMALL_PAD : SMALL_PAD + HALF]])
    end = jnp.concatenate([decoded[SMALL_PAD : SMALL_PAD + HALF], decoded[:SMALL]])
    natural = jnp.where(core == 0, start, end)
    decoded = jnp.stack(exchange_packs(natural.reshape(2, dec_quarter, dec_width), odd))[None]
    grad_input = jnp.stack(
        exchange_packs(grad_input[:enc_half].reshape(2, enc_half // 2, enc_width), odd)
    )[None]
    return (
        decoded,
        grad_input,
        enc_norm_share,
        enc_qkv_share,
        enc_proj_share,
        enc_up_share,
        enc_down_share,
        embed_share,
        dec_vec_share,
        dec_qkv_share,
        dec_proj_share,
        dec_up_share,
        dec_down_share,
    )


def solution(mesh):
    rows = P("img", None, "seq", None)
    tables = P("img", None, None)
    shares = P("img", None)
    return jax.shard_map(
        shards,
        mesh=mesh,
        in_specs=(rows, rows, tables, tables) + (P(),) * 11,
        out_specs=(rows, rows) + (shares,) * 11,
        check_vma=False,
    )
```

```python
import math

import jax
import jax.numpy as jnp
import numpy as np
from jax import lax
from jax.experimental import pallas as pl
from jax.experimental.pallas import tpu as pltpu
from jax.sharding import PartitionSpec as P

HE = 12
HD = 16
PATCHES = 784
SMALL = PATCHES // 4
HALF = PATCHES // 2
SMALL_PAD = 208
BIG_PAD = 400
DEC_PAD = SMALL_PAD + BIG_PAD
ENC_SEG = 80
ENC_PAD = 2 * ENC_SEG

eps_norm = 1e-06
masked_score = -1e30
bf16 = jnp.bfloat16
f32 = jnp.float32


def product(left_side, right_side):
    return jnp.dot(left_side, right_side, preferred_element_type=f32)


def inner_rows(left_side, right_side):
    return lax.dot_general(
        left_side, right_side, (((0,), (0,)), ((), ())), preferred_element_type=f32
    )


def inner_cols(left_side, right_side):
    return lax.dot_general(
        left_side, right_side, (((1,), (1,)), ((), ())), preferred_element_type=f32
    )


def norm_parts(values):
    centered = values - jnp.mean(values, axis=-1, keepdims=True)
    inverse = lax.rsqrt(jnp.mean(centered * centered, axis=-1, keepdims=True) + eps_norm)
    return centered * inverse, inverse


def norm_backward(grad_out, normed, inverse, norm_gain):
    scaled = grad_out * norm_gain
    grad_values = inverse * (
        scaled
        - jnp.mean(scaled, axis=-1, keepdims=True)
        - normed * jnp.mean(scaled * normed, axis=-1, keepdims=True)
    )
    return (
        grad_values,
        jnp.sum(grad_out * normed, axis=0, keepdims=True),
        jnp.sum(grad_out, axis=0, keepdims=True),
    )


def gelu_parts(hidden):
    below = 0.5 + 0.5 * lax.erf(hidden * math.sqrt(0.5))
    density = jnp.exp(hidden * hidden * -0.5) * (1.0 / math.sqrt(2.0 * math.pi))
    return hidden * below, below + hidden * density


def call(kernel, scalars, outs, args, megabytes):
    vmem = pl.BlockSpec(memory_space=pltpu.VMEM)
    smem = pl.BlockSpec(memory_space=pltpu.SMEM)
    return pl.pallas_call(
        kernel,
        out_shape=[jax.ShapeDtypeStruct(shape, kind) for shape, kind in outs],
        in_specs=[smem] * scalars + [vmem] * (len(args) - scalars),
        out_specs=[vmem] * len(outs),
        compiler_params=pltpu.CompilerParams(vmem_limit_bytes=megabytes << 20),
    )(*args)


def lane_masks(head_size, kind):
    lanes = lax.broadcasted_iota(jnp.int32, (1, 128), 1) // head_size
    return [(lanes == head).astype(f32).astype(kind) for head in range(128 // head_size)]


def softmax_rows(scores, scale):
    row_max = jnp.max(scores, axis=1, keepdims=True)
    weights = jnp.exp2((scores - row_max) * (scale * math.log2(math.e)))
    return (weights * (1.0 / jnp.sum(weights, axis=1, keepdims=True))).astype(bf16)


def head_back(probs, grads, values, delta):
    grad_probs = inner_cols(grads, values)
    return (probs.astype(f32) * (grad_probs - delta)).astype(bf16)


def enc_pre_kernel(x, vecs, w_qkv, query, key_value):
    normed, _ = norm_parts(x[...].astype(f32))
    attn_in = (normed * vecs[0:1] + vecs[1:2]).astype(bf16)
    mixed = product(attn_in, w_qkv[...]).astype(bf16)
    width = query.shape[1]
    query[...] = mixed[:, :width]
    key_value[...] = mixed[:, width:]


def enc_main_kernel(
    x, query, own_kv, other_kv, own_ids, all_ids, vecs, w_proj, w_up, w_down, w_embed,
    embedded, att, probs, middle, active, slope, out
):
    width = query.shape[1]
    head_size = width // HE
    bias = jnp.where(own_ids[...] == all_ids[...], 0.0, masked_score)
    masks = lane_masks(head_size, bf16)
    for pair in range(width // 128):
        cols = slice(128 * pair, 128 * pair + 128)
        value_cols = slice(width + 128 * pair, width + 128 * pair + 128)
        keys = jnp.concatenate([own_kv[:, cols], other_kv[:, cols]], axis=0)
        values = jnp.concatenate([own_kv[:, value_cols], other_kv[:, value_cols]], axis=0)
        total = jnp.zeros((query.shape[0], 128), f32)
        for head, mask in enumerate(masks):
            scores = inner_cols(query[:, cols] * mask, keys) + bias
            chances = softmax_rows(scores, 1.0 / math.sqrt(head_size))
            probs[len(masks) * pair + head] = chances
            total += product(chances, values * mask)
        att[:, cols] = total.astype(bf16)
    mid = x[...].astype(f32) + product(att[...], w_proj[...])
    middle[...] = mid
    normed, _ = norm_parts(mid)
    mlp_in = (normed * vecs[2:3] + vecs[3:4]).astype(bf16)
    result, steepness = gelu_parts(product(mlp_in, w_up[...]))
    active[...] = result.astype(bf16)
    slope[...] = steepness.astype(bf16)
    last = mid + product(active[...], w_down[...])
    out[...] = last
    normed, _ = norm_parts(last)
    final = (normed * vecs[4:5] + vecs[5:6]).astype(bf16)
    embedded[...] = product(final, w_embed[...]).astype(bf16)


def chosen_rows(core, visible_rows):
    index = lax.broadcasted_iota(jnp.int32, (DEC_PAD, 1), 0)
    small = index + core * (SMALL + PATCHES)
    big = index + (SMALL - SMALL_PAD) + core * HALF
    row = jnp.where(index < SMALL, small, -1)
    row = jnp.where((index >= SMALL_PAD) & (index < SMALL_PAD + HALF), big, row)
    return (row == visible_rows).astype(f32)


def dec_pre_kernel(core, own, other, rows, code, vecs, w_qkv, dec_input, mixed, big_kv):
    chosen = chosen_rows(core[0], rows[...])
    seen = jnp.sum(chosen, axis=1, keepdims=True)
    tokens = jnp.concatenate([own[...], other[...]], axis=0)
    picked = product(chosen.astype(bf16), tokens)
    values = jnp.where(seen > 0.0, picked, vecs[4:5]) + code[...]
    dec_input[...] = values
    normed, _ = norm_parts(values)
    attn_in = (normed * vecs[0:1] + vecs[1:2]).astype(bf16)
    result = product(attn_in, w_qkv[...]).astype(bf16)
    mixed[...] = result
    big_kv[...] = result[SMALL_PAD:, values.shape[1] :]


def big_bias():
    column = lax.broadcasted_iota(jnp.int32, (1, 2 * BIG_PAD), 1)
    place = jnp.where(column >= BIG_PAD, column - BIG_PAD, column)
    return jnp.where(place < HALF, 0.0, masked_score)


def small_bias():
    column = lax.broadcasted_iota(jnp.int32, (1, SMALL_PAD), 1)
    return jnp.where(column < SMALL, 0.0, masked_score)


def dec_att_kernel(query, key, value, other_key, other_value, att, big_probs, small_probs):
    head_size = query.shape[1] * 4 // HD
    scale = 1.0 / math.sqrt(head_size)
    keys = jnp.concatenate([key[SMALL_PAD:], other_key[...]], axis=0)
    values = jnp.concatenate([value[SMALL_PAD:], other_value[...]], axis=0)
    total = jnp.zeros((BIG_PAD, 128), f32)
    small_total = jnp.zeros((SMALL_PAD, 128), f32)
    for head, mask in enumerate(lane_masks(head_size, bf16)):
        scores = inner_cols(query[SMALL_PAD:] * mask, keys) + big_bias()
        chances = softmax_rows(scores, scale)
        big_probs[head] = chances
        total += product(chances, values * mask)
        scores = inner_cols(query[:SMALL_PAD] * mask, key[:SMALL_PAD]) + small_bias()
        chances = softmax_rows(scores, scale)
        small_probs[head] = chances
        small_total += product(chances, value[:SMALL_PAD] * mask)
    att[:SMALL_PAD] = small_total.astype(bf16)
    att[SMALL_PAD:] = total.astype(bf16)


def dec_mid_kernel(
    dec_input, att, cot, vecs, w_proj, w_up, w_down,
    decoded, grad_middle, grad_att, grad_proj, grad_up, grad_down, vectors
):
    middle = dec_input[...] + product(att[...], w_proj[...])
    normed, inverse = norm_parts(middle)
    mlp_in = (normed * vecs[2:3] + vecs[3:4]).astype(bf16)
    result = middle
    grad_norm = jnp.zeros_like(middle)
    step = 512
    for start in range(0, w_up.shape[1], step):
        cols = slice(start, start + step)
        active, slope = gelu_parts(product(mlp_in, w_up[:, cols]))
        active = active.astype(bf16)
        result += product(active, w_down[cols])
        grad_down[cols] = inner_rows(active, cot[...]).astype(bf16)
        grad_hidden = (slope * inner_cols(cot[...], w_down[cols])).astype(bf16)
        grad_up[:, cols] = inner_rows(mlp_in, grad_hidden).astype(bf16)
        grad_norm += inner_cols(grad_hidden, w_up[:, cols])
    decoded[...] = result.astype(bf16)
    grad_values, gain, shift = norm_backward(grad_norm, normed, inverse, vecs[2:3])
    vectors[0:1] = gain
    vectors[1:2] = shift
    back = cot[...].astype(f32) + grad_values
    grad_middle[...] = back
    low = back.astype(bf16)
    grad_att[...] = inner_cols(low, w_proj[...]).astype(bf16)
    grad_proj[...] = inner_rows(att[...], low).astype(bf16)


def dec_att_back_kernel(
    query, key, value, other_key, other_value, grads, att, big_probs, small_probs,
    grad_query, grad_key, grad_value, leaving_key, leaving_value
):
    head_size = query.shape[1] * 4 // HD
    scale = 1.0 / math.sqrt(head_size)
    keys = jnp.concatenate([key[SMALL_PAD:], other_key[...]], axis=0)
    values = jnp.concatenate([value[SMALL_PAD:], other_value[...]], axis=0)
    overlap = grads[...].astype(f32) * att[...].astype(f32)
    big_q = jnp.zeros((BIG_PAD, 128), f32)
    big_k = jnp.zeros((2 * BIG_PAD, 128), f32)
    big_v = jnp.zeros((2 * BIG_PAD, 128), f32)
    small_q = jnp.zeros((SMALL_PAD, 128), f32)
    small_k = jnp.zeros((SMALL_PAD, 128), f32)
    small_v = jnp.zeros((SMALL_PAD, 128), f32)
    masks = lane_masks(head_size, f32)
    for head, mask in enumerate(lane_masks(head_size, bf16)):
        delta = jnp.sum(overlap * masks[head], axis=1, keepdims=True)
        one_query, one_grad = query[...] * mask, grads[...] * mask
        chances = big_probs[head]
        back = head_back(chances, one_grad[SMALL_PAD:], values, delta[SMALL_PAD:])
        big_q += product(back, keys * mask)
        big_k += inner_rows(back, one_query[SMALL_PAD:])
        big_v += inner_rows(chances, one_grad[SMALL_PAD:])
        chances = small_probs[head]
        back = head_back(chances, one_grad[:SMALL_PAD], value[:SMALL_PAD], delta[:SMALL_PAD])
        small_q += product(back, key[:SMALL_PAD] * mask)
        small_k += inner_rows(back, one_query[:SMALL_PAD])
        small_v += inner_rows(chances, one_grad[:SMALL_PAD])
    grad_query[:SMALL_PAD] = (small_q * scale).astype(bf16)
    grad_query[SMALL_PAD:] = (big_q * scale).astype(bf16)
    grad_key[:SMALL_PAD] = small_k * scale
    grad_key[SMALL_PAD:] = big_k[:BIG_PAD] * scale
    grad_value[:SMALL_PAD] = small_v
    grad_value[SMALL_PAD:] = big_v[:BIG_PAD]
    leaving_key[...] = (big_k[BIG_PAD:] * scale).astype(bf16)
    leaving_value[...] = big_v[BIG_PAD:].astype(bf16)


def dec_post_kernel(
    core, dec_input, grad_middle, grad_query, grad_key, grad_value, arrived_key, arrived_value,
    rows, vecs, w_qkv, own_spread, other_spread, grad_qkv, vectors
):
    width = dec_input.shape[1]
    normed, inverse = norm_parts(dec_input[...])
    attn_in = (normed * vecs[0:1] + vecs[1:2]).astype(bf16)
    key = jnp.concatenate(
        [grad_key[:SMALL_PAD], grad_key[SMALL_PAD:] + arrived_key[...].astype(f32)], axis=0
    ).astype(bf16)
    value = jnp.concatenate(
        [grad_value[:SMALL_PAD], grad_value[SMALL_PAD:] + arrived_value[...].astype(f32)], axis=0
    ).astype(bf16)
    mixed = jnp.concatenate([grad_query[...], key, value], axis=1)
    grad_values, gain, shift = norm_backward(
        inner_cols(mixed, w_qkv[...]), normed, inverse, vecs[0:1]
    )
    back = grad_middle[...] + grad_values
    chosen = chosen_rows(core[0], rows[...])
    seen = jnp.sum(chosen, axis=1, keepdims=True)
    spread = inner_rows(chosen.astype(bf16), back.astype(bf16)).astype(bf16)
    own_spread[...] = spread[:ENC_PAD]
    other_spread[...] = spread[ENC_PAD:]
    vectors[0:1] = gain
    vectors[1:2] = shift
    vectors[2:3] = jnp.sum(jnp.where(seen > 0.0, 0.0, back), axis=0, keepdims=True)
    for start in range(0, 3 * width, width):
        cols = slice(start, start + width)
        grad_qkv[:, cols] = inner_rows(attn_in, mixed[:, cols]).astype(bf16)


def enc_back_kernel(
    own_spread, arrived, out, middle, active, slope, att, probs, query, own_kv, other_kv,
    vecs, w_embed, w_down, w_up, w_proj,
    grad_embed, grad_down, grad_up, grad_proj, grad_middle, grad_query, grad_kv, leaving, vectors
):
    width = query.shape[1]
    head_size = width // HE
    scale = 1.0 / math.sqrt(head_size)
    grad_embedded = own_spread[...] + arrived[...]
    normed, inverse = norm_parts(out[...])
    final = (normed * vecs[4:5] + vecs[5:6]).astype(bf16)
    grad_out, gain, shift = norm_backward(
        inner_cols(grad_embedded, w_embed[...]), normed, inverse, vecs[4:5]
    )
    vectors[2:3] = gain
    vectors[3:4] = shift
    low = grad_out.astype(bf16)
    grad_hidden = (slope[...].astype(f32) * inner_cols(low, w_down[...])).astype(bf16)
    normed, inverse = norm_parts(middle[...])
    mlp_in = (normed * vecs[2:3] + vecs[3:4]).astype(bf16)
    grad_values, gain, shift = norm_backward(
        inner_cols(grad_hidden, w_up[...]), normed, inverse, vecs[2:3]
    )
    vectors[0:1] = gain
    vectors[1:2] = shift
    back = grad_out + grad_values
    grad_middle[...] = back
    low_middle = back.astype(bf16)
    grads = inner_cols(low_middle, w_proj[...]).astype(bf16)
    grad_embed[...] = inner_rows(final, grad_embedded).astype(bf16)
    grad_down[...] = inner_rows(active[...], low).astype(bf16)
    grad_up[...] = inner_rows(mlp_in, grad_hidden).astype(bf16)
    grad_proj[...] = inner_rows(att[...], low_middle).astype(bf16)
    overlap = grads.astype(f32) * att[...].astype(f32)
    masks = lane_masks(head_size, bf16)
    wide_masks = lane_masks(head_size, f32)
    rows = query.shape[0]
    for pair in range(width // 128):
        cols = slice(128 * pair, 128 * pair + 128)
        value_cols = slice(width + 128 * pair, width + 128 * pair + 128)
        keys = jnp.concatenate([own_kv[:, cols], other_kv[:, cols]], axis=0)
        values = jnp.concatenate([own_kv[:, value_cols], other_kv[:, value_cols]], axis=0)
        total_q = jnp.zeros((rows, 128), f32)
        total_k = jnp.zeros((2 * rows, 128), f32)
        total_v = jnp.zeros((2 * rows, 128), f32)
        for head, mask in enumerate(masks):
            delta = jnp.sum(overlap[:, cols] * wide_masks[head], axis=1, keepdims=True)
            one_grad = grads[:, cols] * mask
            chances = probs[len(masks) * pair + head]
            one_back = head_back(chances, one_grad, values, delta)
            total_q += product(one_back, keys * mask)
            total_k += inner_rows(one_back, query[:, cols] * mask)
            total_v += inner_rows(chances, one_grad)
        grad_query[:, cols] = (total_q * scale).astype(bf16)
        grad_kv[:, cols] = total_k[:rows] * scale
        grad_kv[:, value_cols] = total_v[:rows]
        leaving[:, cols] = (total_k[rows:] * scale).astype(bf16)
        leaving[:, value_cols] = total_v[rows:].astype(bf16)


def enc_post_kernel(
    x, grad_middle, grad_query, grad_kv, arrived, vecs, w_qkv, grad_input, grad_qkv, vectors
):
    normed, inverse = norm_parts(x[...].astype(f32))
    attn_in = (normed * vecs[0:1] + vecs[1:2]).astype(bf16)
    key_value = (grad_kv[...] + arrived[...].astype(f32)).astype(bf16)
    mixed = jnp.concatenate([grad_query[...], key_value], axis=1)
    grad_values, gain, shift = norm_backward(
        inner_cols(mixed, w_qkv[...]), normed, inverse, vecs[0:1]
    )
    grad_input[...] = grad_middle[...] + grad_values
    vectors[0:1] = gain
    vectors[1:2] = shift
    grad_qkv[...] = inner_rows(attn_in, mixed).astype(bf16)


def permute(array, where_to):
    seq_count = lax.axis_size("seq")
    img_count = lax.axis_size("img")
    pairs = []
    for seq in range(seq_count):
        for img in range(img_count):
            seq_to, img_to = where_to(seq, img)
            pairs.append((seq * img_count + img, seq_to * img_count + img_to))
    return lax.ppermute(array, ("seq", "img"), pairs)


def swap(array):
    return permute(array, lambda seq, img: (seq, img ^ 1))


def pack_move(turn):
    def where_to(seq, img):
        return (2 * (img & 1) + (turn ^ (seq & 1)), (img & ~1) | (seq >> 1))

    return where_to


def exchange_packs(blocks, odd):
    rounds = [
        permute(jnp.where(odd, blocks[1 - turn], blocks[turn]), pack_move(turn)) for turn in (0, 1)
    ]
    return (jnp.where(odd, rounds[1], rounds[0]), jnp.where(odd, rounds[0], rounds[1]))


def pick(array, index, axis):
    return lax.dynamic_index_in_dim(array, index, axis, keepdims=False)


def pad_rows(array, rows):
    return jnp.pad(array, ((0, rows - array.shape[0]),) + ((0, 0),) * (array.ndim - 1))


def position_table(row_width):
    halfway = row_width // 2
    frequency = np.exp(np.arange(halfway, dtype=np.float64) * (-math.log(10000.0) / halfway))
    angles = np.arange(PATCHES, dtype=np.float64)[:, None] * frequency[None, :]
    return np.concatenate([np.sin(angles), np.cos(angles)], axis=1).astype(np.float32)


def reduce_pair(grad, core):
    images, rows, width = grad.shape
    both = grad.reshape(images // 2, 2, rows, width)
    arrived = swap(pick(both, 1 - core, 1))
    return (pick(both, core, 1).astype(f32) + arrived.astype(f32)).astype(bf16)


def reduce_rest(chunk, seq):
    chips, rows, width = chunk.shape
    high, low = seq // 2, seq % 2
    eighth = -(-rows // 8)
    chunk = jnp.pad(chunk, ((0, 0), (0, 8 * eighth - rows), (0, 0)))
    parts = chunk.reshape(chips, 2, 2, 2, eighth, width)

    def along_x(array):
        return permute(array, lambda s, i: (s ^ 1, i))

    def along_y(array):
        return permute(array, lambda s, i: (s ^ 2, i))

    def add(one, two):
        return (one.astype(f32) + two.astype(f32)).astype(bf16)

    one, two = parts[:, 0], parts[:, 1]
    one = add(pick(one, low, 2), along_x(pick(one, 1 - low, 2)))
    two = add(pick(two, high, 1), along_y(pick(two, 1 - high, 1)))
    one = add(pick(one, high, 1), along_y(pick(one, 1 - high, 1)))
    two = add(pick(two, low, 1), along_x(pick(two, 1 - low, 1)))
    mine = jnp.stack([one, two], axis=1)
    chip = lax.axis_index("img") // 2
    total = pick(mine, chip, 0).astype(f32)
    for step in range(1, chips):
        leaving = pick(mine, (chip + step) % chips, 0)
        arrived = permute(
            leaving,
            lambda s, i, step=step: (s, ((i // 2 + step) % chips) * 2 + (i & 1)),
        )
        total = total + arrived.astype(f32)
    own = total.astype(bf16)
    others = [permute(own, lambda s, i, step=step: (s ^ step, i)) for step in (1, 2, 3)]
    by_xor = jnp.stack([own] + others)
    ordered = jnp.stack([pick(by_xor, seq ^ place, 0) for place in range(4)], axis=1)
    return ordered.reshape(8 * eighth, width)[:rows].astype(f32)


def shards(
    enc_input,
    cotangent,
    enc_image,
    visible_rows,
    enc_norms,
    enc_qkv,
    enc_proj,
    enc_up,
    enc_down,
    embed,
    dec_vecs,
    dec_qkv,
    dec_proj,
    dec_up,
    dec_down,
):
    seq = lax.axis_index("seq")
    img = lax.axis_index("img")
    images = lax.axis_size("img")
    core = img % 2
    odd = seq % 2 == 1
    enc_width = enc_input.shape[3]
    dec_width = dec_vecs.shape[0]
    enc_half = 2 * enc_input.shape[2]
    dec_quarter = cotangent.shape[2]

    enc_vecs = jnp.pad(enc_norms.T, ((0, 2), (0, 0)))
    dec_rows_vecs = jnp.pad(dec_vecs.T, ((0, 3), (0, 0)))
    tables = jnp.stack([enc_image[0], visible_rows[0]])
    other_tables = swap(tables)
    tables = jnp.where(seq // 2 == core, tables, other_tables)
    tables = jnp.where(odd, tables[:, 1], tables[:, 0])
    segments = tables.reshape(2, 2, 2, enc_half // 2)
    segments = jnp.pad(
        segments, ((0, 0),) * 3 + ((0, ENC_SEG - enc_half // 2),), constant_values=-2
    )
    halves = segments.reshape(2, 2, ENC_PAD)
    own = pick(halves, core, 1)
    ids = jnp.concatenate([own, pick(halves, 1 - core, 1)], axis=1)
    row_ids = ids[1:2]
    core_arg = core.reshape(1)

    blocks = jnp.pad(enc_input[0], ((0, 0), (0, ENC_SEG - enc_half // 2), (0, 0)))
    x = jnp.concatenate(exchange_packs(blocks, odd), axis=0)
    cot = jnp.concatenate(exchange_packs(cotangent[0], odd), axis=0)
    cot = jnp.concatenate(
        [
            pad_rows(lax.dynamic_slice_in_dim(cot, core * HALF, SMALL, 0), SMALL_PAD),
            pad_rows(lax.dynamic_slice_in_dim(cot, (1 - core) * SMALL, HALF, 0), BIG_PAD),
        ],
        axis=0,
    )
    enc_hidden_width = enc_up.shape[1]

    enc_query, enc_kv = call(
        enc_pre_kernel,
        0,
        [((ENC_PAD, enc_width), bf16), ((ENC_PAD, 2 * enc_width), bf16)],
        (x, enc_vecs, enc_qkv),
        40,
    )
    enc_other = swap(enc_kv)
    embedded, enc_att, enc_probs, enc_middle, enc_active, enc_slope, enc_out = call(
        enc_main_kernel,
        0,
        [
            ((ENC_PAD, dec_width), bf16),
            ((ENC_PAD, enc_width), bf16),
            ((HE, ENC_PAD, 2 * ENC_PAD), bf16),
            ((ENC_PAD, enc_width), f32),
            ((ENC_PAD, enc_hidden_width), bf16),
            ((ENC_PAD, enc_hidden_width), bf16),
            ((ENC_PAD, enc_width), f32),
        ],
        (
            x, enc_query, enc_kv, enc_other, own[0][:, None], ids[0:1], enc_vecs,
            enc_proj, enc_up, enc_down, embed,
        ),
        48,
    )

    table = position_table(dec_width)
    codes = np.zeros((2, DEC_PAD, dec_width), np.float32)
    for which in range(2):
        codes[which, :SMALL] = table[:SMALL]
        codes[which, SMALL_PAD : SMALL_PAD + HALF] = table[which * HALF : (which + 1) * HALF]
    code = pick(jnp.asarray(codes), core, 0)
    dec_input, dec_mixed, big_kv = call(
        dec_pre_kernel,
        1,
        [
            ((DEC_PAD, dec_width), f32),
            ((DEC_PAD, 3 * dec_width), bf16),
            ((BIG_PAD, 2 * dec_width), bf16),
        ],
        (core_arg, embedded, swap(embedded), row_ids, code, dec_rows_vecs, dec_qkv),
        40,
    )
    other_kv = swap(big_kv)
    groups = dec_width // 128

    def columns(rows, offset=0):
        return pl.BlockSpec((rows, 128), lambda group: (0, offset + group))

    def heads(rows, cols):
        return pl.BlockSpec((HD // groups, rows, cols), lambda group: (group, 0, 0))

    qkv_specs = [
        columns(DEC_PAD),
        columns(DEC_PAD, groups),
        columns(DEC_PAD, 2 * groups),
        columns(BIG_PAD),
        columns(BIG_PAD, groups),
    ]
    qkv_args = (dec_mixed, dec_mixed, dec_mixed, other_kv, other_kv)
    prob_specs = [heads(BIG_PAD, 2 * BIG_PAD), heads(SMALL_PAD, SMALL_PAD)]
    dec_att, big_probs, small_probs = pl.pallas_call(
        dec_att_kernel,
        grid=(groups,),
        in_specs=qkv_specs,
        out_specs=[columns(DEC_PAD)] + prob_specs,
        out_shape=[
            jax.ShapeDtypeStruct((DEC_PAD, dec_width), bf16),
            jax.ShapeDtypeStruct((HD, BIG_PAD, 2 * BIG_PAD), bf16),
            jax.ShapeDtypeStruct((HD, SMALL_PAD, SMALL_PAD), bf16),
        ],
        compiler_params=pltpu.CompilerParams(vmem_limit_bytes=48 << 20),
    )(*qkv_args)
    decoded, grad_dec_middle, dec_grad_att, grad_dec_proj, grad_dec_up, grad_dec_down, vectors_two = call(
        dec_mid_kernel,
        0,
        [
            ((DEC_PAD, dec_width), bf16),
            ((DEC_PAD, dec_width), f32),
            ((DEC_PAD, dec_width), bf16),
            (dec_proj.shape, bf16),
            (dec_up.shape, bf16),
            (dec_down.shape, bf16),
            ((2, dec_width), f32),
        ],
        (dec_input, dec_att, cot, dec_rows_vecs, dec_proj, dec_up, dec_down),
        48,
    )
    grad_specs = [columns(DEC_PAD)] * 3 + [columns(BIG_PAD)] * 2
    grad_query, grad_key, grad_value, leaving_key, leaving_value = pl.pallas_call(
        dec_att_back_kernel,
        grid=(groups,),
        in_specs=qkv_specs + [columns(DEC_PAD)] * 2 + prob_specs,
        out_specs=grad_specs,
        out_shape=[
            jax.ShapeDtypeStruct((DEC_PAD, dec_width), bf16),
            jax.ShapeDtypeStruct((DEC_PAD, dec_width), f32),
            jax.ShapeDtypeStruct((DEC_PAD, dec_width), f32),
            jax.ShapeDtypeStruct((BIG_PAD, dec_width), bf16),
            jax.ShapeDtypeStruct((BIG_PAD, dec_width), bf16),
        ],
        compiler_params=pltpu.CompilerParams(vmem_limit_bytes=48 << 20),
    )(*qkv_args, dec_grad_att, dec_att, big_probs, small_probs)
    own_spread, other_spread, grad_dec_qkv, vectors_one = call(
        dec_post_kernel,
        1,
        [
            ((ENC_PAD, dec_width), bf16),
            ((ENC_PAD, dec_width), bf16),
            (dec_qkv.shape, bf16),
            ((3, dec_width), f32),
        ],
        (
            core_arg, dec_input, grad_dec_middle, grad_query, grad_key, grad_value,
            swap(leaving_key), swap(leaving_value), row_ids, dec_rows_vecs, dec_qkv,
        ),
        48,
    )
    grad_dec_vecs = jnp.concatenate([vectors_one[:2], vectors_two, vectors_one[2:]]).T
    (
        grad_embed, grad_enc_down, grad_enc_up, grad_enc_proj,
        grad_enc_middle, enc_grad_query, enc_grad_kv, enc_leaving, enc_vectors_two,
    ) = call(
        enc_back_kernel,
        0,
        [
            (embed.shape, bf16),
            (enc_down.shape, bf16),
            (enc_up.shape, bf16),
            (enc_proj.shape, bf16),
            ((ENC_PAD, enc_width), f32),
            ((ENC_PAD, enc_width), bf16),
            ((ENC_PAD, 2 * enc_width), f32),
            ((ENC_PAD, 2 * enc_width), bf16),
            ((4, enc_width), f32),
        ],
        (
            own_spread, swap(other_spread), enc_out, enc_middle, enc_active, enc_slope, enc_att,
            enc_probs, enc_query, enc_kv, enc_other, enc_vecs, embed, enc_down, enc_up, enc_proj,
        ),
        56,
    )
    grad_input, grad_enc_qkv, enc_vectors_one = call(
        enc_post_kernel,
        0,
        [((ENC_PAD, enc_width), f32), (enc_qkv.shape, bf16), ((2, enc_width), f32)],
        (x, grad_enc_middle, enc_grad_query, enc_grad_kv, swap(enc_leaving), enc_vecs, enc_qkv),
        48,
    )
    grad_enc_norms = jnp.concatenate([enc_vectors_one, enc_vectors_two]).T

    def to_images(*grads):
        width = min(grad.shape[1] for grad in grads)
        pieces = []
        for grad in grads:
            low = grad.astype(bf16)
            for start in range(0, grad.shape[1], width):
                piece = low[:, start : start + width]
                pieces.append(piece.reshape(images, piece.shape[0] // images, width))
        return jnp.concatenate(pieces, axis=1)

    dec_chunk = to_images(grad_dec_down, grad_dec_up, grad_dec_proj, grad_dec_qkv)
    dec_share = reduce_rest(reduce_pair(dec_chunk, core), seq)
    embed_share = reduce_rest(reduce_pair(to_images(grad_embed), core), seq)
    mlp_share = reduce_rest(reduce_pair(to_images(grad_enc_down, grad_enc_up), core), seq)
    att_share = reduce_rest(reduce_pair(to_images(grad_enc_proj, grad_enc_qkv), core), seq)

    vectors = lax.psum(
        jnp.concatenate([grad_enc_norms.reshape(-1), grad_dec_vecs.reshape(-1)]), ("seq", "img")
    )
    norm_size = grad_enc_norms.size
    enc_norm_share = pick(vectors[:norm_size].reshape(images, -1, grad_enc_norms.shape[1]), img, 0)
    dec_vec_share = pick(vectors[norm_size:].reshape(images, -1, grad_dec_vecs.shape[1]), img, 0)

    def from_images(share, *shapes):
        width = share.shape[1]
        results, start = [], 0
        for rows, columns in shapes:
            count = rows // images
            pieces = []
            for _ in range(columns // width):
                pieces.append(share[start : start + count])
                start += count
            results.append(pieces[0] if len(pieces) == 1 else jnp.concatenate(pieces, axis=1))
        return results

    dec_down_share, dec_up_share, dec_proj_share, dec_qkv_share = from_images(
        dec_share, dec_down.shape, dec_up.shape, dec_proj.shape, dec_qkv.shape
    )
    enc_down_share, enc_up_share = from_images(mlp_share, enc_down.shape, enc_up.shape)
    enc_proj_share, enc_qkv_share = from_images(att_share, enc_proj.shape, enc_qkv.shape)

    start = jnp.concatenate([decoded[:SMALL], decoded[SMALL_PAD : SMALL_PAD + HALF]])
    end = jnp.concatenate([decoded[SMALL_PAD : SMALL_PAD + HALF], decoded[:SMALL]])
    natural = jnp.where(core == 0, start, end)
    decoded = jnp.stack(exchange_packs(natural.reshape(2, dec_quarter, dec_width), odd))[None]
    grad_input = jnp.stack(
        exchange_packs(grad_input.reshape(2, ENC_SEG, enc_width)[:, : enc_half // 2], odd)
    )[None]
    return (
        decoded,
        grad_input,
        enc_norm_share,
        enc_qkv_share,
        enc_proj_share,
        enc_up_share,
        enc_down_share,
        embed_share,
        dec_vec_share,
        dec_qkv_share,
        dec_proj_share,
        dec_up_share,
        dec_down_share,
    )


def solution(mesh):
    rows = P("img", None, "seq", None)
    tables = P("img", None, None)
    shares = P("img", None)
    return jax.shard_map(
        shards,
        mesh=mesh,
        in_specs=(rows, rows, tables, tables) + (P(),) * 11,
        out_specs=(rows, rows) + (shares,) * 11,
        check_vma=False,
    )
```

```python
import functools
import math

import jax
import jax.numpy as jnp
import numpy as np
from jax import lax
from jax.experimental import pallas as pl
from jax.experimental.pallas import tpu as pltpu
from jax.sharding import PartitionSpec as P

HE = 12
HD = 16
PATCHES = 784
SMALL = PATCHES // 4
HALF = PATCHES // 2
SMALL_PAD = 208
BIG_PAD = 400
DEC_PAD = SMALL_PAD + BIG_PAD
ENC_SEG = 80
ENC_PAD = 2 * ENC_SEG

eps_norm = 1e-06
masked_score = -1e30
bf16 = jnp.bfloat16
f32 = jnp.float32


def product(left_side, right_side):
    return jnp.dot(left_side, right_side, preferred_element_type=f32)


def inner_rows(left_side, right_side):
    return lax.dot_general(
        left_side, right_side, (((0,), (0,)), ((), ())), preferred_element_type=f32
    )


def inner_cols(left_side, right_side):
    return lax.dot_general(
        left_side, right_side, (((1,), (1,)), ((), ())), preferred_element_type=f32
    )


def norm_parts(values):
    centered = values - jnp.mean(values, axis=-1, keepdims=True)
    inverse = lax.rsqrt(jnp.mean(centered * centered, axis=-1, keepdims=True) + eps_norm)
    return centered * inverse, inverse


def norm_backward(grad_out, normed, inverse, norm_gain):
    scaled = grad_out * norm_gain
    grad_values = inverse * (
        scaled
        - jnp.mean(scaled, axis=-1, keepdims=True)
        - normed * jnp.mean(scaled * normed, axis=-1, keepdims=True)
    )
    return (
        grad_values,
        jnp.sum(grad_out * normed, axis=0, keepdims=True),
        jnp.sum(grad_out, axis=0, keepdims=True),
    )


def gelu_parts(hidden):
    below = 0.5 + 0.5 * lax.erf(hidden * math.sqrt(0.5))
    density = jnp.exp(hidden * hidden * -0.5) * (1.0 / math.sqrt(2.0 * math.pi))
    return hidden * below, below + hidden * density


LANES = 256
EIGHTH = 48
SUB_ROWS = 8 * EIGHTH


def put(core, dest, offset, grad):
    low = grad.astype(bf16)
    if len(dest) == 1:
        dest[0][...] = low
        return
    keep, leaving = dest
    chips = keep.shape[0]
    count = low.shape[0] // (2 * chips)
    for case in (0, 1):

        @pl.when(core == case)
        def _():
            for image in range(2 * chips):
                ref = keep if image % 2 == case else leaving
                for block in range(low.shape[1] // LANES):
                    start = offset + block * count
                    ref[image // 2, start : start + count, :] = low[
                        image * count : (image + 1) * count, block * LANES : (block + 1) * LANES
                    ]


def image_rows(shape, images):
    return shape[0] // images * (shape[1] // LANES)


class Chunk:
    def __init__(self, images, shapes, spare=0):
        self.images = images
        self.shapes = shapes
        self.offsets = []
        rows = 0
        for shape in shapes:
            self.offsets.append(rows)
            rows += image_rows(shape, images)
        self.used = rows
        rows += spare
        self.direct = all(shape[0] // images % 16 == 0 for shape in shapes)
        unit = SUB_ROWS if self.direct else 8
        self.rows = -(-rows // unit) * unit

    def outs(self):
        if self.direct:
            return [((self.images // 2, self.rows, LANES), bf16)] * 2
        return [(shape, bf16) for shape in self.shapes]

    def dests(self, refs):
        if self.direct:
            return [tuple(refs)] * len(self.shapes)
        return [(ref,) for ref in refs]

    def pair(self, results, core):
        if self.direct:
            return tuple(results)
        pieces = []
        for grad in results:
            for start in range(0, grad.shape[1], LANES):
                piece = grad[:, start : start + LANES]
                pieces.append(piece.reshape(self.images, -1, LANES))
        stacked = jnp.concatenate(pieces, axis=1)
        stacked = jnp.pad(stacked, ((0, 0), (0, self.rows - stacked.shape[1]), (0, 0)))
        both = stacked.reshape(self.images // 2, 2, self.rows, LANES)
        return pick(both, core, 1), pick(both, 1 - core, 1)

    def split(self, share):
        results = []
        for shape, offset in zip(self.shapes, self.offsets):
            count = shape[0] // self.images
            pieces = [
                share[offset + block * count : offset + (block + 1) * count]
                for block in range(shape[1] // LANES)
            ]
            results.append(jnp.concatenate(pieces, axis=1).astype(f32))
        return results


def call(kernel, scalars, outs, args, megabytes):
    vmem = pl.BlockSpec(memory_space=pltpu.VMEM)
    smem = pl.BlockSpec(memory_space=pltpu.SMEM)
    return pl.pallas_call(
        kernel,
        out_shape=[jax.ShapeDtypeStruct(shape, kind) for shape, kind in outs],
        in_specs=[smem] * scalars + [vmem] * (len(args) - scalars),
        out_specs=[vmem] * len(outs),
        compiler_params=pltpu.CompilerParams(vmem_limit_bytes=megabytes << 20),
    )(*args)


def lane_masks(head_size, kind):
    lanes = lax.broadcasted_iota(jnp.int32, (1, 128), 1) // head_size
    return [(lanes == head).astype(f32).astype(kind) for head in range(128 // head_size)]


def softmax_rows(scores, scale):
    row_max = jnp.max(scores, axis=1, keepdims=True)
    weights = jnp.exp2((scores - row_max) * (scale * math.log2(math.e)))
    return (weights * (1.0 / jnp.sum(weights, axis=1, keepdims=True))).astype(bf16)


def head_back(probs, grads, values, delta):
    grad_probs = inner_cols(grads, values)
    return (probs.astype(f32) * (grad_probs - delta)).astype(bf16)


def enc_pre_kernel(x, vecs, w_qkv, query, key_value):
    normed, _ = norm_parts(x[...].astype(f32))
    attn_in = (normed * vecs[0:1] + vecs[1:2]).astype(bf16)
    mixed = product(attn_in, w_qkv[...]).astype(bf16)
    width = query.shape[1]
    query[...] = mixed[:, :width]
    key_value[...] = mixed[:, width:]


def enc_main_kernel(
    x, query, own_kv, other_kv, own_ids, all_ids, vecs, w_proj, w_up, w_down, w_embed,
    embedded, att, probs, middle, active, slope, out
):
    width = query.shape[1]
    head_size = width // HE
    bias = jnp.where(own_ids[...] == all_ids[...], 0.0, masked_score)
    masks = lane_masks(head_size, bf16)
    for pair in range(width // 128):
        cols = slice(128 * pair, 128 * pair + 128)
        value_cols = slice(width + 128 * pair, width + 128 * pair + 128)
        keys = jnp.concatenate([own_kv[:, cols], other_kv[:, cols]], axis=0)
        values = jnp.concatenate([own_kv[:, value_cols], other_kv[:, value_cols]], axis=0)
        total = jnp.zeros((query.shape[0], 128), f32)
        for head, mask in enumerate(masks):
            scores = inner_cols(query[:, cols] * mask, keys) + bias
            chances = softmax_rows(scores, 1.0 / math.sqrt(head_size))
            probs[len(masks) * pair + head] = chances
            total += product(chances, values * mask)
        att[:, cols] = total.astype(bf16)
    mid = x[...].astype(f32) + product(att[...], w_proj[...])
    middle[...] = mid
    normed, _ = norm_parts(mid)
    mlp_in = (normed * vecs[2:3] + vecs[3:4]).astype(bf16)
    result, steepness = gelu_parts(product(mlp_in, w_up[...]))
    active[...] = result.astype(bf16)
    slope[...] = steepness.astype(bf16)
    last = mid + product(active[...], w_down[...])
    out[...] = last
    normed, _ = norm_parts(last)
    final = (normed * vecs[4:5] + vecs[5:6]).astype(bf16)
    embedded[...] = product(final, w_embed[...]).astype(bf16)


def chosen_rows(core, visible_rows):
    index = lax.broadcasted_iota(jnp.int32, (DEC_PAD, 1), 0)
    small = index + core * (SMALL + PATCHES)
    big = index + (SMALL - SMALL_PAD) + core * HALF
    row = jnp.where(index < SMALL, small, -1)
    row = jnp.where((index >= SMALL_PAD) & (index < SMALL_PAD + HALF), big, row)
    return (row == visible_rows).astype(f32)


def dec_pre_kernel(core, own, other, rows, code, vecs, w_qkv, dec_input, mixed, big_kv):
    chosen = chosen_rows(core[0], rows[...])
    seen = jnp.sum(chosen, axis=1, keepdims=True)
    tokens = jnp.concatenate([own[...], other[...]], axis=0)
    picked = product(chosen.astype(bf16), tokens)
    values = jnp.where(seen > 0.0, picked, vecs[4:5]) + code[...]
    dec_input[...] = values
    normed, _ = norm_parts(values)
    attn_in = (normed * vecs[0:1] + vecs[1:2]).astype(bf16)
    result = product(attn_in, w_qkv[...]).astype(bf16)
    mixed[...] = result
    big_kv[...] = result[SMALL_PAD:, values.shape[1] :]


def big_bias():
    column = lax.broadcasted_iota(jnp.int32, (1, 2 * BIG_PAD), 1)
    place = jnp.where(column >= BIG_PAD, column - BIG_PAD, column)
    return jnp.where(place < HALF, 0.0, masked_score)


def small_bias():
    column = lax.broadcasted_iota(jnp.int32, (1, SMALL_PAD), 1)
    return jnp.where(column < SMALL, 0.0, masked_score)


def dec_att_kernel(query, key, value, other_key, other_value, att, big_probs, small_probs):
    head_size = query.shape[1] * 4 // HD
    scale = 1.0 / math.sqrt(head_size)
    keys = jnp.concatenate([key[SMALL_PAD:], other_key[...]], axis=0)
    values = jnp.concatenate([value[SMALL_PAD:], other_value[...]], axis=0)
    total = jnp.zeros((BIG_PAD, 128), f32)
    small_total = jnp.zeros((SMALL_PAD, 128), f32)
    for head, mask in enumerate(lane_masks(head_size, bf16)):
        scores = inner_cols(query[SMALL_PAD:] * mask, keys) + big_bias()
        chances = softmax_rows(scores, scale)
        big_probs[head] = chances
        total += product(chances, values * mask)
        scores = inner_cols(query[:SMALL_PAD] * mask, key[:SMALL_PAD]) + small_bias()
        chances = softmax_rows(scores, scale)
        small_probs[head] = chances
        small_total += product(chances, value[:SMALL_PAD] * mask)
    att[:SMALL_PAD] = small_total.astype(bf16)
    att[SMALL_PAD:] = total.astype(bf16)


def dec_mid_kernel(
    chunk, core, dec_input, att, cot, vecs, w_proj, w_up, w_down,
    decoded, grad_middle, grad_att, vectors, *grads
):
    down_dest, up_dest, proj_dest = chunk.dests(grads)
    down_at, up_at, proj_at = chunk.offsets
    grad_down, grad_up = [], []
    middle = dec_input[...] + product(att[...], w_proj[...])
    normed, inverse = norm_parts(middle)
    mlp_in = (normed * vecs[2:3] + vecs[3:4]).astype(bf16)
    result = middle
    grad_norm = jnp.zeros_like(middle)
    step = 512
    for start in range(0, w_up.shape[1], step):
        cols = slice(start, start + step)
        active, slope = gelu_parts(product(mlp_in, w_up[:, cols]))
        active = active.astype(bf16)
        result += product(active, w_down[cols])
        grad_down.append(inner_rows(active, cot[...]).astype(bf16))
        grad_hidden = (slope * inner_cols(cot[...], w_down[cols])).astype(bf16)
        grad_up.append(inner_rows(mlp_in, grad_hidden).astype(bf16))
        grad_norm += inner_cols(grad_hidden, w_up[:, cols])
    decoded[...] = result.astype(bf16)
    grad_values, gain, shift = norm_backward(grad_norm, normed, inverse, vecs[2:3])
    vectors[0:1] = gain
    vectors[1:2] = shift
    back = cot[...].astype(f32) + grad_values
    grad_middle[...] = back
    low = back.astype(bf16)
    grad_att[...] = inner_cols(low, w_proj[...]).astype(bf16)
    put(core[0], proj_dest, proj_at, inner_rows(att[...], low))
    put(core[0], down_dest, down_at, jnp.concatenate(grad_down, axis=0))
    put(core[0], up_dest, up_at, jnp.concatenate(grad_up, axis=1))


def dec_att_back_kernel(
    query, key, value, other_key, other_value, grads, att, big_probs, small_probs,
    grad_query, grad_key, grad_value, leaving_key, leaving_value
):
    head_size = query.shape[1] * 4 // HD
    scale = 1.0 / math.sqrt(head_size)
    keys = jnp.concatenate([key[SMALL_PAD:], other_key[...]], axis=0)
    values = jnp.concatenate([value[SMALL_PAD:], other_value[...]], axis=0)
    overlap = grads[...].astype(f32) * att[...].astype(f32)
    big_q = jnp.zeros((BIG_PAD, 128), f32)
    big_k = jnp.zeros((2 * BIG_PAD, 128), f32)
    big_v = jnp.zeros((2 * BIG_PAD, 128), f32)
    small_q = jnp.zeros((SMALL_PAD, 128), f32)
    small_k = jnp.zeros((SMALL_PAD, 128), f32)
    small_v = jnp.zeros((SMALL_PAD, 128), f32)
    masks = lane_masks(head_size, f32)
    for head, mask in enumerate(lane_masks(head_size, bf16)):
        delta = jnp.sum(overlap * masks[head], axis=1, keepdims=True)
        one_query, one_grad = query[...] * mask, grads[...] * mask
        chances = big_probs[head]
        back = head_back(chances, one_grad[SMALL_PAD:], values, delta[SMALL_PAD:])
        big_q += product(back, keys * mask)
        big_k += inner_rows(back, one_query[SMALL_PAD:])
        big_v += inner_rows(chances, one_grad[SMALL_PAD:])
        chances = small_probs[head]
        back = head_back(chances, one_grad[:SMALL_PAD], value[:SMALL_PAD], delta[:SMALL_PAD])
        small_q += product(back, key[:SMALL_PAD] * mask)
        small_k += inner_rows(back, one_query[:SMALL_PAD])
        small_v += inner_rows(chances, one_grad[:SMALL_PAD])
    grad_query[:SMALL_PAD] = (small_q * scale).astype(bf16)
    grad_query[SMALL_PAD:] = (big_q * scale).astype(bf16)
    grad_key[:SMALL_PAD] = small_k * scale
    grad_key[SMALL_PAD:] = big_k[:BIG_PAD] * scale
    grad_value[:SMALL_PAD] = small_v
    grad_value[SMALL_PAD:] = big_v[:BIG_PAD]
    leaving_key[...] = (big_k[BIG_PAD:] * scale).astype(bf16)
    leaving_value[...] = big_v[BIG_PAD:].astype(bf16)


def dec_post_kernel(
    chunk, core, dec_input, grad_middle, grad_query, grad_key, grad_value, arrived_key,
    arrived_value, rows, vecs, w_qkv, own_spread, other_spread, vectors, *grads
):
    normed, inverse = norm_parts(dec_input[...])
    attn_in = (normed * vecs[0:1] + vecs[1:2]).astype(bf16)
    key = jnp.concatenate(
        [grad_key[:SMALL_PAD], grad_key[SMALL_PAD:] + arrived_key[...].astype(f32)], axis=0
    ).astype(bf16)
    value = jnp.concatenate(
        [grad_value[:SMALL_PAD], grad_value[SMALL_PAD:] + arrived_value[...].astype(f32)], axis=0
    ).astype(bf16)
    mixed = jnp.concatenate([grad_query[...], key, value], axis=1)
    grad_values, gain, shift = norm_backward(
        inner_cols(mixed, w_qkv[...]), normed, inverse, vecs[0:1]
    )
    back = grad_middle[...] + grad_values
    chosen = chosen_rows(core[0], rows[...])
    seen = jnp.sum(chosen, axis=1, keepdims=True)
    spread = inner_rows(chosen.astype(bf16), back.astype(bf16)).astype(bf16)
    own_spread[...] = spread[:ENC_PAD]
    other_spread[...] = spread[ENC_PAD:]
    vectors[0:1] = gain
    vectors[1:2] = shift
    vectors[2:3] = jnp.sum(jnp.where(seen > 0.0, 0.0, back), axis=0, keepdims=True)
    put(core[0], chunk.dests(grads)[0], chunk.offsets[0], inner_rows(attn_in, mixed))


def enc_mlp_back_kernel(
    first, second, core, own_spread, arrived, out, middle, active, slope,
    vecs, w_embed, w_down, w_up, w_proj, grad_middle, grad_att, vectors, *grads
):
    first_grads, second_grads = grads[: len(first.outs())], grads[len(first.outs()) :]
    grad_embedded = own_spread[...] + arrived[...]
    normed, inverse = norm_parts(out[...])
    grad_out, gain, shift = norm_backward(
        inner_cols(grad_embedded, w_embed[...]), normed, inverse, vecs[4:5]
    )
    vectors[2:3] = gain
    vectors[3:4] = shift
    low = grad_out.astype(bf16)
    put(core[0], first.dests(first_grads)[0], first.offsets[0], inner_rows(active[...], low))
    grad_hidden = (slope[...].astype(f32) * inner_cols(low, w_down[...])).astype(bf16)
    normed, inverse = norm_parts(middle[...])
    mlp_in = (normed * vecs[2:3] + vecs[3:4]).astype(bf16)
    put(
        core[0], second.dests(second_grads)[0], second.offsets[0], inner_rows(mlp_in, grad_hidden)
    )
    grad_values, gain, shift = norm_backward(
        inner_cols(grad_hidden, w_up[...]), normed, inverse, vecs[2:3]
    )
    vectors[0:1] = gain
    vectors[1:2] = shift
    back = grad_out + grad_values
    grad_middle[...] = back
    grad_att[...] = inner_cols(back.astype(bf16), w_proj[...]).astype(bf16)


def enc_att_back_kernel(
    grads, att, probs, query, own_kv, other_kv, grad_query, grad_kv, leaving
):
    width = query.shape[1]
    head_size = width // HE
    scale = 1.0 / math.sqrt(head_size)
    overlap = grads[...].astype(f32) * att[...].astype(f32)
    masks = lane_masks(head_size, bf16)
    wide_masks = lane_masks(head_size, f32)
    rows = query.shape[0]
    for pair in range(width // 128):
        cols = slice(128 * pair, 128 * pair + 128)
        value_cols = slice(width + 128 * pair, width + 128 * pair + 128)
        keys = jnp.concatenate([own_kv[:, cols], other_kv[:, cols]], axis=0)
        values = jnp.concatenate([own_kv[:, value_cols], other_kv[:, value_cols]], axis=0)
        total_q = jnp.zeros((rows, 128), f32)
        total_k = jnp.zeros((2 * rows, 128), f32)
        total_v = jnp.zeros((2 * rows, 128), f32)
        for head, mask in enumerate(masks):
            delta = jnp.sum(overlap[:, cols] * wide_masks[head], axis=1, keepdims=True)
            one_grad = grads[:, cols] * mask
            chances = probs[len(masks) * pair + head]
            one_back = head_back(chances, one_grad, values, delta)
            total_q += product(one_back, keys * mask)
            total_k += inner_rows(one_back, query[:, cols] * mask)
            total_v += inner_rows(chances, one_grad)
        grad_query[:, cols] = (total_q * scale).astype(bf16)
        grad_kv[:, cols] = total_k[:rows] * scale
        grad_kv[:, value_cols] = total_v[:rows]
        leaving[:, cols] = (total_k[rows:] * scale).astype(bf16)
        leaving[:, value_cols] = total_v[rows:].astype(bf16)


def enc_post_kernel(
    chunk, core, x, att, grad_middle, grad_query, grad_kv, arrived, out, own_spread, other_spread,
    vecs, w_qkv, grad_input, vectors, *grads
):
    qkv_dest, proj_dest, embed_dest = chunk.dests(grads)
    normed, _ = norm_parts(out[...])
    final = (normed * vecs[4:5] + vecs[5:6]).astype(bf16)
    put(
        core[0], embed_dest, chunk.offsets[2], inner_rows(final, own_spread[...] + other_spread[...])
    )
    put(
        core[0], proj_dest, chunk.offsets[1],
        inner_rows(att[...], grad_middle[...].astype(bf16)),
    )
    normed, inverse = norm_parts(x[...].astype(f32))
    attn_in = (normed * vecs[0:1] + vecs[1:2]).astype(bf16)
    key_value = (grad_kv[...] + arrived[...].astype(f32)).astype(bf16)
    mixed = jnp.concatenate([grad_query[...], key_value], axis=1)
    grad_values, gain, shift = norm_backward(
        inner_cols(mixed, w_qkv[...]), normed, inverse, vecs[0:1]
    )
    grad_input[...] = grad_middle[...] + grad_values
    vectors[0:1] = gain
    vectors[1:2] = shift
    put(core[0], qkv_dest, chunk.offsets[0], inner_rows(attn_in, mixed))


def permute(array, where_to):
    seq_count = lax.axis_size("seq")
    img_count = lax.axis_size("img")
    pairs = []
    for seq in range(seq_count):
        for img in range(img_count):
            seq_to, img_to = where_to(seq, img)
            pairs.append((seq * img_count + img, seq_to * img_count + img_to))
    return lax.ppermute(array, ("seq", "img"), pairs)


def swap(array):
    return permute(array, lambda seq, img: (seq, img ^ 1))


def pack_move(turn):
    def where_to(seq, img):
        return (2 * (img & 1) + (turn ^ (seq & 1)), (img & ~1) | (seq >> 1))

    return where_to


def exchange_packs(blocks, odd):
    rounds = [
        permute(jnp.where(odd, blocks[1 - turn], blocks[turn]), pack_move(turn)) for turn in (0, 1)
    ]
    return (jnp.where(odd, rounds[1], rounds[0]), jnp.where(odd, rounds[0], rounds[1]))


def pick(array, index, axis):
    return lax.dynamic_index_in_dim(array, index, axis, keepdims=False)


def pad_rows(array, rows):
    return jnp.pad(array, ((0, rows - array.shape[0]),) + ((0, 0),) * (array.ndim - 1))


def position_table(row_width):
    halfway = row_width // 2
    frequency = np.exp(np.arange(halfway, dtype=np.float64) * (-math.log(10000.0) / halfway))
    angles = np.arange(PATCHES, dtype=np.float64)[:, None] * frequency[None, :]
    return np.concatenate([np.sin(angles), np.cos(angles)], axis=1).astype(np.float32)


def reduce_pair(keep, leaving):
    return (keep.astype(f32) + swap(leaving).astype(f32)).astype(bf16)


def reduce_kernel(counts, chips, spare_at, *refs):
    chunks = len(counts)
    keeps, leavings = refs[:chunks], refs[chunks : 2 * chunks]
    spare_keep, spare_leaving, out = refs[2 * chunks : 2 * chunks + 3]
    held, from_pair, first, second, from_chips, gathered = refs[2 * chunks + 3 : 2 * chunks + 9]
    local_sem, spare_sem, pair_sem, first_sem, second_sem, chip_sem, gather_sem = refs[
        2 * chunks + 9 :
    ]
    total = sum(counts)
    seq, img = lax.axis_index("seq"), lax.axis_index("img")
    chip, core = img // 2, img % 2
    high, low = seq // 2, seq % 2
    partner = {"img": img + 1 - 2 * core}
    along_x = {"seq": seq + 1 - 2 * low}
    along_y = {"seq": seq + 2 - 4 * high}
    across = {"seq": 3 - seq}
    others = [
        {"img": lax.rem(chip + step, chips) * 2 + core} for step in range(1, chips)
    ]

    def remote(source, dest, sems, device):
        return pltpu.make_async_remote_copy(
            src_ref=source,
            dst_ref=dest,
            send_sem=sems.at[0],
            recv_sem=sems.at[1],
            device_id=device,
            device_id_type=pl.DeviceIdType.MESH,
        )

    def pair_copies():
        copies = []
        index = 0
        for chunk, count in enumerate(counts):
            for place in range(count):
                last = chunk == chunks - 1 and place == count - 1
                if last:
                    parts = [
                        (
                            keeps[chunk].at[:, place, 0],
                            leavings[chunk].at[:, place, 0],
                            (index, slice(None), 0),
                        ),
                        (
                            spare_keep,
                            spare_leaving,
                            (index, slice(None)) + spare_at,
                        ),
                    ]
                else:
                    parts = [
                        (keeps[chunk].at[:, place], leavings[chunk].at[:, place], (index,))
                    ]
                for part, (keep, leaving, where) in enumerate(parts):
                    local = spare_sem if part else local_sem.at[index]
                    sems = pair_sem.at[total if part else index]
                    copies.append(
                        (
                            pltpu.make_async_copy(keep, held.at[where], local),
                            remote(leaving, from_pair.at[where], sems, partner),
                        )
                    )
                index += 1
        return copies

    def first_copies(i):
        return (
            remote(held.at[i, :, 0, :, 1 - low], first.at[i, 0], first_sem.at[i, 0], along_x),
            remote(held.at[i, :, 1, 1 - high], first.at[i, 1], first_sem.at[i, 1], along_y),
        )

    def second_copies(i):
        return (
            remote(
                held.at[i, :, 0, 1 - high, low], second.at[i, 0], second_sem.at[i, 0], along_y
            ),
            remote(
                held.at[i, :, 1, high, 1 - low], second.at[i, 1], second_sem.at[i, 1], along_x
            ),
        )

    def chip_copies(i):
        return [
            remote(
                held.at[i, device["img"] // 2, :, high, low],
                from_chips.at[i, step],
                chip_sem.at[i, step],
                device,
            )
            for step, device in enumerate(others)
        ]

    def gather_copies(i):
        return [
            remote(
                gathered.at[i, :, high, low],
                gathered.at[i, :, high, low],
                gather_sem.at[i, step],
                device,
            )
            for step, device in enumerate((along_x, along_y, across))
        ]

    def gather_arrivals(i):
        return [
            remote(
                gathered.at[i, :, peer // 2, lax.rem(peer, 2)],
                gathered.at[i, :, peer // 2, lax.rem(peer, 2)],
                gather_sem.at[i, step],
                device,
            )
            for step, (peer, device) in enumerate(
                ((along_x["seq"], along_x), (along_y["seq"], along_y), (3 - seq, across))
            )
        ]

    def add(one, two):
        return (one.astype(f32) + two.astype(f32)).astype(bf16)

    def stage_one(i):
        @pl.when(i < total - 1)
        def _():
            pltpu.make_async_copy(from_pair.at[i], held.at[i], local_sem.at[i]).wait()
            remote(from_pair.at[i], from_pair.at[i], pair_sem.at[i], partner).wait()

        @pl.when(i == total - 1)
        def _():
            for local, away in pairs[-2:]:
                local.wait()
                away.wait()

        for image in range(chips):
            held[i, image] = add(held[i, image], from_pair[i, image])
        for copy in first_copies(i):
            copy.start()

    def stage_two(i):
        for copy in first_copies(i):
            copy.wait_recv()
        held[i, :, 0, :, low] = add(held[i, :, 0, :, low], first[i, 0])
        held[i, :, 1, high] = add(held[i, :, 1, high], first[i, 1])
        for copy in second_copies(i):
            copy.start()

    def stage_chips(i):
        for copy in second_copies(i):
            copy.wait_recv()
        held[i, :, 0, high, low] = add(held[i, :, 0, high, low], second[i, 0])
        held[i, :, 1, high, low] = add(held[i, :, 1, high, low], second[i, 1])
        for copy in chip_copies(i):
            copy.start()

    def stage_gather(i):
        for copy in chip_copies(i):
            copy.wait_recv()
        mine = held[i, chip, :, high, low].astype(f32)
        for step in range(chips - 1):
            mine += from_chips[i, step].astype(f32)
        gathered[i, :, high, low] = mine.astype(bf16)
        for copy in gather_copies(i):
            copy.start()

    def stage_end(i):
        for copy in gather_arrivals(i):
            copy.wait_recv()
        out[i] = gathered[i]
        for copy in (
            *first_copies(i), *second_copies(i), *chip_copies(i), *gather_copies(i)
        ):
            copy.wait_send()

    barrier = pltpu.get_barrier_semaphore()
    for device in (partner, along_x, along_y, across, *others):
        pl.semaphore_signal(
            barrier, inc=1, device_id=device, device_id_type=pl.DeviceIdType.MESH
        )
    pl.semaphore_wait(barrier, 3 + chips)

    pairs = pair_copies()
    for local, away in pairs:
        local.start()
        away.start()

    stages = (stage_one, stage_two, stage_chips, stage_gather, stage_end)

    def step(t, carry):
        for lag, stage in enumerate(stages):
            i = t - lag

            @pl.when((i >= 0) & (i < total))
            def _():
                stage(i)

        return carry

    lax.fori_loop(0, total + len(stages) - 1, step, 0)


def reduce_chunks(pairs, spares, spare_row):
    chips = pairs[0][0].shape[0]
    counts = [keep.shape[1] // SUB_ROWS for keep, _ in pairs]
    total = sum(counts)

    def fold(array):
        return array.reshape(chips, -1, 2, 2, 2, EIGHTH, LANES)

    row = spare_row % SUB_ROWS
    place, start = row // EIGHTH, row % EIGHTH
    spare_at = (place // 4, place // 2 % 2, place % 2, slice(start, start + 16))
    anywhere = pl.BlockSpec(memory_space=pl.ANY)
    block = (EIGHTH, LANES)
    dma = pltpu.SemaphoreType.DMA
    out = pl.pallas_call(
        functools.partial(reduce_kernel, counts, chips, spare_at),
        out_shape=jax.ShapeDtypeStruct((total, 2, 2, 2) + block, bf16),
        in_specs=[anywhere] * (2 * len(pairs) + 2),
        out_specs=pl.BlockSpec(memory_space=pltpu.VMEM),
        scratch_shapes=[
            pltpu.VMEM((total, chips, 2, 2, 2) + block, bf16),
            pltpu.VMEM((total, chips, 2, 2, 2) + block, bf16),
            pltpu.VMEM((total, 2, chips, 2) + block, bf16),
            pltpu.VMEM((total, 2, chips) + block, bf16),
            pltpu.VMEM((total, chips - 1, 2) + block, bf16),
            pltpu.VMEM((total, 2, 2, 2) + block, bf16),
            dma((total,)),
            dma,
            dma((total + 1, 2)),
            dma((total, 2, 2)),
            dma((total, 2, 2)),
            dma((total, chips - 1, 2)),
            dma((total, 3, 2)),
        ],
        compiler_params=pltpu.CompilerParams(
            collective_id=1, has_side_effects=True, vmem_limit_bytes=60 << 20
        ),
    )(*[fold(keep) for keep, _ in pairs], *[fold(leaving) for _, leaving in pairs], *spares)
    shares = []
    start = 0
    for count in counts:
        shares.append(out[start : start + count].reshape(count * SUB_ROWS, LANES))
        start += count
    return shares


def reduce_rest(chunk, seq):
    chips, rows, width = chunk.shape
    high, low = seq // 2, seq % 2
    eighth = rows // 8
    parts = chunk.reshape(chips, 2, 2, 2, eighth, width)

    def along_x(array):
        return permute(array, lambda s, i: (s ^ 1, i))

    def along_y(array):
        return permute(array, lambda s, i: (s ^ 2, i))

    def add(one, two):
        return (one.astype(f32) + two.astype(f32)).astype(bf16)

    one, two = parts[:, 0], parts[:, 1]
    one = add(pick(one, low, 2), along_x(pick(one, 1 - low, 2)))
    two = add(pick(two, high, 1), along_y(pick(two, 1 - high, 1)))
    one = add(pick(one, high, 1), along_y(pick(one, 1 - high, 1)))
    two = add(pick(two, low, 1), along_x(pick(two, 1 - low, 1)))
    mine = jnp.stack([one, two], axis=1)
    chip = lax.axis_index("img") // 2
    total = pick(mine, chip, 0).astype(f32)
    for step in range(1, chips):
        leaving = pick(mine, (chip + step) % chips, 0)
        arrived = permute(
            leaving,
            lambda s, i, step=step: (s, ((i // 2 + step) % chips) * 2 + (i & 1)),
        )
        total = total + arrived.astype(f32)
    own = total.astype(bf16)
    others = [permute(own, lambda s, i, step=step: (s ^ step, i)) for step in (1, 2, 3)]
    by_xor = jnp.stack([own] + others)
    ordered = jnp.stack([pick(by_xor, seq ^ place, 0) for place in range(4)], axis=1)
    return ordered.reshape(rows, width)


def shards(
    enc_input,
    cotangent,
    enc_image,
    visible_rows,
    enc_norms,
    enc_qkv,
    enc_proj,
    enc_up,
    enc_down,
    embed,
    dec_vecs,
    dec_qkv,
    dec_proj,
    dec_up,
    dec_down,
):
    seq = lax.axis_index("seq")
    img = lax.axis_index("img")
    images = lax.axis_size("img")
    core = img % 2
    odd = seq % 2 == 1
    enc_width = enc_input.shape[3]
    dec_width = dec_vecs.shape[0]
    enc_half = 2 * enc_input.shape[2]
    dec_quarter = cotangent.shape[2]

    enc_vecs = jnp.pad(enc_norms.T, ((0, 2), (0, 0)))
    dec_rows_vecs = jnp.pad(dec_vecs.T, ((0, 3), (0, 0)))
    tables = jnp.stack([enc_image[0], visible_rows[0]])
    other_tables = swap(tables)
    tables = jnp.where(seq // 2 == core, tables, other_tables)
    tables = jnp.where(odd, tables[:, 1], tables[:, 0])
    segments = tables.reshape(2, 2, 2, enc_half // 2)
    segments = jnp.pad(
        segments, ((0, 0),) * 3 + ((0, ENC_SEG - enc_half // 2),), constant_values=-2
    )
    halves = segments.reshape(2, 2, ENC_PAD)
    own = pick(halves, core, 1)
    ids = jnp.concatenate([own, pick(halves, 1 - core, 1)], axis=1)
    row_ids = ids[1:2]
    core_arg = core.reshape(1)

    blocks = jnp.pad(enc_input[0], ((0, 0), (0, ENC_SEG - enc_half // 2), (0, 0)))
    x = jnp.concatenate(exchange_packs(blocks, odd), axis=0)
    cot = jnp.concatenate(exchange_packs(cotangent[0], odd), axis=0)
    cot = jnp.concatenate(
        [
            pad_rows(lax.dynamic_slice_in_dim(cot, core * HALF, SMALL, 0), SMALL_PAD),
            pad_rows(lax.dynamic_slice_in_dim(cot, (1 - core) * SMALL, HALF, 0), BIG_PAD),
        ],
        axis=0,
    )
    enc_hidden_width = enc_up.shape[1]

    enc_query, enc_kv = call(
        enc_pre_kernel,
        0,
        [((ENC_PAD, enc_width), bf16), ((ENC_PAD, 2 * enc_width), bf16)],
        (x, enc_vecs, enc_qkv),
        40,
    )
    enc_other = swap(enc_kv)
    embedded, enc_att, enc_probs, enc_middle, enc_active, enc_slope, enc_out = call(
        enc_main_kernel,
        0,
        [
            ((ENC_PAD, dec_width), bf16),
            ((ENC_PAD, enc_width), bf16),
            ((HE, ENC_PAD, 2 * ENC_PAD), bf16),
            ((ENC_PAD, enc_width), f32),
            ((ENC_PAD, enc_hidden_width), bf16),
            ((ENC_PAD, enc_hidden_width), bf16),
            ((ENC_PAD, enc_width), f32),
        ],
        (
            x, enc_query, enc_kv, enc_other, own[0][:, None], ids[0:1], enc_vecs,
            enc_proj, enc_up, enc_down, embed,
        ),
        48,
    )

    table = position_table(dec_width)
    codes = np.zeros((2, DEC_PAD, dec_width), np.float32)
    for which in range(2):
        codes[which, :SMALL] = table[:SMALL]
        codes[which, SMALL_PAD : SMALL_PAD + HALF] = table[which * HALF : (which + 1) * HALF]
    code = pick(jnp.asarray(codes), core, 0)
    dec_input, dec_mixed, big_kv = call(
        dec_pre_kernel,
        1,
        [
            ((DEC_PAD, dec_width), f32),
            ((DEC_PAD, 3 * dec_width), bf16),
            ((BIG_PAD, 2 * dec_width), bf16),
        ],
        (core_arg, embedded, swap(embedded), row_ids, code, dec_rows_vecs, dec_qkv),
        40,
    )
    other_kv = swap(big_kv)
    groups = dec_width // 128

    def columns(rows, offset=0):
        return pl.BlockSpec((rows, 128), lambda group: (0, offset + group))

    def heads(rows, cols):
        return pl.BlockSpec((HD // groups, rows, cols), lambda group: (group, 0, 0))

    qkv_specs = [
        columns(DEC_PAD),
        columns(DEC_PAD, groups),
        columns(DEC_PAD, 2 * groups),
        columns(BIG_PAD),
        columns(BIG_PAD, groups),
    ]
    qkv_args = (dec_mixed, dec_mixed, dec_mixed, other_kv, other_kv)
    prob_specs = [heads(BIG_PAD, 2 * BIG_PAD), heads(SMALL_PAD, SMALL_PAD)]
    dec_att, big_probs, small_probs = pl.pallas_call(
        dec_att_kernel,
        grid=(groups,),
        in_specs=qkv_specs,
        out_specs=[columns(DEC_PAD)] + prob_specs,
        out_shape=[
            jax.ShapeDtypeStruct((DEC_PAD, dec_width), bf16),
            jax.ShapeDtypeStruct((HD, BIG_PAD, 2 * BIG_PAD), bf16),
            jax.ShapeDtypeStruct((HD, SMALL_PAD, SMALL_PAD), bf16),
        ],
        compiler_params=pltpu.CompilerParams(vmem_limit_bytes=48 << 20),
    )(*qkv_args)
    chunk_mid = Chunk(images, [dec_down.shape, dec_up.shape, dec_proj.shape])
    decoded, grad_dec_middle, dec_grad_att, vectors_two, *mid_grads = call(
        functools.partial(dec_mid_kernel, chunk_mid),
        1,
        [
            ((DEC_PAD, dec_width), bf16),
            ((DEC_PAD, dec_width), f32),
            ((DEC_PAD, dec_width), bf16),
            ((2, dec_width), f32),
        ]
        + chunk_mid.outs(),
        (core_arg, dec_input, dec_att, cot, dec_rows_vecs, dec_proj, dec_up, dec_down),
        48,
    )
    grad_specs = [columns(DEC_PAD)] * 3 + [columns(BIG_PAD)] * 2
    grad_query, grad_key, grad_value, leaving_key, leaving_value = pl.pallas_call(
        dec_att_back_kernel,
        grid=(groups,),
        in_specs=qkv_specs + [columns(DEC_PAD)] * 2 + prob_specs,
        out_specs=grad_specs,
        out_shape=[
            jax.ShapeDtypeStruct((DEC_PAD, dec_width), bf16),
            jax.ShapeDtypeStruct((DEC_PAD, dec_width), f32),
            jax.ShapeDtypeStruct((DEC_PAD, dec_width), f32),
            jax.ShapeDtypeStruct((BIG_PAD, dec_width), bf16),
            jax.ShapeDtypeStruct((BIG_PAD, dec_width), bf16),
        ],
        compiler_params=pltpu.CompilerParams(vmem_limit_bytes=48 << 20),
    )(*qkv_args, dec_grad_att, dec_att, big_probs, small_probs)
    chunk_post = Chunk(images, [dec_qkv.shape])
    own_spread, other_spread, vectors_one, *post_grads = call(
        functools.partial(dec_post_kernel, chunk_post),
        1,
        [
            ((ENC_PAD, dec_width), bf16),
            ((ENC_PAD, dec_width), bf16),
            ((3, dec_width), f32),
        ]
        + chunk_post.outs(),
        (
            core_arg, dec_input, grad_dec_middle, grad_query, grad_key, grad_value,
            swap(leaving_key), swap(leaving_value), row_ids, dec_rows_vecs, dec_qkv,
        ),
        48,
    )
    arrived_spread = swap(other_spread)
    chunk_down = Chunk(images, [enc_down.shape])
    chunk_up = Chunk(images, [enc_up.shape])
    grad_enc_middle, enc_grad_att, enc_vectors_two, *mlp_grads = call(
        functools.partial(enc_mlp_back_kernel, chunk_down, chunk_up),
        1,
        [
            ((ENC_PAD, enc_width), f32),
            ((ENC_PAD, enc_width), bf16),
            ((4, enc_width), f32),
        ]
        + chunk_down.outs()
        + chunk_up.outs(),
        (
            core_arg, own_spread, arrived_spread, enc_out, enc_middle, enc_active, enc_slope,
            enc_vecs, embed, enc_down, enc_up, enc_proj,
        ),
        56,
    )
    down_grads, up_grads = mlp_grads[: len(chunk_down.outs())], mlp_grads[len(chunk_down.outs()) :]
    enc_grad_query, enc_grad_kv, enc_leaving = call(
        enc_att_back_kernel,
        0,
        [
            ((ENC_PAD, enc_width), bf16),
            ((ENC_PAD, 2 * enc_width), f32),
            ((ENC_PAD, 2 * enc_width), bf16),
        ],
        (enc_grad_att, enc_att, enc_probs, enc_query, enc_kv, enc_other),
        48,
    )
    chunk_att = Chunk(images, [enc_qkv.shape, enc_proj.shape, embed.shape], 16)
    grad_input, enc_vectors_one, *att_grads = call(
        functools.partial(enc_post_kernel, chunk_att),
        1,
        [((ENC_PAD, enc_width), f32), ((2, enc_width), f32)] + chunk_att.outs(),
        (
            core_arg, x, enc_att, grad_enc_middle, enc_grad_query, enc_grad_kv,
            swap(enc_leaving), enc_out, own_spread, arrived_spread, enc_vecs, enc_qkv,
        ),
        48,
    )

    def by_image(rows):
        flat = rows.reshape(rows.shape[0], images, rows.shape[1] // images)
        return flat.transpose(1, 0, 2).reshape(images, -1)

    vectors = jnp.concatenate(
        [
            by_image(jnp.concatenate([enc_vectors_one, enc_vectors_two])),
            by_image(jnp.concatenate([vectors_one[:2], vectors_two, vectors_one[2:]])),
        ],
        axis=1,
    ).astype(bf16)
    vectors = jnp.pad(vectors, ((0, 0), (0, 16 * LANES - vectors.shape[1])))
    vectors = vectors.reshape(images // 2, 2, 16, LANES)
    vectors = (pick(vectors, core, 1), pick(vectors, 1 - core, 1))
    chunk_pairs = [
        chunk.pair(grads, core)
        for chunk, grads in (
            (chunk_mid, mid_grads),
            (chunk_post, post_grads),
            (chunk_down, down_grads),
            (chunk_up, up_grads),
            (chunk_att, att_grads),
        )
    ]
    if all(chunk.direct for chunk in (chunk_mid, chunk_down)) and images == 8:
        shares = reduce_chunks(chunk_pairs, vectors, chunk_att.used)
    else:
        place = slice(chunk_att.used, chunk_att.used + 16)
        chunk_pairs[-1] = tuple(
            array.at[:, place].set(rows) for array, rows in zip(chunk_pairs[-1], vectors)
        )
        shares = [reduce_rest(reduce_pair(*pair), seq) for pair in chunk_pairs]
    mid_share, post_share, down_share, up_share, att_share = shares
    dec_down_share, dec_up_share, dec_proj_share = chunk_mid.split(mid_share)
    (dec_qkv_share,) = chunk_post.split(post_share)
    (enc_down_share,) = chunk_down.split(down_share)
    (enc_up_share,) = chunk_up.split(up_share)
    enc_qkv_share, enc_proj_share, embed_share = chunk_att.split(att_share)
    vectors = att_share[chunk_att.used : chunk_att.used + 16].reshape(-1).astype(f32)
    enc_count, dec_count = enc_width // images, dec_width // images
    enc_norm_share = vectors[: 6 * enc_count].reshape(6, enc_count).T
    dec_vec_share = vectors[6 * enc_count : 6 * enc_count + 5 * dec_count].reshape(5, dec_count).T

    start = jnp.concatenate([decoded[:SMALL], decoded[SMALL_PAD : SMALL_PAD + HALF]])
    end = jnp.concatenate([decoded[SMALL_PAD : SMALL_PAD + HALF], decoded[:SMALL]])
    natural = jnp.where(core == 0, start, end)
    decoded = jnp.stack(exchange_packs(natural.reshape(2, dec_quarter, dec_width), odd))[None]
    grad_input = jnp.stack(
        exchange_packs(grad_input.reshape(2, ENC_SEG, enc_width)[:, : enc_half // 2], odd)
    )[None]
    return (
        decoded,
        grad_input,
        enc_norm_share,
        enc_qkv_share,
        enc_proj_share,
        enc_up_share,
        enc_down_share,
        embed_share,
        dec_vec_share,
        dec_qkv_share,
        dec_proj_share,
        dec_up_share,
        dec_down_share,
    )


def solution(mesh):
    rows = P("img", None, "seq", None)
    tables = P("img", None, None)
    shares = P("img", None)
    return jax.shard_map(
        shards,
        mesh=mesh,
        in_specs=(rows, rows, tables, tables) + (P(),) * 11,
        out_specs=(rows, rows) + (shares,) * 11,
        check_vma=False,
    )
```

```python
import functools
import math

import jax
import jax.numpy as jnp
import numpy as np
from jax import lax
from jax.experimental import pallas as pl
from jax.experimental.pallas import tpu as pltpu
from jax.sharding import PartitionSpec as P

HE = 12
HD = 16
PATCHES = 784
SMALL = PATCHES // 4
HALF = PATCHES // 2
SMALL_PAD = 208
BIG_PAD = 400
DEC_PAD = SMALL_PAD + BIG_PAD
ENC_SEG = 80
ENC_PAD = 2 * ENC_SEG

eps_norm = 1e-06
masked_score = -1e30
bf16 = jnp.bfloat16
f32 = jnp.float32


def product(left_side, right_side):
    return jnp.dot(left_side, right_side, preferred_element_type=f32)


def inner_rows(left_side, right_side):
    return lax.dot_general(
        left_side, right_side, (((0,), (0,)), ((), ())), preferred_element_type=f32
    )


def inner_cols(left_side, right_side):
    return lax.dot_general(
        left_side, right_side, (((1,), (1,)), ((), ())), preferred_element_type=f32
    )


def norm_parts(values):
    centered = values - jnp.mean(values, axis=-1, keepdims=True)
    inverse = lax.rsqrt(jnp.mean(centered * centered, axis=-1, keepdims=True) + eps_norm)
    return centered * inverse, inverse


def norm_backward(grad_out, normed, inverse, norm_gain):
    scaled = grad_out * norm_gain
    grad_values = inverse * (
        scaled
        - jnp.mean(scaled, axis=-1, keepdims=True)
        - normed * jnp.mean(scaled * normed, axis=-1, keepdims=True)
    )
    return (
        grad_values,
        jnp.sum(grad_out * normed, axis=0, keepdims=True),
        jnp.sum(grad_out, axis=0, keepdims=True),
    )


def gelu_parts(hidden):
    below = 0.5 + 0.5 * lax.erf(hidden * math.sqrt(0.5))
    density = jnp.exp(hidden * hidden * -0.5) * (1.0 / math.sqrt(2.0 * math.pi))
    return hidden * below, below + hidden * density


LANES = 256
EIGHTH = 48
SUB_ROWS = 8 * EIGHTH


def put(core, dest, offset, grad):
    low = grad.astype(bf16)
    if len(dest) == 1:
        dest[0][...] = low
        return
    keep, leaving = dest
    chips = keep.shape[0]
    count = low.shape[0] // (2 * chips)
    for case in (0, 1):

        @pl.when(core == case)
        def _():
            for image in range(2 * chips):
                ref = keep if image % 2 == case else leaving
                for block in range(low.shape[1] // LANES):
                    start = offset + block * count
                    ref[image // 2, start : start + count, :] = low[
                        image * count : (image + 1) * count, block * LANES : (block + 1) * LANES
                    ]


def image_rows(shape, images):
    return shape[0] // images * (shape[1] // LANES)


class Chunk:
    def __init__(self, images, shapes, spare=0):
        self.images = images
        self.shapes = shapes
        self.offsets = []
        rows = 0
        for shape in shapes:
            self.offsets.append(rows)
            rows += image_rows(shape, images)
        self.used = rows
        rows += spare
        self.direct = all(shape[0] // images % 16 == 0 for shape in shapes)
        unit = SUB_ROWS if self.direct else 8
        self.rows = -(-rows // unit) * unit

    def outs(self):
        if self.direct:
            return [((self.images // 2, self.rows, LANES), bf16)] * 2
        return [(shape, bf16) for shape in self.shapes]

    def dests(self, refs):
        if self.direct:
            return [tuple(refs)] * len(self.shapes)
        return [(ref,) for ref in refs]

    def pair(self, results, core):
        if self.direct:
            return tuple(results)
        pieces = []
        for grad in results:
            for start in range(0, grad.shape[1], LANES):
                piece = grad[:, start : start + LANES]
                pieces.append(piece.reshape(self.images, -1, LANES))
        stacked = jnp.concatenate(pieces, axis=1)
        stacked = jnp.pad(stacked, ((0, 0), (0, self.rows - stacked.shape[1]), (0, 0)))
        both = stacked.reshape(self.images // 2, 2, self.rows, LANES)
        return pick(both, core, 1), pick(both, 1 - core, 1)

    def split(self, share):
        results = []
        for shape, offset in zip(self.shapes, self.offsets):
            count = shape[0] // self.images
            pieces = [
                share[offset + block * count : offset + (block + 1) * count]
                for block in range(shape[1] // LANES)
            ]
            results.append(jnp.concatenate(pieces, axis=1).astype(f32))
        return results


def call(kernel, scalars, outs, args, megabytes):
    vmem = pl.BlockSpec(memory_space=pltpu.VMEM)
    smem = pl.BlockSpec(memory_space=pltpu.SMEM)
    return pl.pallas_call(
        kernel,
        out_shape=[jax.ShapeDtypeStruct(shape, kind) for shape, kind in outs],
        in_specs=[smem] * scalars + [vmem] * (len(args) - scalars),
        out_specs=[vmem] * len(outs),
        compiler_params=pltpu.CompilerParams(vmem_limit_bytes=megabytes << 20),
    )(*args)


def lane_masks(head_size, kind):
    lanes = lax.broadcasted_iota(jnp.int32, (1, 128), 1) // head_size
    return [(lanes == head).astype(f32).astype(kind) for head in range(128 // head_size)]


def softmax_rows(scores, scale):
    row_max = jnp.max(scores, axis=1, keepdims=True)
    weights = jnp.exp2((scores - row_max) * (scale * math.log2(math.e)))
    return (weights * (1.0 / jnp.sum(weights, axis=1, keepdims=True))).astype(bf16)


def head_back(probs, grads, values, delta):
    grad_probs = inner_cols(grads, values)
    return (probs.astype(f32) * (grad_probs - delta)).astype(bf16)


def enc_pre_kernel(x, vecs, w_qkv, query, key_value):
    normed, _ = norm_parts(x[...].astype(f32))
    attn_in = (normed * vecs[0:1] + vecs[1:2]).astype(bf16)
    mixed = product(attn_in, w_qkv[...]).astype(bf16)
    width = query.shape[1]
    query[...] = mixed[:, :width]
    key_value[...] = mixed[:, width:]


def enc_main_kernel(
    x, query, own_kv, other_kv, own_ids, all_ids, vecs, w_proj, w_up, w_down, w_embed,
    embedded, att, probs, middle, active, slope, out
):
    width = query.shape[1]
    head_size = width // HE
    bias = jnp.where(own_ids[...] == all_ids[...], 0.0, masked_score)
    masks = lane_masks(head_size, bf16)
    for pair in range(width // 128):
        cols = slice(128 * pair, 128 * pair + 128)
        value_cols = slice(width + 128 * pair, width + 128 * pair + 128)
        keys = jnp.concatenate([own_kv[:, cols], other_kv[:, cols]], axis=0)
        values = jnp.concatenate([own_kv[:, value_cols], other_kv[:, value_cols]], axis=0)
        total = jnp.zeros((query.shape[0], 128), f32)
        for head, mask in enumerate(masks):
            scores = inner_cols(query[:, cols] * mask, keys) + bias
            chances = softmax_rows(scores, 1.0 / math.sqrt(head_size))
            probs[len(masks) * pair + head] = chances
            total += product(chances, values * mask)
        att[:, cols] = total.astype(bf16)
    mid = x[...].astype(f32) + product(att[...], w_proj[...])
    middle[...] = mid
    normed, _ = norm_parts(mid)
    mlp_in = (normed * vecs[2:3] + vecs[3:4]).astype(bf16)
    result, steepness = gelu_parts(product(mlp_in, w_up[...]))
    active[...] = result.astype(bf16)
    slope[...] = steepness.astype(bf16)
    last = mid + product(active[...], w_down[...])
    out[...] = last
    normed, _ = norm_parts(last)
    final = (normed * vecs[4:5] + vecs[5:6]).astype(bf16)
    embedded[...] = product(final, w_embed[...]).astype(bf16)


def enc_lefts_kernel(core, x, middle, active, out, att, vecs, keep, leaving):
    def normed_input(values, row):
        normed, _ = norm_parts(values)
        return (normed * vecs[row : row + 1] + vecs[row + 1 : row + 2]).astype(bf16)

    chips = keep.shape[0]
    start = 0
    for values in (
        active[...],
        normed_input(middle[...], 2),
        att[...],
        normed_input(out[...], 4),
        normed_input(x[...].astype(f32), 0),
    ):
        turned = values.astype(f32).T.astype(bf16)
        count = turned.shape[0] // (2 * chips)
        for case in (0, 1):

            @pl.when(core[0] == case)
            def _():
                for image in range(2 * chips):
                    ref = keep if image % 2 == case else leaving
                    ref[image // 2, start : start + count] = turned[
                        image * count : (image + 1) * count
                    ]

        start += count


def chosen_rows(core, visible_rows):
    index = lax.broadcasted_iota(jnp.int32, (DEC_PAD, 1), 0)
    small = index + core * (SMALL + PATCHES)
    big = index + (SMALL - SMALL_PAD) + core * HALF
    row = jnp.where(index < SMALL, small, -1)
    row = jnp.where((index >= SMALL_PAD) & (index < SMALL_PAD + HALF), big, row)
    return (row == visible_rows).astype(f32)


def dec_pre_kernel(core, own, other, rows, code, vecs, w_qkv, dec_input, mixed, big_kv):
    chosen = chosen_rows(core[0], rows[...])
    seen = jnp.sum(chosen, axis=1, keepdims=True)
    tokens = jnp.concatenate([own[...], other[...]], axis=0)
    picked = product(chosen.astype(bf16), tokens)
    values = jnp.where(seen > 0.0, picked, vecs[4:5]) + code[...]
    dec_input[...] = values
    normed, _ = norm_parts(values)
    attn_in = (normed * vecs[0:1] + vecs[1:2]).astype(bf16)
    result = product(attn_in, w_qkv[...]).astype(bf16)
    mixed[...] = result
    big_kv[...] = result[SMALL_PAD:, values.shape[1] :]


def big_bias():
    column = lax.broadcasted_iota(jnp.int32, (1, 2 * BIG_PAD), 1)
    place = jnp.where(column >= BIG_PAD, column - BIG_PAD, column)
    return jnp.where(place < HALF, 0.0, masked_score)


def small_bias():
    column = lax.broadcasted_iota(jnp.int32, (1, SMALL_PAD), 1)
    return jnp.where(column < SMALL, 0.0, masked_score)


def dec_att_kernel(query, key, value, other_key, other_value, att, big_probs, small_probs):
    head_size = query.shape[1] * 4 // HD
    scale = 1.0 / math.sqrt(head_size)
    keys = jnp.concatenate([key[SMALL_PAD:], other_key[...]], axis=0)
    values = jnp.concatenate([value[SMALL_PAD:], other_value[...]], axis=0)
    total = jnp.zeros((BIG_PAD, 128), f32)
    small_total = jnp.zeros((SMALL_PAD, 128), f32)
    for head, mask in enumerate(lane_masks(head_size, bf16)):
        scores = inner_cols(query[SMALL_PAD:] * mask, keys) + big_bias()
        chances = softmax_rows(scores, scale)
        big_probs[head] = chances
        total += product(chances, values * mask)
        scores = inner_cols(query[:SMALL_PAD] * mask, key[:SMALL_PAD]) + small_bias()
        chances = softmax_rows(scores, scale)
        small_probs[head] = chances
        small_total += product(chances, value[:SMALL_PAD] * mask)
    att[:SMALL_PAD] = small_total.astype(bf16)
    att[SMALL_PAD:] = total.astype(bf16)


def dec_mid_kernel(
    chunk, core, dec_input, att, cot, vecs, w_proj, w_up, w_down,
    decoded, grad_middle, grad_att, vectors, *grads
):
    down_dest, up_dest, proj_dest = chunk.dests(grads)
    down_at, up_at, proj_at = chunk.offsets
    grad_down, grad_up = [], []
    middle = dec_input[...] + product(att[...], w_proj[...])
    normed, inverse = norm_parts(middle)
    mlp_in = (normed * vecs[2:3] + vecs[3:4]).astype(bf16)
    result = middle
    grad_norm = jnp.zeros_like(middle)
    step = 512
    for start in range(0, w_up.shape[1], step):
        cols = slice(start, start + step)
        active, slope = gelu_parts(product(mlp_in, w_up[:, cols]))
        active = active.astype(bf16)
        result += product(active, w_down[cols])
        grad_down.append(inner_rows(active, cot[...]).astype(bf16))
        grad_hidden = (slope * inner_cols(cot[...], w_down[cols])).astype(bf16)
        grad_up.append(inner_rows(mlp_in, grad_hidden).astype(bf16))
        grad_norm += inner_cols(grad_hidden, w_up[:, cols])
    decoded[...] = result.astype(bf16)
    grad_values, gain, shift = norm_backward(grad_norm, normed, inverse, vecs[2:3])
    vectors[0:1] = gain
    vectors[1:2] = shift
    back = cot[...].astype(f32) + grad_values
    grad_middle[...] = back
    low = back.astype(bf16)
    grad_att[...] = inner_cols(low, w_proj[...]).astype(bf16)
    put(core[0], proj_dest, proj_at, inner_rows(att[...], low))
    put(core[0], down_dest, down_at, jnp.concatenate(grad_down, axis=0))
    put(core[0], up_dest, up_at, jnp.concatenate(grad_up, axis=1))


def dec_att_back_kernel(
    query, key, value, other_key, other_value, grads, att, big_probs, small_probs,
    grad_query, grad_key, grad_value, leaving_key, leaving_value
):
    head_size = query.shape[1] * 4 // HD
    scale = 1.0 / math.sqrt(head_size)
    keys = jnp.concatenate([key[SMALL_PAD:], other_key[...]], axis=0)
    values = jnp.concatenate([value[SMALL_PAD:], other_value[...]], axis=0)
    overlap = grads[...].astype(f32) * att[...].astype(f32)
    big_q = jnp.zeros((BIG_PAD, 128), f32)
    big_k = jnp.zeros((2 * BIG_PAD, 128), f32)
    big_v = jnp.zeros((2 * BIG_PAD, 128), f32)
    small_q = jnp.zeros((SMALL_PAD, 128), f32)
    small_k = jnp.zeros((SMALL_PAD, 128), f32)
    small_v = jnp.zeros((SMALL_PAD, 128), f32)
    masks = lane_masks(head_size, f32)
    for head, mask in enumerate(lane_masks(head_size, bf16)):
        delta = jnp.sum(overlap * masks[head], axis=1, keepdims=True)
        one_query, one_grad = query[...] * mask, grads[...] * mask
        chances = big_probs[head]
        back = head_back(chances, one_grad[SMALL_PAD:], values, delta[SMALL_PAD:])
        big_q += product(back, keys * mask)
        big_k += inner_rows(back, one_query[SMALL_PAD:])
        big_v += inner_rows(chances, one_grad[SMALL_PAD:])
        chances = small_probs[head]
        back = head_back(chances, one_grad[:SMALL_PAD], value[:SMALL_PAD], delta[:SMALL_PAD])
        small_q += product(back, key[:SMALL_PAD] * mask)
        small_k += inner_rows(back, one_query[:SMALL_PAD])
        small_v += inner_rows(chances, one_grad[:SMALL_PAD])
    grad_query[:SMALL_PAD] = (small_q * scale).astype(bf16)
    grad_query[SMALL_PAD:] = (big_q * scale).astype(bf16)
    grad_key[:SMALL_PAD] = small_k * scale
    grad_key[SMALL_PAD:] = big_k[:BIG_PAD] * scale
    grad_value[:SMALL_PAD] = small_v
    grad_value[SMALL_PAD:] = big_v[:BIG_PAD]
    leaving_key[...] = (big_k[BIG_PAD:] * scale).astype(bf16)
    leaving_value[...] = big_v[BIG_PAD:].astype(bf16)


def dec_post_kernel(
    chunk, core, dec_input, grad_middle, grad_query, grad_key, grad_value, arrived_key,
    arrived_value, rows, vecs, w_qkv, own_spread, other_spread, vectors, *grads
):
    normed, inverse = norm_parts(dec_input[...])
    attn_in = (normed * vecs[0:1] + vecs[1:2]).astype(bf16)
    key = jnp.concatenate(
        [grad_key[:SMALL_PAD], grad_key[SMALL_PAD:] + arrived_key[...].astype(f32)], axis=0
    ).astype(bf16)
    value = jnp.concatenate(
        [grad_value[:SMALL_PAD], grad_value[SMALL_PAD:] + arrived_value[...].astype(f32)], axis=0
    ).astype(bf16)
    mixed = jnp.concatenate([grad_query[...], key, value], axis=1)
    grad_values, gain, shift = norm_backward(
        inner_cols(mixed, w_qkv[...]), normed, inverse, vecs[0:1]
    )
    back = grad_middle[...] + grad_values
    chosen = chosen_rows(core[0], rows[...])
    seen = jnp.sum(chosen, axis=1, keepdims=True)
    spread = inner_rows(chosen.astype(bf16), back.astype(bf16)).astype(bf16)
    own_spread[...] = spread[:ENC_PAD]
    other_spread[...] = spread[ENC_PAD:]
    vectors[0:1] = gain
    vectors[1:2] = shift
    vectors[2:3] = jnp.sum(jnp.where(seen > 0.0, 0.0, back), axis=0, keepdims=True)
    put(core[0], chunk.dests(grads)[0], chunk.offsets[0], inner_rows(attn_in, mixed))


def enc_mlp_back_kernel(
    first, second, core, own_spread, arrived, out, middle, active, slope,
    vecs, w_embed, w_down, w_up, w_proj, grad_middle, grad_att, vectors, *grads
):
    first_grads, second_grads = grads[: len(first.outs())], grads[len(first.outs()) :]
    grad_embedded = own_spread[...] + arrived[...]
    normed, inverse = norm_parts(out[...])
    grad_out, gain, shift = norm_backward(
        inner_cols(grad_embedded, w_embed[...]), normed, inverse, vecs[4:5]
    )
    vectors[2:3] = gain
    vectors[3:4] = shift
    low = grad_out.astype(bf16)
    put(core[0], first.dests(first_grads)[0], first.offsets[0], inner_rows(active[...], low))
    grad_hidden = (slope[...].astype(f32) * inner_cols(low, w_down[...])).astype(bf16)
    normed, inverse = norm_parts(middle[...])
    mlp_in = (normed * vecs[2:3] + vecs[3:4]).astype(bf16)
    put(
        core[0], second.dests(second_grads)[0], second.offsets[0], inner_rows(mlp_in, grad_hidden)
    )
    grad_values, gain, shift = norm_backward(
        inner_cols(grad_hidden, w_up[...]), normed, inverse, vecs[2:3]
    )
    vectors[0:1] = gain
    vectors[1:2] = shift
    back = grad_out + grad_values
    grad_middle[...] = back
    grad_att[...] = inner_cols(back.astype(bf16), w_proj[...]).astype(bf16)


def enc_att_back_kernel(
    grads, att, probs, query, own_kv, other_kv, grad_query, grad_kv, leaving
):
    width = query.shape[1]
    head_size = width // HE
    scale = 1.0 / math.sqrt(head_size)
    overlap = grads[...].astype(f32) * att[...].astype(f32)
    masks = lane_masks(head_size, bf16)
    wide_masks = lane_masks(head_size, f32)
    rows = query.shape[0]
    for pair in range(width // 128):
        cols = slice(128 * pair, 128 * pair + 128)
        value_cols = slice(width + 128 * pair, width + 128 * pair + 128)
        keys = jnp.concatenate([own_kv[:, cols], other_kv[:, cols]], axis=0)
        values = jnp.concatenate([own_kv[:, value_cols], other_kv[:, value_cols]], axis=0)
        total_q = jnp.zeros((rows, 128), f32)
        total_k = jnp.zeros((2 * rows, 128), f32)
        total_v = jnp.zeros((2 * rows, 128), f32)
        for head, mask in enumerate(masks):
            delta = jnp.sum(overlap[:, cols] * wide_masks[head], axis=1, keepdims=True)
            one_grad = grads[:, cols] * mask
            chances = probs[len(masks) * pair + head]
            one_back = head_back(chances, one_grad, values, delta)
            total_q += product(one_back, keys * mask)
            total_k += inner_rows(one_back, query[:, cols] * mask)
            total_v += inner_rows(chances, one_grad)
        grad_query[:, cols] = (total_q * scale).astype(bf16)
        grad_kv[:, cols] = total_k[:rows] * scale
        grad_kv[:, value_cols] = total_v[:rows]
        leaving[:, cols] = (total_k[rows:] * scale).astype(bf16)
        leaving[:, value_cols] = total_v[rows:].astype(bf16)


def enc_post_kernel(
    chunk, core, x, att, grad_middle, grad_query, grad_kv, arrived, out, own_spread, other_spread,
    vecs, w_qkv, grad_input, vectors, *grads
):
    qkv_dest, proj_dest, embed_dest = chunk.dests(grads)
    normed, _ = norm_parts(out[...])
    final = (normed * vecs[4:5] + vecs[5:6]).astype(bf16)
    put(
        core[0], embed_dest, chunk.offsets[2], inner_rows(final, own_spread[...] + other_spread[...])
    )
    put(
        core[0], proj_dest, chunk.offsets[1],
        inner_rows(att[...], grad_middle[...].astype(bf16)),
    )
    normed, inverse = norm_parts(x[...].astype(f32))
    attn_in = (normed * vecs[0:1] + vecs[1:2]).astype(bf16)
    key_value = (grad_kv[...] + arrived[...].astype(f32)).astype(bf16)
    mixed = jnp.concatenate([grad_query[...], key_value], axis=1)
    grad_values, gain, shift = norm_backward(
        inner_cols(mixed, w_qkv[...]), normed, inverse, vecs[0:1]
    )
    grad_input[...] = grad_middle[...] + grad_values
    vectors[0:1] = gain
    vectors[1:2] = shift
    put(core[0], qkv_dest, chunk.offsets[0], inner_rows(attn_in, mixed))


def permute(array, where_to):
    seq_count = lax.axis_size("seq")
    img_count = lax.axis_size("img")
    pairs = []
    for seq in range(seq_count):
        for img in range(img_count):
            seq_to, img_to = where_to(seq, img)
            pairs.append((seq * img_count + img, seq_to * img_count + img_to))
    return lax.ppermute(array, ("seq", "img"), pairs)


def swap(array):
    return permute(array, lambda seq, img: (seq, img ^ 1))


def pack_move(turn):
    def where_to(seq, img):
        return (2 * (img & 1) + (turn ^ (seq & 1)), (img & ~1) | (seq >> 1))

    return where_to


def exchange_packs(blocks, odd):
    rounds = [
        permute(jnp.where(odd, blocks[1 - turn], blocks[turn]), pack_move(turn)) for turn in (0, 1)
    ]
    return (jnp.where(odd, rounds[1], rounds[0]), jnp.where(odd, rounds[0], rounds[1]))


def pick(array, index, axis):
    return lax.dynamic_index_in_dim(array, index, axis, keepdims=False)


def pad_rows(array, rows):
    return jnp.pad(array, ((0, rows - array.shape[0]),) + ((0, 0),) * (array.ndim - 1))


def position_table(row_width):
    halfway = row_width // 2
    frequency = np.exp(np.arange(halfway, dtype=np.float64) * (-math.log(10000.0) / halfway))
    angles = np.arange(PATCHES, dtype=np.float64)[:, None] * frequency[None, :]
    return np.concatenate([np.sin(angles), np.cos(angles)], axis=1).astype(np.float32)


def reduce_pair(keep, leaving):
    return (keep.astype(f32) + swap(leaving).astype(f32)).astype(bf16)


MID_PIECES, POST_PIECES, DOWN_PIECES, UP_PIECES, ATT_PIECES = 3, 1, 3, 3, 4
DEC_PIECES = MID_PIECES + POST_PIECES
DOWN_AT = DEC_PIECES
UP_AT = DOWN_AT + DOWN_PIECES
ATT_AT = UP_AT + UP_PIECES
PIECES = ATT_AT + ATT_PIECES


class Refs:
    def __init__(self, names, refs):
        self.__dict__.update(zip(names, refs))


def sub_rows(row, count):
    done = 0
    while done < count:
        piece, place = (row + done) // SUB_ROWS, (row + done) % SUB_ROWS
        start = place % EIGHTH
        size = min(count - done, EIGHTH - start)
        place //= EIGHTH
        yield piece, place // 4, place // 2 % 2, place % 2, start, start + size, done
        done += size


def back_kernel(chips, names, *refs):
    r = Refs(names, refs)
    seq, img = lax.axis_index("seq"), lax.axis_index("img")
    chip, core = img // 2, lax.rem(img, 2)
    high, low = seq // 2, lax.rem(seq, 2)
    partner = {"img": img + 1 - 2 * core}
    along_x = {"seq": seq + 1 - 2 * low}
    along_y = {"seq": seq + 2 - 4 * high}
    others = [{"img": lax.rem(chip + step, chips) * 2 + core} for step in range(1, chips)]
    width, wide, narrow = r.w_embed.shape[0], r.w_up.shape[1], r.w_embed.shape[1]
    rows = ENC_PAD

    def remote(source, dest, sems, device):
        return pltpu.make_async_remote_copy(
            src_ref=source,
            dst_ref=dest,
            send_sem=sems.at[0],
            recv_sem=sems.at[1],
            device_id=device,
            device_id_type=pl.DeviceIdType.MESH,
        )

    def add(one, two):
        return (one.astype(f32) + two.astype(f32)).astype(bf16)

    held, first, second, from_chips, gathered = (
        r.held, r.first, r.second, r.from_chips, r.gathered
    )

    def pair_copy(i):
        return remote(r.leaving.at[i], r.from_pair.at[i], r.pair_sem.at[i], partner)

    def first_copies(i):
        return (
            remote(held.at[i, :, 0, :, 1 - low], first.at[i, 0], r.first_sem.at[i, 0], along_x),
            remote(held.at[i, :, 1, 1 - high], first.at[i, 1], r.first_sem.at[i, 1], along_y),
        )

    def second_copies(i):
        return (
            remote(
                held.at[i, :, 0, 1 - high, low], second.at[i, 0], r.second_sem.at[i, 0], along_y
            ),
            remote(
                held.at[i, :, 1, high, 1 - low], second.at[i, 1], r.second_sem.at[i, 1], along_x
            ),
        )

    def chip_copies(i):
        return [
            remote(
                held.at[i, device["img"] // 2, :, high, low],
                from_chips.at[i, step],
                r.chip_sem.at[i, step],
                device,
            )
            for step, device in enumerate(others)
        ]

    def gather_copies(i, arrive):
        x_place = 1 - low if arrive else low
        y_place = 1 - high if arrive else high
        one, two = gathered.at[i, 0, high, x_place], gathered.at[i, 1, y_place, low]
        return (
            remote(one, one, r.gather_sem.at[i, 0], along_x),
            remote(two, two, r.gather_sem.at[i, 1], along_y),
        )

    def spread_copies(i, arrive):
        x_place = 1 - low if arrive else low
        y_place = 1 - high if arrive else high
        one, two = gathered.at[i, 0, y_place], gathered.at[i, 1, :, x_place]
        return (
            remote(one, one, r.gather_sem.at[i, 2], along_y),
            remote(two, two, r.gather_sem.at[i, 3], along_x),
        )

    def share_copy(i):
        return pltpu.make_async_copy(gathered.at[i], r.shares.at[i], r.share_sem.at[i])

    def stage_pair(i):
        pair_copy(i).wait()
        for image in range(chips):
            held[i, image] = add(held[i, image], r.from_pair[i, image])

    def stage_first(i):
        for copy in first_copies(i):
            copy.start()

    def stage_second(i):
        for copy in first_copies(i):
            copy.wait_recv()
        held[i, :, 0, :, low] = add(held[i, :, 0, :, low], first[i, 0])
        held[i, :, 1, high] = add(held[i, :, 1, high], first[i, 1])
        for copy in second_copies(i):
            copy.start()

    def stage_chips(i):
        for copy in second_copies(i):
            copy.wait_recv()
        held[i, :, 0, high, low] = add(held[i, :, 0, high, low], second[i, 0])
        held[i, :, 1, high, low] = add(held[i, :, 1, high, low], second[i, 1])
        for copy in chip_copies(i):
            copy.start()

    def stage_gather(i):
        for copy in chip_copies(i):
            copy.wait_recv()
        mine = held[i, chip, :, high, low].astype(f32)
        for step in range(chips - 1):
            mine += from_chips[i, step].astype(f32)
        gathered[i, :, high, low] = mine.astype(bf16)
        for copy in gather_copies(i, False):
            copy.start()

    def stage_spread(i):
        for copy in gather_copies(i, True):
            copy.wait_recv()
        for copy in spread_copies(i, False):
            copy.start()

    def stage_end(i):
        for copy in spread_copies(i, True):
            copy.wait_recv()
        for copy in (
            *first_copies(i), *second_copies(i), *chip_copies(i), *gather_copies(i, False),
            *spread_copies(i, False),
        ):
            copy.wait_send()
        share_copy(i).start()

    stages = (stage_first, stage_second, stage_chips, stage_gather, stage_spread, stage_end)
    line = []

    def pump(piece):
        line.append(piece)
        for lag in range(len(stages)):
            slot = len(line) - 1 - lag
            if slot >= 0 and line[slot] is not None:
                stages[lag](line[slot])

    def home(turn):
        segment = turn + low - 2 * turn * low
        device = {"seq": 2 * core + segment, "img": 2 * chip + high}
        stays = (high == core) if turn == 0 else None
        return device, segment, stays

    def row_parts(segment):
        start = 288 * segment + 208 * core
        rest = (112 + start) * (1 - segment * core)
        return (
            (pl.ds(pl.multiple_of(start, 16), 112), slice(0, 112)),
            (pl.ds(pl.multiple_of(rest, 16), 208), slice(112, 320)),
        )

    def send_home(act, source_parts, sems):
        for turn in (0, 1):
            device, segment, stays = home(turn)
            for part, (source, dest) in enumerate(source_parts(segment)):
                sem = sems.at[turn, part]
                if stays is None:
                    act(remote(source, dest, sem, device), None)
                else:

                    @pl.when(stays)
                    def _():
                        act(None, pltpu.make_async_copy(source, dest, sem.at[0]))

                    @pl.when(jnp.logical_not(stays))
                    def _():
                        act(remote(source, dest, sem, device), None)

    def start_copy(away, local):
        (local if away is None else away).start()

    def wait_copy(away, local):
        (local if away is None else away).wait()

    def loader(base, items):
        copies = {}
        for index, (name, source, dest) in enumerate(items):
            copies[name] = pltpu.make_async_copy(source, dest, r.load_sem.at[base + index])
            copies[name].start()

        def need(*wanted):
            for name in wanted:
                copies[name].wait()

        return need

    peers = [partner, along_x, along_y, *others]

    def greet(device):
        pl.semaphore_signal(
            barrier, inc=1, device_id=device, device_id_type=pl.DeviceIdType.MESH
        )

    barrier = pltpu.get_barrier_semaphore()
    for device in peers:
        greet(device)
    greet(home(1)[0])

    @pl.when(high != core)
    def _():
        greet(home(0)[0])

    lefts_copy = remote(r.lefts_leaving, r.lefts_other, r.swap_sem.at[0], partner)

    def put_dec(grad, first_image, count, row):
        grad = grad.astype(bf16)
        for case in (0, 1):

            @pl.when(core == case)
            def _():
                for index in range(grad.shape[0] // count):
                    image = first_image + index
                    ref = held if image % 2 == case else r.leaving
                    for block in range(grad.shape[1] // LANES):
                        for piece, half, up, across, begin, end, at in sub_rows(
                            row + block * count, count
                        ):
                            ref[piece, image // 2, half, up, across, begin:end] = grad[
                                index * count + at : index * count + at + end - begin,
                                block * LANES : (block + 1) * LANES,
                            ]

    def decoder(
        dec_input, att, cot, w_proj, w_up, w_down, w_qkv, mixed, other_kv, chances,
        small_chances, decoded, grad_middle, grad_att, grad_mixed, grad_kv, kv_leaving,
    ):
        need = loader(
            0,
            (
                ("dec_input", r.dec_input, dec_input), ("att", r.dec_att, att),
                ("proj", r.dec_proj, w_proj), ("up", r.dec_up, w_up), ("cot", r.cot, cot),
                ("down", r.dec_down, w_down), ("mixed", r.dec_mixed, mixed),
                ("other", r.dec_other_kv, other_kv), ("qkv", r.dec_qkv, w_qkv),
            ),
        )

        def chance_copies(head, slot):
            return (
                pltpu.make_async_copy(
                    r.big_probs.at[head], chances.at[slot], r.chance_sem.at[slot, 0]
                ),
                pltpu.make_async_copy(
                    r.small_probs.at[head], small_chances.at[slot], r.chance_sem.at[slot, 1]
                ),
            )

        for copy in chance_copies(0, 0):
            copy.start()
        pl.semaphore_wait(barrier, len(peers) + 1 + jnp.where(high == core, 0, 1))
        lefts_copy.start()

        need("dec_input", "att", "proj")
        vecs = r.dec_vecs
        middle = dec_input[...] + product(att[...], w_proj[...])
        normed, inverse = norm_parts(middle)
        mlp_in = (normed * vecs[2:3] + vecs[3:4]).astype(bf16)
        result = middle
        grad_norm = jnp.zeros_like(middle)
        step = 2 * w_down.shape[0] // (2 * chips)
        down_count, up_count = step // 2, narrow // (2 * chips)
        up_row = down_count * narrow // LANES
        proj_row = up_row + up_count * w_up.shape[1] // LANES
        need("up", "cot", "down")
        for block in range(w_up.shape[1] // step):
            cols = slice(block * step, (block + 1) * step)
            active, slope = gelu_parts(product(mlp_in, w_up[:, cols]))
            active = active.astype(bf16)
            result += product(active, w_down[cols])
            put_dec(inner_rows(active, cot[...]), 2 * block, down_count, 0)
            grad_hidden = (slope * inner_cols(cot[...], w_down[cols])).astype(bf16)
            put_dec(
                inner_rows(mlp_in, grad_hidden), 0, up_count,
                up_row + up_count * block * step // LANES,
            )
            grad_norm += inner_cols(grad_hidden, w_up[:, cols])
        decoded[...] = result.astype(bf16)

        def decoded_parts(segment):
            return [
                (decoded.at[source], r.home_rows.at[low, dest])
                for source, dest in row_parts(segment)
            ]

        send_home(start_copy, decoded_parts, r.rows_sem)
        grad_values, gain, shift = norm_backward(grad_norm, normed, inverse, vecs[2:3])
        r.vec_own[...] = jnp.zeros(r.vec_own.shape, f32)
        r.vec_own[10:11, :narrow] = gain
        r.vec_own[11:12, :narrow] = shift
        back = cot[...].astype(f32) + grad_values
        grad_middle[...] = back
        back = back.astype(bf16)
        grad_att[...] = inner_cols(back, w_proj[...]).astype(bf16)
        put_dec(inner_rows(att[...], back), 0, up_count, proj_row)
        for i in range(MID_PIECES):
            pair_copy(i).start()

        need("mixed", "other")
        head_size = narrow // HD
        per_group = 128 // head_size
        scale = 1.0 / math.sqrt(head_size)
        masks, wide_masks = lane_masks(head_size, bf16), lane_masks(head_size, f32)

        def group_back(group, last):
            def cols(offset):
                return pl.ds(pl.multiple_of(offset * narrow + group * 128, 128), 128)

            query = mixed[:, cols(0)]
            small_key, small_value = mixed[:SMALL_PAD, cols(1)], mixed[:SMALL_PAD, cols(2)]
            keys = jnp.concatenate([mixed[SMALL_PAD:, cols(1)], other_kv[:, cols(0)]], axis=0)
            values = jnp.concatenate([mixed[SMALL_PAD:, cols(2)], other_kv[:, cols(1)]], axis=0)
            grads = grad_att[:, cols(0)]
            overlap = grads.astype(f32) * att[:, cols(0)].astype(f32)
            big_q = jnp.zeros((BIG_PAD, 128), f32)
            big_k = jnp.zeros((2 * BIG_PAD, 128), f32)
            big_v = jnp.zeros((2 * BIG_PAD, 128), f32)
            small_q = jnp.zeros((SMALL_PAD, 128), f32)
            small_k = jnp.zeros((SMALL_PAD, 128), f32)
            small_v = jnp.zeros((SMALL_PAD, 128), f32)
            for head, mask in enumerate(masks):
                slot = head % 2
                number = group * per_group + head
                for copy in chance_copies(number, slot):
                    copy.wait()
                if head < per_group - 1:
                    for copy in chance_copies(number + 1, 1 - slot):
                        copy.start()
                else:

                    @pl.when(group < last)
                    def _():
                        for copy in chance_copies(number + 1, 1 - slot):
                            copy.start()

                delta = jnp.sum(overlap * wide_masks[head], axis=1, keepdims=True)
                one_query, one_grad = query * mask, grads * mask
                probs = chances[slot]
                one = head_back(probs, one_grad[SMALL_PAD:], values, delta[SMALL_PAD:])
                big_q += product(one, keys * mask)
                big_k += inner_rows(one, one_query[SMALL_PAD:])
                big_v += inner_rows(probs, one_grad[SMALL_PAD:])
                probs = small_chances[slot]
                one = head_back(probs, one_grad[:SMALL_PAD], small_value, delta[:SMALL_PAD])
                small_q += product(one, small_key * mask)
                small_k += inner_rows(one, one_query[:SMALL_PAD])
                small_v += inner_rows(probs, one_grad[:SMALL_PAD])
            grad_mixed[:SMALL_PAD, cols(0)] = (small_q * scale).astype(bf16)
            grad_mixed[SMALL_PAD:, cols(0)] = (big_q * scale).astype(bf16)
            grad_mixed[:SMALL_PAD, cols(1)] = (small_k * scale).astype(bf16)
            grad_mixed[:SMALL_PAD, cols(2)] = small_v.astype(bf16)
            grad_kv[:, cols(0)] = big_k[:BIG_PAD] * scale
            grad_kv[:, cols(1)] = big_v[:BIG_PAD]
            kv_leaving[:, cols(0)] = (big_k[BIG_PAD:] * scale).astype(bf16)
            kv_leaving[:, cols(1)] = big_v[BIG_PAD:].astype(bf16)

        groups = narrow // 128
        for group in range(groups):
            lax.fori_loop(
                group, group + 1, lambda g, c: (group_back(g, groups - 1), c)[1], 0
            )
            if group < MID_PIECES:
                stage_pair(group)
                pump(group)
        kv_copy = remote(kv_leaving, r.dec_kv_in, r.swap_sem.at[1], partner)
        kv_copy.start()
        pump(None)

        normed, inverse = norm_parts(dec_input[...])
        attn_in = (normed * vecs[0:1] + vecs[1:2]).astype(bf16)
        chosen = chosen_rows(core, r.row_ids[...])
        seen = jnp.sum(chosen, axis=1, keepdims=True)
        need("qkv")
        kv_copy.wait()
        grad_mixed[SMALL_PAD:, narrow:] = (grad_kv[...] + r.dec_kv_in[...].astype(f32)).astype(bf16)
        grad_values, gain, shift = norm_backward(
            inner_cols(grad_mixed[...], w_qkv[...]), normed, inverse, vecs[0:1]
        )
        r.vec_own[8:9, :narrow] = gain
        r.vec_own[9:10, :narrow] = shift
        back = grad_middle[...] + grad_values
        spread = inner_rows(chosen.astype(bf16), back.astype(bf16)).astype(bf16)
        r.spread_own[...] = spread[:rows]
        r.spread_leaving[...] = spread[rows:]
        spread_copy.start()
        r.vec_own[12:13, :narrow] = jnp.sum(
            jnp.where(seen > 0.0, 0.0, back), axis=0, keepdims=True
        )
        put_dec(inner_rows(attn_in, grad_mixed[...]), 0, up_count, MID_PIECES * SUB_ROWS)
        pair_copy(MID_PIECES).start()
        send_home(wait_copy, decoded_parts, r.rows_sem)

    spread_copy = remote(r.spread_leaving, r.spread_in, r.swap_sem.at[2], partner)
    dec_rows, big = DEC_PAD, BIG_PAD
    pl.run_scoped(
        decoder,
        pltpu.VMEM((dec_rows, narrow), f32),
        pltpu.VMEM((dec_rows, narrow), bf16),
        pltpu.VMEM((dec_rows, narrow), bf16),
        pltpu.VMEM(r.dec_proj.shape, bf16),
        pltpu.VMEM(r.dec_up.shape, bf16),
        pltpu.VMEM(r.dec_down.shape, bf16),
        pltpu.VMEM(r.dec_qkv.shape, bf16),
        pltpu.VMEM((dec_rows, 3 * narrow), bf16),
        pltpu.VMEM((big, 2 * narrow), bf16),
        pltpu.VMEM((2, big, 2 * big), bf16),
        pltpu.VMEM((2, SMALL_PAD, SMALL_PAD), bf16),
        pltpu.VMEM((dec_rows, narrow), bf16),
        pltpu.VMEM((dec_rows, narrow), f32),
        pltpu.VMEM((dec_rows, narrow), bf16),
        pltpu.VMEM((dec_rows, 3 * narrow), bf16),
        pltpu.VMEM((big, 2 * narrow), f32),
        pltpu.VMEM((big, 2 * narrow), bf16),
    )

    def encoder(
        v_embed, v_down, v_up, v_proj, v_out, v_middle, v_slope, v_att, v_probs, v_query,
        v_own_kv, v_other_kv, v_x, v_lefts, right_own, kv_own, kv_leaving, grad_rows,
    ):
        need = loader(
            9,
            (
                ("embed", r.w_embed, v_embed), ("out", r.out, v_out), ("down", r.w_down, v_down),
                ("slope", r.slope, v_slope), ("lefts", r.lefts_own, v_lefts),
                ("up", r.w_up, v_up), ("middle", r.middle, v_middle), ("proj", r.w_proj, v_proj),
                ("att", r.att, v_att), ("probs", r.probs, v_probs), ("query", r.query, v_query),
                ("own_kv", r.own_kv, v_own_kv), ("other_kv", r.other_kv, v_other_kv),
                ("x", r.x, v_x),
            ),
        )
        vecs = r.enc_vecs
        places = {}
        start = 0
        for name, columns in (
            ("out", width), ("hidden", wide), ("embedded", narrow), ("middle", width),
            ("mixed", 3 * width),
        ):
            places[name] = slice(start, start + columns)
            start += columns
        swaps = {}

        def give(name, value, index):
            cols = places[name]
            if value is not None:
                right_own[:, cols] = value
            swaps[name] = remote(
                right_own.at[:, cols], r.right_other.at[:, cols], r.swap_sem.at[index], partner
            )
            swaps[name].start()

        def weight_grad(name, left, count, row):
            cols = places[name]
            own = v_lefts[:, left : left + count].reshape(chips * count, rows)
            other = r.lefts_other[:, left : left + count].reshape(chips * count, rows)
            for block in range((cols.stop - cols.start) // LANES):
                columns = slice(cols.start + block * LANES, cols.start + (block + 1) * LANES)
                grad = product(own, right_own[:, columns]) + product(
                    other, r.right_other[:, columns]
                )
                grad = grad.astype(bf16)
                for piece, half, up, across, begin, end, at in sub_rows(
                    row + block * count, count
                ):
                    for image in range(chips):
                        held[piece, image, half, up, across, begin:end] = grad[
                            image * count + at : image * count + at + end - begin
                        ]

        lefts = {}
        start = 0
        left_hidden, left_mid = wide // (2 * chips), width // (2 * chips)
        for name, count in (
            ("hidden", left_hidden), ("mlp_in", left_mid), ("att", left_mid), ("final", left_mid),
            ("attn_in", left_mid),
        ):
            lefts[name] = start
            start += count

        spread_copy.wait()
        grad_embedded = r.spread_own[...] + r.spread_in[...]
        give("embedded", grad_embedded, 3)
        need("embed", "out")
        normed, inverse = norm_parts(v_out[...])
        grad_out, gain, shift = norm_backward(
            inner_cols(grad_embedded, v_embed[...]), normed, inverse, vecs[4:5]
        )
        r.vec_own[4:5] = gain
        r.vec_own[5:6] = shift
        grad_low = grad_out.astype(bf16)
        give("out", grad_low, 4)
        need("down", "slope")
        grad_hidden = (v_slope[...].astype(f32) * inner_cols(grad_low, v_down[...])).astype(bf16)
        qkv_copies = [
            pltpu.make_async_copy(
                r.w_qkv.at[:, part * width : (part + 1) * width],
                v_down.at[part * width : (part + 1) * width],
                r.load_sem.at[23 + part],
            )
            for part in range(3)
        ]
        for copy in qkv_copies:
            copy.start()
        give("hidden", grad_hidden, 5)
        stage_pair(MID_PIECES)
        pump(MID_PIECES)
        need("lefts")
        lefts_copy.wait()
        swaps["out"].wait()
        weight_grad("out", lefts["hidden"], left_hidden, DOWN_AT * SUB_ROWS)
        pump(DOWN_AT)
        need("up", "middle", "proj")
        normed, inverse = norm_parts(v_middle[...])
        grad_values, gain, shift = norm_backward(
            inner_cols(grad_hidden, v_up[...]), normed, inverse, vecs[2:3]
        )
        r.vec_own[2:3] = gain
        r.vec_own[3:4] = shift
        grad_middle = grad_out + grad_values
        grad_low = grad_middle.astype(bf16)
        give("middle", grad_low, 6)
        grads = inner_cols(grad_low, v_proj[...]).astype(bf16)

        need("att", "probs", "query", "own_kv", "other_kv")
        head_size = width // HE
        scale = 1.0 / math.sqrt(head_size)
        overlap = grads.astype(f32) * v_att[...].astype(f32)
        masks = lane_masks(head_size, bf16)
        wide_masks = lane_masks(head_size, f32)
        mixed_at = places["mixed"].start
        for pair in range(width // 128):
            cols = slice(128 * pair, 128 * pair + 128)
            value_cols = slice(width + 128 * pair, width + 128 * pair + 128)
            keys = jnp.concatenate([v_own_kv[:, cols], v_other_kv[:, cols]], axis=0)
            values = jnp.concatenate([v_own_kv[:, value_cols], v_other_kv[:, value_cols]], axis=0)
            total_q = jnp.zeros((rows, 128), f32)
            total_k = jnp.zeros((2 * rows, 128), f32)
            total_v = jnp.zeros((2 * rows, 128), f32)
            for head, mask in enumerate(masks):
                delta = jnp.sum(overlap[:, cols] * wide_masks[head], axis=1, keepdims=True)
                one_grad = grads[:, cols] * mask
                chances = v_probs[len(masks) * pair + head]
                one_back = head_back(chances, one_grad, values, delta)
                total_q += product(one_back, keys * mask)
                total_k += inner_rows(one_back, v_query[:, cols] * mask)
                total_v += inner_rows(chances, one_grad)
            right_own[:, mixed_at + 128 * pair : mixed_at + 128 * pair + 128] = (
                total_q * scale
            ).astype(bf16)
            kv_own[:, cols] = total_k[:rows] * scale
            kv_own[:, value_cols] = total_v[:rows]
            kv_leaving[:, cols] = (total_k[rows:] * scale).astype(bf16)
            kv_leaving[:, value_cols] = total_v[rows:].astype(bf16)
        kv_copy = remote(kv_leaving, r.kv_in, r.swap_sem.at[7], partner)
        kv_copy.start()
        pump(DOWN_AT + 1)
        swaps["hidden"].wait()
        weight_grad("hidden", lefts["mlp_in"], left_mid, UP_AT * SUB_ROWS)
        pump(DOWN_AT + 2)

        kv_copy.wait()
        right_own[:, mixed_at + width : mixed_at + 3 * width] = (
            kv_own[...] + r.kv_in[...].astype(f32)
        ).astype(bf16)
        give("mixed", None, 8)
        need("x")
        normed, inverse = norm_parts(v_x[...].astype(f32))
        grad_norm = jnp.zeros((rows, width), f32)
        for part, copy in enumerate(qkv_copies):
            copy.wait()
            place = mixed_at + part * width
            grad_norm += inner_cols(
                right_own[:, place : place + width], v_down[part * width : (part + 1) * width]
            )
        grad_values, gain, shift = norm_backward(grad_norm, normed, inverse, vecs[0:1])
        r.vec_own[0:1] = gain
        r.vec_own[1:2] = shift
        vec_copy = remote(r.vec_own, r.vec_in, r.swap_sem.at[9], partner)
        vec_copy.start()
        grad_values = grad_middle + grad_values
        grad_rows[0] = grad_values[: rows // 2]
        grad_rows[1] = grad_values[rows // 2 :]

        def grad_parts(segment):
            return [(grad_rows.at[segment], r.home_grad.at[low])]

        send_home(start_copy, grad_parts, r.grad_sem)
        pump(UP_AT)
        swaps["middle"].wait()
        swaps["embedded"].wait()
        embed_row = ATT_AT * SUB_ROWS + left_mid * width // LANES
        weight_grad("middle", lefts["att"], left_mid, ATT_AT * SUB_ROWS)
        weight_grad("embedded", lefts["final"], left_mid, embed_row)
        pump(UP_AT + 1)
        swaps["mixed"].wait()
        qkv_row = embed_row + left_mid * narrow // LANES
        weight_grad("mixed", lefts["attn_in"], left_mid, qkv_row)
        pump(UP_AT + 2)
        vec_copy.wait()
        vectors = (r.vec_own[...] + r.vec_in[...]).astype(bf16)
        vec_row = qkv_row + left_mid * 3 * width // LANES
        piece, half, up, across, begin, end, _ = next(iter(sub_rows(vec_row, 16)))
        entry = lax.broadcasted_iota(jnp.int32, (width, LANES), 0)
        lane = lax.broadcasted_iota(jnp.int32, (width, LANES), 1)
        row_index = lax.broadcasted_iota(jnp.int32, (16, LANES), 0)
        narrow_left = narrow // (2 * chips)
        for image in range(chips):
            number = 2 * image + core
            enc_pick = (entry == lane + number * left_mid) & (lane < left_mid)
            dec_pick = (entry == lane + number * narrow_left) & (lane < narrow_left)
            enc_part = product(vectors, enc_pick.astype(f32).astype(bf16))
            dec_part = product(vectors, dec_pick.astype(f32).astype(bf16))
            held[piece, image, half, up, across, begin:end] = jnp.where(
                row_index < 8, enc_part, dec_part
            ).astype(bf16)
        for piece in range(ATT_AT, PIECES):
            pump(piece)
        send_home(wait_copy, grad_parts, r.grad_sem)

    pl.run_scoped(
        encoder,
        pltpu.VMEM(r.w_embed.shape, bf16),
        pltpu.VMEM(r.w_down.shape, bf16),
        pltpu.VMEM(r.w_up.shape, bf16),
        pltpu.VMEM(r.w_proj.shape, bf16),
        pltpu.VMEM(r.out.shape, f32),
        pltpu.VMEM(r.middle.shape, f32),
        pltpu.VMEM(r.slope.shape, bf16),
        pltpu.VMEM(r.att.shape, bf16),
        pltpu.VMEM(r.probs.shape, bf16),
        pltpu.VMEM(r.query.shape, bf16),
        pltpu.VMEM(r.own_kv.shape, bf16),
        pltpu.VMEM(r.other_kv.shape, bf16),
        pltpu.VMEM(r.x.shape, bf16),
        pltpu.VMEM(r.lefts_own.shape, bf16),
        pltpu.VMEM(r.right_other.shape, bf16),
        pltpu.VMEM((rows, 2 * width), f32),
        pltpu.VMEM((rows, 2 * width), bf16),
        pltpu.VMEM((2, ENC_SEG, width), f32),
    )
    for _ in range(len(stages) - 1):
        pump(None)
    lax.fori_loop(0, PIECES, lambda i, c: (share_copy(i).wait(), c)[1], 0)


def back(chips, args):
    anywhere = pl.BlockSpec(memory_space=pl.ANY)
    vmem = pl.BlockSpec(memory_space=pltpu.VMEM)
    block = (EIGHTH, LANES)
    dma = pltpu.SemaphoreType.DMA
    width, narrow = args["w_embed"].shape
    wide = args["w_up"].shape[1]
    rights = width + wide + narrow + width + 3 * width
    outs = {
        "shares": ((PIECES, 2, 2, 2) + block, bf16),
        "home_rows": ((2, 320, narrow), bf16),
        "home_grad": ((2, ENC_SEG, width), f32),
    }
    scratch = {
        "held": pltpu.VMEM((PIECES, chips, 2, 2, 2) + block, bf16),
        "leaving": pltpu.VMEM((DEC_PIECES, chips, 2, 2, 2) + block, bf16),
        "from_pair": pltpu.VMEM((DEC_PIECES, chips, 2, 2, 2) + block, bf16),
        "first": pltpu.VMEM((PIECES, 2, chips, 2) + block, bf16),
        "second": pltpu.VMEM((PIECES, 2, chips) + block, bf16),
        "from_chips": pltpu.VMEM((PIECES, chips - 1, 2) + block, bf16),
        "gathered": pltpu.VMEM((PIECES, 2, 2, 2) + block, bf16),
        "dec_kv_in": pltpu.VMEM((BIG_PAD, 2 * narrow), bf16),
        "spread_own": pltpu.VMEM((ENC_PAD, narrow), bf16),
        "spread_leaving": pltpu.VMEM((ENC_PAD, narrow), bf16),
        "spread_in": pltpu.VMEM((ENC_PAD, narrow), bf16),
        "lefts_other": pltpu.VMEM(args["lefts_own"].shape, bf16),
        "right_other": pltpu.VMEM((ENC_PAD, rights), bf16),
        "kv_in": pltpu.VMEM((ENC_PAD, 2 * width), bf16),
        "vec_own": pltpu.VMEM((16, width), f32),
        "vec_in": pltpu.VMEM((16, width), f32),
        "load_sem": dma((26,)),
        "chance_sem": dma((2, 2)),
        "pair_sem": dma((DEC_PIECES, 2)),
        "first_sem": dma((PIECES, 2, 2)),
        "second_sem": dma((PIECES, 2, 2)),
        "chip_sem": dma((PIECES, chips - 1, 2)),
        "gather_sem": dma((PIECES, 4, 2)),
        "share_sem": dma((PIECES,)),
        "swap_sem": dma((10, 2)),
        "rows_sem": dma((2, 2, 2)),
        "grad_sem": dma((2, 1, 2)),
    }
    names = list(args) + list(outs) + list(scratch)
    in_vmem = ("row_ids", "dec_vecs", "enc_vecs")
    return pl.pallas_call(
        functools.partial(back_kernel, chips, names),
        out_shape=[jax.ShapeDtypeStruct(shape, kind) for shape, kind in outs.values()],
        in_specs=[vmem if name in in_vmem else anywhere for name in args],
        out_specs=[anywhere] * len(outs),
        scratch_shapes=list(scratch.values()),
        compiler_params=pltpu.CompilerParams(
            collective_id=1, has_side_effects=True, vmem_limit_bytes=63 << 20
        ),
    )(*args.values())


def unstack_kernel(counts, enc_count, dec_count, flat, *outs):
    place = 0
    for out, count in zip(outs, counts):
        for block in range(out.shape[1] // LANES):
            out[:, block * LANES : (block + 1) * LANES] = flat[place : place + count].astype(f32)
            place += count
    turned = flat[place : place + 16].astype(f32).T
    outs[-2][...] = turned[:enc_count, :6]
    outs[-1][...] = turned[:dec_count, 8:13]


def reduce_rest(chunk, seq):
    chips, rows, width = chunk.shape
    high, low = seq // 2, seq % 2
    eighth = rows // 8
    parts = chunk.reshape(chips, 2, 2, 2, eighth, width)

    def along_x(array):
        return permute(array, lambda s, i: (s ^ 1, i))

    def along_y(array):
        return permute(array, lambda s, i: (s ^ 2, i))

    def add(one, two):
        return (one.astype(f32) + two.astype(f32)).astype(bf16)

    one, two = parts[:, 0], parts[:, 1]
    one = add(pick(one, low, 2), along_x(pick(one, 1 - low, 2)))
    two = add(pick(two, high, 1), along_y(pick(two, 1 - high, 1)))
    one = add(pick(one, high, 1), along_y(pick(one, 1 - high, 1)))
    two = add(pick(two, low, 1), along_x(pick(two, 1 - low, 1)))
    mine = jnp.stack([one, two], axis=1)
    chip = lax.axis_index("img") // 2
    total = pick(mine, chip, 0).astype(f32)
    for step in range(1, chips):
        leaving = pick(mine, (chip + step) % chips, 0)
        arrived = permute(
            leaving,
            lambda s, i, step=step: (s, ((i // 2 + step) % chips) * 2 + (i & 1)),
        )
        total = total + arrived.astype(f32)
    own = total.astype(bf16)
    others = [permute(own, lambda s, i, step=step: (s ^ step, i)) for step in (1, 2, 3)]
    by_xor = jnp.stack([own] + others)
    ordered = jnp.stack([pick(by_xor, seq ^ place, 0) for place in range(4)], axis=1)
    return ordered.reshape(rows, width)


def shards(
    enc_input,
    cotangent,
    enc_image,
    visible_rows,
    enc_norms,
    enc_qkv,
    enc_proj,
    enc_up,
    enc_down,
    embed,
    dec_vecs,
    dec_qkv,
    dec_proj,
    dec_up,
    dec_down,
):
    seq = lax.axis_index("seq")
    img = lax.axis_index("img")
    images = lax.axis_size("img")
    core = img % 2
    odd = seq % 2 == 1
    enc_width = enc_input.shape[3]
    dec_width = dec_vecs.shape[0]
    enc_half = 2 * enc_input.shape[2]
    dec_quarter = cotangent.shape[2]

    enc_vecs = jnp.pad(enc_norms.T, ((0, 2), (0, 0)))
    dec_rows_vecs = jnp.pad(dec_vecs.T, ((0, 3), (0, 0)))
    tables = jnp.stack([enc_image[0], visible_rows[0]])
    other_tables = swap(tables)
    tables = jnp.where(seq // 2 == core, tables, other_tables)
    tables = jnp.where(odd, tables[:, 1], tables[:, 0])
    segments = tables.reshape(2, 2, 2, enc_half // 2)
    segments = jnp.pad(
        segments, ((0, 0),) * 3 + ((0, ENC_SEG - enc_half // 2),), constant_values=-2
    )
    halves = segments.reshape(2, 2, ENC_PAD)
    own = pick(halves, core, 1)
    ids = jnp.concatenate([own, pick(halves, 1 - core, 1)], axis=1)
    row_ids = ids[1:2]
    core_arg = core.reshape(1)

    blocks = jnp.pad(enc_input[0], ((0, 0), (0, ENC_SEG - enc_half // 2), (0, 0)))
    x = jnp.concatenate(exchange_packs(blocks, odd), axis=0)
    cot = jnp.concatenate(exchange_packs(cotangent[0], odd), axis=0)
    cot = jnp.concatenate(
        [
            pad_rows(lax.dynamic_slice_in_dim(cot, core * HALF, SMALL, 0), SMALL_PAD),
            pad_rows(lax.dynamic_slice_in_dim(cot, (1 - core) * SMALL, HALF, 0), BIG_PAD),
        ],
        axis=0,
    )
    enc_hidden_width = enc_up.shape[1]

    enc_query, enc_kv = call(
        enc_pre_kernel,
        0,
        [((ENC_PAD, enc_width), bf16), ((ENC_PAD, 2 * enc_width), bf16)],
        (x, enc_vecs, enc_qkv),
        40,
    )
    enc_other = swap(enc_kv)
    embedded, enc_att, enc_probs, enc_middle, enc_active, enc_slope, enc_out = call(
        enc_main_kernel,
        0,
        [
            ((ENC_PAD, dec_width), bf16),
            ((ENC_PAD, enc_width), bf16),
            ((HE, ENC_PAD, 2 * ENC_PAD), bf16),
            ((ENC_PAD, enc_width), f32),
            ((ENC_PAD, enc_hidden_width), bf16),
            ((ENC_PAD, enc_hidden_width), bf16),
            ((ENC_PAD, enc_width), f32),
        ],
        (
            x, enc_query, enc_kv, enc_other, own[0][:, None], ids[0:1], enc_vecs,
            enc_proj, enc_up, enc_down, embed,
        ),
        48,
    )

    table = position_table(dec_width)
    codes = np.zeros((2, DEC_PAD, dec_width), np.float32)
    for which in range(2):
        codes[which, :SMALL] = table[:SMALL]
        codes[which, SMALL_PAD : SMALL_PAD + HALF] = table[which * HALF : (which + 1) * HALF]
    code = pick(jnp.asarray(codes), core, 0)
    dec_input, dec_mixed, big_kv = call(
        dec_pre_kernel,
        1,
        [
            ((DEC_PAD, dec_width), f32),
            ((DEC_PAD, 3 * dec_width), bf16),
            ((BIG_PAD, 2 * dec_width), bf16),
        ],
        (core_arg, embedded, swap(embedded), row_ids, code, dec_rows_vecs, dec_qkv),
        40,
    )
    other_kv = swap(big_kv)
    groups = dec_width // 128

    def columns(rows, offset=0):
        return pl.BlockSpec((rows, 128), lambda group: (0, offset + group))

    def heads(rows, cols):
        return pl.BlockSpec((HD // groups, rows, cols), lambda group: (group, 0, 0))

    qkv_specs = [
        columns(DEC_PAD),
        columns(DEC_PAD, groups),
        columns(DEC_PAD, 2 * groups),
        columns(BIG_PAD),
        columns(BIG_PAD, groups),
    ]
    qkv_args = (dec_mixed, dec_mixed, dec_mixed, other_kv, other_kv)
    prob_specs = [heads(BIG_PAD, 2 * BIG_PAD), heads(SMALL_PAD, SMALL_PAD)]
    dec_att, big_probs, small_probs = pl.pallas_call(
        dec_att_kernel,
        grid=(groups,),
        in_specs=qkv_specs,
        out_specs=[columns(DEC_PAD)] + prob_specs,
        out_shape=[
            jax.ShapeDtypeStruct((DEC_PAD, dec_width), bf16),
            jax.ShapeDtypeStruct((HD, BIG_PAD, 2 * BIG_PAD), bf16),
            jax.ShapeDtypeStruct((HD, SMALL_PAD, SMALL_PAD), bf16),
        ],
        compiler_params=pltpu.CompilerParams(vmem_limit_bytes=48 << 20),
    )(*qkv_args)
    chips = images // 2
    if images == 8:
        left_rows = (4 * enc_width + enc_hidden_width) // images
        lefts_keep, lefts_leaving = call(
            enc_lefts_kernel,
            1,
            [((chips, left_rows, ENC_PAD), bf16)] * 2,
            (core_arg, x, enc_middle, enc_active, enc_out, enc_att, enc_vecs),
            40,
        )
        shares, home_rows, home_grad = back(
            chips,
            {
                "dec_input": dec_input,
                "dec_att": dec_att,
                "cot": cot,
                "dec_proj": dec_proj,
                "dec_up": dec_up,
                "dec_down": dec_down,
                "dec_qkv": dec_qkv,
                "dec_mixed": dec_mixed,
                "dec_other_kv": other_kv,
                "big_probs": big_probs,
                "small_probs": small_probs,
                "row_ids": row_ids,
                "dec_vecs": dec_rows_vecs,
                "enc_vecs": enc_vecs,
                "w_embed": embed,
                "w_down": enc_down,
                "w_up": enc_up,
                "w_proj": enc_proj,
                "w_qkv": enc_qkv,
                "out": enc_out,
                "middle": enc_middle,
                "slope": enc_slope,
                "att": enc_att,
                "probs": enc_probs,
                "query": enc_query,
                "own_kv": enc_kv,
                "other_kv": enc_other,
                "x": x,
                "lefts_own": lefts_keep,
                "lefts_leaving": lefts_leaving,
            },
        )
        shapes = (
            dec_down.shape, dec_up.shape, dec_proj.shape, dec_qkv.shape, enc_down.shape,
            enc_up.shape, enc_proj.shape, embed.shape, enc_qkv.shape,
        )
        counts = [shape[0] // images for shape in shapes]
        (
            dec_down_share, dec_up_share, dec_proj_share, dec_qkv_share, enc_down_share,
            enc_up_share, enc_proj_share, embed_share, enc_qkv_share, enc_norm_share,
            dec_vec_share,
        ) = call(
            functools.partial(
                unstack_kernel, counts, enc_width // images, dec_width // images
            ),
            0,
            [((count, shape[1]), f32) for count, shape in zip(counts, shapes)]
            + [((enc_width // images, 6), f32), ((dec_width // images, 5), f32)],
            (shares.reshape(-1, LANES),),
            40,
        )
        grad_input = home_grad[None, :, : enc_half // 2]
        row = jnp.arange(dec_quarter, dtype=jnp.int32)[None, :, None]

        def by_seq(*numbers):
            return jnp.asarray(numbers, jnp.int32)[seq]

        begin = lax.dynamic_slice_in_dim(home_rows, by_seq(0, 18, 0, 6), dec_quarter, 1)
        end = lax.dynamic_slice_in_dim(home_rows, by_seq(12, 18, 0, 14), dec_quarter, 1)
        decoded = jnp.where(row < by_seq(SMALL, dec_quarter, dec_quarter, 98), begin, end)[None]
        return (
            decoded,
            grad_input,
            enc_norm_share,
            enc_qkv_share,
            enc_proj_share,
            enc_up_share,
            enc_down_share,
            embed_share,
            dec_vec_share,
            dec_qkv_share,
            dec_proj_share,
            dec_up_share,
            dec_down_share,
        )

    chunk_mid = Chunk(images, [dec_down.shape, dec_up.shape, dec_proj.shape])
    decoded, grad_dec_middle, dec_grad_att, vectors_two, *mid_grads = call(
        functools.partial(dec_mid_kernel, chunk_mid),
        1,
        [
            ((DEC_PAD, dec_width), bf16),
            ((DEC_PAD, dec_width), f32),
            ((DEC_PAD, dec_width), bf16),
            ((2, dec_width), f32),
        ]
        + chunk_mid.outs(),
        (core_arg, dec_input, dec_att, cot, dec_rows_vecs, dec_proj, dec_up, dec_down),
        48,
    )
    grad_specs = [columns(DEC_PAD)] * 3 + [columns(BIG_PAD)] * 2
    grad_query, grad_key, grad_value, leaving_key, leaving_value = pl.pallas_call(
        dec_att_back_kernel,
        grid=(groups,),
        in_specs=qkv_specs + [columns(DEC_PAD)] * 2 + prob_specs,
        out_specs=grad_specs,
        out_shape=[
            jax.ShapeDtypeStruct((DEC_PAD, dec_width), bf16),
            jax.ShapeDtypeStruct((DEC_PAD, dec_width), f32),
            jax.ShapeDtypeStruct((DEC_PAD, dec_width), f32),
            jax.ShapeDtypeStruct((BIG_PAD, dec_width), bf16),
            jax.ShapeDtypeStruct((BIG_PAD, dec_width), bf16),
        ],
        compiler_params=pltpu.CompilerParams(vmem_limit_bytes=48 << 20),
    )(*qkv_args, dec_grad_att, dec_att, big_probs, small_probs)
    chunk_post = Chunk(images, [dec_qkv.shape])
    own_spread, other_spread, vectors_one, *post_grads = call(
        functools.partial(dec_post_kernel, chunk_post),
        1,
        [
            ((ENC_PAD, dec_width), bf16),
            ((ENC_PAD, dec_width), bf16),
            ((3, dec_width), f32),
        ]
        + chunk_post.outs(),
        (
            core_arg, dec_input, grad_dec_middle, grad_query, grad_key, grad_value,
            swap(leaving_key), swap(leaving_value), row_ids, dec_rows_vecs, dec_qkv,
        ),
        48,
    )
    arrived_spread = swap(other_spread)
    chunk_down = Chunk(images, [enc_down.shape])
    chunk_up = Chunk(images, [enc_up.shape])
    grad_enc_middle, enc_grad_att, enc_vectors_two, *mlp_grads = call(
        functools.partial(enc_mlp_back_kernel, chunk_down, chunk_up),
        1,
        [
            ((ENC_PAD, enc_width), f32),
            ((ENC_PAD, enc_width), bf16),
            ((4, enc_width), f32),
        ]
        + chunk_down.outs()
        + chunk_up.outs(),
        (
            core_arg, own_spread, arrived_spread, enc_out, enc_middle, enc_active, enc_slope,
            enc_vecs, embed, enc_down, enc_up, enc_proj,
        ),
        56,
    )
    down_grads, up_grads = mlp_grads[: len(chunk_down.outs())], mlp_grads[len(chunk_down.outs()) :]
    enc_grad_query, enc_grad_kv, enc_leaving = call(
        enc_att_back_kernel,
        0,
        [
            ((ENC_PAD, enc_width), bf16),
            ((ENC_PAD, 2 * enc_width), f32),
            ((ENC_PAD, 2 * enc_width), bf16),
        ],
        (enc_grad_att, enc_att, enc_probs, enc_query, enc_kv, enc_other),
        48,
    )
    chunk_att = Chunk(images, [enc_qkv.shape, enc_proj.shape, embed.shape], 16)
    grad_input, enc_vectors_one, *att_grads = call(
        functools.partial(enc_post_kernel, chunk_att),
        1,
        [((ENC_PAD, enc_width), f32), ((2, enc_width), f32)] + chunk_att.outs(),
        (
            core_arg, x, enc_att, grad_enc_middle, enc_grad_query, enc_grad_kv,
            swap(enc_leaving), enc_out, own_spread, arrived_spread, enc_vecs, enc_qkv,
        ),
        48,
    )

    def by_image(rows):
        flat = rows.reshape(rows.shape[0], images, rows.shape[1] // images)
        return flat.transpose(1, 0, 2).reshape(images, -1)

    vectors = jnp.concatenate(
        [
            by_image(jnp.concatenate([enc_vectors_one, enc_vectors_two])),
            by_image(jnp.concatenate([vectors_one[:2], vectors_two, vectors_one[2:]])),
        ],
        axis=1,
    ).astype(bf16)
    vectors = jnp.pad(vectors, ((0, 0), (0, 16 * LANES - vectors.shape[1])))
    vectors = vectors.reshape(images // 2, 2, 16, LANES)
    vectors = (pick(vectors, core, 1), pick(vectors, 1 - core, 1))
    chunk_pairs = [
        chunk.pair(grads, core)
        for chunk, grads in (
            (chunk_mid, mid_grads),
            (chunk_post, post_grads),
            (chunk_down, down_grads),
            (chunk_up, up_grads),
            (chunk_att, att_grads),
        )
    ]
    place = slice(chunk_att.used, chunk_att.used + 16)
    chunk_pairs[-1] = tuple(
        array.at[:, place].set(rows) for array, rows in zip(chunk_pairs[-1], vectors)
    )
    shares = [reduce_rest(reduce_pair(*pair), seq) for pair in chunk_pairs]
    mid_share, post_share, down_share, up_share, att_share = shares
    dec_down_share, dec_up_share, dec_proj_share = chunk_mid.split(mid_share)
    (dec_qkv_share,) = chunk_post.split(post_share)
    (enc_down_share,) = chunk_down.split(down_share)
    (enc_up_share,) = chunk_up.split(up_share)
    enc_qkv_share, enc_proj_share, embed_share = chunk_att.split(att_share)
    vectors = att_share[chunk_att.used : chunk_att.used + 16].reshape(-1).astype(f32)
    enc_count, dec_count = enc_width // images, dec_width // images
    enc_norm_share = vectors[: 6 * enc_count].reshape(6, enc_count).T
    dec_vec_share = vectors[6 * enc_count : 6 * enc_count + 5 * dec_count].reshape(5, dec_count).T

    start = jnp.concatenate([decoded[:SMALL], decoded[SMALL_PAD : SMALL_PAD + HALF]])
    end = jnp.concatenate([decoded[SMALL_PAD : SMALL_PAD + HALF], decoded[:SMALL]])
    natural = jnp.where(core == 0, start, end)
    decoded = jnp.stack(exchange_packs(natural.reshape(2, dec_quarter, dec_width), odd))[None]
    grad_input = jnp.stack(
        exchange_packs(grad_input.reshape(2, ENC_SEG, enc_width)[:, : enc_half // 2], odd)
    )[None]
    return (
        decoded,
        grad_input,
        enc_norm_share,
        enc_qkv_share,
        enc_proj_share,
        enc_up_share,
        enc_down_share,
        embed_share,
        dec_vec_share,
        dec_qkv_share,
        dec_proj_share,
        dec_up_share,
        dec_down_share,
    )


def solution(mesh):
    rows = P("img", None, "seq", None)
    tables = P("img", None, None)
    shares = P("img", None)
    return jax.shard_map(
        shards,
        mesh=mesh,
        in_specs=(rows, rows, tables, tables) + (P(),) * 11,
        out_specs=(rows, rows) + (shares,) * 11,
        check_vma=False,
    )
```

```python
import functools
import math

import jax
import jax.numpy as jnp
import numpy as np
from jax import lax
from jax.experimental import pallas as pl
from jax.experimental.pallas import tpu as pltpu
from jax.sharding import PartitionSpec as P

HE = 12
HD = 16
PATCHES = 784
SMALL = PATCHES // 4
HALF = PATCHES // 2
SMALL_PAD = 208
BIG_PAD = 400
DEC_PAD = SMALL_PAD + BIG_PAD
ENC_SEG = 80
ENC_PAD = 2 * ENC_SEG

eps_norm = 1e-06
masked_score = -1e30
bf16 = jnp.bfloat16
f32 = jnp.float32


def product(left_side, right_side):
    return jnp.dot(left_side, right_side, preferred_element_type=f32)


def inner_rows(left_side, right_side):
    return lax.dot_general(
        left_side, right_side, (((0,), (0,)), ((), ())), preferred_element_type=f32
    )


def inner_cols(left_side, right_side):
    return lax.dot_general(
        left_side, right_side, (((1,), (1,)), ((), ())), preferred_element_type=f32
    )


def norm_parts(values):
    centered = values - jnp.mean(values, axis=-1, keepdims=True)
    inverse = lax.rsqrt(jnp.mean(centered * centered, axis=-1, keepdims=True) + eps_norm)
    return centered * inverse, inverse


def norm_backward(grad_out, normed, inverse, norm_gain):
    scaled = grad_out * norm_gain
    grad_values = inverse * (
        scaled
        - jnp.mean(scaled, axis=-1, keepdims=True)
        - normed * jnp.mean(scaled * normed, axis=-1, keepdims=True)
    )
    return (
        grad_values,
        jnp.sum(grad_out * normed, axis=0, keepdims=True),
        jnp.sum(grad_out, axis=0, keepdims=True),
    )


def gelu_parts(hidden):
    below = 0.5 + 0.5 * lax.erf(hidden * math.sqrt(0.5))
    density = jnp.exp(hidden * hidden * -0.5) * (1.0 / math.sqrt(2.0 * math.pi))
    return hidden * below, below + hidden * density


LANES = 256
EIGHTH = 48
SUB_ROWS = 8 * EIGHTH


def put(core, dest, offset, grad):
    low = grad.astype(bf16)
    if len(dest) == 1:
        dest[0][...] = low
        return
    keep, leaving = dest
    chips = keep.shape[0]
    count = low.shape[0] // (2 * chips)
    for case in (0, 1):

        @pl.when(core == case)
        def _():
            for image in range(2 * chips):
                ref = keep if image % 2 == case else leaving
                for block in range(low.shape[1] // LANES):
                    start = offset + block * count
                    ref[image // 2, start : start + count, :] = low[
                        image * count : (image + 1) * count, block * LANES : (block + 1) * LANES
                    ]


def image_rows(shape, images):
    return shape[0] // images * (shape[1] // LANES)


class Chunk:
    def __init__(self, images, shapes, spare=0):
        self.images = images
        self.shapes = shapes
        self.offsets = []
        rows = 0
        for shape in shapes:
            self.offsets.append(rows)
            rows += image_rows(shape, images)
        self.used = rows
        rows += spare
        self.direct = all(shape[0] // images % 16 == 0 for shape in shapes)
        unit = SUB_ROWS if self.direct else 8
        self.rows = -(-rows // unit) * unit

    def outs(self):
        if self.direct:
            return [((self.images // 2, self.rows, LANES), bf16)] * 2
        return [(shape, bf16) for shape in self.shapes]

    def dests(self, refs):
        if self.direct:
            return [tuple(refs)] * len(self.shapes)
        return [(ref,) for ref in refs]

    def pair(self, results, core):
        if self.direct:
            return tuple(results)
        pieces = []
        for grad in results:
            for start in range(0, grad.shape[1], LANES):
                piece = grad[:, start : start + LANES]
                pieces.append(piece.reshape(self.images, -1, LANES))
        stacked = jnp.concatenate(pieces, axis=1)
        stacked = jnp.pad(stacked, ((0, 0), (0, self.rows - stacked.shape[1]), (0, 0)))
        both = stacked.reshape(self.images // 2, 2, self.rows, LANES)
        return pick(both, core, 1), pick(both, 1 - core, 1)

    def split(self, share):
        results = []
        for shape, offset in zip(self.shapes, self.offsets):
            count = shape[0] // self.images
            pieces = [
                share[offset + block * count : offset + (block + 1) * count]
                for block in range(shape[1] // LANES)
            ]
            results.append(jnp.concatenate(pieces, axis=1).astype(f32))
        return results


def call(kernel, scalars, outs, args, megabytes):
    vmem = pl.BlockSpec(memory_space=pltpu.VMEM)
    smem = pl.BlockSpec(memory_space=pltpu.SMEM)
    return pl.pallas_call(
        kernel,
        out_shape=[jax.ShapeDtypeStruct(shape, kind) for shape, kind in outs],
        in_specs=[smem] * scalars + [vmem] * (len(args) - scalars),
        out_specs=[vmem] * len(outs),
        compiler_params=pltpu.CompilerParams(vmem_limit_bytes=megabytes << 20),
    )(*args)


def lane_masks(head_size, kind):
    lanes = lax.broadcasted_iota(jnp.int32, (1, 128), 1) // head_size
    return [(lanes == head).astype(f32).astype(kind) for head in range(128 // head_size)]


def softmax_rows(scores, scale):
    row_max = jnp.max(scores, axis=1, keepdims=True)
    weights = jnp.exp2((scores - row_max) * (scale * math.log2(math.e)))
    return (weights * (1.0 / jnp.sum(weights, axis=1, keepdims=True))).astype(bf16)


def head_back(probs, grads, values, delta):
    grad_probs = inner_cols(grads, values)
    return (probs.astype(f32) * (grad_probs - delta)).astype(bf16)


def enc_pre_kernel(x, vecs, w_qkv, query, key_value):
    normed, _ = norm_parts(x[...].astype(f32))
    attn_in = (normed * vecs[0:1] + vecs[1:2]).astype(bf16)
    mixed = product(attn_in, w_qkv[...]).astype(bf16)
    width = query.shape[1]
    query[...] = mixed[:, :width]
    key_value[...] = mixed[:, width:]


def enc_main_kernel(
    x, query, own_kv, other_kv, own_ids, all_ids, vecs, w_proj, w_up, w_down, w_embed,
    embedded, att, probs, middle, active, slope, out
):
    width = query.shape[1]
    head_size = width // HE
    bias = jnp.where(own_ids[...] == all_ids[...], 0.0, masked_score)
    masks = lane_masks(head_size, bf16)
    for pair in range(width // 128):
        cols = slice(128 * pair, 128 * pair + 128)
        value_cols = slice(width + 128 * pair, width + 128 * pair + 128)
        keys = jnp.concatenate([own_kv[:, cols], other_kv[:, cols]], axis=0)
        values = jnp.concatenate([own_kv[:, value_cols], other_kv[:, value_cols]], axis=0)
        total = jnp.zeros((query.shape[0], 128), f32)
        for head, mask in enumerate(masks):
            scores = inner_cols(query[:, cols] * mask, keys) + bias
            chances = softmax_rows(scores, 1.0 / math.sqrt(head_size))
            probs[len(masks) * pair + head] = chances
            total += product(chances, values * mask)
        att[:, cols] = total.astype(bf16)
    mid = x[...].astype(f32) + product(att[...], w_proj[...])
    middle[...] = mid
    normed, _ = norm_parts(mid)
    mlp_in = (normed * vecs[2:3] + vecs[3:4]).astype(bf16)
    result, steepness = gelu_parts(product(mlp_in, w_up[...]))
    active[...] = result.astype(bf16)
    slope[...] = steepness.astype(bf16)
    last = mid + product(active[...], w_down[...])
    out[...] = last
    normed, _ = norm_parts(last)
    final = (normed * vecs[4:5] + vecs[5:6]).astype(bf16)
    embedded[...] = product(final, w_embed[...]).astype(bf16)


def chosen_rows(core, visible_rows):
    index = lax.broadcasted_iota(jnp.int32, (DEC_PAD, 1), 0)
    small = index + core * (SMALL + PATCHES)
    big = index + (SMALL - SMALL_PAD) + core * HALF
    row = jnp.where(index < SMALL, small, -1)
    row = jnp.where((index >= SMALL_PAD) & (index < SMALL_PAD + HALF), big, row)
    return (row == visible_rows).astype(f32)


def dec_pre_kernel(core, own, other, rows, code, vecs, w_qkv, dec_input, mixed, big_kv):
    chosen = chosen_rows(core[0], rows[...])
    seen = jnp.sum(chosen, axis=1, keepdims=True)
    tokens = jnp.concatenate([own[...], other[...]], axis=0)
    picked = product(chosen.astype(bf16), tokens)
    values = jnp.where(seen > 0.0, picked, vecs[4:5]) + code[...]
    dec_input[...] = values
    normed, _ = norm_parts(values)
    attn_in = (normed * vecs[0:1] + vecs[1:2]).astype(bf16)
    result = product(attn_in, w_qkv[...]).astype(bf16)
    mixed[...] = result
    big_kv[...] = result[SMALL_PAD:, values.shape[1] :]


def big_bias():
    column = lax.broadcasted_iota(jnp.int32, (1, 2 * BIG_PAD), 1)
    place = jnp.where(column >= BIG_PAD, column - BIG_PAD, column)
    return jnp.where(place < HALF, 0.0, masked_score)


def small_bias():
    column = lax.broadcasted_iota(jnp.int32, (1, SMALL_PAD), 1)
    return jnp.where(column < SMALL, 0.0, masked_score)


def dec_att_kernel(query, key, value, other_key, other_value, att, big_probs, small_probs):
    head_size = query.shape[1] * 4 // HD
    scale = 1.0 / math.sqrt(head_size)
    keys = jnp.concatenate([key[SMALL_PAD:], other_key[...]], axis=0)
    values = jnp.concatenate([value[SMALL_PAD:], other_value[...]], axis=0)
    total = jnp.zeros((BIG_PAD, 128), f32)
    small_total = jnp.zeros((SMALL_PAD, 128), f32)
    for head, mask in enumerate(lane_masks(head_size, bf16)):
        scores = inner_cols(query[SMALL_PAD:] * mask, keys) + big_bias()
        chances = softmax_rows(scores, scale)
        big_probs[head] = chances
        total += product(chances, values * mask)
        scores = inner_cols(query[:SMALL_PAD] * mask, key[:SMALL_PAD]) + small_bias()
        chances = softmax_rows(scores, scale)
        small_probs[head] = chances
        small_total += product(chances, value[:SMALL_PAD] * mask)
    att[:SMALL_PAD] = small_total.astype(bf16)
    att[SMALL_PAD:] = total.astype(bf16)


def dec_mid_kernel(
    chunk, core, dec_input, att, cot, vecs, w_proj, w_up, w_down,
    decoded, grad_middle, grad_att, vectors, *grads
):
    down_dest, up_dest, proj_dest = chunk.dests(grads)
    down_at, up_at, proj_at = chunk.offsets
    grad_down, grad_up = [], []
    middle = dec_input[...] + product(att[...], w_proj[...])
    normed, inverse = norm_parts(middle)
    mlp_in = (normed * vecs[2:3] + vecs[3:4]).astype(bf16)
    result = middle
    grad_norm = jnp.zeros_like(middle)
    step = 512
    for start in range(0, w_up.shape[1], step):
        cols = slice(start, start + step)
        active, slope = gelu_parts(product(mlp_in, w_up[:, cols]))
        active = active.astype(bf16)
        result += product(active, w_down[cols])
        grad_down.append(inner_rows(active, cot[...]).astype(bf16))
        grad_hidden = (slope * inner_cols(cot[...], w_down[cols])).astype(bf16)
        grad_up.append(inner_rows(mlp_in, grad_hidden).astype(bf16))
        grad_norm += inner_cols(grad_hidden, w_up[:, cols])
    decoded[...] = result.astype(bf16)
    grad_values, gain, shift = norm_backward(grad_norm, normed, inverse, vecs[2:3])
    vectors[0:1] = gain
    vectors[1:2] = shift
    back = cot[...].astype(f32) + grad_values
    grad_middle[...] = back
    low = back.astype(bf16)
    grad_att[...] = inner_cols(low, w_proj[...]).astype(bf16)
    put(core[0], proj_dest, proj_at, inner_rows(att[...], low))
    put(core[0], down_dest, down_at, jnp.concatenate(grad_down, axis=0))
    put(core[0], up_dest, up_at, jnp.concatenate(grad_up, axis=1))


def dec_att_back_kernel(
    query, key, value, other_key, other_value, grads, att, big_probs, small_probs,
    grad_query, grad_key, grad_value, leaving_key, leaving_value
):
    head_size = query.shape[1] * 4 // HD
    scale = 1.0 / math.sqrt(head_size)
    keys = jnp.concatenate([key[SMALL_PAD:], other_key[...]], axis=0)
    values = jnp.concatenate([value[SMALL_PAD:], other_value[...]], axis=0)
    overlap = grads[...].astype(f32) * att[...].astype(f32)
    big_q = jnp.zeros((BIG_PAD, 128), f32)
    big_k = jnp.zeros((2 * BIG_PAD, 128), f32)
    big_v = jnp.zeros((2 * BIG_PAD, 128), f32)
    small_q = jnp.zeros((SMALL_PAD, 128), f32)
    small_k = jnp.zeros((SMALL_PAD, 128), f32)
    small_v = jnp.zeros((SMALL_PAD, 128), f32)
    masks = lane_masks(head_size, f32)
    for head, mask in enumerate(lane_masks(head_size, bf16)):
        delta = jnp.sum(overlap * masks[head], axis=1, keepdims=True)
        one_query, one_grad = query[...] * mask, grads[...] * mask
        chances = big_probs[head]
        back = head_back(chances, one_grad[SMALL_PAD:], values, delta[SMALL_PAD:])
        big_q += product(back, keys * mask)
        big_k += inner_rows(back, one_query[SMALL_PAD:])
        big_v += inner_rows(chances, one_grad[SMALL_PAD:])
        chances = small_probs[head]
        back = head_back(chances, one_grad[:SMALL_PAD], value[:SMALL_PAD], delta[:SMALL_PAD])
        small_q += product(back, key[:SMALL_PAD] * mask)
        small_k += inner_rows(back, one_query[:SMALL_PAD])
        small_v += inner_rows(chances, one_grad[:SMALL_PAD])
    grad_query[:SMALL_PAD] = (small_q * scale).astype(bf16)
    grad_query[SMALL_PAD:] = (big_q * scale).astype(bf16)
    grad_key[:SMALL_PAD] = small_k * scale
    grad_key[SMALL_PAD:] = big_k[:BIG_PAD] * scale
    grad_value[:SMALL_PAD] = small_v
    grad_value[SMALL_PAD:] = big_v[:BIG_PAD]
    leaving_key[...] = (big_k[BIG_PAD:] * scale).astype(bf16)
    leaving_value[...] = big_v[BIG_PAD:].astype(bf16)


def dec_post_kernel(
    chunk, core, dec_input, grad_middle, grad_query, grad_key, grad_value, arrived_key,
    arrived_value, rows, vecs, w_qkv, own_spread, other_spread, vectors, *grads
):
    normed, inverse = norm_parts(dec_input[...])
    attn_in = (normed * vecs[0:1] + vecs[1:2]).astype(bf16)
    key = jnp.concatenate(
        [grad_key[:SMALL_PAD], grad_key[SMALL_PAD:] + arrived_key[...].astype(f32)], axis=0
    ).astype(bf16)
    value = jnp.concatenate(
        [grad_value[:SMALL_PAD], grad_value[SMALL_PAD:] + arrived_value[...].astype(f32)], axis=0
    ).astype(bf16)
    mixed = jnp.concatenate([grad_query[...], key, value], axis=1)
    grad_values, gain, shift = norm_backward(
        inner_cols(mixed, w_qkv[...]), normed, inverse, vecs[0:1]
    )
    back = grad_middle[...] + grad_values
    chosen = chosen_rows(core[0], rows[...])
    seen = jnp.sum(chosen, axis=1, keepdims=True)
    spread = inner_rows(chosen.astype(bf16), back.astype(bf16)).astype(bf16)
    own_spread[...] = spread[:ENC_PAD]
    other_spread[...] = spread[ENC_PAD:]
    vectors[0:1] = gain
    vectors[1:2] = shift
    vectors[2:3] = jnp.sum(jnp.where(seen > 0.0, 0.0, back), axis=0, keepdims=True)
    put(core[0], chunk.dests(grads)[0], chunk.offsets[0], inner_rows(attn_in, mixed))


def enc_mlp_back_kernel(
    first, second, core, own_spread, arrived, out, middle, active, slope,
    vecs, w_embed, w_down, w_up, w_proj, grad_middle, grad_att, vectors, *grads
):
    first_grads, second_grads = grads[: len(first.outs())], grads[len(first.outs()) :]
    grad_embedded = own_spread[...] + arrived[...]
    normed, inverse = norm_parts(out[...])
    grad_out, gain, shift = norm_backward(
        inner_cols(grad_embedded, w_embed[...]), normed, inverse, vecs[4:5]
    )
    vectors[2:3] = gain
    vectors[3:4] = shift
    low = grad_out.astype(bf16)
    put(core[0], first.dests(first_grads)[0], first.offsets[0], inner_rows(active[...], low))
    grad_hidden = (slope[...].astype(f32) * inner_cols(low, w_down[...])).astype(bf16)
    normed, inverse = norm_parts(middle[...])
    mlp_in = (normed * vecs[2:3] + vecs[3:4]).astype(bf16)
    put(
        core[0], second.dests(second_grads)[0], second.offsets[0], inner_rows(mlp_in, grad_hidden)
    )
    grad_values, gain, shift = norm_backward(
        inner_cols(grad_hidden, w_up[...]), normed, inverse, vecs[2:3]
    )
    vectors[0:1] = gain
    vectors[1:2] = shift
    back = grad_out + grad_values
    grad_middle[...] = back
    grad_att[...] = inner_cols(back.astype(bf16), w_proj[...]).astype(bf16)


def enc_att_back_kernel(
    grads, att, probs, query, own_kv, other_kv, grad_query, grad_kv, leaving
):
    width = query.shape[1]
    head_size = width // HE
    scale = 1.0 / math.sqrt(head_size)
    overlap = grads[...].astype(f32) * att[...].astype(f32)
    masks = lane_masks(head_size, bf16)
    wide_masks = lane_masks(head_size, f32)
    rows = query.shape[0]
    for pair in range(width // 128):
        cols = slice(128 * pair, 128 * pair + 128)
        value_cols = slice(width + 128 * pair, width + 128 * pair + 128)
        keys = jnp.concatenate([own_kv[:, cols], other_kv[:, cols]], axis=0)
        values = jnp.concatenate([own_kv[:, value_cols], other_kv[:, value_cols]], axis=0)
        total_q = jnp.zeros((rows, 128), f32)
        total_k = jnp.zeros((2 * rows, 128), f32)
        total_v = jnp.zeros((2 * rows, 128), f32)
        for head, mask in enumerate(masks):
            delta = jnp.sum(overlap[:, cols] * wide_masks[head], axis=1, keepdims=True)
            one_grad = grads[:, cols] * mask
            chances = probs[len(masks) * pair + head]
            one_back = head_back(chances, one_grad, values, delta)
            total_q += product(one_back, keys * mask)
            total_k += inner_rows(one_back, query[:, cols] * mask)
            total_v += inner_rows(chances, one_grad)
        grad_query[:, cols] = (total_q * scale).astype(bf16)
        grad_kv[:, cols] = total_k[:rows] * scale
        grad_kv[:, value_cols] = total_v[:rows]
        leaving[:, cols] = (total_k[rows:] * scale).astype(bf16)
        leaving[:, value_cols] = total_v[rows:].astype(bf16)


def enc_post_kernel(
    chunk, core, x, att, grad_middle, grad_query, grad_kv, arrived, out, own_spread, other_spread,
    vecs, w_qkv, grad_input, vectors, *grads
):
    qkv_dest, proj_dest, embed_dest = chunk.dests(grads)
    normed, _ = norm_parts(out[...])
    final = (normed * vecs[4:5] + vecs[5:6]).astype(bf16)
    put(
        core[0], embed_dest, chunk.offsets[2], inner_rows(final, own_spread[...] + other_spread[...])
    )
    put(
        core[0], proj_dest, chunk.offsets[1],
        inner_rows(att[...], grad_middle[...].astype(bf16)),
    )
    normed, inverse = norm_parts(x[...].astype(f32))
    attn_in = (normed * vecs[0:1] + vecs[1:2]).astype(bf16)
    key_value = (grad_kv[...] + arrived[...].astype(f32)).astype(bf16)
    mixed = jnp.concatenate([grad_query[...], key_value], axis=1)
    grad_values, gain, shift = norm_backward(
        inner_cols(mixed, w_qkv[...]), normed, inverse, vecs[0:1]
    )
    grad_input[...] = grad_middle[...] + grad_values
    vectors[0:1] = gain
    vectors[1:2] = shift
    put(core[0], qkv_dest, chunk.offsets[0], inner_rows(attn_in, mixed))


def permute(array, where_to):
    seq_count = lax.axis_size("seq")
    img_count = lax.axis_size("img")
    pairs = []
    for seq in range(seq_count):
        for img in range(img_count):
            seq_to, img_to = where_to(seq, img)
            pairs.append((seq * img_count + img, seq_to * img_count + img_to))
    return lax.ppermute(array, ("seq", "img"), pairs)


def swap(array):
    return permute(array, lambda seq, img: (seq, img ^ 1))


def pack_move(turn):
    def where_to(seq, img):
        return (2 * (img & 1) + (turn ^ (seq & 1)), (img & ~1) | (seq >> 1))

    return where_to


def exchange_packs(blocks, odd):
    rounds = [
        permute(jnp.where(odd, blocks[1 - turn], blocks[turn]), pack_move(turn)) for turn in (0, 1)
    ]
    return (jnp.where(odd, rounds[1], rounds[0]), jnp.where(odd, rounds[0], rounds[1]))


def pick(array, index, axis):
    return lax.dynamic_index_in_dim(array, index, axis, keepdims=False)


def pad_rows(array, rows):
    return jnp.pad(array, ((0, rows - array.shape[0]),) + ((0, 0),) * (array.ndim - 1))


def position_table(row_width):
    halfway = row_width // 2
    frequency = np.exp(np.arange(halfway, dtype=np.float64) * (-math.log(10000.0) / halfway))
    angles = np.arange(PATCHES, dtype=np.float64)[:, None] * frequency[None, :]
    return np.concatenate([np.sin(angles), np.cos(angles)], axis=1).astype(np.float32)


def reduce_pair(keep, leaving):
    return (keep.astype(f32) + swap(leaving).astype(f32)).astype(bf16)


MID_PIECES, POST_PIECES, DOWN_PIECES, UP_PIECES, ATT_PIECES = 3, 1, 3, 3, 4
DEC_PIECES = MID_PIECES + POST_PIECES
DOWN_AT = DEC_PIECES
UP_AT = DOWN_AT + DOWN_PIECES
ATT_AT = UP_AT + UP_PIECES
PIECES = ATT_AT + ATT_PIECES


class Refs:
    def __init__(self, names, refs):
        self.__dict__.update(zip(names, refs))


def by_name(items):
    return Refs(items.keys(), items.values())


def sub_rows(row, count):
    done = 0
    while done < count:
        piece, place = (row + done) // SUB_ROWS, (row + done) % SUB_ROWS
        start = place % EIGHTH
        size = min(count - done, EIGHTH - start)
        place //= EIGHTH
        yield piece, place // 4, place // 2 % 2, place % 2, start, start + size, done
        done += size


class Place:
    def __init__(self):
        self.seq, self.img = lax.axis_index("seq"), lax.axis_index("img")
        self.chip, self.core = self.img // 2, lax.rem(self.img, 2)
        self.high, self.low = self.seq // 2, lax.rem(self.seq, 2)
        self.partner = dict(img=self.img + 1 - 2 * self.core)

    def remote(self, source, dest, sems, device):
        return pltpu.make_async_remote_copy(
            src_ref=source,
            dst_ref=dest,
            send_sem=sems.at[0],
            recv_sem=sems.at[1],
            device_id=device,
            device_id_type=pl.DeviceIdType.MESH,
        )

    def home(self, turn):
        segment = turn + self.low - 2 * turn * self.low
        device = dict(seq=2 * self.core + segment, img=2 * self.chip + self.high)
        stays = (self.high == self.core) if turn == 0 else None
        return device, segment, stays

    def send_home(self, act, source_parts, sems):
        for turn in (0, 1):
            device, segment, stays = self.home(turn)
            for part, (source, dest) in enumerate(source_parts(segment)):
                sem = sems.at[turn, part]
                if stays is None:
                    act(self.remote(source, dest, sem, device))
                else:

                    @pl.when(stays)
                    def _():
                        act(pltpu.make_async_copy(source, dest, sem.at[0]))

                    @pl.when(jnp.logical_not(stays))
                    def _():
                        act(self.remote(source, dest, sem, device))

    def greet(self, peers):
        barrier = pltpu.get_barrier_semaphore()

        def signal(device):
            pl.semaphore_signal(
                barrier, inc=1, device_id=device, device_id_type=pl.DeviceIdType.MESH
            )

        for device in peers:
            signal(device)
        signal(self.home(1)[0])

        @pl.when(self.high != self.core)
        def _():
            signal(self.home(0)[0])

        return lambda: pl.semaphore_wait(
            barrier, len(peers) + 1 + jnp.where(self.high == self.core, 0, 1)
        )


def start_copy(copy):
    copy.start()


def wait_copy(copy):
    copy.wait()


def loader(sems, **items):
    copies = {}
    for index, (name, (source, dest)) in enumerate(items.items()):
        copies[name] = pltpu.make_async_copy(source, dest, sems.at[index])
        copies[name].start()
    return by_name(copies)


def ready(*copies):
    for copy in copies:
        copy.wait()


def row_order(core, pad, rows):
    local = lax.broadcasted_iota(jnp.int32, (DEC_PAD, 2 * pad), 0)
    place = lax.broadcasted_iota(jnp.int32, (DEC_PAD, 2 * pad), 1)
    small = local < SMALL_PAD
    natural = jnp.where(small, local + core * HALF, local - SMALL_PAD + (1 - core) * SMALL)
    there = jnp.where(small, local, local - SMALL_PAD + SMALL - HALF) < SMALL
    spot = natural + jnp.where(natural >= rows, pad - rows, 0)
    return ((spot == place) & there).astype(f32).astype(bf16)


def front_kernel(names, *refs):
    r = Refs(names, refs)
    p = Place()
    core, low, high = p.core, p.low, p.high
    width, narrow = r.w_embed.shape
    rows = ENC_PAD
    seg_rows, cot_rows = r.enc_input.shape[1], r.cotangent.shape[1]
    cot_pad = r.cot_send.shape[1]
    load = loader(
        r.load_sem,
        qkv=(r.w_qkv, r.v_qkv),
        proj=(r.w_proj, r.v_proj),
        up=(r.w_up, r.v_up),
        down=(r.w_down, r.v_down),
        embed=(r.w_embed, r.v_embed),
        code=(r.codes.at[core], r.v_code),
        dec_qkv=(r.dec_qkv, r.v_dec_qkv),
    )
    greeted = p.greet([p.partner])
    for block in range(2):
        r.enc_send[block] = jnp.concatenate(
            [
                r.enc_input[block].astype(f32),
                jnp.zeros((ENC_SEG - seg_rows, width), f32),
            ],
            axis=0,
        ).astype(bf16)
    greeted()

    def enc_parts(segment):
        return [(r.enc_send.at[segment], r.v_x.at[low])]

    def cot_parts(segment):
        return [(r.cot_send.at[segment], r.cot_in.at[low])]

    p.send_home(start_copy, enc_parts, r.enc_sem)
    table_copy = p.remote(r.tables.at[1], r.tables_in, r.swap_sem.at[0], p.partner)
    table_copy.start()
    for block in range(2):
        r.cot_send[block] = jnp.concatenate(
            [
                r.cotangent[block].astype(f32),
                jnp.zeros((cot_pad - cot_rows, narrow), f32),
            ],
            axis=0,
        ).astype(bf16)
    p.send_home(start_copy, cot_parts, r.cot_sem)
    enc_vecs, dec_vecs = r.enc_vecs, r.dec_vecs

    stores = []

    def store(source, dest):
        copy = pltpu.make_async_copy(source, dest, r.store_sem.at[len(stores)])
        copy.start()
        stores.append(copy)

    def put_left(values, start):
        chips = r.lefts_keep.shape[0]
        turned = values.astype(f32).T.astype(bf16)
        count = turned.shape[0] // (2 * chips)
        for case in (0, 1):

            @pl.when(core == case)
            def _():
                for image in range(2 * chips):
                    ref = r.lefts_keep if image % 2 == case else r.lefts_leaving
                    ref[image // 2, start : start + count] = turned[
                        image * count : (image + 1) * count
                    ]

    left_hidden = r.w_up.shape[1] // (2 * r.lefts_keep.shape[0])
    left_mid = width // (2 * r.lefts_keep.shape[0])

    def norm_in(values, vecs, row):
        normed, _ = norm_parts(values)
        return (normed * vecs[row : row + 1] + vecs[row + 1 : row + 2]).astype(bf16)

    p.send_home(wait_copy, enc_parts, r.enc_sem)
    x = r.v_x[...].reshape(rows, width).astype(f32)
    attn_in = norm_in(x, enc_vecs, 0)
    ready(load.qkv)
    mixed = product(attn_in, r.v_qkv[...]).astype(bf16)
    r.v_query[...] = mixed[:, :width]
    r.v_own_kv[...] = mixed[:, width:]
    kv_copy = p.remote(r.v_own_kv, r.v_other_kv, r.swap_sem.at[1], p.partner)
    kv_copy.start()
    put_left(attn_in, left_hidden + 3 * left_mid)
    table_copy.wait()
    mine = high == core
    ids = jnp.where(mine, r.tables[0, 0, low], r.tables_in[0, low])
    row_ids = jnp.where(mine, r.tables[0, 1, low], r.tables_in[1, low])
    r.row_ids[...] = row_ids
    across = lax.broadcasted_iota(jnp.int32, (rows, 2 * rows), 1)
    along = lax.broadcasted_iota(jnp.int32, (rows, 2 * rows), 0)
    wide_ids = ids.astype(f32)
    own_ids = jnp.sum(jnp.where(across == along, wide_ids, 0.0), axis=1, keepdims=True)
    bias = jnp.where(own_ids == wide_ids, 0.0, masked_score)
    head_size = width // HE
    masks = lane_masks(head_size, bf16)
    kv_copy.wait()
    for pair in range(width // 128):
        cols = slice(128 * pair, 128 * pair + 128)
        value_cols = slice(width + 128 * pair, width + 128 * pair + 128)
        keys = jnp.concatenate([r.v_own_kv[:, cols], r.v_other_kv[:, cols]], axis=0)
        values = jnp.concatenate([r.v_own_kv[:, value_cols], r.v_other_kv[:, value_cols]], axis=0)
        total = jnp.zeros((rows, 128), f32)
        for head, mask in enumerate(masks):
            scores = inner_cols(r.v_query[:, cols] * mask, keys) + bias
            chances = softmax_rows(scores, 1.0 / math.sqrt(head_size))
            r.v_probs[len(masks) * pair + head] = chances
            total += product(chances, values * mask)
        r.v_att[:, cols] = total.astype(bf16)
    store(r.v_x, r.x)
    store(r.v_query, r.query)
    store(r.v_own_kv, r.own_kv)
    store(r.v_other_kv, r.other_kv)
    store(r.v_probs, r.probs)
    store(r.v_att, r.att)

    ready(load.proj, load.up, load.down, load.embed)
    middle = x + product(r.v_att[...], r.v_proj[...])
    r.v_middle[...] = middle
    store(r.v_middle, r.middle)
    mlp_in = norm_in(middle, enc_vecs, 2)
    active, slope = gelu_parts(product(mlp_in, r.v_up[...]))
    active = active.astype(bf16)
    r.v_slope[...] = slope.astype(bf16)
    store(r.v_slope, r.slope)
    out = middle + product(active, r.v_down[...])
    r.v_out[...] = out
    store(r.v_out, r.out)
    final = norm_in(out, enc_vecs, 4)
    r.emb_own[...] = product(final, r.v_embed[...]).astype(bf16)
    emb_copy = p.remote(r.emb_own, r.emb_in, r.swap_sem.at[2], p.partner)
    emb_copy.start()
    put_left(active, 0)
    put_left(mlp_in, left_hidden)
    put_left(r.v_att[...], left_hidden + left_mid)
    put_left(final, left_hidden + 2 * left_mid)
    store(r.lefts_keep, r.lefts_own)
    lefts_copy = p.remote(r.lefts_leaving, r.lefts_other, r.swap_sem.at[3], p.partner)
    lefts_copy.start()

    chosen = chosen_rows(core, row_ids)
    seen = jnp.sum(chosen, axis=1, keepdims=True)
    ready(load.code, load.dec_qkv)
    emb_copy.wait()
    tokens = jnp.concatenate([r.emb_own[...], r.emb_in[...]], axis=0)
    picked = product(chosen.astype(bf16), tokens)
    values = jnp.where(seen > 0.0, picked, dec_vecs[4:5]) + r.v_code[...]
    r.v_code[...] = values
    store(r.v_code, r.dec_input)
    mixed = product(norm_in(values, dec_vecs, 0), r.v_dec_qkv[...]).astype(bf16)
    r.v_mixed[...] = mixed
    big_copy = p.remote(
        r.v_mixed.at[SMALL_PAD:, narrow:], r.big_in, r.swap_sem.at[4], p.partner
    )
    big_copy.start()
    store(r.v_mixed, r.dec_mixed)

    p.send_home(wait_copy, cot_parts, r.cot_sem)
    moved = product(
        row_order(core, cot_pad, cot_rows), r.cot_in[...].reshape(2 * cot_pad, narrow)
    )
    r.v_cot[...] = moved.astype(bf16)
    store(r.v_cot, r.cot)
    big_copy.wait()
    store(r.big_in, r.dec_other_kv)

    head_size = narrow // HD
    per_group = 128 // head_size
    scale = 1.0 / math.sqrt(head_size)
    masks = lane_masks(head_size, bf16)

    def chance_copies(head, slot):
        return (
            pltpu.make_async_copy(r.chances.at[slot], r.big_probs.at[head], r.chance_sem.at[slot, 0]),
            pltpu.make_async_copy(
                r.small_chances.at[slot], r.small_probs.at[head], r.chance_sem.at[slot, 1]
            ),
        )

    wide_masks = lane_masks(head_size, f32)
    lane = lax.broadcasted_iota(jnp.int32, (1, 128), 1)

    def pad_column(blocks, size, used):
        index = lax.broadcasted_iota(jnp.int32, (blocks * size, 1), 0)
        index = jnp.where(index >= size, index - size, index)
        return jnp.where(index < used, 0.0, masked_score)

    big_pad, small_pad = pad_column(2, BIG_PAD, HALF), pad_column(1, SMALL_PAD, SMALL)

    def weigh(query, key, value, pad, mask, spare):
        one = spare.astype(bf16)
        scores = inner_cols(query * mask + one, key * mask + (pad * spare).astype(bf16))
        row_max = jnp.max(scores, axis=1, keepdims=True)
        weights = jnp.exp2((scores - row_max) * (scale * math.log2(math.e))).astype(bf16)
        mixed = product(weights, value * mask + one)
        return weights, mixed, 1.0 / jnp.sum(mixed * spare, axis=1, keepdims=True)

    def group_forward(group, carry):
        def cols(offset):
            return pl.ds(pl.multiple_of(offset * narrow + group * 128, 128), 128)

        query = r.v_mixed[:, cols(0)]
        small_key, small_value = r.v_mixed[:SMALL_PAD, cols(1)], r.v_mixed[:SMALL_PAD, cols(2)]
        keys = jnp.concatenate([r.v_mixed[SMALL_PAD:, cols(1)], r.big_in[:, cols(0)]], axis=0)
        values = jnp.concatenate([r.v_mixed[SMALL_PAD:, cols(2)], r.big_in[:, cols(1)]], axis=0)
        total = jnp.zeros((BIG_PAD, 128), f32)
        small_total = jnp.zeros((SMALL_PAD, 128), f32)
        inverse = jnp.zeros((BIG_PAD, 128), f32)
        small_inverse = jnp.zeros((SMALL_PAD, 128), f32)
        for head, mask in enumerate(masks):
            slot = head
            number = group * per_group + head

            @pl.when(group > 0)
            def _():
                for copy in chance_copies(number - per_group, slot):
                    copy.wait()

            spare = (lane == (head * head_size + 64) % 128).astype(f32)
            weights, mixed, shrink = weigh(
                query[SMALL_PAD:], keys, values, big_pad, mask, spare
            )
            r.chances[slot] = weights
            shrink = shrink * wide_masks[head]
            inverse += shrink
            total += mixed * shrink
            weights, mixed, shrink = weigh(
                query[:SMALL_PAD], small_key, small_value, small_pad, mask, spare
            )
            r.small_chances[slot] = weights
            shrink = shrink * wide_masks[head]
            small_inverse += shrink
            small_total += mixed * shrink
            for copy in chance_copies(number, slot):
                copy.start()
        r.v_dec_att[:SMALL_PAD, cols(0)] = small_total.astype(bf16)
        r.v_dec_att[SMALL_PAD:, cols(0)] = total.astype(bf16)
        r.v_inverse[:SMALL_PAD, cols(0)] = small_inverse
        r.v_inverse[SMALL_PAD:, cols(0)] = inverse
        return carry

    lax.fori_loop(0, narrow // 128, group_forward, 0)
    store(r.v_dec_att, r.dec_att)
    store(r.v_inverse, r.dec_inverse)
    for slot in range(per_group):
        for copy in chance_copies(HD - per_group + slot, slot):
            copy.wait()
    for copy in stores:
        copy.wait()
    lefts_copy.wait()


def front(args, chips):
    anywhere = pl.BlockSpec(memory_space=pl.ANY)
    vmem = pl.BlockSpec(memory_space=pltpu.VMEM)
    dma = pltpu.SemaphoreType.DMA
    width, narrow = by_name(args).w_embed.shape
    wide = by_name(args).w_up.shape[1]
    left_rows = (4 * width + wide) // (2 * chips)
    cot_pad = DEC_PAD // 2
    outs = dict(
        x=((2, ENC_SEG, width), bf16),
        query=((ENC_PAD, width), bf16),
        own_kv=((ENC_PAD, 2 * width), bf16),
        other_kv=((ENC_PAD, 2 * width), bf16),
        probs=((HE, ENC_PAD, 2 * ENC_PAD), bf16),
        att=((ENC_PAD, width), bf16),
        middle=((ENC_PAD, width), f32),
        slope=((ENC_PAD, wide), bf16),
        out=((ENC_PAD, width), f32),
        lefts_own=((chips, left_rows, ENC_PAD), bf16),
        lefts_other=((chips, left_rows, ENC_PAD), bf16),
        dec_input=((DEC_PAD, narrow), f32),
        dec_mixed=((DEC_PAD, 3 * narrow), bf16),
        cot=((DEC_PAD, narrow), bf16),
        dec_other_kv=((BIG_PAD, 2 * narrow), bf16),
        big_probs=((HD, BIG_PAD, 2 * BIG_PAD), bf16),
        small_probs=((HD, SMALL_PAD, SMALL_PAD), bf16),
        dec_att=((DEC_PAD, narrow), bf16),
        dec_inverse=((DEC_PAD, narrow), f32),
        row_ids=((1, 2 * ENC_PAD), jnp.int32),
    )

    def like(out):
        return pltpu.VMEM(*out)

    scratch = dict(
        enc_send=like(by_name(outs).x),
        cot_send=pltpu.VMEM((2, cot_pad, narrow), bf16),
        cot_in=pltpu.VMEM((2, cot_pad, narrow), bf16),
        tables_in=pltpu.VMEM(by_name(args).tables.shape[1:], jnp.int32),
        v_x=like(by_name(outs).x),
        v_query=like(by_name(outs).query),
        v_own_kv=like(by_name(outs).own_kv),
        v_other_kv=like(by_name(outs).other_kv),
        v_probs=like(by_name(outs).probs),
        v_att=like(by_name(outs).att),
        v_middle=like(by_name(outs).middle),
        v_slope=like(by_name(outs).slope),
        v_out=like(by_name(outs).out),
        lefts_keep=like(by_name(outs).lefts_own),
        lefts_leaving=like(by_name(outs).lefts_own),
        emb_own=pltpu.VMEM((ENC_PAD, narrow), bf16),
        emb_in=pltpu.VMEM((ENC_PAD, narrow), bf16),
        v_code=like(by_name(outs).dec_input),
        v_mixed=like(by_name(outs).dec_mixed),
        v_cot=like(by_name(outs).cot),
        big_in=like(by_name(outs).dec_other_kv),
        chances=pltpu.VMEM((4, BIG_PAD, 2 * BIG_PAD), bf16),
        small_chances=pltpu.VMEM((4, SMALL_PAD, SMALL_PAD), bf16),
        v_dec_att=like(by_name(outs).dec_att),
        v_inverse=like(by_name(outs).dec_inverse),
        v_qkv=pltpu.VMEM(by_name(args).w_qkv.shape, bf16),
        v_proj=pltpu.VMEM(by_name(args).w_proj.shape, bf16),
        v_up=pltpu.VMEM(by_name(args).w_up.shape, bf16),
        v_down=pltpu.VMEM(by_name(args).w_down.shape, bf16),
        v_embed=pltpu.VMEM(by_name(args).w_embed.shape, bf16),
        v_dec_qkv=pltpu.VMEM(by_name(args).dec_qkv.shape, bf16),
        load_sem=dma((7,)),
        store_sem=dma((17,)),
        chance_sem=dma((4, 2)),
        swap_sem=dma((5, 2)),
        enc_sem=dma((2, 1, 2)),
        cot_sem=dma((2, 1, 2)),
    )
    names = list(args) + list(outs) + list(scratch)
    in_vmem = ("enc_input", "cotangent", "tables", "enc_vecs", "dec_vecs")
    results = pl.pallas_call(
        functools.partial(front_kernel, names),
        out_shape=[jax.ShapeDtypeStruct(shape, kind) for shape, kind in outs.values()],
        in_specs=[vmem if name in in_vmem else anywhere for name in args],
        out_specs=[vmem if name == "row_ids" else anywhere for name in outs],
        scratch_shapes=list(scratch.values()),
        compiler_params=pltpu.CompilerParams(
            collective_id=2, has_side_effects=True, vmem_limit_bytes=60 << 20
        ),
    )(*args.values())
    return dict(zip(outs, results))


def back_kernel(chips, names, *refs):
    r = Refs(names, refs)
    p = Place()
    chip, core, high, low = p.chip, p.core, p.high, p.low
    remote, partner = p.remote, p.partner
    along_x = dict(seq=p.seq + 1 - 2 * low)
    along_y = dict(seq=p.seq + 2 - 4 * high)
    others = [dict(img=lax.rem(chip + step, chips) * 2 + core) for step in range(1, chips)]
    width, wide, narrow = r.w_embed.shape[0], r.w_up.shape[1], r.w_embed.shape[1]
    rows = ENC_PAD

    def add(one, two):
        return (one.astype(f32) + two.astype(f32)).astype(bf16)

    held, first, second, from_chips, gathered = (
        r.held, r.first, r.second, r.from_chips, r.gathered
    )

    def pair_copy(i):
        return remote(r.leaving.at[i], r.from_pair.at[i], r.pair_sem.at[i], partner)

    def first_copies(i):
        return (
            remote(held.at[i, :, 0, :, 1 - low], first.at[i, 0], r.first_sem.at[i, 0], along_x),
            remote(held.at[i, :, 1, 1 - high], first.at[i, 1], r.first_sem.at[i, 1], along_y),
        )

    def second_copies(i):
        return (
            remote(
                held.at[i, :, 0, 1 - high, low], second.at[i, 0], r.second_sem.at[i, 0], along_y
            ),
            remote(
                held.at[i, :, 1, high, 1 - low], second.at[i, 1], r.second_sem.at[i, 1], along_x
            ),
        )

    def chip_copies(i):
        return [
            remote(
                held.at[i, device["img"] // 2, :, high, low],
                from_chips.at[i, step],
                r.chip_sem.at[i, step],
                device,
            )
            for step, device in enumerate(others)
        ]

    def gather_copies(i, arrive):
        x_place = 1 - low if arrive else low
        y_place = 1 - high if arrive else high
        one, two = gathered.at[i, 0, high, x_place], gathered.at[i, 1, y_place, low]
        return (
            remote(one, one, r.gather_sem.at[i, 0], along_x),
            remote(two, two, r.gather_sem.at[i, 1], along_y),
        )

    def spread_copies(i, arrive):
        x_place = 1 - low if arrive else low
        y_place = 1 - high if arrive else high
        one, two = gathered.at[i, 0, y_place], gathered.at[i, 1, :, x_place]
        return (
            remote(one, one, r.gather_sem.at[i, 2], along_y),
            remote(two, two, r.gather_sem.at[i, 3], along_x),
        )

    def share_copy(i):
        return pltpu.make_async_copy(gathered.at[i], r.shares.at[i], r.share_sem.at[i])

    def stage_pair(i):
        pair_copy(i).wait()
        for image in range(chips):
            held[i, image] = add(held[i, image], r.from_pair[i, image])

    def stage_first(i):
        for copy in first_copies(i):
            copy.start()

    def stage_second(i):
        for copy in first_copies(i):
            copy.wait_recv()
        held[i, :, 0, :, low] = add(held[i, :, 0, :, low], first[i, 0])
        held[i, :, 1, high] = add(held[i, :, 1, high], first[i, 1])
        for copy in second_copies(i):
            copy.start()

    def stage_chips(i):
        for copy in second_copies(i):
            copy.wait_recv()
        held[i, :, 0, high, low] = add(held[i, :, 0, high, low], second[i, 0])
        held[i, :, 1, high, low] = add(held[i, :, 1, high, low], second[i, 1])
        for copy in chip_copies(i):
            copy.start()

    def stage_gather(i):
        for copy in chip_copies(i):
            copy.wait_recv()
        mine = held[i, chip, :, high, low].astype(f32)
        for step in range(chips - 1):
            mine += from_chips[i, step].astype(f32)
        gathered[i, :, high, low] = mine.astype(bf16)
        for copy in gather_copies(i, False):
            copy.start()

    def stage_spread(i):
        for copy in gather_copies(i, True):
            copy.wait_recv()
        for copy in spread_copies(i, False):
            copy.start()

    def stage_end(i):
        for copy in spread_copies(i, True):
            copy.wait_recv()
        for copy in (
            *first_copies(i), *second_copies(i), *chip_copies(i), *gather_copies(i, False),
            *spread_copies(i, False),
        ):
            copy.wait_send()
        share_copy(i).start()

    stages = (stage_first, stage_second, stage_chips, stage_gather, stage_spread, stage_end)
    line = []

    def pump(piece):
        line.append(piece)
        for lag in range(len(stages)):
            slot = len(line) - 1 - lag
            if slot >= 0 and line[slot] is not None:
                stages[lag](line[slot])

    greeted = p.greet([partner, along_x, along_y, *others])

    def put_dec(grad, first_image, count, row):
        grad = grad.astype(bf16)
        for case in (0, 1):

            @pl.when(core == case)
            def _():
                for index in range(grad.shape[0] // count):
                    image = first_image + index
                    ref = held if image % 2 == case else r.leaving
                    for block in range(grad.shape[1] // LANES):
                        for piece, half, up, across, begin, end, at in sub_rows(
                            row + block * count, count
                        ):
                            ref[piece, image // 2, half, up, across, begin:end] = grad[
                                index * count + at : index * count + at + end - begin,
                                block * LANES : (block + 1) * LANES,
                            ]

    def decoder(
        dec_input, att, inverses, cot, w_proj, w_up, w_down, w_qkv, mixed, other_kv, chances,
        small_chances, decoded, grad_middle, grad_att, grad_mixed, grad_kv, kv_leaving,
    ):
        load = loader(
        r.load_sem,
        dec_input=(r.dec_input, dec_input),
        att=(r.dec_att, att),
        proj=(r.dec_proj, w_proj),
        up=(r.dec_up, w_up),
        cot=(r.cot, cot),
        down=(r.dec_down, w_down),
        mixed=(r.dec_mixed, mixed),
        other=(r.dec_other_kv, other_kv),
        qkv=(r.dec_qkv, w_qkv),
        inverses=(r.dec_inverse, inverses),
    )

        def chance_copies(head, slot):
            return (
                pltpu.make_async_copy(
                    r.big_probs.at[head], chances.at[slot], r.chance_sem.at[slot, 0]
                ),
                pltpu.make_async_copy(
                    r.small_probs.at[head], small_chances.at[slot], r.chance_sem.at[slot, 1]
                ),
            )

        for copy in chance_copies(0, 0):
            copy.start()
        greeted()

        ready(load.dec_input, load.att, load.proj)
        vecs = r.dec_vecs
        middle = dec_input[...] + product(att[...], w_proj[...])
        normed, inverse = norm_parts(middle)
        mlp_in = (normed * vecs[2:3] + vecs[3:4]).astype(bf16)
        result = middle
        grad_norm = jnp.zeros_like(middle)
        step = 2 * w_down.shape[0] // (2 * chips)
        down_count, up_count = step // 2, narrow // (2 * chips)
        up_row = down_count * narrow // LANES
        proj_row = up_row + up_count * w_up.shape[1] // LANES
        ready(load.up, load.cot, load.down)
        for block in range(w_up.shape[1] // step):
            cols = slice(block * step, (block + 1) * step)
            active, slope = gelu_parts(product(mlp_in, w_up[:, cols]))
            active = active.astype(bf16)
            result += product(active, w_down[cols])
            put_dec(inner_rows(active, cot[...]), 2 * block, down_count, 0)
            grad_hidden = (slope * inner_cols(cot[...], w_down[cols])).astype(bf16)
            put_dec(
                inner_rows(mlp_in, grad_hidden), 0, up_count,
                up_row + up_count * block * step // LANES,
            )
            grad_norm += inner_cols(grad_hidden, w_up[:, cols])
        order = row_order(core, DEC_PAD // 2, (SMALL + HALF) // 2)
        decoded[...] = (
            inner_rows(order, result.astype(bf16)).astype(bf16).reshape(2, DEC_PAD // 2, narrow)
        )

        def decoded_parts(segment):
            return [(decoded.at[segment], r.home_rows.at[low])]

        p.send_home(start_copy, decoded_parts, r.rows_sem)
        grad_values, gain, shift = norm_backward(grad_norm, normed, inverse, vecs[2:3])
        r.vec_own[...] = jnp.zeros(r.vec_own.shape, f32)
        r.vec_own[10:11, :narrow] = gain
        r.vec_own[11:12, :narrow] = shift
        back = cot[...].astype(f32) + grad_values
        grad_middle[...] = back
        back = back.astype(bf16)
        ready(load.inverses)
        grad_low = inner_cols(back, w_proj[...]).astype(bf16)
        grad_att[...] = (grad_low.astype(f32) * inverses[...]).astype(bf16)
        put_dec(inner_rows(att[...], back), 0, up_count, proj_row)
        for i in range(MID_PIECES):
            pair_copy(i).start()

        ready(load.mixed, load.other)
        head_size = narrow // HD
        per_group = 128 // head_size
        scale = 1.0 / math.sqrt(head_size)
        masks, wide_masks = lane_masks(head_size, bf16), lane_masks(head_size, f32)

        def group_back(group, last):
            def cols(offset):
                return pl.ds(pl.multiple_of(offset * narrow + group * 128, 128), 128)

            query = mixed[:, cols(0)]
            small_key, small_value = mixed[:SMALL_PAD, cols(1)], mixed[:SMALL_PAD, cols(2)]
            keys = jnp.concatenate([mixed[SMALL_PAD:, cols(1)], other_kv[:, cols(0)]], axis=0)
            values = jnp.concatenate([mixed[SMALL_PAD:, cols(2)], other_kv[:, cols(1)]], axis=0)
            grads = grad_att[:, cols(0)]
            overlap = grads.astype(f32) * att[:, cols(0)].astype(f32)
            def turned(values):
                return values.astype(f32).T.astype(bf16)

            big_query, small_query = turned(query[SMALL_PAD:]), turned(query[:SMALL_PAD])
            big_grad, small_grad = turned(grads[SMALL_PAD:]), turned(grads[:SMALL_PAD])
            big_q = jnp.zeros((BIG_PAD, 128), f32)
            small_q = jnp.zeros((SMALL_PAD, 128), f32)
            big_k, big_v, small_k, small_v = [], [], [], []
            for head, mask in enumerate(masks):
                slot = head % 2
                number = group * per_group + head
                for copy in chance_copies(number, slot):
                    copy.wait()
                if head < per_group - 1:
                    for copy in chance_copies(number + 1, 1 - slot):
                        copy.start()
                else:

                    @pl.when(group < last)
                    def _():
                        for copy in chance_copies(number + 1, 1 - slot):
                            copy.start()

                delta = jnp.sum(overlap * wide_masks[head], axis=1, keepdims=True)
                one_grad = grads * mask
                own = slice(head * head_size, (head + 1) * head_size)
                probs = chances[slot]
                one = head_back(probs, one_grad[SMALL_PAD:], values, delta[SMALL_PAD:])
                big_q += product(one, keys * mask)
                big_k.append(product(big_query[own], one))
                big_v.append(product(big_grad[own], probs))
                probs = small_chances[slot]
                one = head_back(probs, one_grad[:SMALL_PAD], small_value, delta[:SMALL_PAD])
                small_q += product(one, small_key * mask)
                small_k.append(product(small_query[own], one))
                small_v.append(product(small_grad[own], probs))
            big_k, big_v, small_k, small_v = (
                jnp.concatenate(parts, axis=0).T for parts in (big_k, big_v, small_k, small_v)
            )
            grad_mixed[:SMALL_PAD, cols(0)] = (small_q * scale).astype(bf16)
            grad_mixed[SMALL_PAD:, cols(0)] = (big_q * scale).astype(bf16)
            grad_mixed[:SMALL_PAD, cols(1)] = (small_k * scale).astype(bf16)
            grad_mixed[:SMALL_PAD, cols(2)] = small_v.astype(bf16)
            grad_kv[:, cols(0)] = big_k[:BIG_PAD] * scale
            grad_kv[:, cols(1)] = big_v[:BIG_PAD]
            kv_leaving[:, cols(0)] = (big_k[BIG_PAD:] * scale).astype(bf16)
            kv_leaving[:, cols(1)] = big_v[BIG_PAD:].astype(bf16)

        groups = narrow // 128
        for group in range(groups):
            lax.fori_loop(
                group, group + 1, lambda g, c: (group_back(g, groups - 1), c)[1], 0
            )
            if group < MID_PIECES:
                stage_pair(group)
                pump(group)
        kv_copy = remote(kv_leaving, r.dec_kv_in, r.swap_sem.at[1], partner)
        kv_copy.start()
        pump(None)

        normed, inverse = norm_parts(dec_input[...])
        attn_in = (normed * vecs[0:1] + vecs[1:2]).astype(bf16)
        chosen = chosen_rows(core, r.row_ids[...])
        seen = jnp.sum(chosen, axis=1, keepdims=True)
        ready(load.qkv)
        kv_copy.wait()
        grad_mixed[SMALL_PAD:, narrow:] = (grad_kv[...] + r.dec_kv_in[...].astype(f32)).astype(bf16)
        grad_values, gain, shift = norm_backward(
            inner_cols(grad_mixed[...], w_qkv[...]), normed, inverse, vecs[0:1]
        )
        r.vec_own[8:9, :narrow] = gain
        r.vec_own[9:10, :narrow] = shift
        back = grad_middle[...] + grad_values
        spread = inner_rows(chosen.astype(bf16), back.astype(bf16)).astype(bf16)
        r.spread_own[...] = spread[:rows]
        r.spread_leaving[...] = spread[rows:]
        spread_copy.start()
        pump(None)
        r.vec_own[12:13, :narrow] = jnp.sum(
            jnp.where(seen > 0.0, 0.0, back), axis=0, keepdims=True
        )
        put_dec(inner_rows(attn_in, grad_mixed[...]), 0, up_count, MID_PIECES * SUB_ROWS)
        pair_copy(MID_PIECES).start()
        pump(None)
        p.send_home(wait_copy, decoded_parts, r.rows_sem)

    spread_copy = remote(r.spread_leaving, r.spread_in, r.swap_sem.at[2], partner)
    dec_rows, big = DEC_PAD, BIG_PAD
    pl.run_scoped(
        decoder,
        pltpu.VMEM((dec_rows, narrow), f32),
        pltpu.VMEM((dec_rows, narrow), bf16),
        pltpu.VMEM((dec_rows, narrow), f32),
        pltpu.VMEM((dec_rows, narrow), bf16),
        pltpu.VMEM(r.dec_proj.shape, bf16),
        pltpu.VMEM(r.dec_up.shape, bf16),
        pltpu.VMEM(r.dec_down.shape, bf16),
        pltpu.VMEM(r.dec_qkv.shape, bf16),
        pltpu.VMEM((dec_rows, 3 * narrow), bf16),
        pltpu.VMEM((big, 2 * narrow), bf16),
        pltpu.VMEM((2, big, 2 * big), bf16),
        pltpu.VMEM((2, SMALL_PAD, SMALL_PAD), bf16),
        pltpu.VMEM((2, dec_rows // 2, narrow), bf16),
        pltpu.VMEM((dec_rows, narrow), f32),
        pltpu.VMEM((dec_rows, narrow), bf16),
        pltpu.VMEM((dec_rows, 3 * narrow), bf16),
        pltpu.VMEM((big, 2 * narrow), f32),
        pltpu.VMEM((big, 2 * narrow), bf16),
    )

    def encoder(
        v_embed, v_down, v_up, v_proj, v_out, v_middle, v_slope, v_att, v_probs, v_query,
        v_own_kv, v_other_kv, v_x, v_lefts, v_lefts_other, right_own, kv_own, kv_leaving, grad_rows,
    ):
        load = loader(
        r.load_sem.at[10:],
        embed=(r.w_embed, v_embed),
        out=(r.out, v_out),
        down=(r.w_down, v_down),
        slope=(r.slope, v_slope),
        lefts=(r.lefts_own, v_lefts),
        lefts_other=(r.lefts_other, v_lefts_other),
        up=(r.w_up, v_up),
        middle=(r.middle, v_middle),
        proj=(r.w_proj, v_proj),
        att=(r.att, v_att),
        probs=(r.probs, v_probs),
        query=(r.query, v_query),
        own_kv=(r.own_kv, v_own_kv),
        other_kv=(r.other_kv, v_other_kv),
        x=(r.x, v_x),
    )
        vecs = r.enc_vecs
        starts = [0]
        for columns in (width, wide, narrow, width, 3 * width):
            starts.append(starts[-1] + columns)
        out_at, hidden_at, embedded_at, middle_at, all_mixed_at = (
            slice(*pair) for pair in zip(starts, starts[1:])
        )

        def give(cols, value, index):
            if value is not None:
                right_own[:, cols] = value
            copy = remote(
                right_own.at[:, cols], r.right_other.at[:, cols], r.swap_sem.at[index], partner
            )
            copy.start()
            return copy

        def weight_grad(cols, left, count, row):
            own = v_lefts[:, left : left + count].reshape(chips * count, rows)
            other = v_lefts_other[:, left : left + count].reshape(chips * count, rows)
            for block in range((cols.stop - cols.start) // LANES):
                columns = slice(cols.start + block * LANES, cols.start + (block + 1) * LANES)
                grad = product(own, right_own[:, columns]) + product(
                    other, r.right_other[:, columns]
                )
                grad = grad.astype(bf16)
                for piece, half, up, across, begin, end, at in sub_rows(
                    row + block * count, count
                ):
                    for image in range(chips):
                        held[piece, image, half, up, across, begin:end] = grad[
                            image * count + at : image * count + at + end - begin
                        ]

        left_hidden, left_mid = wide // (2 * chips), width // (2 * chips)
        left_mlp = left_hidden
        left_att, left_final, left_attn = (left_hidden + place * left_mid for place in (1, 2, 3))

        spread_copy.wait()
        grad_embedded = r.spread_own[...] + r.spread_in[...]
        embedded_copy = give(embedded_at, grad_embedded, 3)
        ready(load.embed, load.out)
        normed, inverse = norm_parts(v_out[...])
        grad_out, gain, shift = norm_backward(
            inner_cols(grad_embedded, v_embed[...]), normed, inverse, vecs[4:5]
        )
        r.vec_own[4:5] = gain
        r.vec_own[5:6] = shift
        grad_low = grad_out.astype(bf16)
        out_copy = give(out_at, grad_low, 4)
        ready(load.down, load.slope)
        grad_hidden = (v_slope[...].astype(f32) * inner_cols(grad_low, v_down[...])).astype(bf16)
        qkv_copies = [
            pltpu.make_async_copy(
                r.w_qkv.at[:, part * width : (part + 1) * width],
                v_down.at[part * width : (part + 1) * width],
                r.load_sem.at[25 + part],
            )
            for part in range(3)
        ]
        for copy in qkv_copies:
            copy.start()
        hidden_copy = give(hidden_at, grad_hidden, 5)
        stage_pair(MID_PIECES)
        pump(MID_PIECES)
        ready(load.lefts, load.lefts_other)
        out_copy.wait()
        weight_grad(out_at, 0, left_hidden, DOWN_AT * SUB_ROWS)
        pump(DOWN_AT)
        hidden_copy.wait()
        weight_grad(hidden_at, left_mlp, left_mid, UP_AT * SUB_ROWS)
        pump(UP_AT)
        ready(load.up, load.middle, load.proj)
        normed, inverse = norm_parts(v_middle[...])
        grad_values, gain, shift = norm_backward(
            inner_cols(grad_hidden, v_up[...]), normed, inverse, vecs[2:3]
        )
        r.vec_own[2:3] = gain
        r.vec_own[3:4] = shift
        grad_middle = grad_out + grad_values
        grad_low = grad_middle.astype(bf16)
        middle_copy = give(middle_at, grad_low, 6)
        grads = inner_cols(grad_low, v_proj[...]).astype(bf16)

        ready(load.att, load.probs, load.query, load.own_kv, load.other_kv)
        head_size = width // HE
        scale = 1.0 / math.sqrt(head_size)
        overlap = grads.astype(f32) * v_att[...].astype(f32)
        masks = lane_masks(head_size, bf16)
        wide_masks = lane_masks(head_size, f32)
        mixed_at = all_mixed_at.start
        for pair in range(width // 128):
            cols = slice(128 * pair, 128 * pair + 128)
            value_cols = slice(width + 128 * pair, width + 128 * pair + 128)
            keys = jnp.concatenate([v_own_kv[:, cols], v_other_kv[:, cols]], axis=0)
            values = jnp.concatenate([v_own_kv[:, value_cols], v_other_kv[:, value_cols]], axis=0)
            total_q = jnp.zeros((rows, 128), f32)
            total_k = jnp.zeros((2 * rows, 128), f32)
            total_v = jnp.zeros((2 * rows, 128), f32)
            for head, mask in enumerate(masks):
                delta = jnp.sum(overlap[:, cols] * wide_masks[head], axis=1, keepdims=True)
                one_grad = grads[:, cols] * mask
                chances = v_probs[len(masks) * pair + head]
                one_back = head_back(chances, one_grad, values, delta)
                total_q += product(one_back, keys * mask)
                total_k += inner_rows(one_back, v_query[:, cols] * mask)
                total_v += inner_rows(chances, one_grad)
            right_own[:, mixed_at + 128 * pair : mixed_at + 128 * pair + 128] = (
                total_q * scale
            ).astype(bf16)
            kv_own[:, cols] = total_k[:rows] * scale
            kv_own[:, value_cols] = total_v[:rows]
            kv_leaving[:, cols] = (total_k[rows:] * scale).astype(bf16)
            kv_leaving[:, value_cols] = total_v[rows:].astype(bf16)
        kv_copy = remote(kv_leaving, r.kv_in, r.swap_sem.at[7], partner)
        kv_copy.start()
        pump(UP_AT + 1)

        kv_copy.wait()
        right_own[:, mixed_at + width : mixed_at + 3 * width] = (
            kv_own[...] + r.kv_in[...].astype(f32)
        ).astype(bf16)
        mixed_copy = give(all_mixed_at, None, 8)
        ready(load.x)
        normed, inverse = norm_parts(v_x[...].reshape(rows, width).astype(f32))
        grad_norm = jnp.zeros((rows, width), f32)
        for part, copy in enumerate(qkv_copies):
            copy.wait()
            place = mixed_at + part * width
            grad_norm += inner_cols(
                right_own[:, place : place + width], v_down[part * width : (part + 1) * width]
            )
        grad_values, gain, shift = norm_backward(grad_norm, normed, inverse, vecs[0:1])
        r.vec_own[0:1] = gain
        r.vec_own[1:2] = shift
        vec_copy = remote(r.vec_own, r.vec_in, r.swap_sem.at[9], partner)
        vec_copy.start()
        grad_values = grad_middle + grad_values
        grad_rows[0] = grad_values[: rows // 2]
        grad_rows[1] = grad_values[rows // 2 :]

        def grad_parts(segment):
            return [(grad_rows.at[segment], r.home_grad.at[low])]

        p.send_home(start_copy, grad_parts, r.grad_sem)
        pump(UP_AT + 2)
        middle_copy.wait()
        embedded_copy.wait()
        embed_row = ATT_AT * SUB_ROWS + left_mid * width // LANES
        weight_grad(middle_at, left_att, left_mid, ATT_AT * SUB_ROWS)
        weight_grad(embedded_at, left_final, left_mid, embed_row)
        pump(DOWN_AT + 1)
        mixed_copy.wait()
        qkv_row = embed_row + left_mid * narrow // LANES
        weight_grad(all_mixed_at, left_attn, left_mid, qkv_row)
        pump(DOWN_AT + 2)
        vec_copy.wait()
        vectors = (r.vec_own[...] + r.vec_in[...]).astype(bf16)
        vec_row = qkv_row + left_mid * 3 * width // LANES
        piece, half, up, across, begin, end, _ = next(iter(sub_rows(vec_row, 16)))
        entry = lax.broadcasted_iota(jnp.int32, (width, LANES), 0)
        lane = lax.broadcasted_iota(jnp.int32, (width, LANES), 1)
        row_index = lax.broadcasted_iota(jnp.int32, (16, LANES), 0)
        narrow_left = narrow // (2 * chips)
        for image in range(chips):
            number = 2 * image + core
            enc_pick = (entry == lane + number * left_mid) & (lane < left_mid)
            dec_pick = (entry == lane + number * narrow_left) & (lane < narrow_left)
            enc_part = product(vectors, enc_pick.astype(f32).astype(bf16))
            dec_part = product(vectors, dec_pick.astype(f32).astype(bf16))
            held[piece, image, half, up, across, begin:end] = jnp.where(
                row_index < 8, enc_part, dec_part
            ).astype(bf16)
        for piece in range(ATT_AT, PIECES):
            pump(piece)
        p.send_home(wait_copy, grad_parts, r.grad_sem)

    pl.run_scoped(
        encoder,
        pltpu.VMEM(r.w_embed.shape, bf16),
        pltpu.VMEM(r.w_down.shape, bf16),
        pltpu.VMEM(r.w_up.shape, bf16),
        pltpu.VMEM(r.w_proj.shape, bf16),
        pltpu.VMEM(r.out.shape, f32),
        pltpu.VMEM(r.middle.shape, f32),
        pltpu.VMEM(r.slope.shape, bf16),
        pltpu.VMEM(r.att.shape, bf16),
        pltpu.VMEM(r.probs.shape, bf16),
        pltpu.VMEM(r.query.shape, bf16),
        pltpu.VMEM(r.own_kv.shape, bf16),
        pltpu.VMEM(r.other_kv.shape, bf16),
        pltpu.VMEM(r.x.shape, bf16),
        pltpu.VMEM(r.lefts_own.shape, bf16),
        pltpu.VMEM(r.lefts_own.shape, bf16),
        pltpu.VMEM(r.right_other.shape, bf16),
        pltpu.VMEM((rows, 2 * width), f32),
        pltpu.VMEM((rows, 2 * width), bf16),
        pltpu.VMEM((2, ENC_SEG, width), f32),
    )
    for _ in range(len(stages) - 1):
        pump(None)
    lax.fori_loop(0, PIECES, lambda i, c: (share_copy(i).wait(), c)[1], 0)


def back(chips, args):
    anywhere = pl.BlockSpec(memory_space=pl.ANY)
    vmem = pl.BlockSpec(memory_space=pltpu.VMEM)
    block = (EIGHTH, LANES)
    dma = pltpu.SemaphoreType.DMA
    width, narrow = by_name(args).w_embed.shape
    wide = by_name(args).w_up.shape[1]
    rights = width + wide + narrow + width + 3 * width
    outs = dict(
        shares=((PIECES, 2, 2, 2) + block, bf16),
        home_rows=((2, DEC_PAD // 2, narrow), bf16),
        home_grad=((2, ENC_SEG, width), f32),
    )
    scratch = dict(
        held=pltpu.VMEM((PIECES, chips, 2, 2, 2) + block, bf16),
        leaving=pltpu.VMEM((DEC_PIECES, chips, 2, 2, 2) + block, bf16),
        from_pair=pltpu.VMEM((DEC_PIECES, chips, 2, 2, 2) + block, bf16),
        first=pltpu.VMEM((PIECES, 2, chips, 2) + block, bf16),
        second=pltpu.VMEM((PIECES, 2, chips) + block, bf16),
        from_chips=pltpu.VMEM((PIECES, chips - 1, 2) + block, bf16),
        gathered=pltpu.VMEM((PIECES, 2, 2, 2) + block, bf16),
        dec_kv_in=pltpu.VMEM((BIG_PAD, 2 * narrow), bf16),
        spread_own=pltpu.VMEM((ENC_PAD, narrow), bf16),
        spread_leaving=pltpu.VMEM((ENC_PAD, narrow), bf16),
        spread_in=pltpu.VMEM((ENC_PAD, narrow), bf16),
        right_other=pltpu.VMEM((ENC_PAD, rights), bf16),
        kv_in=pltpu.VMEM((ENC_PAD, 2 * width), bf16),
        vec_own=pltpu.VMEM((16, width), f32),
        vec_in=pltpu.VMEM((16, width), f32),
        load_sem=dma((28,)),
        chance_sem=dma((2, 2)),
        pair_sem=dma((DEC_PIECES, 2)),
        first_sem=dma((PIECES, 2, 2)),
        second_sem=dma((PIECES, 2, 2)),
        chip_sem=dma((PIECES, chips - 1, 2)),
        gather_sem=dma((PIECES, 4, 2)),
        share_sem=dma((PIECES,)),
        swap_sem=dma((10, 2)),
        rows_sem=dma((2, 1, 2)),
        grad_sem=dma((2, 1, 2)),
    )
    names = list(args) + list(outs) + list(scratch)
    in_vmem = ("row_ids", "dec_vecs", "enc_vecs")
    return pl.pallas_call(
        functools.partial(back_kernel, chips, names),
        out_shape=[jax.ShapeDtypeStruct(shape, kind) for shape, kind in outs.values()],
        in_specs=[vmem if name in in_vmem else anywhere for name in args],
        out_specs=[anywhere] * len(outs),
        scratch_shapes=list(scratch.values()),
        compiler_params=pltpu.CompilerParams(
            collective_id=1, has_side_effects=True, vmem_limit_bytes=63 << 20
        ),
    )(*args.values())


def unstack_kernel(counts, enc_count, dec_count, flat, *outs):
    place = 0
    for out, count in zip(outs, counts):
        for block in range(out.shape[1] // LANES):
            out[:, block * LANES : (block + 1) * LANES] = flat[place : place + count].astype(f32)
            place += count
    rows = flat[place : place + 16].astype(f32)
    outs[-2][...] = rows[:6, :enc_count]
    outs[-1][...] = rows[8:13, :dec_count]


def reduce_rest(chunk, seq):
    chips, rows, width = chunk.shape
    high, low = seq // 2, seq % 2
    eighth = rows // 8
    parts = chunk.reshape(chips, 2, 2, 2, eighth, width)

    def along_x(array):
        return permute(array, lambda s, i: (s ^ 1, i))

    def along_y(array):
        return permute(array, lambda s, i: (s ^ 2, i))

    def add(one, two):
        return (one.astype(f32) + two.astype(f32)).astype(bf16)

    one, two = parts[:, 0], parts[:, 1]
    one = add(pick(one, low, 2), along_x(pick(one, 1 - low, 2)))
    two = add(pick(two, high, 1), along_y(pick(two, 1 - high, 1)))
    one = add(pick(one, high, 1), along_y(pick(one, 1 - high, 1)))
    two = add(pick(two, low, 1), along_x(pick(two, 1 - low, 1)))
    mine = jnp.stack([one, two], axis=1)
    chip = lax.axis_index("img") // 2
    total = pick(mine, chip, 0).astype(f32)
    for step in range(1, chips):
        leaving = pick(mine, (chip + step) % chips, 0)
        arrived = permute(
            leaving,
            lambda s, i, step=step: (s, ((i // 2 + step) % chips) * 2 + (i & 1)),
        )
        total = total + arrived.astype(f32)
    own = total.astype(bf16)
    others = [permute(own, lambda s, i, step=step: (s ^ step, i)) for step in (1, 2, 3)]
    by_xor = jnp.stack([own] + others)
    ordered = jnp.stack([pick(by_xor, seq ^ place, 0) for place in range(4)], axis=1)
    return ordered.reshape(rows, width)


def shards(
    enc_input,
    cotangent,
    enc_image,
    visible_rows,
    enc_norms,
    enc_qkv,
    enc_proj,
    enc_up,
    enc_down,
    embed,
    dec_vecs,
    dec_qkv,
    dec_proj,
    dec_up,
    dec_down,
):
    seq = lax.axis_index("seq")
    img = lax.axis_index("img")
    images = lax.axis_size("img")
    core = img % 2
    odd = seq % 2 == 1
    enc_width = enc_input.shape[3]
    dec_width = dec_vecs.shape[0]
    enc_half = 2 * enc_input.shape[2]
    dec_quarter = cotangent.shape[2]

    enc_vecs = jnp.pad(enc_norms.T, ((0, 2), (0, 0)))
    dec_rows_vecs = jnp.pad(dec_vecs.T, ((0, 3), (0, 0)))
    table = position_table(dec_width)
    codes = np.zeros((2, DEC_PAD, dec_width), np.float32)
    for which in range(2):
        codes[which, :SMALL] = table[:SMALL]
        codes[which, SMALL_PAD : SMALL_PAD + HALF] = table[which * HALF : (which + 1) * HALF]
    chips = images // 2
    tables = jnp.stack([enc_image[0], visible_rows[0]])
    if images == 8:
        segments = tables.reshape(2, 2, 2, 2, enc_half // 2)
        segments = jnp.pad(
            segments, ((0, 0),) * 4 + ((0, ENC_SEG - enc_half // 2),), constant_values=-2
        )
        segments = segments.reshape(2, 2, 2, ENC_PAD)
        straight = segments.reshape(2, 2, 1, 2 * ENC_PAD)
        crossed = segments[:, :, ::-1].reshape(2, 2, 1, 2 * ENC_PAD)
        ordered = jnp.stack(
            [jnp.where(core == 0, straight, crossed), jnp.where(core == 0, crossed, straight)]
        )
        weights = dict(
            w_embed=embed, w_down=enc_down, w_up=enc_up, w_proj=enc_proj,
            w_qkv=enc_qkv, dec_qkv=dec_qkv, enc_vecs=enc_norms.T, dec_vecs=dec_vecs.T,
        )
        kept = front(
            dict(
                enc_input=enc_input[0], cotangent=cotangent[0], tables=ordered,
                codes=jnp.asarray(codes), **weights,
            ),
            chips,
        )
        shares, home_rows, home_grad = back(
            chips,
            dict(
                **kept, **weights, dec_proj=dec_proj, dec_up=dec_up, dec_down=dec_down
            ),
        )
        shapes = (
            dec_down.shape, dec_up.shape, dec_proj.shape, dec_qkv.shape, enc_down.shape,
            enc_up.shape, enc_proj.shape, embed.shape, enc_qkv.shape,
        )
        counts = [shape[0] // images for shape in shapes]
        (
            dec_down_share, dec_up_share, dec_proj_share, dec_qkv_share, enc_down_share,
            enc_up_share, enc_proj_share, embed_share, enc_qkv_share, enc_norm_share,
            dec_vec_share,
        ) = call(
            functools.partial(
                unstack_kernel, counts, enc_width // images, dec_width // images
            ),
            0,
            [((count, shape[1]), f32) for count, shape in zip(counts, shapes)]
            + [((6, enc_width // images), f32), ((5, dec_width // images), f32)],
            (shares.reshape(-1, LANES),),
            40,
        )
        enc_norm_share, dec_vec_share = enc_norm_share.T, dec_vec_share.T
        grad_input = home_grad[None, :, : enc_half // 2]
        decoded = home_rows[None, :, :dec_quarter]
        return (
            decoded,
            grad_input,
            enc_norm_share,
            enc_qkv_share,
            enc_proj_share,
            enc_up_share,
            enc_down_share,
            embed_share,
            dec_vec_share,
            dec_qkv_share,
            dec_proj_share,
            dec_up_share,
            dec_down_share,
        )

    other_tables = swap(tables)
    tables = jnp.where(seq // 2 == core, tables, other_tables)
    tables = jnp.where(odd, tables[:, 1], tables[:, 0])
    segments = tables.reshape(2, 2, 2, enc_half // 2)
    segments = jnp.pad(
        segments, ((0, 0),) * 3 + ((0, ENC_SEG - enc_half // 2),), constant_values=-2
    )
    halves = segments.reshape(2, 2, ENC_PAD)
    own = pick(halves, core, 1)
    ids = jnp.concatenate([own, pick(halves, 1 - core, 1)], axis=1)
    row_ids = ids[1:2]
    core_arg = core.reshape(1)

    blocks = jnp.pad(enc_input[0], ((0, 0), (0, ENC_SEG - enc_half // 2), (0, 0)))
    x = jnp.concatenate(exchange_packs(blocks, odd), axis=0)
    cot = jnp.concatenate(exchange_packs(cotangent[0], odd), axis=0)
    cot = jnp.concatenate(
        [
            pad_rows(lax.dynamic_slice_in_dim(cot, core * HALF, SMALL, 0), SMALL_PAD),
            pad_rows(lax.dynamic_slice_in_dim(cot, (1 - core) * SMALL, HALF, 0), BIG_PAD),
        ],
        axis=0,
    )
    enc_hidden_width = enc_up.shape[1]

    enc_query, enc_kv = call(
        enc_pre_kernel,
        0,
        [((ENC_PAD, enc_width), bf16), ((ENC_PAD, 2 * enc_width), bf16)],
        (x, enc_vecs, enc_qkv),
        40,
    )
    enc_other = swap(enc_kv)
    embedded, enc_att, enc_probs, enc_middle, enc_active, enc_slope, enc_out = call(
        enc_main_kernel,
        0,
        [
            ((ENC_PAD, dec_width), bf16),
            ((ENC_PAD, enc_width), bf16),
            ((HE, ENC_PAD, 2 * ENC_PAD), bf16),
            ((ENC_PAD, enc_width), f32),
            ((ENC_PAD, enc_hidden_width), bf16),
            ((ENC_PAD, enc_hidden_width), bf16),
            ((ENC_PAD, enc_width), f32),
        ],
        (
            x, enc_query, enc_kv, enc_other, own[0][:, None], ids[0:1], enc_vecs,
            enc_proj, enc_up, enc_down, embed,
        ),
        48,
    )

    code = pick(jnp.asarray(codes), core, 0)
    dec_input, dec_mixed, big_kv = call(
        dec_pre_kernel,
        1,
        [
            ((DEC_PAD, dec_width), f32),
            ((DEC_PAD, 3 * dec_width), bf16),
            ((BIG_PAD, 2 * dec_width), bf16),
        ],
        (core_arg, embedded, swap(embedded), row_ids, code, dec_rows_vecs, dec_qkv),
        40,
    )
    other_kv = swap(big_kv)
    groups = dec_width // 128

    def columns(rows, offset=0):
        return pl.BlockSpec((rows, 128), lambda group: (0, offset + group))

    def heads(rows, cols):
        return pl.BlockSpec((HD // groups, rows, cols), lambda group: (group, 0, 0))

    qkv_specs = [
        columns(DEC_PAD),
        columns(DEC_PAD, groups),
        columns(DEC_PAD, 2 * groups),
        columns(BIG_PAD),
        columns(BIG_PAD, groups),
    ]
    qkv_args = (dec_mixed, dec_mixed, dec_mixed, other_kv, other_kv)
    prob_specs = [heads(BIG_PAD, 2 * BIG_PAD), heads(SMALL_PAD, SMALL_PAD)]
    dec_att, big_probs, small_probs = pl.pallas_call(
        dec_att_kernel,
        grid=(groups,),
        in_specs=qkv_specs,
        out_specs=[columns(DEC_PAD)] + prob_specs,
        out_shape=[
            jax.ShapeDtypeStruct((DEC_PAD, dec_width), bf16),
            jax.ShapeDtypeStruct((HD, BIG_PAD, 2 * BIG_PAD), bf16),
            jax.ShapeDtypeStruct((HD, SMALL_PAD, SMALL_PAD), bf16),
        ],
        compiler_params=pltpu.CompilerParams(vmem_limit_bytes=48 << 20),
    )(*qkv_args)
    chunk_mid = Chunk(images, [dec_down.shape, dec_up.shape, dec_proj.shape])
    decoded, grad_dec_middle, dec_grad_att, vectors_two, *mid_grads = call(
        functools.partial(dec_mid_kernel, chunk_mid),
        1,
        [
            ((DEC_PAD, dec_width), bf16),
            ((DEC_PAD, dec_width), f32),
            ((DEC_PAD, dec_width), bf16),
            ((2, dec_width), f32),
        ]
        + chunk_mid.outs(),
        (core_arg, dec_input, dec_att, cot, dec_rows_vecs, dec_proj, dec_up, dec_down),
        48,
    )
    grad_specs = [columns(DEC_PAD)] * 3 + [columns(BIG_PAD)] * 2
    grad_query, grad_key, grad_value, leaving_key, leaving_value = pl.pallas_call(
        dec_att_back_kernel,
        grid=(groups,),
        in_specs=qkv_specs + [columns(DEC_PAD)] * 2 + prob_specs,
        out_specs=grad_specs,
        out_shape=[
            jax.ShapeDtypeStruct((DEC_PAD, dec_width), bf16),
            jax.ShapeDtypeStruct((DEC_PAD, dec_width), f32),
            jax.ShapeDtypeStruct((DEC_PAD, dec_width), f32),
            jax.ShapeDtypeStruct((BIG_PAD, dec_width), bf16),
            jax.ShapeDtypeStruct((BIG_PAD, dec_width), bf16),
        ],
        compiler_params=pltpu.CompilerParams(vmem_limit_bytes=48 << 20),
    )(*qkv_args, dec_grad_att, dec_att, big_probs, small_probs)
    chunk_post = Chunk(images, [dec_qkv.shape])
    own_spread, other_spread, vectors_one, *post_grads = call(
        functools.partial(dec_post_kernel, chunk_post),
        1,
        [
            ((ENC_PAD, dec_width), bf16),
            ((ENC_PAD, dec_width), bf16),
            ((3, dec_width), f32),
        ]
        + chunk_post.outs(),
        (
            core_arg, dec_input, grad_dec_middle, grad_query, grad_key, grad_value,
            swap(leaving_key), swap(leaving_value), row_ids, dec_rows_vecs, dec_qkv,
        ),
        48,
    )
    arrived_spread = swap(other_spread)
    chunk_down = Chunk(images, [enc_down.shape])
    chunk_up = Chunk(images, [enc_up.shape])
    grad_enc_middle, enc_grad_att, enc_vectors_two, *mlp_grads = call(
        functools.partial(enc_mlp_back_kernel, chunk_down, chunk_up),
        1,
        [
            ((ENC_PAD, enc_width), f32),
            ((ENC_PAD, enc_width), bf16),
            ((4, enc_width), f32),
        ]
        + chunk_down.outs()
        + chunk_up.outs(),
        (
            core_arg, own_spread, arrived_spread, enc_out, enc_middle, enc_active, enc_slope,
            enc_vecs, embed, enc_down, enc_up, enc_proj,
        ),
        56,
    )
    down_grads, up_grads = mlp_grads[: len(chunk_down.outs())], mlp_grads[len(chunk_down.outs()) :]
    enc_grad_query, enc_grad_kv, enc_leaving = call(
        enc_att_back_kernel,
        0,
        [
            ((ENC_PAD, enc_width), bf16),
            ((ENC_PAD, 2 * enc_width), f32),
            ((ENC_PAD, 2 * enc_width), bf16),
        ],
        (enc_grad_att, enc_att, enc_probs, enc_query, enc_kv, enc_other),
        48,
    )
    chunk_att = Chunk(images, [enc_qkv.shape, enc_proj.shape, embed.shape], 16)
    grad_input, enc_vectors_one, *att_grads = call(
        functools.partial(enc_post_kernel, chunk_att),
        1,
        [((ENC_PAD, enc_width), f32), ((2, enc_width), f32)] + chunk_att.outs(),
        (
            core_arg, x, enc_att, grad_enc_middle, enc_grad_query, enc_grad_kv,
            swap(enc_leaving), enc_out, own_spread, arrived_spread, enc_vecs, enc_qkv,
        ),
        48,
    )

    def by_image(rows):
        flat = rows.reshape(rows.shape[0], images, rows.shape[1] // images)
        return flat.transpose(1, 0, 2).reshape(images, -1)

    vectors = jnp.concatenate(
        [
            by_image(jnp.concatenate([enc_vectors_one, enc_vectors_two])),
            by_image(jnp.concatenate([vectors_one[:2], vectors_two, vectors_one[2:]])),
        ],
        axis=1,
    ).astype(bf16)
    vectors = jnp.pad(vectors, ((0, 0), (0, 16 * LANES - vectors.shape[1])))
    vectors = vectors.reshape(images // 2, 2, 16, LANES)
    vectors = (pick(vectors, core, 1), pick(vectors, 1 - core, 1))
    chunk_pairs = [
        chunk.pair(grads, core)
        for chunk, grads in (
            (chunk_mid, mid_grads),
            (chunk_post, post_grads),
            (chunk_down, down_grads),
            (chunk_up, up_grads),
            (chunk_att, att_grads),
        )
    ]
    place = slice(chunk_att.used, chunk_att.used + 16)
    chunk_pairs[-1] = tuple(
        array.at[:, place].set(rows) for array, rows in zip(chunk_pairs[-1], vectors)
    )
    shares = [reduce_rest(reduce_pair(*pair), seq) for pair in chunk_pairs]
    mid_share, post_share, down_share, up_share, att_share = shares
    dec_down_share, dec_up_share, dec_proj_share = chunk_mid.split(mid_share)
    (dec_qkv_share,) = chunk_post.split(post_share)
    (enc_down_share,) = chunk_down.split(down_share)
    (enc_up_share,) = chunk_up.split(up_share)
    enc_qkv_share, enc_proj_share, embed_share = chunk_att.split(att_share)
    vectors = att_share[chunk_att.used : chunk_att.used + 16].reshape(-1).astype(f32)
    enc_count, dec_count = enc_width // images, dec_width // images
    enc_norm_share = vectors[: 6 * enc_count].reshape(6, enc_count).T
    dec_vec_share = vectors[6 * enc_count : 6 * enc_count + 5 * dec_count].reshape(5, dec_count).T

    start = jnp.concatenate([decoded[:SMALL], decoded[SMALL_PAD : SMALL_PAD + HALF]])
    end = jnp.concatenate([decoded[SMALL_PAD : SMALL_PAD + HALF], decoded[:SMALL]])
    natural = jnp.where(core == 0, start, end)
    decoded = jnp.stack(exchange_packs(natural.reshape(2, dec_quarter, dec_width), odd))[None]
    grad_input = jnp.stack(
        exchange_packs(grad_input.reshape(2, ENC_SEG, enc_width)[:, : enc_half // 2], odd)
    )[None]
    return (
        decoded,
        grad_input,
        enc_norm_share,
        enc_qkv_share,
        enc_proj_share,
        enc_up_share,
        enc_down_share,
        embed_share,
        dec_vec_share,
        dec_qkv_share,
        dec_proj_share,
        dec_up_share,
        dec_down_share,
    )


def solution(mesh):
    rows = P("img", None, "seq", None)
    tables = P("img", None, None)
    shares = P("img", None)
    return jax.shard_map(
        shards,
        mesh=mesh,
        in_specs=(rows, rows, tables, tables) + (P(),) * 11,
        out_specs=(rows, rows) + (shares,) * 11,
        check_vma=False,
    )
```

```python
import functools
import math

import jax
import jax.numpy as jnp
import numpy as np
from jax import lax
from jax.experimental import pallas as pl
from jax.experimental.pallas import tpu as pltpu
from jax.sharding import PartitionSpec as P

HE = 12
HD = 16
PATCHES = 784
SMALL = PATCHES // 4
HALF = PATCHES // 2
SMALL_PAD = 208
BIG_PAD = 400
DEC_PAD = SMALL_PAD + BIG_PAD
ENC_SEG = 80
ENC_PAD = 2 * ENC_SEG
BIG_LANES = 896
SMALL_LANES = 256
ENC_LANES = 384
LEFT_LANES = 256

eps_norm = 1e-06
masked_score = -1e30
bf16 = jnp.bfloat16
f32 = jnp.float32


def product(left_side, right_side):
    return jnp.dot(left_side, right_side, preferred_element_type=f32)


def inner_rows(left_side, right_side):
    return lax.dot_general(
        left_side, right_side, (((0,), (0,)), ((), ())), preferred_element_type=f32
    )


def inner_cols(left_side, right_side):
    return lax.dot_general(
        left_side, right_side, (((1,), (1,)), ((), ())), preferred_element_type=f32
    )


def norm_parts(values):
    centered = values - jnp.mean(values, axis=-1, keepdims=True)
    inverse = lax.rsqrt(jnp.mean(centered * centered, axis=-1, keepdims=True) + eps_norm)
    return centered * inverse, inverse


def norm_backward(grad_out, normed, inverse, norm_gain):
    scaled = grad_out * norm_gain
    grad_values = inverse * (
        scaled
        - jnp.mean(scaled, axis=-1, keepdims=True)
        - normed * jnp.mean(scaled * normed, axis=-1, keepdims=True)
    )
    return (
        grad_values,
        jnp.sum(grad_out * normed, axis=0, keepdims=True),
        jnp.sum(grad_out, axis=0, keepdims=True),
    )


def gelu_parts(hidden):
    below = 0.5 + 0.5 * lax.erf(hidden * math.sqrt(0.5))
    density = jnp.exp(hidden * hidden * -0.5) * (1.0 / math.sqrt(2.0 * math.pi))
    return hidden * below, below + hidden * density


LANES = 256
EIGHTH = 48
LAST_EIGHTH = 32
SUB_ROWS = 8 * EIGHTH


def put(core, dest, offset, grad):
    low = grad.astype(bf16)
    if len(dest) == 1:
        dest[0][...] = low
        return
    keep, leaving = dest
    chips = keep.shape[0]
    count = low.shape[0] // (2 * chips)
    for case in (0, 1):

        @pl.when(core == case)
        def _():
            for image in range(2 * chips):
                ref = keep if image % 2 == case else leaving
                for block in range(low.shape[1] // LANES):
                    start = offset + block * count
                    ref[image // 2, start : start + count, :] = low[
                        image * count : (image + 1) * count, block * LANES : (block + 1) * LANES
                    ]


def image_rows(shape, images):
    return shape[0] // images * (shape[1] // LANES)


class Chunk:
    def __init__(self, images, shapes, spare=0):
        self.images = images
        self.shapes = shapes
        self.offsets = []
        rows = 0
        for shape in shapes:
            self.offsets.append(rows)
            rows += image_rows(shape, images)
        self.used = rows
        rows += spare
        self.direct = all(shape[0] // images % 16 == 0 for shape in shapes)
        unit = SUB_ROWS if self.direct else 8
        self.rows = -(-rows // unit) * unit

    def outs(self):
        if self.direct:
            return [((self.images // 2, self.rows, LANES), bf16)] * 2
        return [(shape, bf16) for shape in self.shapes]

    def dests(self, refs):
        if self.direct:
            return [tuple(refs)] * len(self.shapes)
        return [(ref,) for ref in refs]

    def pair(self, results, core):
        if self.direct:
            return tuple(results)
        pieces = []
        for grad in results:
            for start in range(0, grad.shape[1], LANES):
                piece = grad[:, start : start + LANES]
                pieces.append(piece.reshape(self.images, -1, LANES))
        stacked = jnp.concatenate(pieces, axis=1)
        stacked = jnp.pad(stacked, ((0, 0), (0, self.rows - stacked.shape[1]), (0, 0)))
        both = stacked.reshape(self.images // 2, 2, self.rows, LANES)
        return pick(both, core, 1), pick(both, 1 - core, 1)

    def split(self, share):
        results = []
        for shape, offset in zip(self.shapes, self.offsets):
            count = shape[0] // self.images
            pieces = [
                share[offset + block * count : offset + (block + 1) * count]
                for block in range(shape[1] // LANES)
            ]
            results.append(jnp.concatenate(pieces, axis=1).astype(f32))
        return results


def call(kernel, scalars, outs, args, megabytes):
    vmem = pl.BlockSpec(memory_space=pltpu.VMEM)
    smem = pl.BlockSpec(memory_space=pltpu.SMEM)
    return pl.pallas_call(
        kernel,
        out_shape=[jax.ShapeDtypeStruct(shape, kind) for shape, kind in outs],
        in_specs=[smem] * scalars + [vmem] * (len(args) - scalars),
        out_specs=[vmem] * len(outs),
        compiler_params=pltpu.CompilerParams(vmem_limit_bytes=megabytes << 20),
    )(*args)


def lane_masks(head_size, kind):
    lanes = lax.broadcasted_iota(jnp.int32, (1, 128), 1) // head_size
    return [(lanes == head).astype(f32).astype(kind) for head in range(128 // head_size)]


def softmax_rows(scores, scale):
    row_max = jnp.max(scores, axis=1, keepdims=True)
    weights = jnp.exp2((scores - row_max) * (scale * math.log2(math.e)))
    return (weights * (1.0 / jnp.sum(weights, axis=1, keepdims=True))).astype(bf16)


def head_back(probs, grads, values, delta):
    grad_probs = inner_cols(grads, values)
    return (probs.astype(f32) * (grad_probs - delta)).astype(bf16)


def enc_pre_kernel(x, vecs, w_qkv, query, key_value):
    normed, _ = norm_parts(x[...].astype(f32))
    attn_in = (normed * vecs[0:1] + vecs[1:2]).astype(bf16)
    mixed = product(attn_in, w_qkv[...]).astype(bf16)
    width = query.shape[1]
    query[...] = mixed[:, :width]
    key_value[...] = mixed[:, width:]


def enc_main_kernel(
    x, query, own_kv, other_kv, own_ids, all_ids, vecs, w_proj, w_up, w_down, w_embed,
    embedded, att, probs, middle, active, slope, out
):
    width = query.shape[1]
    head_size = width // HE
    bias = jnp.where(own_ids[...] == all_ids[...], 0.0, masked_score)
    masks = lane_masks(head_size, bf16)
    for pair in range(width // 128):
        cols = slice(128 * pair, 128 * pair + 128)
        value_cols = slice(width + 128 * pair, width + 128 * pair + 128)
        keys = jnp.concatenate([own_kv[:, cols], other_kv[:, cols]], axis=0)
        values = jnp.concatenate([own_kv[:, value_cols], other_kv[:, value_cols]], axis=0)
        total = jnp.zeros((query.shape[0], 128), f32)
        for head, mask in enumerate(masks):
            scores = inner_cols(query[:, cols] * mask, keys) + bias
            chances = softmax_rows(scores, 1.0 / math.sqrt(head_size))
            probs[len(masks) * pair + head] = chances
            total += product(chances, values * mask)
        att[:, cols] = total.astype(bf16)
    mid = x[...].astype(f32) + product(att[...], w_proj[...])
    middle[...] = mid
    normed, _ = norm_parts(mid)
    mlp_in = (normed * vecs[2:3] + vecs[3:4]).astype(bf16)
    result, steepness = gelu_parts(product(mlp_in, w_up[...]))
    active[...] = result.astype(bf16)
    slope[...] = steepness.astype(bf16)
    last = mid + product(active[...], w_down[...])
    out[...] = last
    normed, _ = norm_parts(last)
    final = (normed * vecs[4:5] + vecs[5:6]).astype(bf16)
    embedded[...] = product(final, w_embed[...]).astype(bf16)


def chosen_rows(core, visible_rows):
    index = lax.broadcasted_iota(jnp.int32, (DEC_PAD, 1), 0)
    small = index + core * (SMALL + PATCHES)
    big = index + (SMALL - SMALL_PAD) + core * HALF
    row = jnp.where(index < SMALL, small, -1)
    row = jnp.where((index >= SMALL_PAD) & (index < SMALL_PAD + HALF), big, row)
    return (row == visible_rows).astype(f32)


def dec_pre_kernel(core, own, other, rows, code, vecs, w_qkv, dec_input, mixed, big_kv):
    chosen = chosen_rows(core[0], rows[...])
    seen = jnp.sum(chosen, axis=1, keepdims=True)
    tokens = jnp.concatenate([own[...], other[...]], axis=0)
    picked = product(chosen.astype(bf16), tokens)
    values = jnp.where(seen > 0.0, picked, vecs[4:5]) + code[...]
    dec_input[...] = values
    normed, _ = norm_parts(values)
    attn_in = (normed * vecs[0:1] + vecs[1:2]).astype(bf16)
    result = product(attn_in, w_qkv[...]).astype(bf16)
    mixed[...] = result
    big_kv[...] = result[SMALL_PAD:, values.shape[1] :]


def big_bias():
    column = lax.broadcasted_iota(jnp.int32, (1, 2 * BIG_PAD), 1)
    place = jnp.where(column >= BIG_PAD, column - BIG_PAD, column)
    return jnp.where(place < HALF, 0.0, masked_score)


def small_bias():
    column = lax.broadcasted_iota(jnp.int32, (1, SMALL_PAD), 1)
    return jnp.where(column < SMALL, 0.0, masked_score)


def dec_att_kernel(query, key, value, other_key, other_value, att, big_probs, small_probs):
    head_size = query.shape[1] * 4 // HD
    scale = 1.0 / math.sqrt(head_size)
    keys = jnp.concatenate([key[SMALL_PAD:], other_key[...]], axis=0)
    values = jnp.concatenate([value[SMALL_PAD:], other_value[...]], axis=0)
    total = jnp.zeros((BIG_PAD, 128), f32)
    small_total = jnp.zeros((SMALL_PAD, 128), f32)
    for head, mask in enumerate(lane_masks(head_size, bf16)):
        scores = inner_cols(query[SMALL_PAD:] * mask, keys) + big_bias()
        chances = softmax_rows(scores, scale)
        big_probs[head] = chances
        total += product(chances, values * mask)
        scores = inner_cols(query[:SMALL_PAD] * mask, key[:SMALL_PAD]) + small_bias()
        chances = softmax_rows(scores, scale)
        small_probs[head] = chances
        small_total += product(chances, value[:SMALL_PAD] * mask)
    att[:SMALL_PAD] = small_total.astype(bf16)
    att[SMALL_PAD:] = total.astype(bf16)


def dec_mid_kernel(
    chunk, core, dec_input, att, cot, vecs, w_proj, w_up, w_down,
    decoded, grad_middle, grad_att, vectors, *grads
):
    down_dest, up_dest, proj_dest = chunk.dests(grads)
    down_at, up_at, proj_at = chunk.offsets
    grad_down, grad_up = [], []
    middle = dec_input[...] + product(att[...], w_proj[...])
    normed, inverse = norm_parts(middle)
    mlp_in = (normed * vecs[2:3] + vecs[3:4]).astype(bf16)
    result = middle
    grad_norm = jnp.zeros_like(middle)
    step = 512
    for start in range(0, w_up.shape[1], step):
        cols = slice(start, start + step)
        active, slope = gelu_parts(product(mlp_in, w_up[:, cols]))
        active = active.astype(bf16)
        result += product(active, w_down[cols])
        grad_down.append(inner_rows(active, cot[...]).astype(bf16))
        grad_hidden = (slope * inner_cols(cot[...], w_down[cols])).astype(bf16)
        grad_up.append(inner_rows(mlp_in, grad_hidden).astype(bf16))
        grad_norm += inner_cols(grad_hidden, w_up[:, cols])
    decoded[...] = result.astype(bf16)
    grad_values, gain, shift = norm_backward(grad_norm, normed, inverse, vecs[2:3])
    vectors[0:1] = gain
    vectors[1:2] = shift
    back = cot[...].astype(f32) + grad_values
    grad_middle[...] = back
    low = back.astype(bf16)
    grad_att[...] = inner_cols(low, w_proj[...]).astype(bf16)
    put(core[0], proj_dest, proj_at, inner_rows(att[...], low))
    put(core[0], down_dest, down_at, jnp.concatenate(grad_down, axis=0))
    put(core[0], up_dest, up_at, jnp.concatenate(grad_up, axis=1))


def dec_att_back_kernel(
    query, key, value, other_key, other_value, grads, att, big_probs, small_probs,
    grad_query, grad_key, grad_value, leaving_key, leaving_value
):
    head_size = query.shape[1] * 4 // HD
    scale = 1.0 / math.sqrt(head_size)
    keys = jnp.concatenate([key[SMALL_PAD:], other_key[...]], axis=0)
    values = jnp.concatenate([value[SMALL_PAD:], other_value[...]], axis=0)
    overlap = grads[...].astype(f32) * att[...].astype(f32)
    big_q = jnp.zeros((BIG_PAD, 128), f32)
    big_k = jnp.zeros((2 * BIG_PAD, 128), f32)
    big_v = jnp.zeros((2 * BIG_PAD, 128), f32)
    small_q = jnp.zeros((SMALL_PAD, 128), f32)
    small_k = jnp.zeros((SMALL_PAD, 128), f32)
    small_v = jnp.zeros((SMALL_PAD, 128), f32)
    masks = lane_masks(head_size, f32)
    for head, mask in enumerate(lane_masks(head_size, bf16)):
        delta = jnp.sum(overlap * masks[head], axis=1, keepdims=True)
        one_query, one_grad = query[...] * mask, grads[...] * mask
        chances = big_probs[head]
        back = head_back(chances, one_grad[SMALL_PAD:], values, delta[SMALL_PAD:])
        big_q += product(back, keys * mask)
        big_k += inner_rows(back, one_query[SMALL_PAD:])
        big_v += inner_rows(chances, one_grad[SMALL_PAD:])
        chances = small_probs[head]
        back = head_back(chances, one_grad[:SMALL_PAD], value[:SMALL_PAD], delta[:SMALL_PAD])
        small_q += product(back, key[:SMALL_PAD] * mask)
        small_k += inner_rows(back, one_query[:SMALL_PAD])
        small_v += inner_rows(chances, one_grad[:SMALL_PAD])
    grad_query[:SMALL_PAD] = (small_q * scale).astype(bf16)
    grad_query[SMALL_PAD:] = (big_q * scale).astype(bf16)
    grad_key[:SMALL_PAD] = small_k * scale
    grad_key[SMALL_PAD:] = big_k[:BIG_PAD] * scale
    grad_value[:SMALL_PAD] = small_v
    grad_value[SMALL_PAD:] = big_v[:BIG_PAD]
    leaving_key[...] = (big_k[BIG_PAD:] * scale).astype(bf16)
    leaving_value[...] = big_v[BIG_PAD:].astype(bf16)


def dec_post_kernel(
    chunk, core, dec_input, grad_middle, grad_query, grad_key, grad_value, arrived_key,
    arrived_value, rows, vecs, w_qkv, own_spread, other_spread, vectors, *grads
):
    normed, inverse = norm_parts(dec_input[...])
    attn_in = (normed * vecs[0:1] + vecs[1:2]).astype(bf16)
    key = jnp.concatenate(
        [grad_key[:SMALL_PAD], grad_key[SMALL_PAD:] + arrived_key[...].astype(f32)], axis=0
    ).astype(bf16)
    value = jnp.concatenate(
        [grad_value[:SMALL_PAD], grad_value[SMALL_PAD:] + arrived_value[...].astype(f32)], axis=0
    ).astype(bf16)
    mixed = jnp.concatenate([grad_query[...], key, value], axis=1)
    grad_values, gain, shift = norm_backward(
        inner_cols(mixed, w_qkv[...]), normed, inverse, vecs[0:1]
    )
    back = grad_middle[...] + grad_values
    chosen = chosen_rows(core[0], rows[...])
    seen = jnp.sum(chosen, axis=1, keepdims=True)
    spread = inner_rows(chosen.astype(bf16), back.astype(bf16)).astype(bf16)
    own_spread[...] = spread[:ENC_PAD]
    other_spread[...] = spread[ENC_PAD:]
    vectors[0:1] = gain
    vectors[1:2] = shift
    vectors[2:3] = jnp.sum(jnp.where(seen > 0.0, 0.0, back), axis=0, keepdims=True)
    put(core[0], chunk.dests(grads)[0], chunk.offsets[0], inner_rows(attn_in, mixed))


def enc_mlp_back_kernel(
    first, second, core, own_spread, arrived, out, middle, active, slope,
    vecs, w_embed, w_down, w_up, w_proj, grad_middle, grad_att, vectors, *grads
):
    first_grads, second_grads = grads[: len(first.outs())], grads[len(first.outs()) :]
    grad_embedded = own_spread[...] + arrived[...]
    normed, inverse = norm_parts(out[...])
    grad_out, gain, shift = norm_backward(
        inner_cols(grad_embedded, w_embed[...]), normed, inverse, vecs[4:5]
    )
    vectors[2:3] = gain
    vectors[3:4] = shift
    low = grad_out.astype(bf16)
    put(core[0], first.dests(first_grads)[0], first.offsets[0], inner_rows(active[...], low))
    grad_hidden = (slope[...].astype(f32) * inner_cols(low, w_down[...])).astype(bf16)
    normed, inverse = norm_parts(middle[...])
    mlp_in = (normed * vecs[2:3] + vecs[3:4]).astype(bf16)
    put(
        core[0], second.dests(second_grads)[0], second.offsets[0], inner_rows(mlp_in, grad_hidden)
    )
    grad_values, gain, shift = norm_backward(
        inner_cols(grad_hidden, w_up[...]), normed, inverse, vecs[2:3]
    )
    vectors[0:1] = gain
    vectors[1:2] = shift
    back = grad_out + grad_values
    grad_middle[...] = back
    grad_att[...] = inner_cols(back.astype(bf16), w_proj[...]).astype(bf16)


def enc_att_back_kernel(
    grads, att, probs, query, own_kv, other_kv, grad_query, grad_kv, leaving
):
    width = query.shape[1]
    head_size = width // HE
    scale = 1.0 / math.sqrt(head_size)
    overlap = grads[...].astype(f32) * att[...].astype(f32)
    masks = lane_masks(head_size, bf16)
    wide_masks = lane_masks(head_size, f32)
    rows = query.shape[0]
    for pair in range(width // 128):
        cols = slice(128 * pair, 128 * pair + 128)
        value_cols = slice(width + 128 * pair, width + 128 * pair + 128)
        keys = jnp.concatenate([own_kv[:, cols], other_kv[:, cols]], axis=0)
        values = jnp.concatenate([own_kv[:, value_cols], other_kv[:, value_cols]], axis=0)
        total_q = jnp.zeros((rows, 128), f32)
        total_k = jnp.zeros((2 * rows, 128), f32)
        total_v = jnp.zeros((2 * rows, 128), f32)
        for head, mask in enumerate(masks):
            delta = jnp.sum(overlap[:, cols] * wide_masks[head], axis=1, keepdims=True)
            one_grad = grads[:, cols] * mask
            chances = probs[len(masks) * pair + head]
            one_back = head_back(chances, one_grad, values, delta)
            total_q += product(one_back, keys * mask)
            total_k += inner_rows(one_back, query[:, cols] * mask)
            total_v += inner_rows(chances, one_grad)
        grad_query[:, cols] = (total_q * scale).astype(bf16)
        grad_kv[:, cols] = total_k[:rows] * scale
        grad_kv[:, value_cols] = total_v[:rows]
        leaving[:, cols] = (total_k[rows:] * scale).astype(bf16)
        leaving[:, value_cols] = total_v[rows:].astype(bf16)


def enc_post_kernel(
    chunk, core, x, att, grad_middle, grad_query, grad_kv, arrived, out, own_spread, other_spread,
    vecs, w_qkv, grad_input, vectors, *grads
):
    qkv_dest, proj_dest, embed_dest = chunk.dests(grads)
    normed, _ = norm_parts(out[...])
    final = (normed * vecs[4:5] + vecs[5:6]).astype(bf16)
    put(
        core[0], embed_dest, chunk.offsets[2], inner_rows(final, own_spread[...] + other_spread[...])
    )
    put(
        core[0], proj_dest, chunk.offsets[1],
        inner_rows(att[...], grad_middle[...].astype(bf16)),
    )
    normed, inverse = norm_parts(x[...].astype(f32))
    attn_in = (normed * vecs[0:1] + vecs[1:2]).astype(bf16)
    key_value = (grad_kv[...] + arrived[...].astype(f32)).astype(bf16)
    mixed = jnp.concatenate([grad_query[...], key_value], axis=1)
    grad_values, gain, shift = norm_backward(
        inner_cols(mixed, w_qkv[...]), normed, inverse, vecs[0:1]
    )
    grad_input[...] = grad_middle[...] + grad_values
    vectors[0:1] = gain
    vectors[1:2] = shift
    put(core[0], qkv_dest, chunk.offsets[0], inner_rows(attn_in, mixed))


def permute(array, where_to):
    seq_count = lax.axis_size("seq")
    img_count = lax.axis_size("img")
    pairs = []
    for seq in range(seq_count):
        for img in range(img_count):
            seq_to, img_to = where_to(seq, img)
            pairs.append((seq * img_count + img, seq_to * img_count + img_to))
    return lax.ppermute(array, ("seq", "img"), pairs)


def swap(array):
    return permute(array, lambda seq, img: (seq, img ^ 1))


def pack_move(turn):
    def where_to(seq, img):
        return (2 * (img & 1) + (turn ^ (seq & 1)), (img & ~1) | (seq >> 1))

    return where_to


def exchange_packs(blocks, odd):
    rounds = [
        permute(jnp.where(odd, blocks[1 - turn], blocks[turn]), pack_move(turn)) for turn in (0, 1)
    ]
    return (jnp.where(odd, rounds[1], rounds[0]), jnp.where(odd, rounds[0], rounds[1]))


def pick(array, index, axis):
    return lax.dynamic_index_in_dim(array, index, axis, keepdims=False)


def pad_rows(array, rows):
    return jnp.pad(array, ((0, rows - array.shape[0]),) + ((0, 0),) * (array.ndim - 1))


def position_table(row_width):
    halfway = row_width // 2
    frequency = np.exp(np.arange(halfway, dtype=np.float64) * (-math.log(10000.0) / halfway))
    angles = np.arange(PATCHES, dtype=np.float64)[:, None] * frequency[None, :]
    return np.concatenate([np.sin(angles), np.cos(angles)], axis=1).astype(np.float32)


def reduce_pair(keep, leaving):
    return (keep.astype(f32) + swap(leaving).astype(f32)).astype(bf16)


MID_PIECES, POST_PIECES, DOWN_PIECES, UP_PIECES, ATT_PIECES = 3, 1, 3, 3, 4
DEC_PIECES = MID_PIECES + POST_PIECES
DOWN_AT = DEC_PIECES
UP_AT = DOWN_AT + DOWN_PIECES
ATT_AT = UP_AT + UP_PIECES
PIECES = ATT_AT + ATT_PIECES
FAR = (0, MID_PIECES)


class Refs:
    def __init__(self, names, refs):
        self.__dict__.update(zip(names, refs))


def by_name(items):
    return Refs(items.keys(), items.values())


def piece_rows(piece):
    return LAST_EIGHTH if piece == PIECES - 1 else EIGHTH


def sub_rows(row, count):
    done = 0
    while done < count:
        piece = min((row + done) // SUB_ROWS, PIECES - 1)
        place, height = row + done - piece * SUB_ROWS, piece_rows(piece)
        start = place % height
        size = min(count - done, height - start)
        place //= height
        yield piece, place // 4, place // 2 % 2, place % 2, start, start + size, done
        done += size


class Place:
    def __init__(self):
        self.seq, self.img = lax.axis_index("seq"), lax.axis_index("img")
        self.chip, self.core = self.img // 2, lax.rem(self.img, 2)
        self.high, self.low = self.seq // 2, lax.rem(self.seq, 2)
        self.partner = dict(img=self.img + 1 - 2 * self.core)

    def remote(self, source, dest, sems, device):
        return pltpu.make_async_remote_copy(
            src_ref=source,
            dst_ref=dest,
            send_sem=sems.at[0],
            recv_sem=sems.at[1],
            device_id=device,
            device_id_type=pl.DeviceIdType.MESH,
        )

    def home(self, turn):
        segment = turn + self.low - 2 * turn * self.low
        device = dict(seq=2 * self.core + segment, img=2 * self.chip + self.high)
        stays = (self.high == self.core) if turn == 0 else None
        return device, segment, stays

    def send_home(self, act, source_parts, sems):
        for turn in (0, 1):
            device, segment, stays = self.home(turn)
            for part, (source, dest) in enumerate(source_parts(segment)):
                sem = sems.at[turn, part]
                if stays is None:
                    act(self.remote(source, dest, sem, device))
                else:

                    @pl.when(stays)
                    def _():
                        act(pltpu.make_async_copy(source, dest, sem.at[0]))

                    @pl.when(jnp.logical_not(stays))
                    def _():
                        act(self.remote(source, dest, sem, device))

    def greet(self, peers):
        barrier = pltpu.get_barrier_semaphore()

        def signal(device):
            pl.semaphore_signal(
                barrier, inc=1, device_id=device, device_id_type=pl.DeviceIdType.MESH
            )

        for device in peers:
            signal(device)
        signal(self.home(1)[0])

        @pl.when(self.high != self.core)
        def _():
            signal(self.home(0)[0])

        return lambda: pl.semaphore_wait(
            barrier, len(peers) + 1 + jnp.where(self.high == self.core, 0, 1)
        )


def start_copy(copy):
    copy.start()


def wait_copy(copy):
    copy.wait()


def loader(sems, **items):
    copies = {}
    for index, (name, (source, dest)) in enumerate(items.items()):
        copies[name] = pltpu.make_async_copy(source, dest, sems.at[index])
        copies[name].start()
    return by_name(copies)


def ready(*copies):
    for copy in copies:
        copy.wait()


def row_order(core, pad, rows):
    local = lax.broadcasted_iota(jnp.int32, (DEC_PAD, 2 * pad), 0)
    place = lax.broadcasted_iota(jnp.int32, (DEC_PAD, 2 * pad), 1)
    small = local < SMALL_PAD
    natural = jnp.where(small, local + core * HALF, local - SMALL_PAD + (1 - core) * SMALL)
    there = jnp.where(small, local, local - SMALL_PAD + SMALL - HALF) < SMALL
    spot = natural + jnp.where(natural >= rows, pad - rows, 0)
    return ((spot == place) & there).astype(f32).astype(bf16)


def front_kernel(names, *refs):
    r = Refs(names, refs)
    p = Place()
    core, low, high = p.core, p.low, p.high
    width, narrow = r.w_embed.shape
    rows = ENC_PAD
    seg_rows, cot_rows = r.enc_input.shape[1], r.cotangent.shape[1]
    cot_pad = r.cot_send.shape[1]
    load = loader(
        r.load_sem,
        qkv=(r.w_qkv, r.v_qkv),
        proj=(r.w_proj, r.v_proj),
        up=(r.w_up, r.v_up),
        down=(r.w_down, r.v_down),
        embed=(r.w_embed, r.v_embed),
        code=(r.codes.at[core], r.v_code),
        dec_qkv=(r.dec_qkv, r.v_dec_qkv),
    )
    greeted = p.greet([p.partner])
    for block in range(2):
        r.enc_send[block] = jnp.concatenate(
            [
                r.enc_input[block].astype(f32),
                jnp.zeros((ENC_SEG - seg_rows, width), f32),
            ],
            axis=0,
        ).astype(bf16)
    greeted()

    def enc_parts(segment):
        return [(r.enc_send.at[segment], r.v_x.at[low])]

    def cot_parts(segment):
        return [(r.cot_send.at[segment], r.cot_in.at[low])]

    p.send_home(start_copy, enc_parts, r.enc_sem)
    table_copy = p.remote(r.tables.at[1], r.tables_in, r.swap_sem.at[0], p.partner)
    table_copy.start()
    for block in range(2):
        r.cot_send[block] = jnp.concatenate(
            [
                r.cotangent[block].astype(f32),
                jnp.zeros((cot_pad - cot_rows, narrow), f32),
            ],
            axis=0,
        ).astype(bf16)
    p.send_home(start_copy, cot_parts, r.cot_sem)
    enc_vecs, dec_vecs = r.enc_vecs, r.dec_vecs

    stores = []

    def store(source, dest):
        copy = pltpu.make_async_copy(source, dest, r.store_sem.at[len(stores)])
        copy.start()
        stores.append(copy)

    def put_left(values, start):
        chips = r.lefts_keep.shape[0]
        turned = values.astype(f32).T.astype(bf16)
        count = turned.shape[0] // (2 * chips)
        for case in (0, 1):

            @pl.when(core == case)
            def _():
                for image in range(2 * chips):
                    ref = r.lefts_keep if image % 2 == case else r.lefts_leaving
                    ref[image // 2, start : start + count, :rows] = turned[
                        image * count : (image + 1) * count
                    ]

    left_hidden = r.w_up.shape[1] // (2 * r.lefts_keep.shape[0])
    left_mid = width // (2 * r.lefts_keep.shape[0])

    def norm_in(values, vecs, row):
        normed, _ = norm_parts(values)
        return (normed * vecs[row : row + 1] + vecs[row + 1 : row + 2]).astype(bf16)

    p.send_home(wait_copy, enc_parts, r.enc_sem)
    x = r.v_x[...].reshape(rows, width).astype(f32)
    attn_in = norm_in(x, enc_vecs, 0)
    ready(load.qkv)
    mixed = product(attn_in, r.v_qkv[...]).astype(bf16)
    r.v_query[...] = mixed[:, :width]
    r.v_own_kv[...] = mixed[:, width:]
    kv_copy = p.remote(r.v_own_kv, r.v_other_kv, r.swap_sem.at[1], p.partner)
    kv_copy.start()
    put_left(attn_in, left_hidden + 3 * left_mid)
    table_copy.wait()
    mine = high == core
    ids = jnp.where(mine, r.tables[0, 0, low], r.tables_in[0, low])
    row_ids = jnp.where(mine, r.tables[0, 1, low], r.tables_in[1, low])
    r.row_ids[...] = row_ids
    across = lax.broadcasted_iota(jnp.int32, (rows, 2 * rows), 1)
    along = lax.broadcasted_iota(jnp.int32, (rows, 2 * rows), 0)
    wide_ids = ids.astype(f32)
    own_ids = jnp.sum(jnp.where(across == along, wide_ids, 0.0), axis=1, keepdims=True)
    bias = jnp.where(own_ids == wide_ids, 0.0, masked_score)
    head_size = width // HE
    masks = lane_masks(head_size, bf16)
    kv_copy.wait()
    for pair in range(width // 128):
        cols = slice(128 * pair, 128 * pair + 128)
        value_cols = slice(width + 128 * pair, width + 128 * pair + 128)
        keys = jnp.concatenate([r.v_own_kv[:, cols], r.v_other_kv[:, cols]], axis=0)
        values = jnp.concatenate([r.v_own_kv[:, value_cols], r.v_other_kv[:, value_cols]], axis=0)
        total = jnp.zeros((rows, 128), f32)
        for head, mask in enumerate(masks):
            scores = inner_cols(r.v_query[:, cols] * mask, keys) + bias
            chances = softmax_rows(scores, 1.0 / math.sqrt(head_size))
            r.v_probs[len(masks) * pair + head, :, : 2 * rows] = chances
            total += product(chances, values * mask)
        r.v_att[:, cols] = total.astype(bf16)
    store(r.v_x, r.x)
    store(r.v_query, r.query)
    store(r.v_own_kv, r.own_kv)
    store(r.v_other_kv, r.other_kv)
    store(r.v_probs, r.probs)
    store(r.v_att, r.att)

    ready(load.proj, load.up, load.down, load.embed)
    middle = x + product(r.v_att[...], r.v_proj[...])
    r.v_middle[...] = middle
    store(r.v_middle, r.middle)
    mlp_in = norm_in(middle, enc_vecs, 2)
    active, slope = gelu_parts(product(mlp_in, r.v_up[...]))
    active = active.astype(bf16)
    r.v_slope[...] = slope.astype(bf16)
    store(r.v_slope, r.slope)
    out = middle + product(active, r.v_down[...])
    r.v_out[...] = out
    store(r.v_out, r.out)
    final = norm_in(out, enc_vecs, 4)
    r.emb_own[...] = product(final, r.v_embed[...]).astype(bf16)
    emb_copy = p.remote(r.emb_own, r.emb_in, r.swap_sem.at[2], p.partner)
    emb_copy.start()
    put_left(active, 0)
    put_left(mlp_in, left_hidden)
    put_left(r.v_att[...], left_hidden + left_mid)
    put_left(final, left_hidden + 2 * left_mid)
    store(r.lefts_keep, r.lefts_own)
    lefts_copy = p.remote(r.lefts_leaving, r.lefts_other, r.swap_sem.at[3], p.partner)
    lefts_copy.start()

    chosen = chosen_rows(core, row_ids)
    seen = jnp.sum(chosen, axis=1, keepdims=True)
    ready(load.code, load.dec_qkv)
    emb_copy.wait()
    tokens = jnp.concatenate([r.emb_own[...], r.emb_in[...]], axis=0)
    picked = product(chosen.astype(bf16), tokens)
    values = jnp.where(seen > 0.0, picked, dec_vecs[4:5]) + r.v_code[...]
    r.v_code[...] = values
    store(r.v_code, r.dec_input)
    mixed = product(norm_in(values, dec_vecs, 0), r.v_dec_qkv[...]).astype(bf16)
    r.v_mixed[...] = mixed
    big_copy = p.remote(
        r.v_mixed.at[SMALL_PAD:, narrow:], r.big_in, r.swap_sem.at[4], p.partner
    )
    big_copy.start()
    store(r.v_mixed, r.dec_mixed)

    p.send_home(wait_copy, cot_parts, r.cot_sem)
    moved = product(
        row_order(core, cot_pad, cot_rows), r.cot_in[...].reshape(2 * cot_pad, narrow)
    )
    r.v_cot[...] = moved.astype(bf16)
    store(r.v_cot, r.cot)
    big_copy.wait()
    store(r.big_in, r.dec_other_kv)

    head_size = narrow // HD
    per_group = 128 // head_size
    scale = 1.0 / math.sqrt(head_size)
    masks = lane_masks(head_size, bf16)

    def chance_copies(head, slot):
        return (
            pltpu.make_async_copy(r.chances.at[slot], r.big_probs.at[head], r.chance_sem.at[slot, 0]),
            pltpu.make_async_copy(
                r.small_chances.at[slot], r.small_probs.at[head], r.chance_sem.at[slot, 1]
            ),
        )

    wide_masks = lane_masks(head_size, f32)
    lane = lax.broadcasted_iota(jnp.int32, (1, 128), 1)

    def pad_column(blocks, size, used):
        index = lax.broadcasted_iota(jnp.int32, (blocks * size, 1), 0)
        index = jnp.where(index >= size, index - size, index)
        return jnp.where(index < used, 0.0, masked_score)

    big_pad, small_pad = pad_column(2, BIG_PAD, HALF), pad_column(1, SMALL_PAD, SMALL)

    def weigh(query, key, value, pad, mask, spare):
        one = spare.astype(bf16)
        scores = inner_cols(query * mask + one, key * mask + (pad * spare).astype(bf16))
        row_max = jnp.max(scores, axis=1, keepdims=True)
        weights = jnp.exp2((scores - row_max) * (scale * math.log2(math.e))).astype(bf16)
        mixed = product(weights, value * mask + one)
        return weights, mixed, 1.0 / jnp.sum(mixed * spare, axis=1, keepdims=True)

    def group_forward(group, carry):
        def cols(offset):
            return pl.ds(pl.multiple_of(offset * narrow + group * 128, 128), 128)

        query = r.v_mixed[:, cols(0)]
        small_key, small_value = r.v_mixed[:SMALL_PAD, cols(1)], r.v_mixed[:SMALL_PAD, cols(2)]
        keys = jnp.concatenate([r.v_mixed[SMALL_PAD:, cols(1)], r.big_in[:, cols(0)]], axis=0)
        values = jnp.concatenate([r.v_mixed[SMALL_PAD:, cols(2)], r.big_in[:, cols(1)]], axis=0)
        total = jnp.zeros((BIG_PAD, 128), f32)
        small_total = jnp.zeros((SMALL_PAD, 128), f32)
        inverse = jnp.zeros((BIG_PAD, 128), f32)
        small_inverse = jnp.zeros((SMALL_PAD, 128), f32)
        for head, mask in enumerate(masks):
            slot = head
            number = group * per_group + head

            @pl.when(group > 0)
            def _():
                for copy in chance_copies(number - per_group, slot):
                    copy.wait()

            spare = (lane == (head * head_size + 64) % 128).astype(f32)
            weights, mixed, shrink = weigh(
                query[SMALL_PAD:], keys, values, big_pad, mask, spare
            )
            r.chances[slot, :, : 2 * BIG_PAD] = weights
            shrink = shrink * wide_masks[head]
            inverse += shrink
            total += mixed * shrink
            weights, mixed, shrink = weigh(
                query[:SMALL_PAD], small_key, small_value, small_pad, mask, spare
            )
            r.small_chances[slot, :, :SMALL_PAD] = weights
            shrink = shrink * wide_masks[head]
            small_inverse += shrink
            small_total += mixed * shrink
            for copy in chance_copies(number, slot):
                copy.start()
        r.v_dec_att[:SMALL_PAD, cols(0)] = small_total.astype(bf16)
        r.v_dec_att[SMALL_PAD:, cols(0)] = total.astype(bf16)
        r.v_inverse[:SMALL_PAD, cols(0)] = small_inverse
        r.v_inverse[SMALL_PAD:, cols(0)] = inverse
        return carry

    lax.fori_loop(0, narrow // 128, group_forward, 0)
    store(r.v_dec_att, r.dec_att)
    store(r.v_inverse, r.dec_inverse)
    for slot in range(per_group):
        for copy in chance_copies(HD - per_group + slot, slot):
            copy.wait()
    for copy in stores:
        copy.wait()
    lefts_copy.wait()


def front(args, chips):
    anywhere = pl.BlockSpec(memory_space=pl.ANY)
    vmem = pl.BlockSpec(memory_space=pltpu.VMEM)
    dma = pltpu.SemaphoreType.DMA
    width, narrow = by_name(args).w_embed.shape
    wide = by_name(args).w_up.shape[1]
    left_rows = (4 * width + wide) // (2 * chips)
    cot_pad = DEC_PAD // 2
    outs = dict(
        x=((2, ENC_SEG, width), bf16),
        query=((ENC_PAD, width), bf16),
        own_kv=((ENC_PAD, 2 * width), bf16),
        other_kv=((ENC_PAD, 2 * width), bf16),
        probs=((HE, ENC_PAD, ENC_LANES), bf16),
        att=((ENC_PAD, width), bf16),
        middle=((ENC_PAD, width), f32),
        slope=((ENC_PAD, wide), bf16),
        out=((ENC_PAD, width), f32),
        lefts_own=((chips, left_rows, LEFT_LANES), bf16),
        lefts_other=((chips, left_rows, LEFT_LANES), bf16),
        dec_input=((DEC_PAD, narrow), f32),
        dec_mixed=((DEC_PAD, 3 * narrow), bf16),
        cot=((DEC_PAD, narrow), bf16),
        dec_other_kv=((BIG_PAD, 2 * narrow), bf16),
        big_probs=((HD, BIG_PAD, BIG_LANES), bf16),
        small_probs=((HD, SMALL_PAD, SMALL_LANES), bf16),
        dec_att=((DEC_PAD, narrow), bf16),
        dec_inverse=((DEC_PAD, narrow), f32),
        row_ids=((1, 2 * ENC_PAD), jnp.int32),
    )

    def like(out):
        return pltpu.VMEM(*out)

    scratch = dict(
        enc_send=like(by_name(outs).x),
        cot_send=pltpu.VMEM((2, cot_pad, narrow), bf16),
        cot_in=pltpu.VMEM((2, cot_pad, narrow), bf16),
        tables_in=pltpu.VMEM(by_name(args).tables.shape[1:], jnp.int32),
        v_x=like(by_name(outs).x),
        v_query=like(by_name(outs).query),
        v_own_kv=like(by_name(outs).own_kv),
        v_other_kv=like(by_name(outs).other_kv),
        v_probs=like(by_name(outs).probs),
        v_att=like(by_name(outs).att),
        v_middle=like(by_name(outs).middle),
        v_slope=like(by_name(outs).slope),
        v_out=like(by_name(outs).out),
        lefts_keep=like(by_name(outs).lefts_own),
        lefts_leaving=like(by_name(outs).lefts_own),
        emb_own=pltpu.VMEM((ENC_PAD, narrow), bf16),
        emb_in=pltpu.VMEM((ENC_PAD, narrow), bf16),
        v_code=like(by_name(outs).dec_input),
        v_mixed=like(by_name(outs).dec_mixed),
        v_cot=like(by_name(outs).cot),
        big_in=like(by_name(outs).dec_other_kv),
        chances=pltpu.VMEM((4, BIG_PAD, BIG_LANES), bf16),
        small_chances=pltpu.VMEM((4, SMALL_PAD, SMALL_LANES), bf16),
        v_dec_att=like(by_name(outs).dec_att),
        v_inverse=like(by_name(outs).dec_inverse),
        v_qkv=pltpu.VMEM(by_name(args).w_qkv.shape, bf16),
        v_proj=pltpu.VMEM(by_name(args).w_proj.shape, bf16),
        v_up=pltpu.VMEM(by_name(args).w_up.shape, bf16),
        v_down=pltpu.VMEM(by_name(args).w_down.shape, bf16),
        v_embed=pltpu.VMEM(by_name(args).w_embed.shape, bf16),
        v_dec_qkv=pltpu.VMEM(by_name(args).dec_qkv.shape, bf16),
        load_sem=dma((7,)),
        store_sem=dma((17,)),
        chance_sem=dma((4, 2)),
        swap_sem=dma((5, 2)),
        enc_sem=dma((2, 1, 2)),
        cot_sem=dma((2, 1, 2)),
    )
    names = list(args) + list(outs) + list(scratch)
    in_vmem = ("enc_input", "cotangent", "tables", "enc_vecs", "dec_vecs")
    results = pl.pallas_call(
        functools.partial(front_kernel, names),
        out_shape=[jax.ShapeDtypeStruct(shape, kind) for shape, kind in outs.values()],
        in_specs=[vmem if name in in_vmem else anywhere for name in args],
        out_specs=[vmem if name == "row_ids" else anywhere for name in outs],
        scratch_shapes=list(scratch.values()),
        compiler_params=pltpu.CompilerParams(
            collective_id=2, has_side_effects=True, vmem_limit_bytes=60 << 20
        ),
    )(*args.values())
    return dict(zip(outs, results))


def back_kernel(chips, names, *refs):
    r = Refs(names, refs)
    p = Place()
    chip, core, high, low = p.chip, p.core, p.high, p.low
    remote, partner = p.remote, p.partner
    along_x = dict(seq=p.seq + 1 - 2 * low)
    along_y = dict(seq=p.seq + 2 - 4 * high)
    others = [dict(img=lax.rem(chip + step, chips) * 2 + core) for step in range(1, chips)]
    width, wide, narrow = r.w_embed.shape[0], r.w_up.shape[1], r.w_embed.shape[1]
    rows = ENC_PAD

    def add(one, two):
        return (one.astype(f32) + two.astype(f32)).astype(bf16)

    held, first, second, from_chips, gathered = (
        r.held, r.first, r.second, r.from_chips, r.gathered
    )

    def pair_copy(i):
        return remote(r.leaving.at[i], r.from_pair.at[i], r.pair_sem.at[i], partner)

    def first_copies(i):
        n = slice(0, piece_rows(i))
        return (
            remote(
                held.at[i, :, 0, :, 1 - low, n], first.at[i, 0, :, :, n], r.first_sem.at[i, 0],
                along_x,
            ),
            remote(
                held.at[i, :, 1, 1 - high, :, n], first.at[i, 1, :, :, n], r.first_sem.at[i, 1],
                along_y,
            ),
        )

    def second_copies(i):
        n = slice(0, piece_rows(i))
        return (
            remote(
                held.at[i, :, 0, 1 - high, low, n], second.at[i, 0, :, n], r.second_sem.at[i, 0],
                along_y,
            ),
            remote(
                held.at[i, :, 1, high, 1 - low, n], second.at[i, 1, :, n], r.second_sem.at[i, 1],
                along_x,
            ),
        )

    def chip_copies(i):
        n = slice(0, piece_rows(i))
        return [
            remote(
                held.at[i, device["img"] // 2, :, high, low, n],
                from_chips.at[i, step, :, n],
                r.chip_sem.at[i, step],
                device,
            )
            for step, device in enumerate(others)
        ]

    def gather_copies(i, arrive):
        n = slice(0, piece_rows(i))
        x_place = 1 - low if arrive else low
        y_place = 1 - high if arrive else high
        one, two = gathered.at[i, 0, high, x_place, n], gathered.at[i, 1, y_place, low, n]
        return (
            remote(one, one, r.gather_sem.at[i, 0], along_x),
            remote(two, two, r.gather_sem.at[i, 1], along_y),
        )

    def spread_copies(i, arrive):
        n = slice(0, piece_rows(i))
        x_place = 1 - low if arrive else low
        y_place = 1 - high if arrive else high
        one, two = gathered.at[i, 0, y_place, :, n], gathered.at[i, 1, :, x_place, n]
        return (
            remote(one, one, r.gather_sem.at[i, 2], along_y),
            remote(two, two, r.gather_sem.at[i, 3], along_x),
        )

    def share_copy(i):
        return pltpu.make_async_copy(gathered.at[i], r.shares.at[i], r.share_sem.at[i])

    def stage_pair(i):
        pair_copy(i).wait()
        for image in range(chips):
            held[i, image] = add(held[i, image], r.from_pair[i, image])

    def stage_first(i):
        for copy in first_copies(i):
            copy.start()

    def stage_second(i):
        for copy in first_copies(i):
            copy.wait_recv()
        n = slice(0, piece_rows(i))
        held[i, :, 0, :, low, n] = add(held[i, :, 0, :, low, n], first[i, 0, :, :, n])
        held[i, :, 1, high, :, n] = add(held[i, :, 1, high, :, n], first[i, 1, :, :, n])
        for copy in second_copies(i):
            copy.start()

    def stage_chips(i):
        for copy in second_copies(i):
            copy.wait_recv()
        n = slice(0, piece_rows(i))
        held[i, :, 0, high, low, n] = add(held[i, :, 0, high, low, n], second[i, 0, :, n])
        held[i, :, 1, high, low, n] = add(held[i, :, 1, high, low, n], second[i, 1, :, n])
        for copy in chip_copies(i):
            copy.start()

    def stage_gather(i):
        for copy in chip_copies(i):
            copy.wait_recv()
        n = slice(0, piece_rows(i))
        mine = held[i, chip, :, high, low, n].astype(f32)
        for step in range(chips - 1):
            mine += from_chips[i, step, :, n].astype(f32)
        gathered[i, :, high, low, n] = mine.astype(bf16)
        for copy in gather_copies(i, False):
            copy.start()

    def stage_spread(i):
        for copy in gather_copies(i, True):
            copy.wait_recv()
        for copy in spread_copies(i, False):
            copy.start()

    def stage_end(i):
        for copy in spread_copies(i, True):
            copy.wait_recv()
        for copy in (
            *first_copies(i), *second_copies(i), *chip_copies(i), *gather_copies(i, False),
            *spread_copies(i, False),
        ):
            copy.wait_send()
        share_copy(i).start()

    def far_copies(i):
        return [
            remote(source, dest, r.far_sem.at[FAR.index(i), step, part], device)
            for step, device in enumerate(others)
            for part, (source, dest) in enumerate(
                (
                    (held.at[i, device["img"] // 2, :, 0], first.at[i, :, 1 + step]),
                    (held.at[i, device["img"] // 2, :, 1, 0], second.at[i, :, 1 + step]),
                    (held.at[i, device["img"] // 2, :, 1, 1], from_chips.at[i, step]),
                )
            )
        ]

    def far_start(i):
        for copy in far_copies(i):
            copy.start()

    def far_first_copies(i):
        return (
            remote(held.at[i, chip, 0, :, 1 - low], first.at[i, 0, 0], r.first_sem.at[i, 0], along_x),
            remote(held.at[i, chip, 1, 1 - high], first.at[i, 1, 0], r.first_sem.at[i, 1], along_y),
        )

    def far_second_copies(i):
        return (
            remote(
                held.at[i, chip, 0, 1 - high, low], second.at[i, 0, 0], r.second_sem.at[i, 0],
                along_y,
            ),
            remote(
                held.at[i, chip, 1, high, 1 - low], second.at[i, 1, 0], r.second_sem.at[i, 1],
                along_x,
            ),
        )

    def far_first(i):
        for copy in far_copies(i):
            copy.wait_recv()

        def total(mine, *arrived):
            mine = mine.astype(f32)
            for one in arrived:
                mine += one.astype(f32)
            return mine.astype(bf16)

        steps = range(chips - 1)
        held[i, chip, :, 0] = total(held[i, chip, :, 0], *(first[i, :, 1 + k] for k in steps))
        held[i, chip, :, 1, 0] = total(
            held[i, chip, :, 1, 0], *(second[i, :, 1 + k] for k in steps)
        )
        held[i, chip, :, 1, 1] = total(
            held[i, chip, :, 1, 1], *(from_chips[i, k] for k in steps)
        )
        for copy in far_first_copies(i):
            copy.start()

    def far_second(i):
        for copy in far_first_copies(i):
            copy.wait_recv()
        held[i, chip, 0, :, low] = add(held[i, chip, 0, :, low], first[i, 0, 0])
        held[i, chip, 1, high] = add(held[i, chip, 1, high], first[i, 1, 0])
        for copy in far_second_copies(i):
            copy.start()

    def far_gather(i):
        for copy in far_second_copies(i):
            copy.wait_recv()
        gathered[i, 0, high, low] = add(held[i, chip, 0, high, low], second[i, 0, 0])
        gathered[i, 1, high, low] = add(held[i, chip, 1, high, low], second[i, 1, 0])
        for copy in gather_copies(i, False):
            copy.start()

    def far_end(i):
        for copy in spread_copies(i, True):
            copy.wait_recv()
        for copy in (
            *far_copies(i), *far_first_copies(i), *far_second_copies(i),
            *gather_copies(i, False), *spread_copies(i, False),
        ):
            copy.wait_send()
        share_copy(i).start()

    stages = (stage_first, stage_second, stage_chips, stage_gather, stage_spread, stage_end)
    far_stages = (far_first, far_second, far_gather, stage_spread, far_end)
    line = []

    def pump(piece):
        line.append(piece)
        for lag in range(len(stages)):
            slot = len(line) - 1 - lag
            if slot >= 0 and line[slot] is not None:
                course = far_stages if line[slot] in FAR else stages
                if lag < len(course):
                    course[lag](line[slot])

    greeted = p.greet([partner, along_x, along_y, *others])

    def put_dec(grad, first_image, count, row):
        grad = grad.astype(bf16)
        for case in (0, 1):

            @pl.when(core == case)
            def _():
                for index in range(grad.shape[0] // count):
                    image = first_image + index
                    ref = held if image % 2 == case else r.leaving
                    for block in range(grad.shape[1] // LANES):
                        for piece, half, up, across, begin, end, at in sub_rows(
                            row + block * count, count
                        ):
                            ref[piece, image // 2, half, up, across, begin:end] = grad[
                                index * count + at : index * count + at + end - begin,
                                block * LANES : (block + 1) * LANES,
                            ]

    def decoder(
        dec_input, att, inverses, cot, w_proj, w_up, w_down, w_qkv, mixed, other_kv, chances,
        small_chances, decoded, grad_middle, grad_att, grad_mixed, grad_kv, kv_leaving,
    ):
        load = loader(
        r.load_sem,
        dec_input=(r.dec_input, dec_input),
        att=(r.dec_att, att),
        proj=(r.dec_proj, w_proj),
        up=(r.dec_up, w_up),
        cot=(r.cot, cot),
        down=(r.dec_down, w_down),
        mixed=(r.dec_mixed, mixed),
        other=(r.dec_other_kv, other_kv),
        qkv=(r.dec_qkv, w_qkv),
        inverses=(r.dec_inverse, inverses),
    )

        def chance_copies(head, slot):
            return (
                pltpu.make_async_copy(
                    r.big_probs.at[head], chances.at[slot], r.chance_sem.at[slot, 0]
                ),
                pltpu.make_async_copy(
                    r.small_probs.at[head], small_chances.at[slot], r.chance_sem.at[slot, 1]
                ),
            )

        for copy in chance_copies(0, 0):
            copy.start()
        greeted()

        ready(load.dec_input, load.att, load.proj)
        vecs = r.dec_vecs
        middle = dec_input[...] + product(att[...], w_proj[...])
        normed, inverse = norm_parts(middle)
        mlp_in = (normed * vecs[2:3] + vecs[3:4]).astype(bf16)
        result = middle
        grad_norm = jnp.zeros_like(middle)
        step = 2 * w_down.shape[0] // (2 * chips)
        down_count, up_count = step // 2, narrow // (2 * chips)
        up_row = down_count * narrow // LANES
        proj_row = up_row + up_count * w_up.shape[1] // LANES
        ready(load.up, load.cot, load.down)
        for copy in early_loads():
            copy.start()
        for block in range(w_up.shape[1] // step):
            cols = slice(block * step, (block + 1) * step)
            active, slope = gelu_parts(product(mlp_in, w_up[:, cols]))
            active = active.astype(bf16)
            result += product(active, w_down[cols])
            put_dec(inner_rows(active, cot[...]), 2 * block, down_count, 0)
            grad_hidden = (slope * inner_cols(cot[...], w_down[cols])).astype(bf16)
            put_dec(
                inner_rows(mlp_in, grad_hidden), 0, up_count,
                up_row + up_count * block * step // LANES,
            )
            grad_norm += inner_cols(grad_hidden, w_up[:, cols])
        order = row_order(core, DEC_PAD // 2, (SMALL + HALF) // 2)
        decoded[...] = (
            inner_rows(order, result.astype(bf16)).astype(bf16).reshape(2, DEC_PAD // 2, narrow)
        )

        def decoded_parts(segment):
            return [(decoded.at[segment], r.home_rows.at[low])]

        p.send_home(start_copy, decoded_parts, r.rows_sem)
        grad_values, gain, shift = norm_backward(grad_norm, normed, inverse, vecs[2:3])
        r.vec_own[...] = jnp.zeros(r.vec_own.shape, f32)
        r.vec_own[10:11, :narrow] = gain
        r.vec_own[11:12, :narrow] = shift
        back = cot[...].astype(f32) + grad_values
        grad_middle[...] = back
        back = back.astype(bf16)
        ready(load.inverses)
        grad_low = inner_cols(back, w_proj[...]).astype(bf16)
        grad_att[...] = (grad_low.astype(f32) * inverses[...]).astype(bf16)
        put_dec(inner_rows(att[...], back), 0, up_count, proj_row)
        for i in range(MID_PIECES):
            pair_copy(i).start()

        ready(load.mixed, load.other)
        head_size = narrow // HD
        per_group = 128 // head_size
        scale = 1.0 / math.sqrt(head_size)
        masks, wide_masks = lane_masks(head_size, bf16), lane_masks(head_size, f32)

        def group_back(group, last):
            def cols(offset):
                return pl.ds(pl.multiple_of(offset * narrow + group * 128, 128), 128)

            query = mixed[:, cols(0)]
            small_key, small_value = mixed[:SMALL_PAD, cols(1)], mixed[:SMALL_PAD, cols(2)]
            keys = jnp.concatenate([mixed[SMALL_PAD:, cols(1)], other_kv[:, cols(0)]], axis=0)
            values = jnp.concatenate([mixed[SMALL_PAD:, cols(2)], other_kv[:, cols(1)]], axis=0)
            grads = grad_att[:, cols(0)]
            overlap = grads.astype(f32) * att[:, cols(0)].astype(f32)
            def turned(values):
                return values.astype(f32).T.astype(bf16)

            big_query, small_query = turned(query[SMALL_PAD:]), turned(query[:SMALL_PAD])
            big_grad, small_grad = turned(grads[SMALL_PAD:]), turned(grads[:SMALL_PAD])
            big_q = jnp.zeros((BIG_PAD, 128), f32)
            small_q = jnp.zeros((SMALL_PAD, 128), f32)
            big_k, big_v, small_k, small_v = [], [], [], []
            for head, mask in enumerate(masks):
                slot = head % 2
                number = group * per_group + head
                for copy in chance_copies(number, slot):
                    copy.wait()
                if head < per_group - 1:
                    for copy in chance_copies(number + 1, 1 - slot):
                        copy.start()
                else:

                    @pl.when(group < last)
                    def _():
                        for copy in chance_copies(number + 1, 1 - slot):
                            copy.start()

                delta = jnp.sum(overlap * wide_masks[head], axis=1, keepdims=True)
                one_grad = grads * mask
                own = slice(head * head_size, (head + 1) * head_size)
                probs = chances[slot, :, : 2 * BIG_PAD]
                one = head_back(probs, one_grad[SMALL_PAD:], values, delta[SMALL_PAD:])
                big_q += product(one, keys * mask)
                big_k.append(product(big_query[own], one))
                big_v.append(product(big_grad[own], probs))
                probs = small_chances[slot, :, :SMALL_PAD]
                one = head_back(probs, one_grad[:SMALL_PAD], small_value, delta[:SMALL_PAD])
                small_q += product(one, small_key * mask)
                small_k.append(product(small_query[own], one))
                small_v.append(product(small_grad[own], probs))
            big_k, big_v, small_k, small_v = (
                jnp.concatenate(parts, axis=0).T for parts in (big_k, big_v, small_k, small_v)
            )
            grad_mixed[:SMALL_PAD, cols(0)] = (small_q * scale).astype(bf16)
            grad_mixed[SMALL_PAD:, cols(0)] = (big_q * scale).astype(bf16)
            grad_mixed[:SMALL_PAD, cols(1)] = (small_k * scale).astype(bf16)
            grad_mixed[:SMALL_PAD, cols(2)] = small_v.astype(bf16)
            grad_kv[:, cols(0)] = big_k[:BIG_PAD] * scale
            grad_kv[:, cols(1)] = big_v[:BIG_PAD]
            kv_leaving[:, cols(0)] = (big_k[BIG_PAD:] * scale).astype(bf16)
            kv_leaving[:, cols(1)] = big_v[BIG_PAD:].astype(bf16)

        def kv_copies(group):
            for which in range(2):
                cols = slice(which * narrow + group * 128, which * narrow + (group + 1) * 128)
                yield remote(
                    kv_leaving.at[:, cols], r.dec_kv_in.at[:, cols], r.kv_sem.at[group, which],
                    partner,
                )

        groups = narrow // 128
        for group in range(groups):
            lax.fori_loop(
                group, group + 1, lambda g, c: (group_back(g, groups - 1), c)[1], 0
            )
            for copy in kv_copies(group):
                copy.start()
            if group == 0:
                stage_pair(0)
                far_start(0)
                stage_pair(1)
                pump(1)
            if group == 1:
                stage_pair(2)
                pump(2)
            if group == 2:
                pump(None)
        pump(None)

        normed, inverse = norm_parts(dec_input[...])
        attn_in = (normed * vecs[0:1] + vecs[1:2]).astype(bf16)
        chosen = chosen_rows(core, r.row_ids[...])
        seen = jnp.sum(chosen, axis=1, keepdims=True)
        ready(load.qkv)
        for group in range(groups):
            for copy in kv_copies(group):
                copy.wait()
        grad_mixed[SMALL_PAD:, narrow:] = (grad_kv[...] + r.dec_kv_in[...].astype(f32)).astype(bf16)
        grad_values, gain, shift = norm_backward(
            inner_cols(grad_mixed[...], w_qkv[...]), normed, inverse, vecs[0:1]
        )
        r.vec_own[8:9, :narrow] = gain
        r.vec_own[9:10, :narrow] = shift
        back = grad_middle[...] + grad_values
        spread = inner_rows(chosen.astype(bf16), back.astype(bf16)).astype(bf16)
        r.spread_own[...] = spread[:rows]
        r.spread_leaving[...] = spread[rows:]
        spread_copy.start()
        pump(0)
        r.vec_own[12:13, :narrow] = jnp.sum(
            jnp.where(seen > 0.0, 0.0, back), axis=0, keepdims=True
        )
        put_dec(inner_rows(attn_in, grad_mixed[...]), 0, up_count, MID_PIECES * SUB_ROWS)
        pair_copy(MID_PIECES).start()
        pump(None)
        p.send_home(wait_copy, decoded_parts, r.rows_sem)

    def early_loads():
        return [
            pltpu.make_async_copy(source, dest, r.load_sem.at[10 + index])
            for index, (source, dest) in enumerate(
                (
                    (r.w_embed, r.v_embed), (r.out, r.v_out),
                )
            )
        ]

    spread_copy = remote(r.spread_leaving, r.spread_in, r.swap_sem.at[2], partner)
    dec_rows, big = DEC_PAD, BIG_PAD
    pl.run_scoped(
        decoder,
        pltpu.VMEM((dec_rows, narrow), f32),
        pltpu.VMEM((dec_rows, narrow), bf16),
        pltpu.VMEM((dec_rows, narrow), f32),
        pltpu.VMEM((dec_rows, narrow), bf16),
        pltpu.VMEM(r.dec_proj.shape, bf16),
        pltpu.VMEM(r.dec_up.shape, bf16),
        pltpu.VMEM(r.dec_down.shape, bf16),
        pltpu.VMEM(r.dec_qkv.shape, bf16),
        pltpu.VMEM((dec_rows, 3 * narrow), bf16),
        pltpu.VMEM((big, 2 * narrow), bf16),
        pltpu.VMEM((2, big, BIG_LANES), bf16),
        pltpu.VMEM((2, SMALL_PAD, SMALL_LANES), bf16),
        pltpu.VMEM((2, dec_rows // 2, narrow), bf16),
        pltpu.VMEM((dec_rows, narrow), f32),
        pltpu.VMEM((dec_rows, narrow), bf16),
        pltpu.VMEM((dec_rows, 3 * narrow), bf16),
        pltpu.VMEM((big, 2 * narrow), f32),
        pltpu.VMEM((big, 2 * narrow), bf16),
    )

    def encoder(
        v_down, v_slope, v_up, v_proj, v_middle, v_att, v_probs, v_query,
        v_own_kv, v_other_kv, v_x, v_lefts, v_lefts_other, right_own, kv_own, kv_leaving, grad_rows,
    ):
        load = loader(
        r.load_sem.at[12:],
        down=(r.w_down, v_down),
        slope=(r.slope, v_slope),
        lefts=(r.lefts_own, v_lefts),
        lefts_other=(r.lefts_other, v_lefts_other),
        up=(r.w_up, v_up),
        middle=(r.middle, v_middle),
        proj=(r.w_proj, v_proj),
        att=(r.att, v_att),
        probs=(r.probs, v_probs),
        query=(r.query, v_query),
        own_kv=(r.own_kv, v_own_kv),
        other_kv=(r.other_kv, v_other_kv),
        x=(r.x, v_x),
    )
        early = early_loads()
        vecs = r.enc_vecs
        starts = [0]
        for columns in (width, wide, narrow, width, 3 * width):
            starts.append(starts[-1] + columns)
        out_at, hidden_at, embedded_at, middle_at, all_mixed_at = (
            slice(*pair) for pair in zip(starts, starts[1:])
        )

        def give(cols, value, index):
            if value is not None:
                right_own[:, cols] = value
            copy = remote(
                right_own.at[:, cols], r.right_other.at[:, cols], r.swap_sem.at[index], partner
            )
            copy.start()
            return copy

        def weight_grad(cols, left, count, row, first_block=0, blocks=None):
            last_block = (
                (cols.stop - cols.start) // LANES if blocks is None else first_block + blocks
            )
            own = v_lefts[:, left : left + count, :rows].reshape(chips * count, rows)
            other = v_lefts_other[:, left : left + count, :rows].reshape(chips * count, rows)
            for block in range(first_block, last_block):
                columns = slice(cols.start + block * LANES, cols.start + (block + 1) * LANES)
                grad = product(own, right_own[:, columns]) + product(
                    other, r.right_other[:, columns]
                )
                grad = grad.astype(bf16)
                for piece, half, up, across, begin, end, at in sub_rows(
                    row + block * count, count
                ):
                    for image in range(chips):
                        held[piece, image, half, up, across, begin:end] = grad[
                            image * count + at : image * count + at + end - begin
                        ]

        left_hidden, left_mid = wide // (2 * chips), width // (2 * chips)
        left_mlp = left_hidden
        left_att, left_final, left_attn = (left_hidden + place * left_mid for place in (1, 2, 3))

        spread_copy.wait()
        grad_embedded = r.spread_own[...] + r.spread_in[...]
        embedded_copy = give(embedded_at, grad_embedded, 3)
        stage_pair(MID_PIECES)
        far_start(MID_PIECES)
        ready(*early)
        normed, inverse = norm_parts(r.v_out[...])
        grad_out, gain, shift = norm_backward(
            inner_cols(grad_embedded, r.v_embed[...]), normed, inverse, vecs[4:5]
        )
        r.vec_own[4:5] = gain
        r.vec_own[5:6] = shift
        grad_low = grad_out.astype(bf16)
        out_copy = give(out_at, grad_low, 4)
        ready(load.down, load.slope)
        grad_hidden = (v_slope[...].astype(f32) * inner_cols(grad_low, v_down[...])).astype(bf16)
        qkv_copies = [
            pltpu.make_async_copy(
                r.w_qkv.at[:, part * width : (part + 1) * width],
                v_down.at[part * width : (part + 1) * width],
                r.load_sem.at[25 + part],
            )
            for part in range(3)
        ]
        for copy in qkv_copies:
            copy.start()
        hidden_copy = give(hidden_at, grad_hidden, 5)
        ready(load.lefts, load.lefts_other)
        out_copy.wait()
        weight_grad(out_at, 0, left_hidden, DOWN_AT * SUB_ROWS, 0, 1)
        pump(DOWN_AT)
        weight_grad(out_at, 0, left_hidden, DOWN_AT * SUB_ROWS, 1, 2)
        ready(load.up, load.middle, load.proj)
        normed, inverse = norm_parts(v_middle[...])
        grad_values, gain, shift = norm_backward(
            inner_cols(grad_hidden, v_up[...]), normed, inverse, vecs[2:3]
        )
        r.vec_own[2:3] = gain
        r.vec_own[3:4] = shift
        grad_middle = grad_out + grad_values
        grad_low = grad_middle.astype(bf16)
        middle_copy = give(middle_at, grad_low, 6)
        grads = inner_cols(grad_low, v_proj[...]).astype(bf16)
        pump(DOWN_AT + 1)

        ready(load.att, load.probs, load.query, load.own_kv, load.other_kv)
        head_size = width // HE
        scale = 1.0 / math.sqrt(head_size)
        overlap = grads.astype(f32) * v_att[...].astype(f32)
        masks = lane_masks(head_size, bf16)
        wide_masks = lane_masks(head_size, f32)
        mixed_at = all_mixed_at.start
        for pair in range(width // 128):
            cols = slice(128 * pair, 128 * pair + 128)
            value_cols = slice(width + 128 * pair, width + 128 * pair + 128)
            keys = jnp.concatenate([v_own_kv[:, cols], v_other_kv[:, cols]], axis=0)
            values = jnp.concatenate([v_own_kv[:, value_cols], v_other_kv[:, value_cols]], axis=0)
            total_q = jnp.zeros((rows, 128), f32)
            total_k = jnp.zeros((2 * rows, 128), f32)
            total_v = jnp.zeros((2 * rows, 128), f32)
            for head, mask in enumerate(masks):
                delta = jnp.sum(overlap[:, cols] * wide_masks[head], axis=1, keepdims=True)
                one_grad = grads[:, cols] * mask
                chances = v_probs[len(masks) * pair + head, :, : 2 * rows]
                one_back = head_back(chances, one_grad, values, delta)
                total_q += product(one_back, keys * mask)
                total_k += inner_rows(one_back, v_query[:, cols] * mask)
                total_v += inner_rows(chances, one_grad)
            right_own[:, mixed_at + 128 * pair : mixed_at + 128 * pair + 128] = (
                total_q * scale
            ).astype(bf16)
            kv_own[:, cols] = total_k[:rows] * scale
            kv_own[:, value_cols] = total_v[:rows]
            kv_leaving[:, cols] = (total_k[rows:] * scale).astype(bf16)
            kv_leaving[:, value_cols] = total_v[rows:].astype(bf16)
        kv_copy = remote(kv_leaving, r.kv_in, r.swap_sem.at[7], partner)
        kv_copy.start()
        pump(DOWN_AT + 2)
        hidden_copy.wait()
        weight_grad(hidden_at, left_mlp, left_mid, UP_AT * SUB_ROWS)
        pump(MID_PIECES)

        kv_copy.wait()
        right_own[:, mixed_at + width : mixed_at + 3 * width] = (
            kv_own[...] + r.kv_in[...].astype(f32)
        ).astype(bf16)
        mixed_copy = give(all_mixed_at, None, 8)
        ready(load.x)
        normed, inverse = norm_parts(v_x[...].reshape(rows, width).astype(f32))
        grad_norm = jnp.zeros((rows, width), f32)
        for part, copy in enumerate(qkv_copies):
            copy.wait()
            place = mixed_at + part * width
            grad_norm += inner_cols(
                right_own[:, place : place + width], v_down[part * width : (part + 1) * width]
            )
        grad_values, gain, shift = norm_backward(grad_norm, normed, inverse, vecs[0:1])
        r.vec_own[0:1] = gain
        r.vec_own[1:2] = shift
        vec_copy = remote(r.vec_own, r.vec_in, r.swap_sem.at[9], partner)
        vec_copy.start()
        grad_values = grad_middle + grad_values
        grad_rows[0] = grad_values[: rows // 2]
        grad_rows[1] = grad_values[rows // 2 :]

        def grad_parts(segment):
            return [(grad_rows.at[segment], r.home_grad.at[low])]

        p.send_home(start_copy, grad_parts, r.grad_sem)
        pump(UP_AT)
        middle_copy.wait()
        embedded_copy.wait()
        embed_row = ATT_AT * SUB_ROWS + left_mid * width // LANES
        weight_grad(middle_at, left_att, left_mid, ATT_AT * SUB_ROWS)
        weight_grad(embedded_at, left_final, left_mid, embed_row)
        pump(UP_AT + 1)
        mixed_copy.wait()
        qkv_row = embed_row + left_mid * narrow // LANES
        weight_grad(all_mixed_at, left_attn, left_mid, qkv_row)
        pump(UP_AT + 2)
        vec_copy.wait()
        vectors = (r.vec_own[...] + r.vec_in[...]).astype(bf16)
        vec_row = qkv_row + left_mid * 3 * width // LANES
        piece, half, up, across, begin, end, _ = next(iter(sub_rows(vec_row, 16)))
        entry = lax.broadcasted_iota(jnp.int32, (width, LANES), 0)
        lane = lax.broadcasted_iota(jnp.int32, (width, LANES), 1)
        row_index = lax.broadcasted_iota(jnp.int32, (16, LANES), 0)
        narrow_left = narrow // (2 * chips)
        for image in range(chips):
            number = 2 * image + core
            enc_pick = (entry == lane + number * left_mid) & (lane < left_mid)
            dec_pick = (entry == lane + number * narrow_left) & (lane < narrow_left)
            enc_part = product(vectors, enc_pick.astype(f32).astype(bf16))
            dec_part = product(vectors, dec_pick.astype(f32).astype(bf16))
            held[piece, image, half, up, across, begin:end] = jnp.where(
                row_index < 8, enc_part, dec_part
            ).astype(bf16)
        for piece in range(ATT_AT, PIECES):
            pump(piece)
        p.send_home(wait_copy, grad_parts, r.grad_sem)

    pl.run_scoped(
        encoder,
        pltpu.VMEM(r.w_down.shape, bf16),
        pltpu.VMEM(r.slope.shape, bf16),
        pltpu.VMEM(r.w_up.shape, bf16),
        pltpu.VMEM(r.w_proj.shape, bf16),
        pltpu.VMEM(r.middle.shape, f32),
        pltpu.VMEM(r.att.shape, bf16),
        pltpu.VMEM(r.probs.shape, bf16),
        pltpu.VMEM(r.query.shape, bf16),
        pltpu.VMEM(r.own_kv.shape, bf16),
        pltpu.VMEM(r.other_kv.shape, bf16),
        pltpu.VMEM(r.x.shape, bf16),
        pltpu.VMEM(r.lefts_own.shape, bf16),
        pltpu.VMEM(r.lefts_own.shape, bf16),
        pltpu.VMEM(r.right_other.shape, bf16),
        pltpu.VMEM((rows, 2 * width), f32),
        pltpu.VMEM((rows, 2 * width), bf16),
        pltpu.VMEM((2, ENC_SEG, width), f32),
    )
    for _ in range(len(stages) - 1):
        pump(None)
    lax.fori_loop(0, PIECES, lambda i, c: (share_copy(i).wait(), c)[1], 0)


def back(chips, args):
    anywhere = pl.BlockSpec(memory_space=pl.ANY)
    vmem = pl.BlockSpec(memory_space=pltpu.VMEM)
    block = (EIGHTH, LANES)
    dma = pltpu.SemaphoreType.DMA
    width, narrow = by_name(args).w_embed.shape
    wide = by_name(args).w_up.shape[1]
    rights = width + wide + narrow + width + 3 * width
    outs = dict(
        shares=((PIECES, 2, 2, 2) + block, bf16),
        home_rows=((2, DEC_PAD // 2, narrow), bf16),
        home_grad=((2, ENC_SEG, width), f32),
    )
    scratch = dict(
        held=pltpu.VMEM((PIECES, chips, 2, 2, 2) + block, bf16),
        v_embed=pltpu.VMEM(by_name(args).w_embed.shape, bf16),
        v_out=pltpu.VMEM(by_name(args).out.shape, f32),
        leaving=pltpu.VMEM((DEC_PIECES, chips, 2, 2, 2) + block, bf16),
        from_pair=pltpu.VMEM((DEC_PIECES, chips, 2, 2, 2) + block, bf16),
        first=pltpu.VMEM((PIECES, 2, chips, 2) + block, bf16),
        second=pltpu.VMEM((PIECES, 2, chips) + block, bf16),
        from_chips=pltpu.VMEM((PIECES, chips - 1, 2) + block, bf16),
        gathered=pltpu.VMEM((PIECES, 2, 2, 2) + block, bf16),
        dec_kv_in=pltpu.VMEM((BIG_PAD, 2 * narrow), bf16),
        spread_own=pltpu.VMEM((ENC_PAD, narrow), bf16),
        spread_leaving=pltpu.VMEM((ENC_PAD, narrow), bf16),
        spread_in=pltpu.VMEM((ENC_PAD, narrow), bf16),
        right_other=pltpu.VMEM((ENC_PAD, rights), bf16),
        kv_in=pltpu.VMEM((ENC_PAD, 2 * width), bf16),
        vec_own=pltpu.VMEM((16, width), f32),
        vec_in=pltpu.VMEM((16, width), f32),
        load_sem=dma((28,)),
        chance_sem=dma((2, 2)),
        pair_sem=dma((DEC_PIECES, 2)),
        first_sem=dma((PIECES, 2, 2)),
        second_sem=dma((PIECES, 2, 2)),
        chip_sem=dma((PIECES, chips - 1, 2)),
        gather_sem=dma((PIECES, 4, 2)),
        share_sem=dma((PIECES,)),
        far_sem=dma((len(FAR), chips - 1, 3, 2)),
        swap_sem=dma((10, 2)),
        kv_sem=dma((4, 2, 2)),
        rows_sem=dma((2, 1, 2)),
        grad_sem=dma((2, 1, 2)),
    )
    names = list(args) + list(outs) + list(scratch)
    in_vmem = ("row_ids", "dec_vecs", "enc_vecs")
    return pl.pallas_call(
        functools.partial(back_kernel, chips, names),
        out_shape=[jax.ShapeDtypeStruct(shape, kind) for shape, kind in outs.values()],
        in_specs=[vmem if name in in_vmem else anywhere for name in args],
        out_specs=[anywhere] * len(outs),
        scratch_shapes=list(scratch.values()),
        compiler_params=pltpu.CompilerParams(
            collective_id=1, has_side_effects=True, vmem_limit_bytes=63 << 20
        ),
    )(*args.values())


def unstack_kernel(counts, enc_count, dec_count, flat, *outs):
    def runs(row, count):
        for piece, half, up, across, begin, end, at in sub_rows(row, count):
            start = piece * SUB_ROWS + (4 * half + 2 * up + across) * EIGHTH + begin
            yield flat[start : start + end - begin].astype(f32), at

    row = 0
    for out, count in zip(outs, counts):
        for block in range(out.shape[1] // LANES):
            for values, at in runs(row, count):
                out[at : at + values.shape[0], block * LANES : (block + 1) * LANES] = values
            row += count
    ((rows, _),) = runs(row, 16)
    outs[-2][...] = rows[:6, :enc_count]
    outs[-1][...] = rows[8:13, :dec_count]


def reduce_rest(chunk, seq):
    chips, rows, width = chunk.shape
    high, low = seq // 2, seq % 2
    eighth = rows // 8
    parts = chunk.reshape(chips, 2, 2, 2, eighth, width)

    def along_x(array):
        return permute(array, lambda s, i: (s ^ 1, i))

    def along_y(array):
        return permute(array, lambda s, i: (s ^ 2, i))

    def add(one, two):
        return (one.astype(f32) + two.astype(f32)).astype(bf16)

    one, two = parts[:, 0], parts[:, 1]
    one = add(pick(one, low, 2), along_x(pick(one, 1 - low, 2)))
    two = add(pick(two, high, 1), along_y(pick(two, 1 - high, 1)))
    one = add(pick(one, high, 1), along_y(pick(one, 1 - high, 1)))
    two = add(pick(two, low, 1), along_x(pick(two, 1 - low, 1)))
    mine = jnp.stack([one, two], axis=1)
    chip = lax.axis_index("img") // 2
    total = pick(mine, chip, 0).astype(f32)
    for step in range(1, chips):
        leaving = pick(mine, (chip + step) % chips, 0)
        arrived = permute(
            leaving,
            lambda s, i, step=step: (s, ((i // 2 + step) % chips) * 2 + (i & 1)),
        )
        total = total + arrived.astype(f32)
    own = total.astype(bf16)
    others = [permute(own, lambda s, i, step=step: (s ^ step, i)) for step in (1, 2, 3)]
    by_xor = jnp.stack([own] + others)
    ordered = jnp.stack([pick(by_xor, seq ^ place, 0) for place in range(4)], axis=1)
    return ordered.reshape(rows, width)


def shards(
    enc_input,
    cotangent,
    enc_image,
    visible_rows,
    enc_norms,
    enc_qkv,
    enc_proj,
    enc_up,
    enc_down,
    embed,
    dec_vecs,
    dec_qkv,
    dec_proj,
    dec_up,
    dec_down,
):
    seq = lax.axis_index("seq")
    img = lax.axis_index("img")
    images = lax.axis_size("img")
    core = img % 2
    odd = seq % 2 == 1
    enc_width = enc_input.shape[3]
    dec_width = dec_vecs.shape[0]
    enc_half = 2 * enc_input.shape[2]
    dec_quarter = cotangent.shape[2]

    enc_vecs = jnp.pad(enc_norms.T, ((0, 2), (0, 0)))
    dec_rows_vecs = jnp.pad(dec_vecs.T, ((0, 3), (0, 0)))
    table = position_table(dec_width)
    codes = np.zeros((2, DEC_PAD, dec_width), np.float32)
    for which in range(2):
        codes[which, :SMALL] = table[:SMALL]
        codes[which, SMALL_PAD : SMALL_PAD + HALF] = table[which * HALF : (which + 1) * HALF]
    chips = images // 2
    tables = jnp.stack([enc_image[0], visible_rows[0]])
    if images == 8:
        segments = tables.reshape(2, 2, 2, 2, enc_half // 2)
        segments = jnp.pad(
            segments, ((0, 0),) * 4 + ((0, ENC_SEG - enc_half // 2),), constant_values=-2
        )
        segments = segments.reshape(2, 2, 2, ENC_PAD)
        straight = segments.reshape(2, 2, 1, 2 * ENC_PAD)
        crossed = segments[:, :, ::-1].reshape(2, 2, 1, 2 * ENC_PAD)
        ordered = jnp.stack(
            [jnp.where(core == 0, straight, crossed), jnp.where(core == 0, crossed, straight)]
        )
        weights = dict(
            w_embed=embed, w_down=enc_down, w_up=enc_up, w_proj=enc_proj,
            w_qkv=enc_qkv, dec_qkv=dec_qkv, enc_vecs=enc_norms.T, dec_vecs=dec_vecs.T,
        )
        kept = front(
            dict(
                enc_input=enc_input[0], cotangent=cotangent[0], tables=ordered,
                codes=jnp.asarray(codes), **weights,
            ),
            chips,
        )
        shares, home_rows, home_grad = back(
            chips,
            dict(
                **kept, **weights, dec_proj=dec_proj, dec_up=dec_up, dec_down=dec_down
            ),
        )
        shapes = (
            dec_down.shape, dec_up.shape, dec_proj.shape, dec_qkv.shape, enc_down.shape,
            enc_up.shape, enc_proj.shape, embed.shape, enc_qkv.shape,
        )
        counts = [shape[0] // images for shape in shapes]
        (
            dec_down_share, dec_up_share, dec_proj_share, dec_qkv_share, enc_down_share,
            enc_up_share, enc_proj_share, embed_share, enc_qkv_share, enc_norm_share,
            dec_vec_share,
        ) = call(
            functools.partial(
                unstack_kernel, counts, enc_width // images, dec_width // images
            ),
            0,
            [((count, shape[1]), f32) for count, shape in zip(counts, shapes)]
            + [((6, enc_width // images), f32), ((5, dec_width // images), f32)],
            (shares.reshape(-1, LANES),),
            40,
        )
        enc_norm_share, dec_vec_share = enc_norm_share.T, dec_vec_share.T
        grad_input = home_grad[None, :, : enc_half // 2]
        decoded = home_rows[None, :, :dec_quarter]
        return (
            decoded,
            grad_input,
            enc_norm_share,
            enc_qkv_share,
            enc_proj_share,
            enc_up_share,
            enc_down_share,
            embed_share,
            dec_vec_share,
            dec_qkv_share,
            dec_proj_share,
            dec_up_share,
            dec_down_share,
        )

    other_tables = swap(tables)
    tables = jnp.where(seq // 2 == core, tables, other_tables)
    tables = jnp.where(odd, tables[:, 1], tables[:, 0])
    segments = tables.reshape(2, 2, 2, enc_half // 2)
    segments = jnp.pad(
        segments, ((0, 0),) * 3 + ((0, ENC_SEG - enc_half // 2),), constant_values=-2
    )
    halves = segments.reshape(2, 2, ENC_PAD)
    own = pick(halves, core, 1)
    ids = jnp.concatenate([own, pick(halves, 1 - core, 1)], axis=1)
    row_ids = ids[1:2]
    core_arg = core.reshape(1)

    blocks = jnp.pad(enc_input[0], ((0, 0), (0, ENC_SEG - enc_half // 2), (0, 0)))
    x = jnp.concatenate(exchange_packs(blocks, odd), axis=0)
    cot = jnp.concatenate(exchange_packs(cotangent[0], odd), axis=0)
    cot = jnp.concatenate(
        [
            pad_rows(lax.dynamic_slice_in_dim(cot, core * HALF, SMALL, 0), SMALL_PAD),
            pad_rows(lax.dynamic_slice_in_dim(cot, (1 - core) * SMALL, HALF, 0), BIG_PAD),
        ],
        axis=0,
    )
    enc_hidden_width = enc_up.shape[1]

    enc_query, enc_kv = call(
        enc_pre_kernel,
        0,
        [((ENC_PAD, enc_width), bf16), ((ENC_PAD, 2 * enc_width), bf16)],
        (x, enc_vecs, enc_qkv),
        40,
    )
    enc_other = swap(enc_kv)
    embedded, enc_att, enc_probs, enc_middle, enc_active, enc_slope, enc_out = call(
        enc_main_kernel,
        0,
        [
            ((ENC_PAD, dec_width), bf16),
            ((ENC_PAD, enc_width), bf16),
            ((HE, ENC_PAD, 2 * ENC_PAD), bf16),
            ((ENC_PAD, enc_width), f32),
            ((ENC_PAD, enc_hidden_width), bf16),
            ((ENC_PAD, enc_hidden_width), bf16),
            ((ENC_PAD, enc_width), f32),
        ],
        (
            x, enc_query, enc_kv, enc_other, own[0][:, None], ids[0:1], enc_vecs,
            enc_proj, enc_up, enc_down, embed,
        ),
        48,
    )

    code = pick(jnp.asarray(codes), core, 0)
    dec_input, dec_mixed, big_kv = call(
        dec_pre_kernel,
        1,
        [
            ((DEC_PAD, dec_width), f32),
            ((DEC_PAD, 3 * dec_width), bf16),
            ((BIG_PAD, 2 * dec_width), bf16),
        ],
        (core_arg, embedded, swap(embedded), row_ids, code, dec_rows_vecs, dec_qkv),
        40,
    )
    other_kv = swap(big_kv)
    groups = dec_width // 128

    def columns(rows, offset=0):
        return pl.BlockSpec((rows, 128), lambda group: (0, offset + group))

    def heads(rows, cols):
        return pl.BlockSpec((HD // groups, rows, cols), lambda group: (group, 0, 0))

    qkv_specs = [
        columns(DEC_PAD),
        columns(DEC_PAD, groups),
        columns(DEC_PAD, 2 * groups),
        columns(BIG_PAD),
        columns(BIG_PAD, groups),
    ]
    qkv_args = (dec_mixed, dec_mixed, dec_mixed, other_kv, other_kv)
    prob_specs = [heads(BIG_PAD, 2 * BIG_PAD), heads(SMALL_PAD, SMALL_PAD)]
    dec_att, big_probs, small_probs = pl.pallas_call(
        dec_att_kernel,
        grid=(groups,),
        in_specs=qkv_specs,
        out_specs=[columns(DEC_PAD)] + prob_specs,
        out_shape=[
            jax.ShapeDtypeStruct((DEC_PAD, dec_width), bf16),
            jax.ShapeDtypeStruct((HD, BIG_PAD, 2 * BIG_PAD), bf16),
            jax.ShapeDtypeStruct((HD, SMALL_PAD, SMALL_PAD), bf16),
        ],
        compiler_params=pltpu.CompilerParams(vmem_limit_bytes=48 << 20),
    )(*qkv_args)
    chunk_mid = Chunk(images, [dec_down.shape, dec_up.shape, dec_proj.shape])
    decoded, grad_dec_middle, dec_grad_att, vectors_two, *mid_grads = call(
        functools.partial(dec_mid_kernel, chunk_mid),
        1,
        [
            ((DEC_PAD, dec_width), bf16),
            ((DEC_PAD, dec_width), f32),
            ((DEC_PAD, dec_width), bf16),
            ((2, dec_width), f32),
        ]
        + chunk_mid.outs(),
        (core_arg, dec_input, dec_att, cot, dec_rows_vecs, dec_proj, dec_up, dec_down),
        48,
    )
    grad_specs = [columns(DEC_PAD)] * 3 + [columns(BIG_PAD)] * 2
    grad_query, grad_key, grad_value, leaving_key, leaving_value = pl.pallas_call(
        dec_att_back_kernel,
        grid=(groups,),
        in_specs=qkv_specs + [columns(DEC_PAD)] * 2 + prob_specs,
        out_specs=grad_specs,
        out_shape=[
            jax.ShapeDtypeStruct((DEC_PAD, dec_width), bf16),
            jax.ShapeDtypeStruct((DEC_PAD, dec_width), f32),
            jax.ShapeDtypeStruct((DEC_PAD, dec_width), f32),
            jax.ShapeDtypeStruct((BIG_PAD, dec_width), bf16),
            jax.ShapeDtypeStruct((BIG_PAD, dec_width), bf16),
        ],
        compiler_params=pltpu.CompilerParams(vmem_limit_bytes=48 << 20),
    )(*qkv_args, dec_grad_att, dec_att, big_probs, small_probs)
    chunk_post = Chunk(images, [dec_qkv.shape])
    own_spread, other_spread, vectors_one, *post_grads = call(
        functools.partial(dec_post_kernel, chunk_post),
        1,
        [
            ((ENC_PAD, dec_width), bf16),
            ((ENC_PAD, dec_width), bf16),
            ((3, dec_width), f32),
        ]
        + chunk_post.outs(),
        (
            core_arg, dec_input, grad_dec_middle, grad_query, grad_key, grad_value,
            swap(leaving_key), swap(leaving_value), row_ids, dec_rows_vecs, dec_qkv,
        ),
        48,
    )
    arrived_spread = swap(other_spread)
    chunk_down = Chunk(images, [enc_down.shape])
    chunk_up = Chunk(images, [enc_up.shape])
    grad_enc_middle, enc_grad_att, enc_vectors_two, *mlp_grads = call(
        functools.partial(enc_mlp_back_kernel, chunk_down, chunk_up),
        1,
        [
            ((ENC_PAD, enc_width), f32),
            ((ENC_PAD, enc_width), bf16),
            ((4, enc_width), f32),
        ]
        + chunk_down.outs()
        + chunk_up.outs(),
        (
            core_arg, own_spread, arrived_spread, enc_out, enc_middle, enc_active, enc_slope,
            enc_vecs, embed, enc_down, enc_up, enc_proj,
        ),
        56,
    )
    down_grads, up_grads = mlp_grads[: len(chunk_down.outs())], mlp_grads[len(chunk_down.outs()) :]
    enc_grad_query, enc_grad_kv, enc_leaving = call(
        enc_att_back_kernel,
        0,
        [
            ((ENC_PAD, enc_width), bf16),
            ((ENC_PAD, 2 * enc_width), f32),
            ((ENC_PAD, 2 * enc_width), bf16),
        ],
        (enc_grad_att, enc_att, enc_probs, enc_query, enc_kv, enc_other),
        48,
    )
    chunk_att = Chunk(images, [enc_qkv.shape, enc_proj.shape, embed.shape], 16)
    grad_input, enc_vectors_one, *att_grads = call(
        functools.partial(enc_post_kernel, chunk_att),
        1,
        [((ENC_PAD, enc_width), f32), ((2, enc_width), f32)] + chunk_att.outs(),
        (
            core_arg, x, enc_att, grad_enc_middle, enc_grad_query, enc_grad_kv,
            swap(enc_leaving), enc_out, own_spread, arrived_spread, enc_vecs, enc_qkv,
        ),
        48,
    )

    def by_image(rows):
        flat = rows.reshape(rows.shape[0], images, rows.shape[1] // images)
        return flat.transpose(1, 0, 2).reshape(images, -1)

    vectors = jnp.concatenate(
        [
            by_image(jnp.concatenate([enc_vectors_one, enc_vectors_two])),
            by_image(jnp.concatenate([vectors_one[:2], vectors_two, vectors_one[2:]])),
        ],
        axis=1,
    ).astype(bf16)
    vectors = jnp.pad(vectors, ((0, 0), (0, 16 * LANES - vectors.shape[1])))
    vectors = vectors.reshape(images // 2, 2, 16, LANES)
    vectors = (pick(vectors, core, 1), pick(vectors, 1 - core, 1))
    chunk_pairs = [
        chunk.pair(grads, core)
        for chunk, grads in (
            (chunk_mid, mid_grads),
            (chunk_post, post_grads),
            (chunk_down, down_grads),
            (chunk_up, up_grads),
            (chunk_att, att_grads),
        )
    ]
    place = slice(chunk_att.used, chunk_att.used + 16)
    chunk_pairs[-1] = tuple(
        array.at[:, place].set(rows) for array, rows in zip(chunk_pairs[-1], vectors)
    )
    shares = [reduce_rest(reduce_pair(*pair), seq) for pair in chunk_pairs]
    mid_share, post_share, down_share, up_share, att_share = shares
    dec_down_share, dec_up_share, dec_proj_share = chunk_mid.split(mid_share)
    (dec_qkv_share,) = chunk_post.split(post_share)
    (enc_down_share,) = chunk_down.split(down_share)
    (enc_up_share,) = chunk_up.split(up_share)
    enc_qkv_share, enc_proj_share, embed_share = chunk_att.split(att_share)
    vectors = att_share[chunk_att.used : chunk_att.used + 16].reshape(-1).astype(f32)
    enc_count, dec_count = enc_width // images, dec_width // images
    enc_norm_share = vectors[: 6 * enc_count].reshape(6, enc_count).T
    dec_vec_share = vectors[6 * enc_count : 6 * enc_count + 5 * dec_count].reshape(5, dec_count).T

    start = jnp.concatenate([decoded[:SMALL], decoded[SMALL_PAD : SMALL_PAD + HALF]])
    end = jnp.concatenate([decoded[SMALL_PAD : SMALL_PAD + HALF], decoded[:SMALL]])
    natural = jnp.where(core == 0, start, end)
    decoded = jnp.stack(exchange_packs(natural.reshape(2, dec_quarter, dec_width), odd))[None]
    grad_input = jnp.stack(
        exchange_packs(grad_input.reshape(2, ENC_SEG, enc_width)[:, : enc_half // 2], odd)
    )[None]
    return (
        decoded,
        grad_input,
        enc_norm_share,
        enc_qkv_share,
        enc_proj_share,
        enc_up_share,
        enc_down_share,
        embed_share,
        dec_vec_share,
        dec_qkv_share,
        dec_proj_share,
        dec_up_share,
        dec_down_share,
    )


def solution(mesh):
    rows = P("img", None, "seq", None)
    tables = P("img", None, None)
    shares = P("img", None)
    return jax.shard_map(
        shards,
        mesh=mesh,
        in_specs=(rows, rows, tables, tables) + (P(),) * 11,
        out_specs=(rows, rows) + (shares,) * 11,
        check_vma=False,
    )
```

```python
import functools
import math

import jax
import jax.numpy as jnp
import numpy as np
from jax import lax
from jax.experimental import pallas as pl
from jax.experimental.pallas import tpu as pltpu
from jax.sharding import PartitionSpec as P

HE = 12
HD = 16
PATCHES = 784
SMALL = PATCHES // 4
HALF = PATCHES // 2
SMALL_PAD = 208
BIG_PAD = 400
DEC_PAD = SMALL_PAD + BIG_PAD
ENC_SEG = 80
ENC_PAD = 2 * ENC_SEG
BIG_LANES = 896
SMALL_LANES = 256
ENC_LANES = 384
LEFT_LANES = 256

eps_norm = 1e-06
masked_score = -1e30
bf16 = jnp.bfloat16
f32 = jnp.float32


def product(left_side, right_side):
    return jnp.dot(left_side, right_side, preferred_element_type=f32)


def inner_rows(left_side, right_side):
    return lax.dot_general(
        left_side, right_side, (((0,), (0,)), ((), ())), preferred_element_type=f32
    )


def inner_cols(left_side, right_side):
    return lax.dot_general(
        left_side, right_side, (((1,), (1,)), ((), ())), preferred_element_type=f32
    )


def norm_parts(values):
    centered = values - jnp.mean(values, axis=-1, keepdims=True)
    inverse = lax.rsqrt(jnp.mean(centered * centered, axis=-1, keepdims=True) + eps_norm)
    return centered * inverse, inverse


def norm_backward(grad_out, normed, inverse, norm_gain):
    scaled = grad_out * norm_gain
    grad_values = inverse * (
        scaled
        - jnp.mean(scaled, axis=-1, keepdims=True)
        - normed * jnp.mean(scaled * normed, axis=-1, keepdims=True)
    )
    return (
        grad_values,
        jnp.sum(grad_out * normed, axis=0, keepdims=True),
        jnp.sum(grad_out, axis=0, keepdims=True),
    )


def gelu_parts(hidden):
    below = 0.5 + 0.5 * lax.erf(hidden * math.sqrt(0.5))
    density = jnp.exp(hidden * hidden * -0.5) * (1.0 / math.sqrt(2.0 * math.pi))
    return hidden * below, below + hidden * density


LANES = 256
EIGHTH = 48
LAST_EIGHTH = 32
SUB_ROWS = 8 * EIGHTH


def put(core, dest, offset, grad):
    low = grad.astype(bf16)
    if len(dest) == 1:
        dest[0][...] = low
        return
    keep, leaving = dest
    chips = keep.shape[0]
    count = low.shape[0] // (2 * chips)
    for case in (0, 1):

        @pl.when(core == case)
        def _():
            for image in range(2 * chips):
                ref = keep if image % 2 == case else leaving
                for block in range(low.shape[1] // LANES):
                    start = offset + block * count
                    ref[image // 2, start : start + count, :] = low[
                        image * count : (image + 1) * count, block * LANES : (block + 1) * LANES
                    ]


def image_rows(shape, images):
    return shape[0] // images * (shape[1] // LANES)


class Chunk:
    def __init__(self, images, shapes, spare=0):
        self.images = images
        self.shapes = shapes
        self.offsets = []
        rows = 0
        for shape in shapes:
            self.offsets.append(rows)
            rows += image_rows(shape, images)
        self.used = rows
        rows += spare
        self.direct = all(shape[0] // images % 16 == 0 for shape in shapes)
        unit = SUB_ROWS if self.direct else 8
        self.rows = -(-rows // unit) * unit

    def outs(self):
        if self.direct:
            return [((self.images // 2, self.rows, LANES), bf16)] * 2
        return [(shape, bf16) for shape in self.shapes]

    def dests(self, refs):
        if self.direct:
            return [tuple(refs)] * len(self.shapes)
        return [(ref,) for ref in refs]

    def pair(self, results, core):
        if self.direct:
            return tuple(results)
        pieces = []
        for grad in results:
            for start in range(0, grad.shape[1], LANES):
                piece = grad[:, start : start + LANES]
                pieces.append(piece.reshape(self.images, -1, LANES))
        stacked = jnp.concatenate(pieces, axis=1)
        stacked = jnp.pad(stacked, ((0, 0), (0, self.rows - stacked.shape[1]), (0, 0)))
        both = stacked.reshape(self.images // 2, 2, self.rows, LANES)
        return pick(both, core, 1), pick(both, 1 - core, 1)

    def split(self, share):
        results = []
        for shape, offset in zip(self.shapes, self.offsets):
            count = shape[0] // self.images
            pieces = [
                share[offset + block * count : offset + (block + 1) * count]
                for block in range(shape[1] // LANES)
            ]
            results.append(jnp.concatenate(pieces, axis=1).astype(f32))
        return results


def call(kernel, scalars, outs, args, megabytes):
    vmem = pl.BlockSpec(memory_space=pltpu.VMEM)
    smem = pl.BlockSpec(memory_space=pltpu.SMEM)
    return pl.pallas_call(
        kernel,
        out_shape=[jax.ShapeDtypeStruct(shape, kind) for shape, kind in outs],
        in_specs=[smem] * scalars + [vmem] * (len(args) - scalars),
        out_specs=[vmem] * len(outs),
        compiler_params=pltpu.CompilerParams(vmem_limit_bytes=megabytes << 20),
    )(*args)


def lane_masks(head_size, kind):
    lanes = lax.broadcasted_iota(jnp.int32, (1, 128), 1) // head_size
    return [(lanes == head).astype(f32).astype(kind) for head in range(128 // head_size)]


def softmax_rows(scores, scale):
    row_max = jnp.max(scores, axis=1, keepdims=True)
    weights = jnp.exp2((scores - row_max) * (scale * math.log2(math.e)))
    return (weights * (1.0 / jnp.sum(weights, axis=1, keepdims=True))).astype(bf16)


def head_back(probs, grads, values, delta):
    grad_probs = inner_cols(grads, values)
    return (probs.astype(f32) * (grad_probs - delta)).astype(bf16)


def enc_pre_kernel(x, vecs, w_qkv, query, key_value):
    normed, _ = norm_parts(x[...].astype(f32))
    attn_in = (normed * vecs[0:1] + vecs[1:2]).astype(bf16)
    mixed = product(attn_in, w_qkv[...]).astype(bf16)
    width = query.shape[1]
    query[...] = mixed[:, :width]
    key_value[...] = mixed[:, width:]


def enc_main_kernel(
    x, query, own_kv, other_kv, own_ids, all_ids, vecs, w_proj, w_up, w_down, w_embed,
    embedded, att, probs, middle, active, slope, out
):
    width = query.shape[1]
    head_size = width // HE
    bias = jnp.where(own_ids[...] == all_ids[...], 0.0, masked_score)
    masks = lane_masks(head_size, bf16)
    for pair in range(width // 128):
        cols = slice(128 * pair, 128 * pair + 128)
        value_cols = slice(width + 128 * pair, width + 128 * pair + 128)
        keys = jnp.concatenate([own_kv[:, cols], other_kv[:, cols]], axis=0)
        values = jnp.concatenate([own_kv[:, value_cols], other_kv[:, value_cols]], axis=0)
        total = jnp.zeros((query.shape[0], 128), f32)
        for head, mask in enumerate(masks):
            scores = inner_cols(query[:, cols] * mask, keys) + bias
            chances = softmax_rows(scores, 1.0 / math.sqrt(head_size))
            probs[len(masks) * pair + head] = chances
            total += product(chances, values * mask)
        att[:, cols] = total.astype(bf16)
    mid = x[...].astype(f32) + product(att[...], w_proj[...])
    middle[...] = mid
    normed, _ = norm_parts(mid)
    mlp_in = (normed * vecs[2:3] + vecs[3:4]).astype(bf16)
    result, steepness = gelu_parts(product(mlp_in, w_up[...]))
    active[...] = result.astype(bf16)
    slope[...] = steepness.astype(bf16)
    last = mid + product(active[...], w_down[...])
    out[...] = last
    normed, _ = norm_parts(last)
    final = (normed * vecs[4:5] + vecs[5:6]).astype(bf16)
    embedded[...] = product(final, w_embed[...]).astype(bf16)


def chosen_rows(core, visible_rows):
    index = lax.broadcasted_iota(jnp.int32, (DEC_PAD, 1), 0)
    small = index + core * (SMALL + PATCHES)
    big = index + (SMALL - SMALL_PAD) + core * HALF
    row = jnp.where(index < SMALL, small, -1)
    row = jnp.where((index >= SMALL_PAD) & (index < SMALL_PAD + HALF), big, row)
    return (row == visible_rows).astype(f32)


def dec_pre_kernel(core, own, other, rows, code, vecs, w_qkv, dec_input, mixed, big_kv):
    chosen = chosen_rows(core[0], rows[...])
    seen = jnp.sum(chosen, axis=1, keepdims=True)
    tokens = jnp.concatenate([own[...], other[...]], axis=0)
    picked = product(chosen.astype(bf16), tokens)
    values = jnp.where(seen > 0.0, picked, vecs[4:5]) + code[...]
    dec_input[...] = values
    normed, _ = norm_parts(values)
    attn_in = (normed * vecs[0:1] + vecs[1:2]).astype(bf16)
    result = product(attn_in, w_qkv[...]).astype(bf16)
    mixed[...] = result
    big_kv[...] = result[SMALL_PAD:, values.shape[1] :]


def big_bias():
    column = lax.broadcasted_iota(jnp.int32, (1, 2 * BIG_PAD), 1)
    place = jnp.where(column >= BIG_PAD, column - BIG_PAD, column)
    return jnp.where(place < HALF, 0.0, masked_score)


def small_bias():
    column = lax.broadcasted_iota(jnp.int32, (1, SMALL_PAD), 1)
    return jnp.where(column < SMALL, 0.0, masked_score)


def dec_att_kernel(query, key, value, other_key, other_value, att, big_probs, small_probs):
    head_size = query.shape[1] * 4 // HD
    scale = 1.0 / math.sqrt(head_size)
    keys = jnp.concatenate([key[SMALL_PAD:], other_key[...]], axis=0)
    values = jnp.concatenate([value[SMALL_PAD:], other_value[...]], axis=0)
    total = jnp.zeros((BIG_PAD, 128), f32)
    small_total = jnp.zeros((SMALL_PAD, 128), f32)
    for head, mask in enumerate(lane_masks(head_size, bf16)):
        scores = inner_cols(query[SMALL_PAD:] * mask, keys) + big_bias()
        chances = softmax_rows(scores, scale)
        big_probs[head] = chances
        total += product(chances, values * mask)
        scores = inner_cols(query[:SMALL_PAD] * mask, key[:SMALL_PAD]) + small_bias()
        chances = softmax_rows(scores, scale)
        small_probs[head] = chances
        small_total += product(chances, value[:SMALL_PAD] * mask)
    att[:SMALL_PAD] = small_total.astype(bf16)
    att[SMALL_PAD:] = total.astype(bf16)


def dec_mid_kernel(
    chunk, core, dec_input, att, cot, vecs, w_proj, w_up, w_down,
    decoded, grad_middle, grad_att, vectors, *grads
):
    down_dest, up_dest, proj_dest = chunk.dests(grads)
    down_at, up_at, proj_at = chunk.offsets
    grad_down, grad_up = [], []
    middle = dec_input[...] + product(att[...], w_proj[...])
    normed, inverse = norm_parts(middle)
    mlp_in = (normed * vecs[2:3] + vecs[3:4]).astype(bf16)
    result = middle
    grad_norm = jnp.zeros_like(middle)
    step = 512
    for start in range(0, w_up.shape[1], step):
        cols = slice(start, start + step)
        active, slope = gelu_parts(product(mlp_in, w_up[:, cols]))
        active = active.astype(bf16)
        result += product(active, w_down[cols])
        grad_down.append(inner_rows(active, cot[...]).astype(bf16))
        grad_hidden = (slope * inner_cols(cot[...], w_down[cols])).astype(bf16)
        grad_up.append(inner_rows(mlp_in, grad_hidden).astype(bf16))
        grad_norm += inner_cols(grad_hidden, w_up[:, cols])
    decoded[...] = result.astype(bf16)
    grad_values, gain, shift = norm_backward(grad_norm, normed, inverse, vecs[2:3])
    vectors[0:1] = gain
    vectors[1:2] = shift
    back = cot[...].astype(f32) + grad_values
    grad_middle[...] = back
    low = back.astype(bf16)
    grad_att[...] = inner_cols(low, w_proj[...]).astype(bf16)
    put(core[0], proj_dest, proj_at, inner_rows(att[...], low))
    put(core[0], down_dest, down_at, jnp.concatenate(grad_down, axis=0))
    put(core[0], up_dest, up_at, jnp.concatenate(grad_up, axis=1))


def dec_att_back_kernel(
    query, key, value, other_key, other_value, grads, att, big_probs, small_probs,
    grad_query, grad_key, grad_value, leaving_key, leaving_value
):
    head_size = query.shape[1] * 4 // HD
    scale = 1.0 / math.sqrt(head_size)
    keys = jnp.concatenate([key[SMALL_PAD:], other_key[...]], axis=0)
    values = jnp.concatenate([value[SMALL_PAD:], other_value[...]], axis=0)
    overlap = grads[...].astype(f32) * att[...].astype(f32)
    big_q = jnp.zeros((BIG_PAD, 128), f32)
    big_k = jnp.zeros((2 * BIG_PAD, 128), f32)
    big_v = jnp.zeros((2 * BIG_PAD, 128), f32)
    small_q = jnp.zeros((SMALL_PAD, 128), f32)
    small_k = jnp.zeros((SMALL_PAD, 128), f32)
    small_v = jnp.zeros((SMALL_PAD, 128), f32)
    masks = lane_masks(head_size, f32)
    for head, mask in enumerate(lane_masks(head_size, bf16)):
        delta = jnp.sum(overlap * masks[head], axis=1, keepdims=True)
        one_query, one_grad = query[...] * mask, grads[...] * mask
        chances = big_probs[head]
        back = head_back(chances, one_grad[SMALL_PAD:], values, delta[SMALL_PAD:])
        big_q += product(back, keys * mask)
        big_k += inner_rows(back, one_query[SMALL_PAD:])
        big_v += inner_rows(chances, one_grad[SMALL_PAD:])
        chances = small_probs[head]
        back = head_back(chances, one_grad[:SMALL_PAD], value[:SMALL_PAD], delta[:SMALL_PAD])
        small_q += product(back, key[:SMALL_PAD] * mask)
        small_k += inner_rows(back, one_query[:SMALL_PAD])
        small_v += inner_rows(chances, one_grad[:SMALL_PAD])
    grad_query[:SMALL_PAD] = (small_q * scale).astype(bf16)
    grad_query[SMALL_PAD:] = (big_q * scale).astype(bf16)
    grad_key[:SMALL_PAD] = small_k * scale
    grad_key[SMALL_PAD:] = big_k[:BIG_PAD] * scale
    grad_value[:SMALL_PAD] = small_v
    grad_value[SMALL_PAD:] = big_v[:BIG_PAD]
    leaving_key[...] = (big_k[BIG_PAD:] * scale).astype(bf16)
    leaving_value[...] = big_v[BIG_PAD:].astype(bf16)


def dec_post_kernel(
    chunk, core, dec_input, grad_middle, grad_query, grad_key, grad_value, arrived_key,
    arrived_value, rows, vecs, w_qkv, own_spread, other_spread, vectors, *grads
):
    normed, inverse = norm_parts(dec_input[...])
    attn_in = (normed * vecs[0:1] + vecs[1:2]).astype(bf16)
    key = jnp.concatenate(
        [grad_key[:SMALL_PAD], grad_key[SMALL_PAD:] + arrived_key[...].astype(f32)], axis=0
    ).astype(bf16)
    value = jnp.concatenate(
        [grad_value[:SMALL_PAD], grad_value[SMALL_PAD:] + arrived_value[...].astype(f32)], axis=0
    ).astype(bf16)
    mixed = jnp.concatenate([grad_query[...], key, value], axis=1)
    grad_values, gain, shift = norm_backward(
        inner_cols(mixed, w_qkv[...]), normed, inverse, vecs[0:1]
    )
    back = grad_middle[...] + grad_values
    chosen = chosen_rows(core[0], rows[...])
    seen = jnp.sum(chosen, axis=1, keepdims=True)
    spread = inner_rows(chosen.astype(bf16), back.astype(bf16)).astype(bf16)
    own_spread[...] = spread[:ENC_PAD]
    other_spread[...] = spread[ENC_PAD:]
    vectors[0:1] = gain
    vectors[1:2] = shift
    vectors[2:3] = jnp.sum(jnp.where(seen > 0.0, 0.0, back), axis=0, keepdims=True)
    put(core[0], chunk.dests(grads)[0], chunk.offsets[0], inner_rows(attn_in, mixed))


def enc_mlp_back_kernel(
    first, second, core, own_spread, arrived, out, middle, active, slope,
    vecs, w_embed, w_down, w_up, w_proj, grad_middle, grad_att, vectors, *grads
):
    first_grads, second_grads = grads[: len(first.outs())], grads[len(first.outs()) :]
    grad_embedded = own_spread[...] + arrived[...]
    normed, inverse = norm_parts(out[...])
    grad_out, gain, shift = norm_backward(
        inner_cols(grad_embedded, w_embed[...]), normed, inverse, vecs[4:5]
    )
    vectors[2:3] = gain
    vectors[3:4] = shift
    low = grad_out.astype(bf16)
    put(core[0], first.dests(first_grads)[0], first.offsets[0], inner_rows(active[...], low))
    grad_hidden = (slope[...].astype(f32) * inner_cols(low, w_down[...])).astype(bf16)
    normed, inverse = norm_parts(middle[...])
    mlp_in = (normed * vecs[2:3] + vecs[3:4]).astype(bf16)
    put(
        core[0], second.dests(second_grads)[0], second.offsets[0], inner_rows(mlp_in, grad_hidden)
    )
    grad_values, gain, shift = norm_backward(
        inner_cols(grad_hidden, w_up[...]), normed, inverse, vecs[2:3]
    )
    vectors[0:1] = gain
    vectors[1:2] = shift
    back = grad_out + grad_values
    grad_middle[...] = back
    grad_att[...] = inner_cols(back.astype(bf16), w_proj[...]).astype(bf16)


def enc_att_back_kernel(
    grads, att, probs, query, own_kv, other_kv, grad_query, grad_kv, leaving
):
    width = query.shape[1]
    head_size = width // HE
    scale = 1.0 / math.sqrt(head_size)
    overlap = grads[...].astype(f32) * att[...].astype(f32)
    masks = lane_masks(head_size, bf16)
    wide_masks = lane_masks(head_size, f32)
    rows = query.shape[0]
    for pair in range(width // 128):
        cols = slice(128 * pair, 128 * pair + 128)
        value_cols = slice(width + 128 * pair, width + 128 * pair + 128)
        keys = jnp.concatenate([own_kv[:, cols], other_kv[:, cols]], axis=0)
        values = jnp.concatenate([own_kv[:, value_cols], other_kv[:, value_cols]], axis=0)
        total_q = jnp.zeros((rows, 128), f32)
        total_k = jnp.zeros((2 * rows, 128), f32)
        total_v = jnp.zeros((2 * rows, 128), f32)
        for head, mask in enumerate(masks):
            delta = jnp.sum(overlap[:, cols] * wide_masks[head], axis=1, keepdims=True)
            one_grad = grads[:, cols] * mask
            chances = probs[len(masks) * pair + head]
            one_back = head_back(chances, one_grad, values, delta)
            total_q += product(one_back, keys * mask)
            total_k += inner_rows(one_back, query[:, cols] * mask)
            total_v += inner_rows(chances, one_grad)
        grad_query[:, cols] = (total_q * scale).astype(bf16)
        grad_kv[:, cols] = total_k[:rows] * scale
        grad_kv[:, value_cols] = total_v[:rows]
        leaving[:, cols] = (total_k[rows:] * scale).astype(bf16)
        leaving[:, value_cols] = total_v[rows:].astype(bf16)


def enc_post_kernel(
    chunk, core, x, att, grad_middle, grad_query, grad_kv, arrived, out, own_spread, other_spread,
    vecs, w_qkv, grad_input, vectors, *grads
):
    qkv_dest, proj_dest, embed_dest = chunk.dests(grads)
    normed, _ = norm_parts(out[...])
    final = (normed * vecs[4:5] + vecs[5:6]).astype(bf16)
    put(
        core[0], embed_dest, chunk.offsets[2], inner_rows(final, own_spread[...] + other_spread[...])
    )
    put(
        core[0], proj_dest, chunk.offsets[1],
        inner_rows(att[...], grad_middle[...].astype(bf16)),
    )
    normed, inverse = norm_parts(x[...].astype(f32))
    attn_in = (normed * vecs[0:1] + vecs[1:2]).astype(bf16)
    key_value = (grad_kv[...] + arrived[...].astype(f32)).astype(bf16)
    mixed = jnp.concatenate([grad_query[...], key_value], axis=1)
    grad_values, gain, shift = norm_backward(
        inner_cols(mixed, w_qkv[...]), normed, inverse, vecs[0:1]
    )
    grad_input[...] = grad_middle[...] + grad_values
    vectors[0:1] = gain
    vectors[1:2] = shift
    put(core[0], qkv_dest, chunk.offsets[0], inner_rows(attn_in, mixed))


def permute(array, where_to):
    seq_count = lax.axis_size("seq")
    img_count = lax.axis_size("img")
    pairs = []
    for seq in range(seq_count):
        for img in range(img_count):
            seq_to, img_to = where_to(seq, img)
            pairs.append((seq * img_count + img, seq_to * img_count + img_to))
    return lax.ppermute(array, ("seq", "img"), pairs)


def swap(array):
    return permute(array, lambda seq, img: (seq, img ^ 1))


def pack_move(turn):
    def where_to(seq, img):
        return (2 * (img & 1) + (turn ^ (seq & 1)), (img & ~1) | (seq >> 1))

    return where_to


def exchange_packs(blocks, odd):
    rounds = [
        permute(jnp.where(odd, blocks[1 - turn], blocks[turn]), pack_move(turn)) for turn in (0, 1)
    ]
    return (jnp.where(odd, rounds[1], rounds[0]), jnp.where(odd, rounds[0], rounds[1]))


def pick(array, index, axis):
    return lax.dynamic_index_in_dim(array, index, axis, keepdims=False)


def pad_rows(array, rows):
    return jnp.pad(array, ((0, rows - array.shape[0]),) + ((0, 0),) * (array.ndim - 1))


def position_table(row_width):
    halfway = row_width // 2
    frequency = np.exp(np.arange(halfway, dtype=np.float64) * (-math.log(10000.0) / halfway))
    angles = np.arange(PATCHES, dtype=np.float64)[:, None] * frequency[None, :]
    return np.concatenate([np.sin(angles), np.cos(angles)], axis=1).astype(np.float32)


def reduce_pair(keep, leaving):
    return (keep.astype(f32) + swap(leaving).astype(f32)).astype(bf16)


MID_PIECES, POST_PIECES, DOWN_PIECES, UP_PIECES, ATT_PIECES = 3, 1, 3, 3, 4
DEC_PIECES = MID_PIECES + POST_PIECES
DOWN_AT = DEC_PIECES
UP_AT = DOWN_AT + DOWN_PIECES
ATT_AT = UP_AT + UP_PIECES
PIECES = ATT_AT + ATT_PIECES
FAR = (0, MID_PIECES, DOWN_AT + 1)


class Refs:
    def __init__(self, names, refs):
        self.__dict__.update(zip(names, refs))


def by_name(items):
    return Refs(items.keys(), items.values())


def piece_rows(piece):
    return LAST_EIGHTH if piece == PIECES - 1 else EIGHTH


def sub_rows(row, count):
    done = 0
    while done < count:
        piece = min((row + done) // SUB_ROWS, PIECES - 1)
        place, height = row + done - piece * SUB_ROWS, piece_rows(piece)
        start = place % height
        size = min(count - done, height - start)
        place //= height
        yield piece, place // 4, place // 2 % 2, place % 2, start, start + size, done
        done += size


class Place:
    def __init__(self):
        self.seq, self.img = lax.axis_index("seq"), lax.axis_index("img")
        self.chip, self.core = self.img // 2, lax.rem(self.img, 2)
        self.high, self.low = self.seq // 2, lax.rem(self.seq, 2)
        self.partner = dict(img=self.img + 1 - 2 * self.core)

    def remote(self, source, dest, sems, device):
        return pltpu.make_async_remote_copy(
            src_ref=source,
            dst_ref=dest,
            send_sem=sems.at[0],
            recv_sem=sems.at[1],
            device_id=device,
            device_id_type=pl.DeviceIdType.MESH,
        )

    def home(self, turn):
        segment = turn + self.low - 2 * turn * self.low
        device = dict(seq=2 * self.core + segment, img=2 * self.chip + self.high)
        stays = (self.high == self.core) if turn == 0 else None
        return device, segment, stays

    def send_home(self, act, source_parts, sems):
        for turn in (0, 1):
            device, segment, stays = self.home(turn)
            for part, (source, dest) in enumerate(source_parts(segment)):
                sem = sems.at[turn, part]
                if stays is None:
                    act(self.remote(source, dest, sem, device))
                else:

                    @pl.when(stays)
                    def _():
                        act(pltpu.make_async_copy(source, dest, sem.at[0]))

                    @pl.when(jnp.logical_not(stays))
                    def _():
                        act(self.remote(source, dest, sem, device))

    def greet(self, peers):
        barrier = pltpu.get_barrier_semaphore()

        def signal(device):
            pl.semaphore_signal(
                barrier, inc=1, device_id=device, device_id_type=pl.DeviceIdType.MESH
            )

        for device in peers:
            signal(device)
        signal(self.home(1)[0])

        @pl.when(self.high != self.core)
        def _():
            signal(self.home(0)[0])

        return lambda: pl.semaphore_wait(
            barrier, len(peers) + 1 + jnp.where(self.high == self.core, 0, 1)
        )


def start_copy(copy):
    copy.start()


def wait_copy(copy):
    copy.wait()


def loader(sems, **items):
    copies = {}
    for index, (name, (source, dest)) in enumerate(items.items()):
        copies[name] = pltpu.make_async_copy(source, dest, sems.at[index])
        copies[name].start()
    return by_name(copies)


def ready(*copies):
    for copy in copies:
        copy.wait()


def row_order(core, pad, rows):
    local = lax.broadcasted_iota(jnp.int32, (DEC_PAD, 2 * pad), 0)
    place = lax.broadcasted_iota(jnp.int32, (DEC_PAD, 2 * pad), 1)
    small = local < SMALL_PAD
    natural = jnp.where(small, local + core * HALF, local - SMALL_PAD + (1 - core) * SMALL)
    there = jnp.where(small, local, local - SMALL_PAD + SMALL - HALF) < SMALL
    spot = natural + jnp.where(natural >= rows, pad - rows, 0)
    return ((spot == place) & there).astype(f32).astype(bf16)


def front_kernel(names, *refs):
    r = Refs(names, refs)
    p = Place()
    core, low, high = p.core, p.low, p.high
    width, narrow = r.w_embed.shape
    rows = ENC_PAD
    seg_rows, cot_rows = r.enc_input.shape[1], r.cotangent.shape[1]
    cot_pad = r.cot_send.shape[1]
    load = loader(
        r.load_sem,
        qkv=(r.w_qkv, r.v_qkv),
        proj=(r.w_proj, r.v_proj),
        up=(r.w_up, r.v_up),
        down=(r.w_down, r.v_down),
        embed=(r.w_embed, r.v_embed),
        code=(r.codes.at[core], r.v_code),
        dec_qkv=(r.dec_qkv, r.v_dec_qkv),
    )
    greeted = p.greet([p.partner])
    for block in range(2):
        r.enc_send[block] = jnp.concatenate(
            [
                r.enc_input[block].astype(f32),
                jnp.zeros((ENC_SEG - seg_rows, width), f32),
            ],
            axis=0,
        ).astype(bf16)
    greeted()

    def enc_parts(segment):
        return [(r.enc_send.at[segment], r.v_x.at[low])]

    def cot_parts(segment):
        return [(r.cot_send.at[segment], r.cot_in.at[low])]

    p.send_home(start_copy, enc_parts, r.enc_sem)
    table_copy = p.remote(r.tables.at[1], r.tables_in, r.swap_sem.at[0], p.partner)
    table_copy.start()
    for block in range(2):
        r.cot_send[block] = jnp.concatenate(
            [
                r.cotangent[block].astype(f32),
                jnp.zeros((cot_pad - cot_rows, narrow), f32),
            ],
            axis=0,
        ).astype(bf16)
    p.send_home(start_copy, cot_parts, r.cot_sem)
    enc_vecs, dec_vecs = r.enc_vecs, r.dec_vecs

    stores = []

    def store(source, dest):
        copy = pltpu.make_async_copy(source, dest, r.store_sem.at[len(stores)])
        copy.start()
        stores.append(copy)

    def put_left(values, start):
        chips = r.lefts_keep.shape[0]
        turned = values.astype(f32).T.astype(bf16)
        count = turned.shape[0] // (2 * chips)
        for case in (0, 1):

            @pl.when(core == case)
            def _():
                for image in range(2 * chips):
                    ref = r.lefts_keep if image % 2 == case else r.lefts_leaving
                    ref[image // 2, start : start + count, :rows] = turned[
                        image * count : (image + 1) * count
                    ]

    left_hidden = r.w_up.shape[1] // (2 * r.lefts_keep.shape[0])
    left_mid = width // (2 * r.lefts_keep.shape[0])

    def norm_in(values, vecs, row):
        normed, _ = norm_parts(values)
        return (normed * vecs[row : row + 1] + vecs[row + 1 : row + 2]).astype(bf16)

    p.send_home(wait_copy, enc_parts, r.enc_sem)
    x = r.v_x[...].reshape(rows, width).astype(f32)
    attn_in = norm_in(x, enc_vecs, 0)
    ready(load.qkv)
    mixed = product(attn_in, r.v_qkv[...]).astype(bf16)
    r.v_query[...] = mixed[:, :width]
    r.v_own_kv[...] = mixed[:, width:]
    kv_copy = p.remote(r.v_own_kv, r.v_other_kv, r.swap_sem.at[1], p.partner)
    kv_copy.start()
    put_left(attn_in, left_hidden + 3 * left_mid)
    table_copy.wait()
    mine = high == core
    ids = jnp.where(mine, r.tables[0, 0, low], r.tables_in[0, low])
    row_ids = jnp.where(mine, r.tables[0, 1, low], r.tables_in[1, low])
    r.row_ids[...] = row_ids
    across = lax.broadcasted_iota(jnp.int32, (rows, 2 * rows), 1)
    along = lax.broadcasted_iota(jnp.int32, (rows, 2 * rows), 0)
    wide_ids = ids.astype(f32)
    own_ids = jnp.sum(jnp.where(across == along, wide_ids, 0.0), axis=1, keepdims=True)
    bias = jnp.where(own_ids == wide_ids, 0.0, masked_score)
    head_size = width // HE
    masks = lane_masks(head_size, bf16)
    kv_copy.wait()
    for pair in range(width // 128):
        cols = slice(128 * pair, 128 * pair + 128)
        value_cols = slice(width + 128 * pair, width + 128 * pair + 128)
        keys = jnp.concatenate([r.v_own_kv[:, cols], r.v_other_kv[:, cols]], axis=0)
        values = jnp.concatenate([r.v_own_kv[:, value_cols], r.v_other_kv[:, value_cols]], axis=0)
        total = jnp.zeros((rows, 128), f32)
        for head, mask in enumerate(masks):
            scores = inner_cols(r.v_query[:, cols] * mask, keys) + bias
            chances = softmax_rows(scores, 1.0 / math.sqrt(head_size))
            r.v_probs[len(masks) * pair + head, :, : 2 * rows] = chances
            total += product(chances, values * mask)
        r.v_att[:, cols] = total.astype(bf16)
    store(r.v_x, r.x)
    store(r.v_query, r.query)
    store(r.v_own_kv, r.own_kv)
    store(r.v_other_kv, r.other_kv)
    store(r.v_probs, r.probs)
    store(r.v_att, r.att)

    ready(load.proj, load.up, load.down, load.embed)
    middle = x + product(r.v_att[...], r.v_proj[...])
    r.v_middle[...] = middle
    store(r.v_middle, r.middle)
    mlp_in = norm_in(middle, enc_vecs, 2)
    active, slope = gelu_parts(product(mlp_in, r.v_up[...]))
    active = active.astype(bf16)
    r.v_slope[...] = slope.astype(bf16)
    store(r.v_slope, r.slope)
    out = middle + product(active, r.v_down[...])
    r.v_out[...] = out
    store(r.v_out, r.out)
    final = norm_in(out, enc_vecs, 4)
    r.emb_own[...] = product(final, r.v_embed[...]).astype(bf16)
    emb_copy = p.remote(r.emb_own, r.emb_in, r.swap_sem.at[2], p.partner)
    emb_copy.start()
    put_left(active, 0)
    put_left(mlp_in, left_hidden)
    put_left(r.v_att[...], left_hidden + left_mid)
    put_left(final, left_hidden + 2 * left_mid)
    store(r.lefts_keep, r.lefts_own)
    lefts_copy = p.remote(r.lefts_leaving, r.lefts_other, r.swap_sem.at[3], p.partner)
    lefts_copy.start()

    chosen = chosen_rows(core, row_ids)
    seen = jnp.sum(chosen, axis=1, keepdims=True)
    ready(load.code, load.dec_qkv)
    emb_copy.wait()
    tokens = jnp.concatenate([r.emb_own[...], r.emb_in[...]], axis=0)
    picked = product(chosen.astype(bf16), tokens)
    values = jnp.where(seen > 0.0, picked, dec_vecs[4:5]) + r.v_code[...]
    r.v_code[...] = values
    store(r.v_code, r.dec_input)
    mixed = product(norm_in(values, dec_vecs, 0), r.v_dec_qkv[...]).astype(bf16)
    r.v_mixed[...] = mixed
    big_copy = p.remote(
        r.v_mixed.at[SMALL_PAD:, narrow:], r.big_in, r.swap_sem.at[4], p.partner
    )
    big_copy.start()
    store(r.v_mixed, r.dec_mixed)

    p.send_home(wait_copy, cot_parts, r.cot_sem)
    moved = product(
        row_order(core, cot_pad, cot_rows), r.cot_in[...].reshape(2 * cot_pad, narrow)
    )
    r.v_cot[...] = moved.astype(bf16)
    store(r.v_cot, r.cot)
    big_copy.wait()
    store(r.big_in, r.dec_other_kv)

    head_size = narrow // HD
    per_group = 128 // head_size
    scale = 1.0 / math.sqrt(head_size)
    masks = lane_masks(head_size, bf16)

    def chance_copies(head, slot):
        return (
            pltpu.make_async_copy(r.chances.at[slot], r.big_probs.at[head], r.chance_sem.at[slot, 0]),
            pltpu.make_async_copy(
                r.small_chances.at[slot], r.small_probs.at[head], r.chance_sem.at[slot, 1]
            ),
        )

    wide_masks = lane_masks(head_size, f32)
    lane = lax.broadcasted_iota(jnp.int32, (1, 128), 1)

    def pad_column(blocks, size, used):
        index = lax.broadcasted_iota(jnp.int32, (blocks * size, 1), 0)
        index = jnp.where(index >= size, index - size, index)
        return jnp.where(index < used, 0.0, masked_score)

    big_pad, small_pad = pad_column(2, BIG_PAD, HALF), pad_column(1, SMALL_PAD, SMALL)

    def weigh(query, key, value, pad, mask, spare):
        one = spare.astype(bf16)
        scores = inner_cols(query * mask + one, key * mask + (pad * spare).astype(bf16))
        row_max = jnp.max(scores, axis=1, keepdims=True)
        weights = jnp.exp2((scores - row_max) * (scale * math.log2(math.e))).astype(bf16)
        mixed = product(weights, value * mask + one)
        return weights, mixed, 1.0 / jnp.sum(mixed * spare, axis=1, keepdims=True)

    def group_forward(group, carry):
        def cols(offset):
            return pl.ds(pl.multiple_of(offset * narrow + group * 128, 128), 128)

        query = r.v_mixed[:, cols(0)]
        small_key, small_value = r.v_mixed[:SMALL_PAD, cols(1)], r.v_mixed[:SMALL_PAD, cols(2)]
        keys = jnp.concatenate([r.v_mixed[SMALL_PAD:, cols(1)], r.big_in[:, cols(0)]], axis=0)
        values = jnp.concatenate([r.v_mixed[SMALL_PAD:, cols(2)], r.big_in[:, cols(1)]], axis=0)
        total = jnp.zeros((BIG_PAD, 128), f32)
        small_total = jnp.zeros((SMALL_PAD, 128), f32)
        inverse = jnp.zeros((BIG_PAD, 128), f32)
        small_inverse = jnp.zeros((SMALL_PAD, 128), f32)
        for head, mask in enumerate(masks):
            slot = head
            number = group * per_group + head

            @pl.when(group > 0)
            def _():
                for copy in chance_copies(number - per_group, slot):
                    copy.wait()

            spare = (lane == (head * head_size + 64) % 128).astype(f32)
            weights, mixed, shrink = weigh(
                query[SMALL_PAD:], keys, values, big_pad, mask, spare
            )
            r.chances[slot, :, : 2 * BIG_PAD] = weights
            shrink = shrink * wide_masks[head]
            inverse += shrink
            total += mixed * shrink
            weights, mixed, shrink = weigh(
                query[:SMALL_PAD], small_key, small_value, small_pad, mask, spare
            )
            r.small_chances[slot, :, :SMALL_PAD] = weights
            shrink = shrink * wide_masks[head]
            small_inverse += shrink
            small_total += mixed * shrink
            for copy in chance_copies(number, slot):
                copy.start()
        r.v_dec_att[:SMALL_PAD, cols(0)] = small_total.astype(bf16)
        r.v_dec_att[SMALL_PAD:, cols(0)] = total.astype(bf16)
        r.v_inverse[:SMALL_PAD, cols(0)] = small_inverse
        r.v_inverse[SMALL_PAD:, cols(0)] = inverse
        return carry

    lax.fori_loop(0, narrow // 128, group_forward, 0)
    store(r.v_dec_att, r.dec_att)
    store(r.v_inverse, r.dec_inverse)
    for slot in range(per_group):
        for copy in chance_copies(HD - per_group + slot, slot):
            copy.wait()
    for copy in stores:
        copy.wait()
    lefts_copy.wait()


def front(args, chips):
    anywhere = pl.BlockSpec(memory_space=pl.ANY)
    vmem = pl.BlockSpec(memory_space=pltpu.VMEM)
    dma = pltpu.SemaphoreType.DMA
    width, narrow = by_name(args).w_embed.shape
    wide = by_name(args).w_up.shape[1]
    left_rows = (4 * width + wide) // (2 * chips)
    cot_pad = DEC_PAD // 2
    outs = dict(
        x=((2, ENC_SEG, width), bf16),
        query=((ENC_PAD, width), bf16),
        own_kv=((ENC_PAD, 2 * width), bf16),
        other_kv=((ENC_PAD, 2 * width), bf16),
        probs=((HE, ENC_PAD, ENC_LANES), bf16),
        att=((ENC_PAD, width), bf16),
        middle=((ENC_PAD, width), f32),
        slope=((ENC_PAD, wide), bf16),
        out=((ENC_PAD, width), f32),
        lefts_own=((chips, left_rows, LEFT_LANES), bf16),
        lefts_other=((chips, left_rows, LEFT_LANES), bf16),
        dec_input=((DEC_PAD, narrow), f32),
        dec_mixed=((DEC_PAD, 3 * narrow), bf16),
        cot=((DEC_PAD, narrow), bf16),
        dec_other_kv=((BIG_PAD, 2 * narrow), bf16),
        big_probs=((HD, BIG_PAD, BIG_LANES), bf16),
        small_probs=((HD, SMALL_PAD, SMALL_LANES), bf16),
        dec_att=((DEC_PAD, narrow), bf16),
        dec_inverse=((DEC_PAD, narrow), f32),
        row_ids=((1, 2 * ENC_PAD), jnp.int32),
    )

    def like(out):
        return pltpu.VMEM(*out)

    scratch = dict(
        enc_send=like(by_name(outs).x),
        cot_send=pltpu.VMEM((2, cot_pad, narrow), bf16),
        cot_in=pltpu.VMEM((2, cot_pad, narrow), bf16),
        tables_in=pltpu.VMEM(by_name(args).tables.shape[1:], jnp.int32),
        v_x=like(by_name(outs).x),
        v_query=like(by_name(outs).query),
        v_own_kv=like(by_name(outs).own_kv),
        v_other_kv=like(by_name(outs).other_kv),
        v_probs=like(by_name(outs).probs),
        v_att=like(by_name(outs).att),
        v_middle=like(by_name(outs).middle),
        v_slope=like(by_name(outs).slope),
        v_out=like(by_name(outs).out),
        lefts_keep=like(by_name(outs).lefts_own),
        lefts_leaving=like(by_name(outs).lefts_own),
        emb_own=pltpu.VMEM((ENC_PAD, narrow), bf16),
        emb_in=pltpu.VMEM((ENC_PAD, narrow), bf16),
        v_code=like(by_name(outs).dec_input),
        v_mixed=like(by_name(outs).dec_mixed),
        v_cot=like(by_name(outs).cot),
        big_in=like(by_name(outs).dec_other_kv),
        chances=pltpu.VMEM((4, BIG_PAD, BIG_LANES), bf16),
        small_chances=pltpu.VMEM((4, SMALL_PAD, SMALL_LANES), bf16),
        v_dec_att=like(by_name(outs).dec_att),
        v_inverse=like(by_name(outs).dec_inverse),
        v_qkv=pltpu.VMEM(by_name(args).w_qkv.shape, bf16),
        v_proj=pltpu.VMEM(by_name(args).w_proj.shape, bf16),
        v_up=pltpu.VMEM(by_name(args).w_up.shape, bf16),
        v_down=pltpu.VMEM(by_name(args).w_down.shape, bf16),
        v_embed=pltpu.VMEM(by_name(args).w_embed.shape, bf16),
        v_dec_qkv=pltpu.VMEM(by_name(args).dec_qkv.shape, bf16),
        load_sem=dma((7,)),
        store_sem=dma((17,)),
        chance_sem=dma((4, 2)),
        swap_sem=dma((5, 2)),
        enc_sem=dma((2, 1, 2)),
        cot_sem=dma((2, 1, 2)),
    )
    names = list(args) + list(outs) + list(scratch)
    in_vmem = ("enc_input", "cotangent", "tables", "enc_vecs", "dec_vecs")
    results = pl.pallas_call(
        functools.partial(front_kernel, names),
        out_shape=[jax.ShapeDtypeStruct(shape, kind) for shape, kind in outs.values()],
        in_specs=[vmem if name in in_vmem else anywhere for name in args],
        out_specs=[vmem if name == "row_ids" else anywhere for name in outs],
        scratch_shapes=list(scratch.values()),
        compiler_params=pltpu.CompilerParams(
            collective_id=2, has_side_effects=True, vmem_limit_bytes=60 << 20
        ),
    )(*args.values())
    return dict(zip(outs, results))


def back_kernel(chips, names, *refs):
    r = Refs(names, refs)
    p = Place()
    chip, core, high, low = p.chip, p.core, p.high, p.low
    remote, partner = p.remote, p.partner
    along_x = dict(seq=p.seq + 1 - 2 * low)
    along_y = dict(seq=p.seq + 2 - 4 * high)
    others = [dict(img=lax.rem(chip + step, chips) * 2 + core) for step in range(1, chips)]
    width, wide, narrow = r.w_embed.shape[0], r.w_up.shape[1], r.w_embed.shape[1]
    rows = ENC_PAD

    def add(one, two):
        return (one.astype(f32) + two.astype(f32)).astype(bf16)

    held, first, second, from_chips, gathered = (
        r.held, r.first, r.second, r.from_chips, r.gathered
    )

    def pair_copy(i):
        return remote(r.leaving.at[i], r.from_pair.at[i], r.pair_sem.at[i], partner)

    def first_copies(i):
        n = slice(0, piece_rows(i))
        return (
            remote(
                held.at[i, :, 0, :, 1 - low, n], first.at[i, 0, :, :, n], r.first_sem.at[i, 0],
                along_x,
            ),
            remote(
                held.at[i, :, 1, 1 - high, :, n], first.at[i, 1, :, :, n], r.first_sem.at[i, 1],
                along_y,
            ),
        )

    def second_copies(i):
        n = slice(0, piece_rows(i))
        return (
            remote(
                held.at[i, :, 0, 1 - high, low, n], second.at[i, 0, :, n], r.second_sem.at[i, 0],
                along_y,
            ),
            remote(
                held.at[i, :, 1, high, 1 - low, n], second.at[i, 1, :, n], r.second_sem.at[i, 1],
                along_x,
            ),
        )

    def chip_copies(i):
        n = slice(0, piece_rows(i))
        return [
            remote(
                held.at[i, device["img"] // 2, :, high, low, n],
                from_chips.at[i, step, :, n],
                r.chip_sem.at[i, step],
                device,
            )
            for step, device in enumerate(others)
        ]

    def gather_copies(i, arrive):
        n = slice(0, piece_rows(i))
        x_place = 1 - low if arrive else low
        y_place = 1 - high if arrive else high
        one, two = gathered.at[i, 0, high, x_place, n], gathered.at[i, 1, y_place, low, n]
        return (
            remote(one, one, r.gather_sem.at[i, 0], along_x),
            remote(two, two, r.gather_sem.at[i, 1], along_y),
        )

    def spread_copies(i, arrive):
        n = slice(0, piece_rows(i))
        x_place = 1 - low if arrive else low
        y_place = 1 - high if arrive else high
        one, two = gathered.at[i, 0, y_place, :, n], gathered.at[i, 1, :, x_place, n]
        return (
            remote(one, one, r.gather_sem.at[i, 2], along_y),
            remote(two, two, r.gather_sem.at[i, 3], along_x),
        )

    def share_copy(i):
        return pltpu.make_async_copy(gathered.at[i], r.shares.at[i], r.share_sem.at[i])

    def stage_pair(i):
        pair_copy(i).wait()
        for image in range(chips):
            held[i, image] = add(held[i, image], r.from_pair[i, image])

    def stage_first(i):
        for copy in first_copies(i):
            copy.start()

    def stage_second(i):
        for copy in first_copies(i):
            copy.wait_recv()
        n = slice(0, piece_rows(i))
        held[i, :, 0, :, low, n] = add(held[i, :, 0, :, low, n], first[i, 0, :, :, n])
        held[i, :, 1, high, :, n] = add(held[i, :, 1, high, :, n], first[i, 1, :, :, n])
        for copy in second_copies(i):
            copy.start()

    def stage_chips(i):
        for copy in second_copies(i):
            copy.wait_recv()
        n = slice(0, piece_rows(i))
        held[i, :, 0, high, low, n] = add(held[i, :, 0, high, low, n], second[i, 0, :, n])
        held[i, :, 1, high, low, n] = add(held[i, :, 1, high, low, n], second[i, 1, :, n])
        for copy in chip_copies(i):
            copy.start()

    def stage_gather(i):
        for copy in chip_copies(i):
            copy.wait_recv()
        n = slice(0, piece_rows(i))
        mine = held[i, chip, :, high, low, n].astype(f32)
        for step in range(chips - 1):
            mine += from_chips[i, step, :, n].astype(f32)
        gathered[i, :, high, low, n] = mine.astype(bf16)
        for copy in gather_copies(i, False):
            copy.start()

    def stage_spread(i):
        for copy in gather_copies(i, True):
            copy.wait_recv()
        for copy in spread_copies(i, False):
            copy.start()

    def stage_end(i):
        for copy in spread_copies(i, True):
            copy.wait_recv()
        for copy in (
            *first_copies(i), *second_copies(i), *chip_copies(i), *gather_copies(i, False),
            *spread_copies(i, False),
        ):
            copy.wait_send()
        share_copy(i).start()

    def far_copies(i, begin=0, end=None):
        spots = [
            (step, part, device, source, dest)
            for step, device in enumerate(others)
            for part, (source, dest) in enumerate(
                (
                    (held.at[i, device["img"] // 2, :, 0], first.at[i, :, 1 + step]),
                    (held.at[i, device["img"] // 2, :, 1, 0], second.at[i, :, 1 + step]),
                    (held.at[i, device["img"] // 2, :, 1, 1], from_chips.at[i, step]),
                )
            )
        ]
        return [
            remote(source, dest, r.far_sem.at[FAR.index(i), step, part], device)
            for step, part, device, source, dest in spots[begin:end]
        ]

    def far_start(i, begin=0, end=None):
        for copy in far_copies(i, begin, end):
            copy.start()

    def far_first_copies(i):
        return (
            remote(held.at[i, chip, 0, :, 1 - low], first.at[i, 0, 0], r.first_sem.at[i, 0], along_x),
            remote(held.at[i, chip, 1, 1 - high], first.at[i, 1, 0], r.first_sem.at[i, 1], along_y),
        )

    def far_second_copies(i):
        return (
            remote(
                held.at[i, chip, 0, 1 - high, low], second.at[i, 0, 0], r.second_sem.at[i, 0],
                along_y,
            ),
            remote(
                held.at[i, chip, 1, high, 1 - low], second.at[i, 1, 0], r.second_sem.at[i, 1],
                along_x,
            ),
        )

    def far_first(i):
        for copy in far_copies(i):
            copy.wait_recv()

        def total(mine, *arrived):
            mine = mine.astype(f32)
            for one in arrived:
                mine += one.astype(f32)
            return mine.astype(bf16)

        steps = range(chips - 1)
        held[i, chip, :, 0] = total(held[i, chip, :, 0], *(first[i, :, 1 + k] for k in steps))
        held[i, chip, :, 1, 0] = total(
            held[i, chip, :, 1, 0], *(second[i, :, 1 + k] for k in steps)
        )
        held[i, chip, :, 1, 1] = total(
            held[i, chip, :, 1, 1], *(from_chips[i, k] for k in steps)
        )
        for copy in far_first_copies(i):
            copy.start()

    def far_second(i):
        for copy in far_first_copies(i):
            copy.wait_recv()
        held[i, chip, 0, :, low] = add(held[i, chip, 0, :, low], first[i, 0, 0])
        held[i, chip, 1, high] = add(held[i, chip, 1, high], first[i, 1, 0])
        for copy in far_second_copies(i):
            copy.start()

    def far_gather(i):
        for copy in far_second_copies(i):
            copy.wait_recv()
        gathered[i, 0, high, low] = add(held[i, chip, 0, high, low], second[i, 0, 0])
        gathered[i, 1, high, low] = add(held[i, chip, 1, high, low], second[i, 1, 0])
        for copy in gather_copies(i, False):
            copy.start()

    def far_end(i):
        for copy in spread_copies(i, True):
            copy.wait_recv()
        for copy in (
            *far_copies(i), *far_first_copies(i), *far_second_copies(i),
            *gather_copies(i, False), *spread_copies(i, False),
        ):
            copy.wait_send()
        share_copy(i).start()

    stages = (stage_first, stage_second, stage_chips, stage_gather, stage_spread, stage_end)
    far_stages = (far_first, far_second, far_gather, stage_spread, far_end)
    line = []

    def pump(piece):
        line.append(piece)
        for lag in range(len(stages)):
            slot = len(line) - 1 - lag
            if slot >= 0 and line[slot] is not None:
                course = far_stages if line[slot] in FAR else stages
                if lag < len(course):
                    course[lag](line[slot])

    greeted = p.greet([partner, along_x, along_y, *others])

    def put_dec(grad, first_image, count, row):
        grad = grad.astype(bf16)
        for case in (0, 1):

            @pl.when(core == case)
            def _():
                for index in range(grad.shape[0] // count):
                    image = first_image + index
                    ref = held if image % 2 == case else r.leaving
                    for block in range(grad.shape[1] // LANES):
                        for piece, half, up, across, begin, end, at in sub_rows(
                            row + block * count, count
                        ):
                            ref[piece, image // 2, half, up, across, begin:end] = grad[
                                index * count + at : index * count + at + end - begin,
                                block * LANES : (block + 1) * LANES,
                            ]

    def decoder(
        dec_input, att, inverses, cot, w_proj, w_up, w_down, w_qkv, mixed, other_kv, chances,
        small_chances, decoded, grad_middle, grad_att, grad_mixed, grad_kv, kv_leaving,
    ):
        load = loader(
        r.load_sem,
        dec_input=(r.dec_input, dec_input),
        att=(r.dec_att, att),
        proj=(r.dec_proj, w_proj),
        up=(r.dec_up, w_up),
        cot=(r.cot, cot),
        down=(r.dec_down, w_down),
        mixed=(r.dec_mixed, mixed),
        other=(r.dec_other_kv, other_kv),
        qkv=(r.dec_qkv, w_qkv),
        inverses=(r.dec_inverse, inverses),
    )

        def chance_copies(head, slot):
            return (
                pltpu.make_async_copy(
                    r.big_probs.at[head], chances.at[slot], r.chance_sem.at[slot, 0]
                ),
                pltpu.make_async_copy(
                    r.small_probs.at[head], small_chances.at[slot], r.chance_sem.at[slot, 1]
                ),
            )

        for copy in chance_copies(0, 0):
            copy.start()
        greeted()

        ready(load.dec_input, load.att, load.proj)
        vecs = r.dec_vecs
        middle = dec_input[...] + product(att[...], w_proj[...])
        normed, inverse = norm_parts(middle)
        mlp_in = (normed * vecs[2:3] + vecs[3:4]).astype(bf16)
        result = middle
        grad_norm = jnp.zeros_like(middle)
        step = 2 * w_down.shape[0] // (2 * chips)
        down_count, up_count = step // 2, narrow // (2 * chips)
        up_row = down_count * narrow // LANES
        proj_row = up_row + up_count * w_up.shape[1] // LANES
        ready(load.up, load.cot, load.down)
        for copy in early_loads():
            copy.start()
        for block in range(w_up.shape[1] // step):
            cols = slice(block * step, (block + 1) * step)
            active, slope = gelu_parts(product(mlp_in, w_up[:, cols]))
            active = active.astype(bf16)
            result += product(active, w_down[cols])
            put_dec(inner_rows(active, cot[...]), 2 * block, down_count, 0)
            grad_hidden = (slope * inner_cols(cot[...], w_down[cols])).astype(bf16)
            put_dec(
                inner_rows(mlp_in, grad_hidden), 0, up_count,
                up_row + up_count * block * step // LANES,
            )
            grad_norm += inner_cols(grad_hidden, w_up[:, cols])
        order = row_order(core, DEC_PAD // 2, (SMALL + HALF) // 2)
        decoded[...] = (
            inner_rows(order, result.astype(bf16)).astype(bf16).reshape(2, DEC_PAD // 2, narrow)
        )

        def decoded_parts(segment):
            return [(decoded.at[segment], r.home_rows.at[low])]

        p.send_home(start_copy, decoded_parts, r.rows_sem)
        grad_values, gain, shift = norm_backward(grad_norm, normed, inverse, vecs[2:3])
        r.vec_own[...] = jnp.zeros(r.vec_own.shape, f32)
        r.vec_own[10:11, :narrow] = gain
        r.vec_own[11:12, :narrow] = shift
        back = cot[...].astype(f32) + grad_values
        grad_middle[...] = back
        back = back.astype(bf16)
        ready(load.inverses)
        grad_low = inner_cols(back, w_proj[...]).astype(bf16)
        grad_att[...] = (grad_low.astype(f32) * inverses[...]).astype(bf16)
        put_dec(inner_rows(att[...], back), 0, up_count, proj_row)
        for i in range(MID_PIECES):
            pair_copy(i).start()

        ready(load.mixed, load.other)
        head_size = narrow // HD
        per_group = 128 // head_size
        scale = 1.0 / math.sqrt(head_size)
        masks, wide_masks = lane_masks(head_size, bf16), lane_masks(head_size, f32)

        def group_back(group, last):
            def cols(offset):
                return pl.ds(pl.multiple_of(offset * narrow + group * 128, 128), 128)

            query = mixed[:, cols(0)]
            small_key, small_value = mixed[:SMALL_PAD, cols(1)], mixed[:SMALL_PAD, cols(2)]
            keys = jnp.concatenate([mixed[SMALL_PAD:, cols(1)], other_kv[:, cols(0)]], axis=0)
            values = jnp.concatenate([mixed[SMALL_PAD:, cols(2)], other_kv[:, cols(1)]], axis=0)
            grads = grad_att[:, cols(0)]
            overlap = grads.astype(f32) * att[:, cols(0)].astype(f32)
            def turned(values):
                return values.astype(f32).T.astype(bf16)

            big_query, small_query = turned(query[SMALL_PAD:]), turned(query[:SMALL_PAD])
            big_grad, small_grad = turned(grads[SMALL_PAD:]), turned(grads[:SMALL_PAD])
            big_q = jnp.zeros((BIG_PAD, 128), f32)
            small_q = jnp.zeros((SMALL_PAD, 128), f32)
            big_k, big_v, small_k, small_v = [], [], [], []
            for head, mask in enumerate(masks):
                slot = head % 2
                number = group * per_group + head
                for copy in chance_copies(number, slot):
                    copy.wait()
                if head < per_group - 1:
                    for copy in chance_copies(number + 1, 1 - slot):
                        copy.start()
                else:

                    @pl.when(group < last)
                    def _():
                        for copy in chance_copies(number + 1, 1 - slot):
                            copy.start()

                delta = jnp.sum(overlap * wide_masks[head], axis=1, keepdims=True)
                one_grad = grads * mask
                own = slice(head * head_size, (head + 1) * head_size)
                probs = chances[slot, :, : 2 * BIG_PAD]
                one = head_back(probs, one_grad[SMALL_PAD:], values, delta[SMALL_PAD:])
                big_q += product(one, keys * mask)
                big_k.append(product(big_query[own], one))
                big_v.append(product(big_grad[own], probs))
                probs = small_chances[slot, :, :SMALL_PAD]
                one = head_back(probs, one_grad[:SMALL_PAD], small_value, delta[:SMALL_PAD])
                small_q += product(one, small_key * mask)
                small_k.append(product(small_query[own], one))
                small_v.append(product(small_grad[own], probs))
            big_k, big_v, small_k, small_v = (
                jnp.concatenate(parts, axis=0).T for parts in (big_k, big_v, small_k, small_v)
            )
            grad_mixed[:SMALL_PAD, cols(0)] = (small_q * scale).astype(bf16)
            grad_mixed[SMALL_PAD:, cols(0)] = (big_q * scale).astype(bf16)
            grad_mixed[:SMALL_PAD, cols(1)] = (small_k * scale).astype(bf16)
            grad_mixed[:SMALL_PAD, cols(2)] = small_v.astype(bf16)
            grad_kv[:, cols(0)] = big_k[:BIG_PAD] * scale
            grad_kv[:, cols(1)] = big_v[:BIG_PAD]
            kv_leaving[:, cols(0)] = (big_k[BIG_PAD:] * scale).astype(bf16)
            kv_leaving[:, cols(1)] = big_v[BIG_PAD:].astype(bf16)

        def kv_copies(group):
            for which in range(2):
                cols = slice(which * narrow + group * 128, which * narrow + (group + 1) * 128)
                yield remote(
                    kv_leaving.at[:, cols], r.dec_kv_in.at[:, cols], r.kv_sem.at[group, which],
                    partner,
                )

        groups = narrow // 128
        for group in range(groups):
            lax.fori_loop(
                group, group + 1, lambda g, c: (group_back(g, groups - 1), c)[1], 0
            )
            for copy in kv_copies(group):
                copy.start()
            if group == 0:
                stage_pair(0)
                far_start(0)
                stage_pair(1)
                pump(1)
            if group == 1:
                stage_pair(2)
                pump(2)
            if group == 2:
                pump(None)
        pump(None)

        normed, inverse = norm_parts(dec_input[...])
        attn_in = (normed * vecs[0:1] + vecs[1:2]).astype(bf16)
        chosen = chosen_rows(core, r.row_ids[...])
        seen = jnp.sum(chosen, axis=1, keepdims=True)
        ready(load.qkv)
        for group in range(groups):
            for copy in kv_copies(group):
                copy.wait()
        grad_mixed[SMALL_PAD:, narrow:] = (grad_kv[...] + r.dec_kv_in[...].astype(f32)).astype(bf16)
        grad_values, gain, shift = norm_backward(
            inner_cols(grad_mixed[...], w_qkv[...]), normed, inverse, vecs[0:1]
        )
        r.vec_own[8:9, :narrow] = gain
        r.vec_own[9:10, :narrow] = shift
        back = grad_middle[...] + grad_values
        spread = inner_rows(chosen.astype(bf16), back.astype(bf16)).astype(bf16)
        r.spread_own[...] = spread[:rows]
        r.spread_leaving[...] = spread[rows:]
        spread_copy.start()
        pump(0)
        r.vec_own[12:13, :narrow] = jnp.sum(
            jnp.where(seen > 0.0, 0.0, back), axis=0, keepdims=True
        )
        put_dec(inner_rows(attn_in, grad_mixed[...]), 0, up_count, MID_PIECES * SUB_ROWS)
        pair_copy(MID_PIECES).start()
        pump(None)
        p.send_home(wait_copy, decoded_parts, r.rows_sem)

    def early_loads():
        return [
            pltpu.make_async_copy(source, dest, r.load_sem.at[10 + index])
            for index, (source, dest) in enumerate(
                (
                    (r.w_embed, r.v_embed), (r.out, r.v_out),
                )
            )
        ]

    spread_copy = remote(r.spread_leaving, r.spread_in, r.swap_sem.at[2], partner)
    dec_rows, big = DEC_PAD, BIG_PAD
    pl.run_scoped(
        decoder,
        pltpu.VMEM((dec_rows, narrow), f32),
        pltpu.VMEM((dec_rows, narrow), bf16),
        pltpu.VMEM((dec_rows, narrow), f32),
        pltpu.VMEM((dec_rows, narrow), bf16),
        pltpu.VMEM(r.dec_proj.shape, bf16),
        pltpu.VMEM(r.dec_up.shape, bf16),
        pltpu.VMEM(r.dec_down.shape, bf16),
        pltpu.VMEM(r.dec_qkv.shape, bf16),
        pltpu.VMEM((dec_rows, 3 * narrow), bf16),
        pltpu.VMEM((big, 2 * narrow), bf16),
        pltpu.VMEM((2, big, BIG_LANES), bf16),
        pltpu.VMEM((2, SMALL_PAD, SMALL_LANES), bf16),
        pltpu.VMEM((2, dec_rows // 2, narrow), bf16),
        pltpu.VMEM((dec_rows, narrow), f32),
        pltpu.VMEM((dec_rows, narrow), bf16),
        pltpu.VMEM((dec_rows, 3 * narrow), bf16),
        pltpu.VMEM((big, 2 * narrow), f32),
        pltpu.VMEM((big, 2 * narrow), bf16),
    )

    def encoder(
        v_down, v_slope, v_up, v_proj, v_middle, v_att, v_probs, v_query,
        v_own_kv, v_other_kv, v_x, v_lefts, v_lefts_other, right_own, kv_own, kv_leaving, grad_rows,
    ):
        load = loader(
        r.load_sem.at[12:],
        down=(r.w_down, v_down),
        slope=(r.slope, v_slope),
        lefts=(r.lefts_own, v_lefts),
        lefts_other=(r.lefts_other, v_lefts_other),
        up=(r.w_up, v_up),
        middle=(r.middle, v_middle),
        proj=(r.w_proj, v_proj),
        att=(r.att, v_att),
        probs=(r.probs, v_probs),
        query=(r.query, v_query),
        own_kv=(r.own_kv, v_own_kv),
        other_kv=(r.other_kv, v_other_kv),
        x=(r.x, v_x),
    )
        early = early_loads()
        vecs = r.enc_vecs
        starts = [0]
        for columns in (width, wide, narrow, width, 3 * width):
            starts.append(starts[-1] + columns)
        out_at, hidden_at, embedded_at, middle_at, all_mixed_at = (
            slice(*pair) for pair in zip(starts, starts[1:])
        )

        def give(cols, value, index):
            if value is not None:
                right_own[:, cols] = value
            copy = remote(
                right_own.at[:, cols], r.right_other.at[:, cols], r.swap_sem.at[index], partner
            )
            copy.start()
            return copy

        def weight_grad(cols, left, count, row, first_block=0, blocks=None):
            last_block = (
                (cols.stop - cols.start) // LANES if blocks is None else first_block + blocks
            )
            own = v_lefts[:, left : left + count, :rows].reshape(chips * count, rows)
            other = v_lefts_other[:, left : left + count, :rows].reshape(chips * count, rows)
            for block in range(first_block, last_block):
                columns = slice(cols.start + block * LANES, cols.start + (block + 1) * LANES)
                grad = product(own, right_own[:, columns]) + product(
                    other, r.right_other[:, columns]
                )
                grad = grad.astype(bf16)
                for piece, half, up, across, begin, end, at in sub_rows(
                    row + block * count, count
                ):
                    for image in range(chips):
                        held[piece, image, half, up, across, begin:end] = grad[
                            image * count + at : image * count + at + end - begin
                        ]

        left_hidden, left_mid = wide // (2 * chips), width // (2 * chips)
        left_mlp = left_hidden
        left_att, left_final, left_attn = (left_hidden + place * left_mid for place in (1, 2, 3))

        spread_copy.wait()
        grad_embedded = r.spread_own[...] + r.spread_in[...]
        embedded_copy = give(embedded_at, grad_embedded, 3)
        stage_pair(MID_PIECES)
        far_start(MID_PIECES)
        ready(*early)
        normed, inverse = norm_parts(r.v_out[...])
        grad_out, gain, shift = norm_backward(
            inner_cols(grad_embedded, r.v_embed[...]), normed, inverse, vecs[4:5]
        )
        r.vec_own[4:5] = gain
        r.vec_own[5:6] = shift
        grad_low = grad_out.astype(bf16)
        out_copy = give(out_at, grad_low, 4)
        ready(load.down, load.slope)
        grad_hidden = (v_slope[...].astype(f32) * inner_cols(grad_low, v_down[...])).astype(bf16)
        qkv_copies = [
            pltpu.make_async_copy(
                r.w_qkv.at[:, part * width : (part + 1) * width],
                v_down.at[part * width : (part + 1) * width],
                r.load_sem.at[25 + part],
            )
            for part in range(3)
        ]
        for copy in qkv_copies:
            copy.start()
        hidden_copy = give(hidden_at, grad_hidden, 5)
        ready(load.lefts, load.lefts_other)
        out_copy.wait()
        weight_grad(out_at, 0, left_hidden, DOWN_AT * SUB_ROWS, 0, 1)
        pump(DOWN_AT)
        weight_grad(out_at, 0, left_hidden, DOWN_AT * SUB_ROWS, 1, 2)
        ready(load.up, load.middle, load.proj)
        normed, inverse = norm_parts(v_middle[...])
        grad_values, gain, shift = norm_backward(
            inner_cols(grad_hidden, v_up[...]), normed, inverse, vecs[2:3]
        )
        r.vec_own[2:3] = gain
        r.vec_own[3:4] = shift
        grad_middle = grad_out + grad_values
        grad_low = grad_middle.astype(bf16)
        middle_copy = give(middle_at, grad_low, 6)
        grads = inner_cols(grad_low, v_proj[...]).astype(bf16)
        pump(DOWN_AT + 2)

        ready(load.att, load.probs, load.query, load.own_kv, load.other_kv)
        head_size = width // HE
        scale = 1.0 / math.sqrt(head_size)
        overlap = grads.astype(f32) * v_att[...].astype(f32)
        masks = lane_masks(head_size, bf16)
        wide_masks = lane_masks(head_size, f32)
        mixed_at = all_mixed_at.start
        for pair in range(width // 128):
            cols = slice(128 * pair, 128 * pair + 128)
            value_cols = slice(width + 128 * pair, width + 128 * pair + 128)
            keys = jnp.concatenate([v_own_kv[:, cols], v_other_kv[:, cols]], axis=0)
            values = jnp.concatenate([v_own_kv[:, value_cols], v_other_kv[:, value_cols]], axis=0)
            total_q = jnp.zeros((rows, 128), f32)
            total_k = jnp.zeros((2 * rows, 128), f32)
            total_v = jnp.zeros((2 * rows, 128), f32)
            for head, mask in enumerate(masks):
                delta = jnp.sum(overlap[:, cols] * wide_masks[head], axis=1, keepdims=True)
                one_grad = grads[:, cols] * mask
                chances = v_probs[len(masks) * pair + head, :, : 2 * rows]
                one_back = head_back(chances, one_grad, values, delta)
                total_q += product(one_back, keys * mask)
                total_k += inner_rows(one_back, v_query[:, cols] * mask)
                total_v += inner_rows(chances, one_grad)
            right_own[:, mixed_at + 128 * pair : mixed_at + 128 * pair + 128] = (
                total_q * scale
            ).astype(bf16)
            kv_own[:, cols] = total_k[:rows] * scale
            kv_own[:, value_cols] = total_v[:rows]
            kv_leaving[:, cols] = (total_k[rows:] * scale).astype(bf16)
            kv_leaving[:, value_cols] = total_v[rows:].astype(bf16)
        kv_copy = remote(kv_leaving, r.kv_in, r.swap_sem.at[7], partner)
        kv_copy.start()
        pump(MID_PIECES)
        hidden_copy.wait()
        weight_grad(hidden_at, left_mlp, left_mid, UP_AT * SUB_ROWS)
        late = DOWN_AT + 1
        pump(UP_AT)
        far_start(late, 0, 2)

        kv_copy.wait()
        right_own[:, mixed_at + width : mixed_at + 3 * width] = (
            kv_own[...] + r.kv_in[...].astype(f32)
        ).astype(bf16)
        mixed_copy = give(all_mixed_at, None, 8)
        ready(load.x)
        normed, inverse = norm_parts(v_x[...].reshape(rows, width).astype(f32))
        grad_norm = jnp.zeros((rows, width), f32)
        for part, copy in enumerate(qkv_copies):
            copy.wait()
            place = mixed_at + part * width
            grad_norm += inner_cols(
                right_own[:, place : place + width], v_down[part * width : (part + 1) * width]
            )
        grad_values, gain, shift = norm_backward(grad_norm, normed, inverse, vecs[0:1])
        r.vec_own[0:1] = gain
        r.vec_own[1:2] = shift
        vec_copy = remote(r.vec_own, r.vec_in, r.swap_sem.at[9], partner)
        vec_copy.start()
        grad_values = grad_middle + grad_values
        grad_rows[0] = grad_values[: rows // 2]
        grad_rows[1] = grad_values[rows // 2 :]

        def grad_parts(segment):
            return [(grad_rows.at[segment], r.home_grad.at[low])]

        p.send_home(start_copy, grad_parts, r.grad_sem)
        pump(UP_AT + 1)
        far_start(late, 2, 4)
        middle_copy.wait()
        embedded_copy.wait()
        embed_row = ATT_AT * SUB_ROWS + left_mid * width // LANES
        weight_grad(middle_at, left_att, left_mid, ATT_AT * SUB_ROWS)
        weight_grad(embedded_at, left_final, left_mid, embed_row)
        pump(UP_AT + 2)
        far_start(late, 4, 6)
        mixed_copy.wait()
        qkv_row = embed_row + left_mid * narrow // LANES
        weight_grad(all_mixed_at, left_attn, left_mid, qkv_row)
        pump(ATT_AT)
        far_start(late, 6, 8)
        vec_copy.wait()
        vectors = (r.vec_own[...] + r.vec_in[...]).astype(bf16)
        vec_row = qkv_row + left_mid * 3 * width // LANES
        piece, half, up, across, begin, end, _ = next(iter(sub_rows(vec_row, 16)))
        entry = lax.broadcasted_iota(jnp.int32, (width, LANES), 0)
        lane = lax.broadcasted_iota(jnp.int32, (width, LANES), 1)
        row_index = lax.broadcasted_iota(jnp.int32, (16, LANES), 0)
        narrow_left = narrow // (2 * chips)
        for image in range(chips):
            number = 2 * image + core
            enc_pick = (entry == lane + number * left_mid) & (lane < left_mid)
            dec_pick = (entry == lane + number * narrow_left) & (lane < narrow_left)
            enc_part = product(vectors, enc_pick.astype(f32).astype(bf16))
            dec_part = product(vectors, dec_pick.astype(f32).astype(bf16))
            held[piece, image, half, up, across, begin:end] = jnp.where(
                row_index < 8, enc_part, dec_part
            ).astype(bf16)
        pump(ATT_AT + 1)
        far_start(late, 8, 9)
        for piece in (ATT_AT + 2, late, PIECES - 1):
            pump(piece)
        p.send_home(wait_copy, grad_parts, r.grad_sem)

    pl.run_scoped(
        encoder,
        pltpu.VMEM(r.w_down.shape, bf16),
        pltpu.VMEM(r.slope.shape, bf16),
        pltpu.VMEM(r.w_up.shape, bf16),
        pltpu.VMEM(r.w_proj.shape, bf16),
        pltpu.VMEM(r.middle.shape, f32),
        pltpu.VMEM(r.att.shape, bf16),
        pltpu.VMEM(r.probs.shape, bf16),
        pltpu.VMEM(r.query.shape, bf16),
        pltpu.VMEM(r.own_kv.shape, bf16),
        pltpu.VMEM(r.other_kv.shape, bf16),
        pltpu.VMEM(r.x.shape, bf16),
        pltpu.VMEM(r.lefts_own.shape, bf16),
        pltpu.VMEM(r.lefts_own.shape, bf16),
        pltpu.VMEM(r.right_other.shape, bf16),
        pltpu.VMEM((rows, 2 * width), f32),
        pltpu.VMEM((rows, 2 * width), bf16),
        pltpu.VMEM((2, ENC_SEG, width), f32),
    )
    for _ in range(len(stages) - 1):
        pump(None)
    lax.fori_loop(0, PIECES, lambda i, c: (share_copy(i).wait(), c)[1], 0)


def back(chips, args):
    anywhere = pl.BlockSpec(memory_space=pl.ANY)
    vmem = pl.BlockSpec(memory_space=pltpu.VMEM)
    block = (EIGHTH, LANES)
    dma = pltpu.SemaphoreType.DMA
    width, narrow = by_name(args).w_embed.shape
    wide = by_name(args).w_up.shape[1]
    rights = width + wide + narrow + width + 3 * width
    outs = dict(
        shares=((PIECES, 2, 2, 2) + block, bf16),
        home_rows=((2, DEC_PAD // 2, narrow), bf16),
        home_grad=((2, ENC_SEG, width), f32),
    )
    scratch = dict(
        held=pltpu.VMEM((PIECES, chips, 2, 2, 2) + block, bf16),
        v_embed=pltpu.VMEM(by_name(args).w_embed.shape, bf16),
        v_out=pltpu.VMEM(by_name(args).out.shape, f32),
        leaving=pltpu.VMEM((DEC_PIECES, chips, 2, 2, 2) + block, bf16),
        from_pair=pltpu.VMEM((DEC_PIECES, chips, 2, 2, 2) + block, bf16),
        first=pltpu.VMEM((PIECES, 2, chips, 2) + block, bf16),
        second=pltpu.VMEM((PIECES, 2, chips) + block, bf16),
        from_chips=pltpu.VMEM((PIECES, chips - 1, 2) + block, bf16),
        gathered=pltpu.VMEM((PIECES, 2, 2, 2) + block, bf16),
        dec_kv_in=pltpu.VMEM((BIG_PAD, 2 * narrow), bf16),
        spread_own=pltpu.VMEM((ENC_PAD, narrow), bf16),
        spread_leaving=pltpu.VMEM((ENC_PAD, narrow), bf16),
        spread_in=pltpu.VMEM((ENC_PAD, narrow), bf16),
        right_other=pltpu.VMEM((ENC_PAD, rights), bf16),
        kv_in=pltpu.VMEM((ENC_PAD, 2 * width), bf16),
        vec_own=pltpu.VMEM((16, width), f32),
        vec_in=pltpu.VMEM((16, width), f32),
        load_sem=dma((28,)),
        chance_sem=dma((2, 2)),
        pair_sem=dma((DEC_PIECES, 2)),
        first_sem=dma((PIECES, 2, 2)),
        second_sem=dma((PIECES, 2, 2)),
        chip_sem=dma((PIECES, chips - 1, 2)),
        gather_sem=dma((PIECES, 4, 2)),
        share_sem=dma((PIECES,)),
        far_sem=dma((len(FAR), chips - 1, 3, 2)),
        swap_sem=dma((10, 2)),
        kv_sem=dma((4, 2, 2)),
        rows_sem=dma((2, 1, 2)),
        grad_sem=dma((2, 1, 2)),
    )
    names = list(args) + list(outs) + list(scratch)
    in_vmem = ("row_ids", "dec_vecs", "enc_vecs")
    return pl.pallas_call(
        functools.partial(back_kernel, chips, names),
        out_shape=[jax.ShapeDtypeStruct(shape, kind) for shape, kind in outs.values()],
        in_specs=[vmem if name in in_vmem else anywhere for name in args],
        out_specs=[anywhere] * len(outs),
        scratch_shapes=list(scratch.values()),
        compiler_params=pltpu.CompilerParams(
            collective_id=1, has_side_effects=True, vmem_limit_bytes=63 << 20
        ),
    )(*args.values())


def unstack_kernel(counts, enc_count, dec_count, flat, *outs):
    def runs(row, count):
        for piece, half, up, across, begin, end, at in sub_rows(row, count):
            start = piece * SUB_ROWS + (4 * half + 2 * up + across) * EIGHTH + begin
            yield flat[start : start + end - begin].astype(f32), at

    row = 0
    for out, count in zip(outs, counts):
        for block in range(out.shape[1] // LANES):
            for values, at in runs(row, count):
                out[at : at + values.shape[0], block * LANES : (block + 1) * LANES] = values
            row += count
    ((rows, _),) = runs(row, 16)
    outs[-2][...] = rows[:6, :enc_count]
    outs[-1][...] = rows[8:13, :dec_count]


def reduce_rest(chunk, seq):
    chips, rows, width = chunk.shape
    high, low = seq // 2, seq % 2
    eighth = rows // 8
    parts = chunk.reshape(chips, 2, 2, 2, eighth, width)

    def along_x(array):
        return permute(array, lambda s, i: (s ^ 1, i))

    def along_y(array):
        return permute(array, lambda s, i: (s ^ 2, i))

    def add(one, two):
        return (one.astype(f32) + two.astype(f32)).astype(bf16)

    one, two = parts[:, 0], parts[:, 1]
    one = add(pick(one, low, 2), along_x(pick(one, 1 - low, 2)))
    two = add(pick(two, high, 1), along_y(pick(two, 1 - high, 1)))
    one = add(pick(one, high, 1), along_y(pick(one, 1 - high, 1)))
    two = add(pick(two, low, 1), along_x(pick(two, 1 - low, 1)))
    mine = jnp.stack([one, two], axis=1)
    chip = lax.axis_index("img") // 2
    total = pick(mine, chip, 0).astype(f32)
    for step in range(1, chips):
        leaving = pick(mine, (chip + step) % chips, 0)
        arrived = permute(
            leaving,
            lambda s, i, step=step: (s, ((i // 2 + step) % chips) * 2 + (i & 1)),
        )
        total = total + arrived.astype(f32)
    own = total.astype(bf16)
    others = [permute(own, lambda s, i, step=step: (s ^ step, i)) for step in (1, 2, 3)]
    by_xor = jnp.stack([own] + others)
    ordered = jnp.stack([pick(by_xor, seq ^ place, 0) for place in range(4)], axis=1)
    return ordered.reshape(rows, width)


def shards(
    enc_input,
    cotangent,
    enc_image,
    visible_rows,
    enc_norms,
    enc_qkv,
    enc_proj,
    enc_up,
    enc_down,
    embed,
    dec_vecs,
    dec_qkv,
    dec_proj,
    dec_up,
    dec_down,
):
    seq = lax.axis_index("seq")
    img = lax.axis_index("img")
    images = lax.axis_size("img")
    core = img % 2
    odd = seq % 2 == 1
    enc_width = enc_input.shape[3]
    dec_width = dec_vecs.shape[0]
    enc_half = 2 * enc_input.shape[2]
    dec_quarter = cotangent.shape[2]

    enc_vecs = jnp.pad(enc_norms.T, ((0, 2), (0, 0)))
    dec_rows_vecs = jnp.pad(dec_vecs.T, ((0, 3), (0, 0)))
    table = position_table(dec_width)
    codes = np.zeros((2, DEC_PAD, dec_width), np.float32)
    for which in range(2):
        codes[which, :SMALL] = table[:SMALL]
        codes[which, SMALL_PAD : SMALL_PAD + HALF] = table[which * HALF : (which + 1) * HALF]
    chips = images // 2
    tables = jnp.stack([enc_image[0], visible_rows[0]])
    if images == 8:
        segments = tables.reshape(2, 2, 2, 2, enc_half // 2)
        segments = jnp.pad(
            segments, ((0, 0),) * 4 + ((0, ENC_SEG - enc_half // 2),), constant_values=-2
        )
        segments = segments.reshape(2, 2, 2, ENC_PAD)
        straight = segments.reshape(2, 2, 1, 2 * ENC_PAD)
        crossed = segments[:, :, ::-1].reshape(2, 2, 1, 2 * ENC_PAD)
        ordered = jnp.stack(
            [jnp.where(core == 0, straight, crossed), jnp.where(core == 0, crossed, straight)]
        )
        weights = dict(
            w_embed=embed, w_down=enc_down, w_up=enc_up, w_proj=enc_proj,
            w_qkv=enc_qkv, dec_qkv=dec_qkv, enc_vecs=enc_norms.T, dec_vecs=dec_vecs.T,
        )
        kept = front(
            dict(
                enc_input=enc_input[0], cotangent=cotangent[0], tables=ordered,
                codes=jnp.asarray(codes), **weights,
            ),
            chips,
        )
        shares, home_rows, home_grad = back(
            chips,
            dict(
                **kept, **weights, dec_proj=dec_proj, dec_up=dec_up, dec_down=dec_down
            ),
        )
        shapes = (
            dec_down.shape, dec_up.shape, dec_proj.shape, dec_qkv.shape, enc_down.shape,
            enc_up.shape, enc_proj.shape, embed.shape, enc_qkv.shape,
        )
        counts = [shape[0] // images for shape in shapes]
        (
            dec_down_share, dec_up_share, dec_proj_share, dec_qkv_share, enc_down_share,
            enc_up_share, enc_proj_share, embed_share, enc_qkv_share, enc_norm_share,
            dec_vec_share,
        ) = call(
            functools.partial(
                unstack_kernel, counts, enc_width // images, dec_width // images
            ),
            0,
            [((count, shape[1]), f32) for count, shape in zip(counts, shapes)]
            + [((6, enc_width // images), f32), ((5, dec_width // images), f32)],
            (shares.reshape(-1, LANES),),
            40,
        )
        enc_norm_share, dec_vec_share = enc_norm_share.T, dec_vec_share.T
        grad_input = home_grad[None, :, : enc_half // 2]
        decoded = home_rows[None, :, :dec_quarter]
        return (
            decoded,
            grad_input,
            enc_norm_share,
            enc_qkv_share,
            enc_proj_share,
            enc_up_share,
            enc_down_share,
            embed_share,
            dec_vec_share,
            dec_qkv_share,
            dec_proj_share,
            dec_up_share,
            dec_down_share,
        )

    other_tables = swap(tables)
    tables = jnp.where(seq // 2 == core, tables, other_tables)
    tables = jnp.where(odd, tables[:, 1], tables[:, 0])
    segments = tables.reshape(2, 2, 2, enc_half // 2)
    segments = jnp.pad(
        segments, ((0, 0),) * 3 + ((0, ENC_SEG - enc_half // 2),), constant_values=-2
    )
    halves = segments.reshape(2, 2, ENC_PAD)
    own = pick(halves, core, 1)
    ids = jnp.concatenate([own, pick(halves, 1 - core, 1)], axis=1)
    row_ids = ids[1:2]
    core_arg = core.reshape(1)

    blocks = jnp.pad(enc_input[0], ((0, 0), (0, ENC_SEG - enc_half // 2), (0, 0)))
    x = jnp.concatenate(exchange_packs(blocks, odd), axis=0)
    cot = jnp.concatenate(exchange_packs(cotangent[0], odd), axis=0)
    cot = jnp.concatenate(
        [
            pad_rows(lax.dynamic_slice_in_dim(cot, core * HALF, SMALL, 0), SMALL_PAD),
            pad_rows(lax.dynamic_slice_in_dim(cot, (1 - core) * SMALL, HALF, 0), BIG_PAD),
        ],
        axis=0,
    )
    enc_hidden_width = enc_up.shape[1]

    enc_query, enc_kv = call(
        enc_pre_kernel,
        0,
        [((ENC_PAD, enc_width), bf16), ((ENC_PAD, 2 * enc_width), bf16)],
        (x, enc_vecs, enc_qkv),
        40,
    )
    enc_other = swap(enc_kv)
    embedded, enc_att, enc_probs, enc_middle, enc_active, enc_slope, enc_out = call(
        enc_main_kernel,
        0,
        [
            ((ENC_PAD, dec_width), bf16),
            ((ENC_PAD, enc_width), bf16),
            ((HE, ENC_PAD, 2 * ENC_PAD), bf16),
            ((ENC_PAD, enc_width), f32),
            ((ENC_PAD, enc_hidden_width), bf16),
            ((ENC_PAD, enc_hidden_width), bf16),
            ((ENC_PAD, enc_width), f32),
        ],
        (
            x, enc_query, enc_kv, enc_other, own[0][:, None], ids[0:1], enc_vecs,
            enc_proj, enc_up, enc_down, embed,
        ),
        48,
    )

    code = pick(jnp.asarray(codes), core, 0)
    dec_input, dec_mixed, big_kv = call(
        dec_pre_kernel,
        1,
        [
            ((DEC_PAD, dec_width), f32),
            ((DEC_PAD, 3 * dec_width), bf16),
            ((BIG_PAD, 2 * dec_width), bf16),
        ],
        (core_arg, embedded, swap(embedded), row_ids, code, dec_rows_vecs, dec_qkv),
        40,
    )
    other_kv = swap(big_kv)
    groups = dec_width // 128

    def columns(rows, offset=0):
        return pl.BlockSpec((rows, 128), lambda group: (0, offset + group))

    def heads(rows, cols):
        return pl.BlockSpec((HD // groups, rows, cols), lambda group: (group, 0, 0))

    qkv_specs = [
        columns(DEC_PAD),
        columns(DEC_PAD, groups),
        columns(DEC_PAD, 2 * groups),
        columns(BIG_PAD),
        columns(BIG_PAD, groups),
    ]
    qkv_args = (dec_mixed, dec_mixed, dec_mixed, other_kv, other_kv)
    prob_specs = [heads(BIG_PAD, 2 * BIG_PAD), heads(SMALL_PAD, SMALL_PAD)]
    dec_att, big_probs, small_probs = pl.pallas_call(
        dec_att_kernel,
        grid=(groups,),
        in_specs=qkv_specs,
        out_specs=[columns(DEC_PAD)] + prob_specs,
        out_shape=[
            jax.ShapeDtypeStruct((DEC_PAD, dec_width), bf16),
            jax.ShapeDtypeStruct((HD, BIG_PAD, 2 * BIG_PAD), bf16),
            jax.ShapeDtypeStruct((HD, SMALL_PAD, SMALL_PAD), bf16),
        ],
        compiler_params=pltpu.CompilerParams(vmem_limit_bytes=48 << 20),
    )(*qkv_args)
    chunk_mid = Chunk(images, [dec_down.shape, dec_up.shape, dec_proj.shape])
    decoded, grad_dec_middle, dec_grad_att, vectors_two, *mid_grads = call(
        functools.partial(dec_mid_kernel, chunk_mid),
        1,
        [
            ((DEC_PAD, dec_width), bf16),
            ((DEC_PAD, dec_width), f32),
            ((DEC_PAD, dec_width), bf16),
            ((2, dec_width), f32),
        ]
        + chunk_mid.outs(),
        (core_arg, dec_input, dec_att, cot, dec_rows_vecs, dec_proj, dec_up, dec_down),
        48,
    )
    grad_specs = [columns(DEC_PAD)] * 3 + [columns(BIG_PAD)] * 2
    grad_query, grad_key, grad_value, leaving_key, leaving_value = pl.pallas_call(
        dec_att_back_kernel,
        grid=(groups,),
        in_specs=qkv_specs + [columns(DEC_PAD)] * 2 + prob_specs,
        out_specs=grad_specs,
        out_shape=[
            jax.ShapeDtypeStruct((DEC_PAD, dec_width), bf16),
            jax.ShapeDtypeStruct((DEC_PAD, dec_width), f32),
            jax.ShapeDtypeStruct((DEC_PAD, dec_width), f32),
            jax.ShapeDtypeStruct((BIG_PAD, dec_width), bf16),
            jax.ShapeDtypeStruct((BIG_PAD, dec_width), bf16),
        ],
        compiler_params=pltpu.CompilerParams(vmem_limit_bytes=48 << 20),
    )(*qkv_args, dec_grad_att, dec_att, big_probs, small_probs)
    chunk_post = Chunk(images, [dec_qkv.shape])
    own_spread, other_spread, vectors_one, *post_grads = call(
        functools.partial(dec_post_kernel, chunk_post),
        1,
        [
            ((ENC_PAD, dec_width), bf16),
            ((ENC_PAD, dec_width), bf16),
            ((3, dec_width), f32),
        ]
        + chunk_post.outs(),
        (
            core_arg, dec_input, grad_dec_middle, grad_query, grad_key, grad_value,
            swap(leaving_key), swap(leaving_value), row_ids, dec_rows_vecs, dec_qkv,
        ),
        48,
    )
    arrived_spread = swap(other_spread)
    chunk_down = Chunk(images, [enc_down.shape])
    chunk_up = Chunk(images, [enc_up.shape])
    grad_enc_middle, enc_grad_att, enc_vectors_two, *mlp_grads = call(
        functools.partial(enc_mlp_back_kernel, chunk_down, chunk_up),
        1,
        [
            ((ENC_PAD, enc_width), f32),
            ((ENC_PAD, enc_width), bf16),
            ((4, enc_width), f32),
        ]
        + chunk_down.outs()
        + chunk_up.outs(),
        (
            core_arg, own_spread, arrived_spread, enc_out, enc_middle, enc_active, enc_slope,
            enc_vecs, embed, enc_down, enc_up, enc_proj,
        ),
        56,
    )
    down_grads, up_grads = mlp_grads[: len(chunk_down.outs())], mlp_grads[len(chunk_down.outs()) :]
    enc_grad_query, enc_grad_kv, enc_leaving = call(
        enc_att_back_kernel,
        0,
        [
            ((ENC_PAD, enc_width), bf16),
            ((ENC_PAD, 2 * enc_width), f32),
            ((ENC_PAD, 2 * enc_width), bf16),
        ],
        (enc_grad_att, enc_att, enc_probs, enc_query, enc_kv, enc_other),
        48,
    )
    chunk_att = Chunk(images, [enc_qkv.shape, enc_proj.shape, embed.shape], 16)
    grad_input, enc_vectors_one, *att_grads = call(
        functools.partial(enc_post_kernel, chunk_att),
        1,
        [((ENC_PAD, enc_width), f32), ((2, enc_width), f32)] + chunk_att.outs(),
        (
            core_arg, x, enc_att, grad_enc_middle, enc_grad_query, enc_grad_kv,
            swap(enc_leaving), enc_out, own_spread, arrived_spread, enc_vecs, enc_qkv,
        ),
        48,
    )

    def by_image(rows):
        flat = rows.reshape(rows.shape[0], images, rows.shape[1] // images)
        return flat.transpose(1, 0, 2).reshape(images, -1)

    vectors = jnp.concatenate(
        [
            by_image(jnp.concatenate([enc_vectors_one, enc_vectors_two])),
            by_image(jnp.concatenate([vectors_one[:2], vectors_two, vectors_one[2:]])),
        ],
        axis=1,
    ).astype(bf16)
    vectors = jnp.pad(vectors, ((0, 0), (0, 16 * LANES - vectors.shape[1])))
    vectors = vectors.reshape(images // 2, 2, 16, LANES)
    vectors = (pick(vectors, core, 1), pick(vectors, 1 - core, 1))
    chunk_pairs = [
        chunk.pair(grads, core)
        for chunk, grads in (
            (chunk_mid, mid_grads),
            (chunk_post, post_grads),
            (chunk_down, down_grads),
            (chunk_up, up_grads),
            (chunk_att, att_grads),
        )
    ]
    place = slice(chunk_att.used, chunk_att.used + 16)
    chunk_pairs[-1] = tuple(
        array.at[:, place].set(rows) for array, rows in zip(chunk_pairs[-1], vectors)
    )
    shares = [reduce_rest(reduce_pair(*pair), seq) for pair in chunk_pairs]
    mid_share, post_share, down_share, up_share, att_share = shares
    dec_down_share, dec_up_share, dec_proj_share = chunk_mid.split(mid_share)
    (dec_qkv_share,) = chunk_post.split(post_share)
    (enc_down_share,) = chunk_down.split(down_share)
    (enc_up_share,) = chunk_up.split(up_share)
    enc_qkv_share, enc_proj_share, embed_share = chunk_att.split(att_share)
    vectors = att_share[chunk_att.used : chunk_att.used + 16].reshape(-1).astype(f32)
    enc_count, dec_count = enc_width // images, dec_width // images
    enc_norm_share = vectors[: 6 * enc_count].reshape(6, enc_count).T
    dec_vec_share = vectors[6 * enc_count : 6 * enc_count + 5 * dec_count].reshape(5, dec_count).T

    start = jnp.concatenate([decoded[:SMALL], decoded[SMALL_PAD : SMALL_PAD + HALF]])
    end = jnp.concatenate([decoded[SMALL_PAD : SMALL_PAD + HALF], decoded[:SMALL]])
    natural = jnp.where(core == 0, start, end)
    decoded = jnp.stack(exchange_packs(natural.reshape(2, dec_quarter, dec_width), odd))[None]
    grad_input = jnp.stack(
        exchange_packs(grad_input.reshape(2, ENC_SEG, enc_width)[:, : enc_half // 2], odd)
    )[None]
    return (
        decoded,
        grad_input,
        enc_norm_share,
        enc_qkv_share,
        enc_proj_share,
        enc_up_share,
        enc_down_share,
        embed_share,
        dec_vec_share,
        dec_qkv_share,
        dec_proj_share,
        dec_up_share,
        dec_down_share,
    )


def solution(mesh):
    rows = P("img", None, "seq", None)
    tables = P("img", None, None)
    shares = P("img", None)
    return jax.shard_map(
        shards,
        mesh=mesh,
        in_specs=(rows, rows, tables, tables) + (P(),) * 11,
        out_specs=(rows, rows) + (shares,) * 11,
        check_vma=False,
    )
```

```python
import functools
import math

import jax
import jax.numpy as jnp
import numpy as np
from jax import lax
from jax.experimental import pallas as pl
from jax.experimental.pallas import tpu as pltpu
from jax.sharding import PartitionSpec as P

HE = 12
HD = 16
PATCHES = 784
SMALL = PATCHES // 4
HALF = PATCHES // 2
SMALL_PAD = 208
BIG_PAD = 400
DEC_PAD = SMALL_PAD + BIG_PAD
ENC_SEG = 80
ENC_PAD = 2 * ENC_SEG
BIG_LANES = 896
SMALL_LANES = 256
ENC_LANES = 384
LEFT_LANES = 256

eps_norm = 1e-06
masked_score = -1e30
bf16 = jnp.bfloat16
f32 = jnp.float32


def product(left_side, right_side):
    return jnp.dot(left_side, right_side, preferred_element_type=f32)


def inner_rows(left_side, right_side):
    return lax.dot_general(
        left_side, right_side, (((0,), (0,)), ((), ())), preferred_element_type=f32
    )


def inner_cols(left_side, right_side):
    return lax.dot_general(
        left_side, right_side, (((1,), (1,)), ((), ())), preferred_element_type=f32
    )


def norm_parts(values):
    centered = values - jnp.mean(values, axis=-1, keepdims=True)
    inverse = lax.rsqrt(jnp.mean(centered * centered, axis=-1, keepdims=True) + eps_norm)
    return centered * inverse, inverse


def norm_backward(grad_out, normed, inverse, norm_gain):
    scaled = grad_out * norm_gain
    grad_values = inverse * (
        scaled
        - jnp.mean(scaled, axis=-1, keepdims=True)
        - normed * jnp.mean(scaled * normed, axis=-1, keepdims=True)
    )
    return (
        grad_values,
        jnp.sum(grad_out * normed, axis=0, keepdims=True),
        jnp.sum(grad_out, axis=0, keepdims=True),
    )


def gelu_parts(hidden):
    below = 0.5 + 0.5 * lax.erf(hidden * math.sqrt(0.5))
    density = jnp.exp(hidden * hidden * -0.5) * (1.0 / math.sqrt(2.0 * math.pi))
    return hidden * below, below + hidden * density


LANES = 256
EIGHTH = 48
LAST_EIGHTH = 32
SUB_ROWS = 8 * EIGHTH


def put(core, dest, offset, grad):
    low = grad.astype(bf16)
    if len(dest) == 1:
        dest[0][...] = low
        return
    keep, leaving = dest
    chips = keep.shape[0]
    count = low.shape[0] // (2 * chips)
    for case in (0, 1):

        @pl.when(core == case)
        def _():
            for image in range(2 * chips):
                ref = keep if image % 2 == case else leaving
                for block in range(low.shape[1] // LANES):
                    start = offset + block * count
                    ref[image // 2, start : start + count, :] = low[
                        image * count : (image + 1) * count, block * LANES : (block + 1) * LANES
                    ]


def image_rows(shape, images):
    return shape[0] // images * (shape[1] // LANES)


class Chunk:
    def __init__(self, images, shapes, spare=0):
        self.images = images
        self.shapes = shapes
        self.offsets = []
        rows = 0
        for shape in shapes:
            self.offsets.append(rows)
            rows += image_rows(shape, images)
        self.used = rows
        rows += spare
        self.direct = all(shape[0] // images % 16 == 0 for shape in shapes)
        unit = SUB_ROWS if self.direct else 8
        self.rows = -(-rows // unit) * unit

    def outs(self):
        if self.direct:
            return [((self.images // 2, self.rows, LANES), bf16)] * 2
        return [(shape, bf16) for shape in self.shapes]

    def dests(self, refs):
        if self.direct:
            return [tuple(refs)] * len(self.shapes)
        return [(ref,) for ref in refs]

    def pair(self, results, core):
        if self.direct:
            return tuple(results)
        pieces = []
        for grad in results:
            for start in range(0, grad.shape[1], LANES):
                piece = grad[:, start : start + LANES]
                pieces.append(piece.reshape(self.images, -1, LANES))
        stacked = jnp.concatenate(pieces, axis=1)
        stacked = jnp.pad(stacked, ((0, 0), (0, self.rows - stacked.shape[1]), (0, 0)))
        both = stacked.reshape(self.images // 2, 2, self.rows, LANES)
        return pick(both, core, 1), pick(both, 1 - core, 1)

    def split(self, share):
        results = []
        for shape, offset in zip(self.shapes, self.offsets):
            count = shape[0] // self.images
            pieces = [
                share[offset + block * count : offset + (block + 1) * count]
                for block in range(shape[1] // LANES)
            ]
            results.append(jnp.concatenate(pieces, axis=1).astype(f32))
        return results


def call(kernel, scalars, outs, args, megabytes):
    vmem = pl.BlockSpec(memory_space=pltpu.VMEM)
    smem = pl.BlockSpec(memory_space=pltpu.SMEM)
    return pl.pallas_call(
        kernel,
        out_shape=[jax.ShapeDtypeStruct(shape, kind) for shape, kind in outs],
        in_specs=[smem] * scalars + [vmem] * (len(args) - scalars),
        out_specs=[vmem] * len(outs),
        compiler_params=pltpu.CompilerParams(vmem_limit_bytes=megabytes << 20),
    )(*args)


def lane_masks(head_size, kind):
    lanes = lax.broadcasted_iota(jnp.int32, (1, 128), 1) // head_size
    return [(lanes == head).astype(f32).astype(kind) for head in range(128 // head_size)]


def softmax_rows(scores, scale):
    row_max = jnp.max(scores, axis=1, keepdims=True)
    weights = jnp.exp2((scores - row_max) * (scale * math.log2(math.e)))
    return (weights * (1.0 / jnp.sum(weights, axis=1, keepdims=True))).astype(bf16)


def head_back(probs, grads, values, delta):
    grad_probs = inner_cols(grads, values)
    return (probs.astype(f32) * (grad_probs - delta)).astype(bf16)


def enc_pre_kernel(x, vecs, w_qkv, query, key_value):
    normed, _ = norm_parts(x[...].astype(f32))
    attn_in = (normed * vecs[0:1] + vecs[1:2]).astype(bf16)
    mixed = product(attn_in, w_qkv[...]).astype(bf16)
    width = query.shape[1]
    query[...] = mixed[:, :width]
    key_value[...] = mixed[:, width:]


def enc_main_kernel(
    x, query, own_kv, other_kv, own_ids, all_ids, vecs, w_proj, w_up, w_down, w_embed,
    embedded, att, probs, middle, active, slope, out
):
    width = query.shape[1]
    head_size = width // HE
    bias = jnp.where(own_ids[...] == all_ids[...], 0.0, masked_score)
    masks = lane_masks(head_size, bf16)
    for pair in range(width // 128):
        cols = slice(128 * pair, 128 * pair + 128)
        value_cols = slice(width + 128 * pair, width + 128 * pair + 128)
        keys = jnp.concatenate([own_kv[:, cols], other_kv[:, cols]], axis=0)
        values = jnp.concatenate([own_kv[:, value_cols], other_kv[:, value_cols]], axis=0)
        total = jnp.zeros((query.shape[0], 128), f32)
        for head, mask in enumerate(masks):
            scores = inner_cols(query[:, cols] * mask, keys) + bias
            chances = softmax_rows(scores, 1.0 / math.sqrt(head_size))
            probs[len(masks) * pair + head] = chances
            total += product(chances, values * mask)
        att[:, cols] = total.astype(bf16)
    mid = x[...].astype(f32) + product(att[...], w_proj[...])
    middle[...] = mid
    normed, _ = norm_parts(mid)
    mlp_in = (normed * vecs[2:3] + vecs[3:4]).astype(bf16)
    result, steepness = gelu_parts(product(mlp_in, w_up[...]))
    active[...] = result.astype(bf16)
    slope[...] = steepness.astype(bf16)
    last = mid + product(active[...], w_down[...])
    out[...] = last
    normed, _ = norm_parts(last)
    final = (normed * vecs[4:5] + vecs[5:6]).astype(bf16)
    embedded[...] = product(final, w_embed[...]).astype(bf16)


def chosen_rows(core, visible_rows):
    index = lax.broadcasted_iota(jnp.int32, (DEC_PAD, 1), 0)
    small = index + core * (SMALL + PATCHES)
    big = index + (SMALL - SMALL_PAD) + core * HALF
    row = jnp.where(index < SMALL, small, -1)
    row = jnp.where((index >= SMALL_PAD) & (index < SMALL_PAD + HALF), big, row)
    return (row == visible_rows).astype(f32)


def dec_pre_kernel(core, own, other, rows, code, vecs, w_qkv, dec_input, mixed, big_kv):
    chosen = chosen_rows(core[0], rows[...])
    seen = jnp.sum(chosen, axis=1, keepdims=True)
    tokens = jnp.concatenate([own[...], other[...]], axis=0)
    picked = product(chosen.astype(bf16), tokens)
    values = jnp.where(seen > 0.0, picked, vecs[4:5]) + code[...]
    dec_input[...] = values
    normed, _ = norm_parts(values)
    attn_in = (normed * vecs[0:1] + vecs[1:2]).astype(bf16)
    result = product(attn_in, w_qkv[...]).astype(bf16)
    mixed[...] = result
    big_kv[...] = result[SMALL_PAD:, values.shape[1] :]


def big_bias():
    column = lax.broadcasted_iota(jnp.int32, (1, 2 * BIG_PAD), 1)
    place = jnp.where(column >= BIG_PAD, column - BIG_PAD, column)
    return jnp.where(place < HALF, 0.0, masked_score)


def small_bias():
    column = lax.broadcasted_iota(jnp.int32, (1, SMALL_PAD), 1)
    return jnp.where(column < SMALL, 0.0, masked_score)


def dec_att_kernel(query, key, value, other_key, other_value, att, big_probs, small_probs):
    head_size = query.shape[1] * 4 // HD
    scale = 1.0 / math.sqrt(head_size)
    keys = jnp.concatenate([key[SMALL_PAD:], other_key[...]], axis=0)
    values = jnp.concatenate([value[SMALL_PAD:], other_value[...]], axis=0)
    total = jnp.zeros((BIG_PAD, 128), f32)
    small_total = jnp.zeros((SMALL_PAD, 128), f32)
    for head, mask in enumerate(lane_masks(head_size, bf16)):
        scores = inner_cols(query[SMALL_PAD:] * mask, keys) + big_bias()
        chances = softmax_rows(scores, scale)
        big_probs[head] = chances
        total += product(chances, values * mask)
        scores = inner_cols(query[:SMALL_PAD] * mask, key[:SMALL_PAD]) + small_bias()
        chances = softmax_rows(scores, scale)
        small_probs[head] = chances
        small_total += product(chances, value[:SMALL_PAD] * mask)
    att[:SMALL_PAD] = small_total.astype(bf16)
    att[SMALL_PAD:] = total.astype(bf16)


def dec_mid_kernel(
    chunk, core, dec_input, att, cot, vecs, w_proj, w_up, w_down,
    decoded, grad_middle, grad_att, vectors, *grads
):
    down_dest, up_dest, proj_dest = chunk.dests(grads)
    down_at, up_at, proj_at = chunk.offsets
    grad_down, grad_up = [], []
    middle = dec_input[...] + product(att[...], w_proj[...])
    normed, inverse = norm_parts(middle)
    mlp_in = (normed * vecs[2:3] + vecs[3:4]).astype(bf16)
    result = middle
    grad_norm = jnp.zeros_like(middle)
    step = 512
    for start in range(0, w_up.shape[1], step):
        cols = slice(start, start + step)
        active, slope = gelu_parts(product(mlp_in, w_up[:, cols]))
        active = active.astype(bf16)
        result += product(active, w_down[cols])
        grad_down.append(inner_rows(active, cot[...]).astype(bf16))
        grad_hidden = (slope * inner_cols(cot[...], w_down[cols])).astype(bf16)
        grad_up.append(inner_rows(mlp_in, grad_hidden).astype(bf16))
        grad_norm += inner_cols(grad_hidden, w_up[:, cols])
    decoded[...] = result.astype(bf16)
    grad_values, gain, shift = norm_backward(grad_norm, normed, inverse, vecs[2:3])
    vectors[0:1] = gain
    vectors[1:2] = shift
    back = cot[...].astype(f32) + grad_values
    grad_middle[...] = back
    low = back.astype(bf16)
    grad_att[...] = inner_cols(low, w_proj[...]).astype(bf16)
    put(core[0], proj_dest, proj_at, inner_rows(att[...], low))
    put(core[0], down_dest, down_at, jnp.concatenate(grad_down, axis=0))
    put(core[0], up_dest, up_at, jnp.concatenate(grad_up, axis=1))


def dec_att_back_kernel(
    query, key, value, other_key, other_value, grads, att, big_probs, small_probs,
    grad_query, grad_key, grad_value, leaving_key, leaving_value
):
    head_size = query.shape[1] * 4 // HD
    scale = 1.0 / math.sqrt(head_size)
    keys = jnp.concatenate([key[SMALL_PAD:], other_key[...]], axis=0)
    values = jnp.concatenate([value[SMALL_PAD:], other_value[...]], axis=0)
    overlap = grads[...].astype(f32) * att[...].astype(f32)
    big_q = jnp.zeros((BIG_PAD, 128), f32)
    big_k = jnp.zeros((2 * BIG_PAD, 128), f32)
    big_v = jnp.zeros((2 * BIG_PAD, 128), f32)
    small_q = jnp.zeros((SMALL_PAD, 128), f32)
    small_k = jnp.zeros((SMALL_PAD, 128), f32)
    small_v = jnp.zeros((SMALL_PAD, 128), f32)
    masks = lane_masks(head_size, f32)
    for head, mask in enumerate(lane_masks(head_size, bf16)):
        delta = jnp.sum(overlap * masks[head], axis=1, keepdims=True)
        one_query, one_grad = query[...] * mask, grads[...] * mask
        chances = big_probs[head]
        back = head_back(chances, one_grad[SMALL_PAD:], values, delta[SMALL_PAD:])
        big_q += product(back, keys * mask)
        big_k += inner_rows(back, one_query[SMALL_PAD:])
        big_v += inner_rows(chances, one_grad[SMALL_PAD:])
        chances = small_probs[head]
        back = head_back(chances, one_grad[:SMALL_PAD], value[:SMALL_PAD], delta[:SMALL_PAD])
        small_q += product(back, key[:SMALL_PAD] * mask)
        small_k += inner_rows(back, one_query[:SMALL_PAD])
        small_v += inner_rows(chances, one_grad[:SMALL_PAD])
    grad_query[:SMALL_PAD] = (small_q * scale).astype(bf16)
    grad_query[SMALL_PAD:] = (big_q * scale).astype(bf16)
    grad_key[:SMALL_PAD] = small_k * scale
    grad_key[SMALL_PAD:] = big_k[:BIG_PAD] * scale
    grad_value[:SMALL_PAD] = small_v
    grad_value[SMALL_PAD:] = big_v[:BIG_PAD]
    leaving_key[...] = (big_k[BIG_PAD:] * scale).astype(bf16)
    leaving_value[...] = big_v[BIG_PAD:].astype(bf16)


def dec_post_kernel(
    chunk, core, dec_input, grad_middle, grad_query, grad_key, grad_value, arrived_key,
    arrived_value, rows, vecs, w_qkv, own_spread, other_spread, vectors, *grads
):
    normed, inverse = norm_parts(dec_input[...])
    attn_in = (normed * vecs[0:1] + vecs[1:2]).astype(bf16)
    key = jnp.concatenate(
        [grad_key[:SMALL_PAD], grad_key[SMALL_PAD:] + arrived_key[...].astype(f32)], axis=0
    ).astype(bf16)
    value = jnp.concatenate(
        [grad_value[:SMALL_PAD], grad_value[SMALL_PAD:] + arrived_value[...].astype(f32)], axis=0
    ).astype(bf16)
    mixed = jnp.concatenate([grad_query[...], key, value], axis=1)
    grad_values, gain, shift = norm_backward(
        inner_cols(mixed, w_qkv[...]), normed, inverse, vecs[0:1]
    )
    back = grad_middle[...] + grad_values
    chosen = chosen_rows(core[0], rows[...])
    seen = jnp.sum(chosen, axis=1, keepdims=True)
    spread = inner_rows(chosen.astype(bf16), back.astype(bf16)).astype(bf16)
    own_spread[...] = spread[:ENC_PAD]
    other_spread[...] = spread[ENC_PAD:]
    vectors[0:1] = gain
    vectors[1:2] = shift
    vectors[2:3] = jnp.sum(jnp.where(seen > 0.0, 0.0, back), axis=0, keepdims=True)
    put(core[0], chunk.dests(grads)[0], chunk.offsets[0], inner_rows(attn_in, mixed))


def enc_mlp_back_kernel(
    first, second, core, own_spread, arrived, out, middle, active, slope,
    vecs, w_embed, w_down, w_up, w_proj, grad_middle, grad_att, vectors, *grads
):
    first_grads, second_grads = grads[: len(first.outs())], grads[len(first.outs()) :]
    grad_embedded = own_spread[...] + arrived[...]
    normed, inverse = norm_parts(out[...])
    grad_out, gain, shift = norm_backward(
        inner_cols(grad_embedded, w_embed[...]), normed, inverse, vecs[4:5]
    )
    vectors[2:3] = gain
    vectors[3:4] = shift
    low = grad_out.astype(bf16)
    put(core[0], first.dests(first_grads)[0], first.offsets[0], inner_rows(active[...], low))
    grad_hidden = (slope[...].astype(f32) * inner_cols(low, w_down[...])).astype(bf16)
    normed, inverse = norm_parts(middle[...])
    mlp_in = (normed * vecs[2:3] + vecs[3:4]).astype(bf16)
    put(
        core[0], second.dests(second_grads)[0], second.offsets[0], inner_rows(mlp_in, grad_hidden)
    )
    grad_values, gain, shift = norm_backward(
        inner_cols(grad_hidden, w_up[...]), normed, inverse, vecs[2:3]
    )
    vectors[0:1] = gain
    vectors[1:2] = shift
    back = grad_out + grad_values
    grad_middle[...] = back
    grad_att[...] = inner_cols(back.astype(bf16), w_proj[...]).astype(bf16)


def enc_att_back_kernel(
    grads, att, probs, query, own_kv, other_kv, grad_query, grad_kv, leaving
):
    width = query.shape[1]
    head_size = width // HE
    scale = 1.0 / math.sqrt(head_size)
    overlap = grads[...].astype(f32) * att[...].astype(f32)
    masks = lane_masks(head_size, bf16)
    wide_masks = lane_masks(head_size, f32)
    rows = query.shape[0]
    for pair in range(width // 128):
        cols = slice(128 * pair, 128 * pair + 128)
        value_cols = slice(width + 128 * pair, width + 128 * pair + 128)
        keys = jnp.concatenate([own_kv[:, cols], other_kv[:, cols]], axis=0)
        values = jnp.concatenate([own_kv[:, value_cols], other_kv[:, value_cols]], axis=0)
        total_q = jnp.zeros((rows, 128), f32)
        total_k = jnp.zeros((2 * rows, 128), f32)
        total_v = jnp.zeros((2 * rows, 128), f32)
        for head, mask in enumerate(masks):
            delta = jnp.sum(overlap[:, cols] * wide_masks[head], axis=1, keepdims=True)
            one_grad = grads[:, cols] * mask
            chances = probs[len(masks) * pair + head]
            one_back = head_back(chances, one_grad, values, delta)
            total_q += product(one_back, keys * mask)
            total_k += inner_rows(one_back, query[:, cols] * mask)
            total_v += inner_rows(chances, one_grad)
        grad_query[:, cols] = (total_q * scale).astype(bf16)
        grad_kv[:, cols] = total_k[:rows] * scale
        grad_kv[:, value_cols] = total_v[:rows]
        leaving[:, cols] = (total_k[rows:] * scale).astype(bf16)
        leaving[:, value_cols] = total_v[rows:].astype(bf16)


def enc_post_kernel(
    chunk, core, x, att, grad_middle, grad_query, grad_kv, arrived, out, own_spread, other_spread,
    vecs, w_qkv, grad_input, vectors, *grads
):
    qkv_dest, proj_dest, embed_dest = chunk.dests(grads)
    normed, _ = norm_parts(out[...])
    final = (normed * vecs[4:5] + vecs[5:6]).astype(bf16)
    put(
        core[0], embed_dest, chunk.offsets[2], inner_rows(final, own_spread[...] + other_spread[...])
    )
    put(
        core[0], proj_dest, chunk.offsets[1],
        inner_rows(att[...], grad_middle[...].astype(bf16)),
    )
    normed, inverse = norm_parts(x[...].astype(f32))
    attn_in = (normed * vecs[0:1] + vecs[1:2]).astype(bf16)
    key_value = (grad_kv[...] + arrived[...].astype(f32)).astype(bf16)
    mixed = jnp.concatenate([grad_query[...], key_value], axis=1)
    grad_values, gain, shift = norm_backward(
        inner_cols(mixed, w_qkv[...]), normed, inverse, vecs[0:1]
    )
    grad_input[...] = grad_middle[...] + grad_values
    vectors[0:1] = gain
    vectors[1:2] = shift
    put(core[0], qkv_dest, chunk.offsets[0], inner_rows(attn_in, mixed))


def permute(array, where_to):
    seq_count = lax.axis_size("seq")
    img_count = lax.axis_size("img")
    pairs = []
    for seq in range(seq_count):
        for img in range(img_count):
            seq_to, img_to = where_to(seq, img)
            pairs.append((seq * img_count + img, seq_to * img_count + img_to))
    return lax.ppermute(array, ("seq", "img"), pairs)


def swap(array):
    return permute(array, lambda seq, img: (seq, img ^ 1))


def pack_move(turn):
    def where_to(seq, img):
        return (2 * (img & 1) + (turn ^ (seq & 1)), (img & ~1) | (seq >> 1))

    return where_to


def exchange_packs(blocks, odd):
    rounds = [
        permute(jnp.where(odd, blocks[1 - turn], blocks[turn]), pack_move(turn)) for turn in (0, 1)
    ]
    return (jnp.where(odd, rounds[1], rounds[0]), jnp.where(odd, rounds[0], rounds[1]))


def pick(array, index, axis):
    return lax.dynamic_index_in_dim(array, index, axis, keepdims=False)


def pad_rows(array, rows):
    return jnp.pad(array, ((0, rows - array.shape[0]),) + ((0, 0),) * (array.ndim - 1))


def position_table(row_width):
    halfway = row_width // 2
    frequency = np.exp(np.arange(halfway, dtype=np.float64) * (-math.log(10000.0) / halfway))
    angles = np.arange(PATCHES, dtype=np.float64)[:, None] * frequency[None, :]
    return np.concatenate([np.sin(angles), np.cos(angles)], axis=1).astype(np.float32)


def reduce_pair(keep, leaving):
    return (keep.astype(f32) + swap(leaving).astype(f32)).astype(bf16)


MID_PIECES, POST_PIECES, DOWN_PIECES, UP_PIECES, ATT_PIECES = 3, 1, 3, 3, 4
DEC_PIECES = MID_PIECES + POST_PIECES
DOWN_AT = DEC_PIECES
UP_AT = DOWN_AT + DOWN_PIECES
ATT_AT = UP_AT + UP_PIECES
PIECES = ATT_AT + ATT_PIECES
FAR = (0, MID_PIECES, DOWN_AT + 1)


class Refs:
    def __init__(self, names, refs):
        self.__dict__.update(zip(names, refs))


def by_name(items):
    return Refs(items.keys(), items.values())


def piece_rows(piece):
    return LAST_EIGHTH if piece == PIECES - 1 else EIGHTH


def sub_rows(row, count):
    done = 0
    while done < count:
        piece = min((row + done) // SUB_ROWS, PIECES - 1)
        place, height = row + done - piece * SUB_ROWS, piece_rows(piece)
        start = place % height
        size = min(count - done, height - start)
        place //= height
        yield piece, place // 4, place // 2 % 2, place % 2, start, start + size, done
        done += size


class Place:
    def __init__(self):
        self.seq, self.img = lax.axis_index("seq"), lax.axis_index("img")
        self.chip, self.core = self.img // 2, lax.rem(self.img, 2)
        self.high, self.low = self.seq // 2, lax.rem(self.seq, 2)
        self.partner = dict(img=self.img + 1 - 2 * self.core)

    def remote(self, source, dest, sems, device):
        return pltpu.make_async_remote_copy(
            src_ref=source,
            dst_ref=dest,
            send_sem=sems.at[0],
            recv_sem=sems.at[1],
            device_id=device,
            device_id_type=pl.DeviceIdType.MESH,
        )

    def home(self, turn):
        segment = turn + self.low - 2 * turn * self.low
        device = dict(seq=2 * self.core + segment, img=2 * self.chip + self.high)
        stays = (self.high == self.core) if turn == 0 else None
        return device, segment, stays

    def send_home(self, act, source_parts, sems):
        for turn in (0, 1):
            device, segment, stays = self.home(turn)
            for part, (source, dest) in enumerate(source_parts(segment)):
                sem = sems.at[turn, part]
                if stays is None:
                    act(self.remote(source, dest, sem, device))
                else:

                    @pl.when(stays)
                    def _():
                        act(pltpu.make_async_copy(source, dest, sem.at[0]))

                    @pl.when(jnp.logical_not(stays))
                    def _():
                        act(self.remote(source, dest, sem, device))

    def greet(self, peers):
        barrier = pltpu.get_barrier_semaphore()

        def signal(device):
            pl.semaphore_signal(
                barrier, inc=1, device_id=device, device_id_type=pl.DeviceIdType.MESH
            )

        for device in peers:
            signal(device)
        signal(self.home(1)[0])

        @pl.when(self.high != self.core)
        def _():
            signal(self.home(0)[0])

        return lambda: pl.semaphore_wait(
            barrier, len(peers) + 1 + jnp.where(self.high == self.core, 0, 1)
        )


def start_copy(copy):
    copy.start()


def wait_copy(copy):
    copy.wait()


def loader(sems, **items):
    copies = {}
    for index, (name, (source, dest)) in enumerate(items.items()):
        copies[name] = pltpu.make_async_copy(source, dest, sems.at[index])
        copies[name].start()
    return by_name(copies)


def ready(*copies):
    for copy in copies:
        copy.wait()


def row_order(core, pad, rows):
    local = lax.broadcasted_iota(jnp.int32, (DEC_PAD, 2 * pad), 0)
    place = lax.broadcasted_iota(jnp.int32, (DEC_PAD, 2 * pad), 1)
    small = local < SMALL_PAD
    natural = jnp.where(small, local + core * HALF, local - SMALL_PAD + (1 - core) * SMALL)
    there = jnp.where(small, local, local - SMALL_PAD + SMALL - HALF) < SMALL
    spot = natural + jnp.where(natural >= rows, pad - rows, 0)
    return ((spot == place) & there).astype(f32).astype(bf16)


def front_kernel(names, *refs):
    r = Refs(names, refs)
    p = Place()
    core, low, high = p.core, p.low, p.high
    width, narrow = r.w_embed.shape
    rows = ENC_PAD
    seg_rows, cot_rows = r.enc_input.shape[1], r.cotangent.shape[1]
    cot_pad = r.cot_send.shape[1]
    load = loader(
        r.load_sem,
        qkv=(r.w_qkv, r.v_qkv),
        proj=(r.w_proj, r.v_proj),
        up=(r.w_up, r.v_up),
        down=(r.w_down, r.v_down),
        embed=(r.w_embed, r.v_embed),
        code=(r.codes.at[core], r.v_code),
        dec_qkv=(r.dec_qkv, r.v_dec_qkv),
    )
    greeted = p.greet([p.partner])
    for block in range(2):
        r.enc_send[block] = jnp.concatenate(
            [
                r.enc_input[block].astype(f32),
                jnp.zeros((ENC_SEG - seg_rows, width), f32),
            ],
            axis=0,
        ).astype(bf16)
    greeted()

    def enc_parts(segment):
        return [(r.enc_send.at[segment], r.v_x.at[low])]

    def cot_parts(segment):
        return [(r.cot_send.at[segment], r.cot_in.at[low])]

    p.send_home(start_copy, enc_parts, r.enc_sem)
    table_copy = p.remote(r.tables.at[1], r.tables_in, r.swap_sem.at[0], p.partner)
    table_copy.start()
    for block in range(2):
        r.cot_send[block] = jnp.concatenate(
            [
                r.cotangent[block].astype(f32),
                jnp.zeros((cot_pad - cot_rows, narrow), f32),
            ],
            axis=0,
        ).astype(bf16)
    p.send_home(start_copy, cot_parts, r.cot_sem)
    enc_vecs, dec_vecs = r.enc_vecs, r.dec_vecs

    stores = []

    def store(source, dest):
        copy = pltpu.make_async_copy(source, dest, r.store_sem.at[len(stores)])
        copy.start()
        stores.append(copy)

    def put_left(values, start):
        chips = r.lefts_keep.shape[0]
        turned = values.astype(f32).T.astype(bf16)
        count = turned.shape[0] // (2 * chips)
        for case in (0, 1):

            @pl.when(core == case)
            def _():
                for image in range(2 * chips):
                    ref = r.lefts_keep if image % 2 == case else r.lefts_leaving
                    ref[image // 2, start : start + count, :rows] = turned[
                        image * count : (image + 1) * count
                    ]

    left_hidden = r.w_up.shape[1] // (2 * r.lefts_keep.shape[0])
    left_mid = width // (2 * r.lefts_keep.shape[0])

    def norm_in(values, vecs, row):
        normed, _ = norm_parts(values)
        return (normed * vecs[row : row + 1] + vecs[row + 1 : row + 2]).astype(bf16)

    p.send_home(wait_copy, enc_parts, r.enc_sem)
    x = r.v_x[...].reshape(rows, width).astype(f32)
    attn_in = norm_in(x, enc_vecs, 0)
    ready(load.qkv)
    mixed = product(attn_in, r.v_qkv[...]).astype(bf16)
    r.v_query[...] = mixed[:, :width]
    r.v_own_kv[...] = mixed[:, width:]
    kv_copy = p.remote(r.v_own_kv, r.v_other_kv, r.swap_sem.at[1], p.partner)
    kv_copy.start()
    put_left(attn_in, left_hidden + 3 * left_mid)
    table_copy.wait()
    mine = high == core
    ids = jnp.where(mine, r.tables[0, 0, low], r.tables_in[0, low])
    row_ids = jnp.where(mine, r.tables[0, 1, low], r.tables_in[1, low])
    r.row_ids[...] = row_ids
    across = lax.broadcasted_iota(jnp.int32, (rows, 2 * rows), 1)
    along = lax.broadcasted_iota(jnp.int32, (rows, 2 * rows), 0)
    wide_ids = ids.astype(f32)
    own_ids = jnp.sum(jnp.where(across == along, wide_ids, 0.0), axis=1, keepdims=True)
    bias = jnp.where(own_ids == wide_ids, 0.0, masked_score)
    head_size = width // HE
    masks = lane_masks(head_size, bf16)
    kv_copy.wait()
    for pair in range(width // 128):
        cols = slice(128 * pair, 128 * pair + 128)
        value_cols = slice(width + 128 * pair, width + 128 * pair + 128)
        keys = jnp.concatenate([r.v_own_kv[:, cols], r.v_other_kv[:, cols]], axis=0)
        values = jnp.concatenate([r.v_own_kv[:, value_cols], r.v_other_kv[:, value_cols]], axis=0)
        total = jnp.zeros((rows, 128), f32)
        for head, mask in enumerate(masks):
            scores = inner_cols(r.v_query[:, cols] * mask, keys) + bias
            chances = softmax_rows(scores, 1.0 / math.sqrt(head_size))
            r.v_probs[len(masks) * pair + head, :, : 2 * rows] = chances
            total += product(chances, values * mask)
        r.v_att[:, cols] = total.astype(bf16)
    store(r.v_x, r.x)
    store(r.v_query, r.query)
    store(r.v_own_kv, r.own_kv)
    store(r.v_other_kv, r.other_kv)
    store(r.v_probs, r.probs)
    store(r.v_att, r.att)

    ready(load.proj, load.up, load.down, load.embed)
    middle = x + product(r.v_att[...], r.v_proj[...])
    r.v_middle[...] = middle
    store(r.v_middle, r.middle)
    mlp_in = norm_in(middle, enc_vecs, 2)
    active, slope = gelu_parts(product(mlp_in, r.v_up[...]))
    active = active.astype(bf16)
    r.v_slope[...] = slope.astype(bf16)
    store(r.v_slope, r.slope)
    out = middle + product(active, r.v_down[...])
    r.v_out[...] = out
    store(r.v_out, r.out)
    final = norm_in(out, enc_vecs, 4)
    r.emb_own[...] = product(final, r.v_embed[...]).astype(bf16)
    emb_copy = p.remote(r.emb_own, r.emb_in, r.swap_sem.at[2], p.partner)
    emb_copy.start()
    put_left(active, 0)
    put_left(mlp_in, left_hidden)
    put_left(r.v_att[...], left_hidden + left_mid)
    put_left(final, left_hidden + 2 * left_mid)
    store(r.lefts_keep, r.lefts_own)
    lefts_copy = p.remote(r.lefts_leaving, r.lefts_other, r.swap_sem.at[3], p.partner)
    lefts_copy.start()

    chosen = chosen_rows(core, row_ids)
    seen = jnp.sum(chosen, axis=1, keepdims=True)
    ready(load.code, load.dec_qkv)
    emb_copy.wait()
    tokens = jnp.concatenate([r.emb_own[...], r.emb_in[...]], axis=0)
    picked = product(chosen.astype(bf16), tokens)
    values = jnp.where(seen > 0.0, picked, dec_vecs[4:5]) + r.v_code[...]
    r.v_code[...] = values
    store(r.v_code, r.dec_input)
    mixed = product(norm_in(values, dec_vecs, 0), r.v_dec_qkv[...]).astype(bf16)
    r.v_mixed[...] = mixed
    big_copy = p.remote(
        r.v_mixed.at[SMALL_PAD:, narrow:], r.big_in, r.swap_sem.at[4], p.partner
    )
    big_copy.start()
    store(r.v_mixed, r.dec_mixed)

    p.send_home(wait_copy, cot_parts, r.cot_sem)
    moved = product(
        row_order(core, cot_pad, cot_rows), r.cot_in[...].reshape(2 * cot_pad, narrow)
    )
    r.v_cot[...] = moved.astype(bf16)
    store(r.v_cot, r.cot)
    big_copy.wait()
    store(r.big_in, r.dec_other_kv)

    head_size = narrow // HD
    per_group = 128 // head_size
    scale = 1.0 / math.sqrt(head_size)
    masks = lane_masks(head_size, bf16)

    def chance_copies(head, slot):
        return (
            pltpu.make_async_copy(r.chances.at[slot], r.big_probs.at[head], r.chance_sem.at[slot, 0]),
            pltpu.make_async_copy(
                r.small_chances.at[slot], r.small_probs.at[head], r.chance_sem.at[slot, 1]
            ),
        )

    wide_masks = lane_masks(head_size, f32)
    lane = lax.broadcasted_iota(jnp.int32, (1, 128), 1)

    def pad_column(blocks, size, used):
        index = lax.broadcasted_iota(jnp.int32, (blocks * size, 1), 0)
        index = jnp.where(index >= size, index - size, index)
        return jnp.where(index < used, 0.0, masked_score)

    big_pad, small_pad = pad_column(2, BIG_PAD, HALF), pad_column(1, SMALL_PAD, SMALL)

    def weigh(query, key, value, pad, mask, spare):
        one = spare.astype(bf16)
        scores = inner_cols(query * mask + one, key * mask + (pad * spare).astype(bf16))
        row_max = jnp.max(scores, axis=1, keepdims=True)
        weights = jnp.exp2((scores - row_max) * (scale * math.log2(math.e))).astype(bf16)
        mixed = product(weights, value * mask + one)
        return weights, mixed, 1.0 / jnp.sum(mixed * spare, axis=1, keepdims=True)

    def group_forward(group, carry):
        def cols(offset):
            return pl.ds(pl.multiple_of(offset * narrow + group * 128, 128), 128)

        query = r.v_mixed[:, cols(0)]
        small_key, small_value = r.v_mixed[:SMALL_PAD, cols(1)], r.v_mixed[:SMALL_PAD, cols(2)]
        keys = jnp.concatenate([r.v_mixed[SMALL_PAD:, cols(1)], r.big_in[:, cols(0)]], axis=0)
        values = jnp.concatenate([r.v_mixed[SMALL_PAD:, cols(2)], r.big_in[:, cols(1)]], axis=0)
        total = jnp.zeros((BIG_PAD, 128), f32)
        small_total = jnp.zeros((SMALL_PAD, 128), f32)
        inverse = jnp.zeros((BIG_PAD, 128), f32)
        small_inverse = jnp.zeros((SMALL_PAD, 128), f32)
        for head, mask in enumerate(masks):
            slot = head
            number = group * per_group + head

            @pl.when(group > 0)
            def _():
                for copy in chance_copies(number - per_group, slot):
                    copy.wait()

            spare = (lane == (head * head_size + 64) % 128).astype(f32)
            weights, mixed, shrink = weigh(
                query[SMALL_PAD:], keys, values, big_pad, mask, spare
            )
            r.chances[slot, :, : 2 * BIG_PAD] = weights
            shrink = shrink * wide_masks[head]
            inverse += shrink
            total += mixed * shrink
            weights, mixed, shrink = weigh(
                query[:SMALL_PAD], small_key, small_value, small_pad, mask, spare
            )
            r.small_chances[slot, :, :SMALL_PAD] = weights
            shrink = shrink * wide_masks[head]
            small_inverse += shrink
            small_total += mixed * shrink
            for copy in chance_copies(number, slot):
                copy.start()
        r.v_dec_att[:SMALL_PAD, cols(0)] = small_total.astype(bf16)
        r.v_dec_att[SMALL_PAD:, cols(0)] = total.astype(bf16)
        r.v_inverse[:SMALL_PAD, cols(0)] = small_inverse
        r.v_inverse[SMALL_PAD:, cols(0)] = inverse
        return carry

    lax.fori_loop(0, narrow // 128, group_forward, 0)
    store(r.v_dec_att, r.dec_att)
    store(r.v_inverse, r.dec_inverse)
    for slot in range(per_group):
        for copy in chance_copies(HD - per_group + slot, slot):
            copy.wait()
    for copy in stores:
        copy.wait()
    lefts_copy.wait()


def front(args, chips):
    anywhere = pl.BlockSpec(memory_space=pl.ANY)
    vmem = pl.BlockSpec(memory_space=pltpu.VMEM)
    dma = pltpu.SemaphoreType.DMA
    width, narrow = by_name(args).w_embed.shape
    wide = by_name(args).w_up.shape[1]
    left_rows = (4 * width + wide) // (2 * chips)
    cot_pad = DEC_PAD // 2
    outs = dict(
        x=((2, ENC_SEG, width), bf16),
        query=((ENC_PAD, width), bf16),
        own_kv=((ENC_PAD, 2 * width), bf16),
        other_kv=((ENC_PAD, 2 * width), bf16),
        probs=((HE, ENC_PAD, ENC_LANES), bf16),
        att=((ENC_PAD, width), bf16),
        middle=((ENC_PAD, width), f32),
        slope=((ENC_PAD, wide), bf16),
        out=((ENC_PAD, width), f32),
        lefts_own=((chips, left_rows, LEFT_LANES), bf16),
        lefts_other=((chips, left_rows, LEFT_LANES), bf16),
        dec_input=((DEC_PAD, narrow), f32),
        dec_mixed=((DEC_PAD, 3 * narrow), bf16),
        cot=((DEC_PAD, narrow), bf16),
        dec_other_kv=((BIG_PAD, 2 * narrow), bf16),
        big_probs=((HD, BIG_PAD, BIG_LANES), bf16),
        small_probs=((HD, SMALL_PAD, SMALL_LANES), bf16),
        dec_att=((DEC_PAD, narrow), bf16),
        dec_inverse=((DEC_PAD, narrow), f32),
        row_ids=((1, 2 * ENC_PAD), jnp.int32),
    )

    def like(out):
        return pltpu.VMEM(*out)

    scratch = dict(
        enc_send=like(by_name(outs).x),
        cot_send=pltpu.VMEM((2, cot_pad, narrow), bf16),
        cot_in=pltpu.VMEM((2, cot_pad, narrow), bf16),
        tables_in=pltpu.VMEM(by_name(args).tables.shape[1:], jnp.int32),
        v_x=like(by_name(outs).x),
        v_query=like(by_name(outs).query),
        v_own_kv=like(by_name(outs).own_kv),
        v_other_kv=like(by_name(outs).other_kv),
        v_probs=like(by_name(outs).probs),
        v_att=like(by_name(outs).att),
        v_middle=like(by_name(outs).middle),
        v_slope=like(by_name(outs).slope),
        v_out=like(by_name(outs).out),
        lefts_keep=like(by_name(outs).lefts_own),
        lefts_leaving=like(by_name(outs).lefts_own),
        emb_own=pltpu.VMEM((ENC_PAD, narrow), bf16),
        emb_in=pltpu.VMEM((ENC_PAD, narrow), bf16),
        v_code=like(by_name(outs).dec_input),
        v_mixed=like(by_name(outs).dec_mixed),
        v_cot=like(by_name(outs).cot),
        big_in=like(by_name(outs).dec_other_kv),
        chances=pltpu.VMEM((4, BIG_PAD, BIG_LANES), bf16),
        small_chances=pltpu.VMEM((4, SMALL_PAD, SMALL_LANES), bf16),
        v_dec_att=like(by_name(outs).dec_att),
        v_inverse=like(by_name(outs).dec_inverse),
        v_qkv=pltpu.VMEM(by_name(args).w_qkv.shape, bf16),
        v_proj=pltpu.VMEM(by_name(args).w_proj.shape, bf16),
        v_up=pltpu.VMEM(by_name(args).w_up.shape, bf16),
        v_down=pltpu.VMEM(by_name(args).w_down.shape, bf16),
        v_embed=pltpu.VMEM(by_name(args).w_embed.shape, bf16),
        v_dec_qkv=pltpu.VMEM(by_name(args).dec_qkv.shape, bf16),
        load_sem=dma((7,)),
        store_sem=dma((17,)),
        chance_sem=dma((4, 2)),
        swap_sem=dma((5, 2)),
        enc_sem=dma((2, 1, 2)),
        cot_sem=dma((2, 1, 2)),
    )
    names = list(args) + list(outs) + list(scratch)
    in_vmem = ("enc_input", "cotangent", "tables", "enc_vecs", "dec_vecs")
    results = pl.pallas_call(
        functools.partial(front_kernel, names),
        out_shape=[jax.ShapeDtypeStruct(shape, kind) for shape, kind in outs.values()],
        in_specs=[vmem if name in in_vmem else anywhere for name in args],
        out_specs=[vmem if name == "row_ids" else anywhere for name in outs],
        scratch_shapes=list(scratch.values()),
        compiler_params=pltpu.CompilerParams(
            collective_id=2, has_side_effects=True, vmem_limit_bytes=60 << 20
        ),
    )(*args.values())
    return dict(zip(outs, results))


def back_kernel(chips, names, *refs):
    r = Refs(names, refs)
    p = Place()
    chip, core, high, low = p.chip, p.core, p.high, p.low
    remote, partner = p.remote, p.partner
    along_x = dict(seq=p.seq + 1 - 2 * low)
    along_y = dict(seq=p.seq + 2 - 4 * high)
    others = [dict(img=lax.rem(chip + step, chips) * 2 + core) for step in range(1, chips)]
    width, wide, narrow = r.w_embed.shape[0], r.w_up.shape[1], r.w_embed.shape[1]
    rows = ENC_PAD

    def add(one, two):
        return (one.astype(f32) + two.astype(f32)).astype(bf16)

    held, first, second, from_chips, gathered = (
        r.held, r.first, r.second, r.from_chips, r.gathered
    )

    def pair_copy(i):
        return remote(r.leaving.at[i], r.from_pair.at[i], r.pair_sem.at[i], partner)

    def first_copies(i):
        n = slice(0, piece_rows(i))
        return (
            remote(
                held.at[i, :, 0, :, 1 - low, n], first.at[i, 0, :, :, n], r.first_sem.at[i, 0],
                along_x,
            ),
            remote(
                held.at[i, :, 1, 1 - high, :, n], first.at[i, 1, :, :, n], r.first_sem.at[i, 1],
                along_y,
            ),
        )

    def second_copies(i):
        n = slice(0, piece_rows(i))
        return (
            remote(
                held.at[i, :, 0, 1 - high, low, n], second.at[i, 0, :, n], r.second_sem.at[i, 0],
                along_y,
            ),
            remote(
                held.at[i, :, 1, high, 1 - low, n], second.at[i, 1, :, n], r.second_sem.at[i, 1],
                along_x,
            ),
        )

    def chip_copies(i):
        n = slice(0, piece_rows(i))
        return [
            remote(
                held.at[i, device["img"] // 2, :, high, low, n],
                from_chips.at[i, step, :, n],
                r.chip_sem.at[i, step],
                device,
            )
            for step, device in enumerate(others)
        ]

    def gather_copies(i, arrive):
        n = slice(0, piece_rows(i))
        x_place = 1 - low if arrive else low
        y_place = 1 - high if arrive else high
        one, two = gathered.at[i, 0, high, x_place, n], gathered.at[i, 1, y_place, low, n]
        return (
            remote(one, one, r.gather_sem.at[i, 0], along_x),
            remote(two, two, r.gather_sem.at[i, 1], along_y),
        )

    def spread_copies(i, arrive):
        n = slice(0, piece_rows(i))
        x_place = 1 - low if arrive else low
        y_place = 1 - high if arrive else high
        one, two = gathered.at[i, 0, y_place, :, n], gathered.at[i, 1, :, x_place, n]
        return (
            remote(one, one, r.gather_sem.at[i, 2], along_y),
            remote(two, two, r.gather_sem.at[i, 3], along_x),
        )

    def share_copy(i):
        return pltpu.make_async_copy(gathered.at[i], r.shares.at[i], r.share_sem.at[i])

    def stage_pair(i):
        pair_copy(i).wait()
        for image in range(chips):
            held[i, image] = add(held[i, image], r.from_pair[i, image])

    def stage_first(i):
        for copy in first_copies(i):
            copy.start()

    def stage_second(i):
        for copy in first_copies(i):
            copy.wait_recv()
        n = slice(0, piece_rows(i))
        held[i, :, 0, :, low, n] = add(held[i, :, 0, :, low, n], first[i, 0, :, :, n])
        held[i, :, 1, high, :, n] = add(held[i, :, 1, high, :, n], first[i, 1, :, :, n])
        for copy in second_copies(i):
            copy.start()

    def stage_chips(i):
        for copy in second_copies(i):
            copy.wait_recv()
        n = slice(0, piece_rows(i))
        held[i, :, 0, high, low, n] = add(held[i, :, 0, high, low, n], second[i, 0, :, n])
        held[i, :, 1, high, low, n] = add(held[i, :, 1, high, low, n], second[i, 1, :, n])
        for copy in chip_copies(i):
            copy.start()

    def stage_gather(i):
        for copy in chip_copies(i):
            copy.wait_recv()
        n = slice(0, piece_rows(i))
        mine = held[i, chip, :, high, low, n].astype(f32)
        for step in range(chips - 1):
            mine += from_chips[i, step, :, n].astype(f32)
        gathered[i, :, high, low, n] = mine.astype(bf16)
        for copy in gather_copies(i, False):
            copy.start()

    def stage_spread(i):
        for copy in gather_copies(i, True):
            copy.wait_recv()
        for copy in spread_copies(i, False):
            copy.start()

    def stage_end(i):
        for copy in spread_copies(i, True):
            copy.wait_recv()
        for copy in (
            *first_copies(i), *second_copies(i), *chip_copies(i), *gather_copies(i, False),
            *spread_copies(i, False),
        ):
            copy.wait_send()
        share_copy(i).start()

    def far_copies(i, begin=0, end=None):
        spots = [
            (step, part, device, source, dest)
            for step, device in enumerate(others)
            for part, (source, dest) in enumerate(
                (
                    (held.at[i, device["img"] // 2, :, 0], first.at[i, :, 1 + step]),
                    (held.at[i, device["img"] // 2, :, 1, 0], second.at[i, :, 1 + step]),
                    (held.at[i, device["img"] // 2, :, 1, 1], from_chips.at[i, step]),
                )
            )
        ]
        return [
            remote(source, dest, r.far_sem.at[FAR.index(i), step, part], device)
            for step, part, device, source, dest in spots[begin:end]
        ]

    def far_start(i, begin=0, end=None):
        for copy in far_copies(i, begin, end):
            copy.start()

    def far_first_copies(i):
        return (
            remote(held.at[i, chip, 0, :, 1 - low], first.at[i, 0, 0], r.first_sem.at[i, 0], along_x),
            remote(held.at[i, chip, 1, 1 - high], first.at[i, 1, 0], r.first_sem.at[i, 1], along_y),
        )

    def far_second_copies(i):
        return (
            remote(
                held.at[i, chip, 0, 1 - high, low], second.at[i, 0, 0], r.second_sem.at[i, 0],
                along_y,
            ),
            remote(
                held.at[i, chip, 1, high, 1 - low], second.at[i, 1, 0], r.second_sem.at[i, 1],
                along_x,
            ),
        )

    def far_first(i):
        for copy in far_copies(i):
            copy.wait_recv()

        def total(mine, *arrived):
            mine = mine.astype(f32)
            for one in arrived:
                mine += one.astype(f32)
            return mine.astype(bf16)

        steps = range(chips - 1)
        held[i, chip, :, 0] = total(held[i, chip, :, 0], *(first[i, :, 1 + k] for k in steps))
        held[i, chip, :, 1, 0] = total(
            held[i, chip, :, 1, 0], *(second[i, :, 1 + k] for k in steps)
        )
        held[i, chip, :, 1, 1] = total(
            held[i, chip, :, 1, 1], *(from_chips[i, k] for k in steps)
        )
        for copy in far_first_copies(i):
            copy.start()

    def far_second(i):
        for copy in far_first_copies(i):
            copy.wait_recv()
        held[i, chip, 0, :, low] = add(held[i, chip, 0, :, low], first[i, 0, 0])
        held[i, chip, 1, high] = add(held[i, chip, 1, high], first[i, 1, 0])
        for copy in far_second_copies(i):
            copy.start()

    def far_gather(i):
        for copy in far_second_copies(i):
            copy.wait_recv()
        gathered[i, 0, high, low] = add(held[i, chip, 0, high, low], second[i, 0, 0])
        gathered[i, 1, high, low] = add(held[i, chip, 1, high, low], second[i, 1, 0])
        for copy in gather_copies(i, False):
            copy.start()

    def far_end(i):
        for copy in spread_copies(i, True):
            copy.wait_recv()
        for copy in (
            *far_copies(i), *far_first_copies(i), *far_second_copies(i),
            *gather_copies(i, False), *spread_copies(i, False),
        ):
            copy.wait_send()
        share_copy(i).start()

    stages = (stage_first, stage_second, stage_chips, stage_gather, stage_spread, stage_end)
    far_stages = (far_first, far_second, far_gather, stage_spread, far_end)
    line = []

    def pump(piece):
        line.append(piece)
        for lag in range(len(stages)):
            slot = len(line) - 1 - lag
            if slot >= 0 and line[slot] is not None:
                course = far_stages if line[slot] in FAR else stages
                if lag < len(course):
                    course[lag](line[slot])

    greeted = p.greet([partner, along_x, along_y, *others])

    def put_dec(grad, first_image, count, row):
        grad = grad.astype(bf16)
        for case in (0, 1):

            @pl.when(core == case)
            def _():
                for index in range(grad.shape[0] // count):
                    image = first_image + index
                    ref = held if image % 2 == case else r.leaving
                    for block in range(grad.shape[1] // LANES):
                        for piece, half, up, across, begin, end, at in sub_rows(
                            row + block * count, count
                        ):
                            ref[piece, image // 2, half, up, across, begin:end] = grad[
                                index * count + at : index * count + at + end - begin,
                                block * LANES : (block + 1) * LANES,
                            ]

    def decoder(
        dec_input, att, inverses, cot, w_proj, w_up, w_down, w_qkv, mixed, other_kv, chances,
        small_chances, decoded, grad_middle, grad_att, grad_mixed, grad_kv, kv_leaving,
    ):
        load = loader(
        r.load_sem,
        dec_input=(r.dec_input, dec_input),
        att=(r.dec_att, att),
        proj=(r.dec_proj, w_proj),
        up=(r.dec_up, w_up),
        cot=(r.cot, cot),
        down=(r.dec_down, w_down),
        mixed=(r.dec_mixed, mixed),
        other=(r.dec_other_kv, other_kv),
        qkv=(r.dec_qkv, w_qkv),
        inverses=(r.dec_inverse, inverses),
    )

        def chance_copies(head, slot):
            return (
                pltpu.make_async_copy(
                    r.big_probs.at[head], chances.at[slot], r.chance_sem.at[slot, 0]
                ),
                pltpu.make_async_copy(
                    r.small_probs.at[head], small_chances.at[slot], r.chance_sem.at[slot, 1]
                ),
            )

        for copy in chance_copies(0, 0):
            copy.start()
        greeted()

        ready(load.dec_input, load.att, load.proj)
        vecs = r.dec_vecs
        middle = dec_input[...] + product(att[...], w_proj[...])
        normed, inverse = norm_parts(middle)
        mlp_in = (normed * vecs[2:3] + vecs[3:4]).astype(bf16)
        result = middle
        grad_norm = jnp.zeros_like(middle)
        step = 2 * w_down.shape[0] // (2 * chips)
        down_count, up_count = step // 2, narrow // (2 * chips)
        up_row = down_count * narrow // LANES
        proj_row = up_row + up_count * w_up.shape[1] // LANES
        ready(load.up, load.cot, load.down)
        for copy in early_loads():
            copy.start()
        for block in range(w_up.shape[1] // step):
            cols = slice(block * step, (block + 1) * step)
            active, slope = gelu_parts(product(mlp_in, w_up[:, cols]))
            active = active.astype(bf16)
            result += product(active, w_down[cols])
            put_dec(inner_rows(active, cot[...]), 2 * block, down_count, 0)
            grad_hidden = (slope * inner_cols(cot[...], w_down[cols])).astype(bf16)
            put_dec(
                inner_rows(mlp_in, grad_hidden), 0, up_count,
                up_row + up_count * block * step // LANES,
            )
            grad_norm += inner_cols(grad_hidden, w_up[:, cols])
        order = row_order(core, DEC_PAD // 2, (SMALL + HALF) // 2)
        decoded[...] = (
            inner_rows(order, result.astype(bf16)).astype(bf16).reshape(2, DEC_PAD // 2, narrow)
        )

        def decoded_parts(segment):
            return [(decoded.at[segment], r.home_rows.at[low])]

        p.send_home(start_copy, decoded_parts, r.rows_sem)
        grad_values, gain, shift = norm_backward(grad_norm, normed, inverse, vecs[2:3])
        r.vec_own[...] = jnp.zeros(r.vec_own.shape, f32)
        r.vec_own[10:11, :narrow] = gain
        r.vec_own[11:12, :narrow] = shift
        back = cot[...].astype(f32) + grad_values
        grad_middle[...] = back
        back = back.astype(bf16)
        ready(load.inverses)
        grad_low = inner_cols(back, w_proj[...]).astype(bf16)
        grad_att[...] = (grad_low.astype(f32) * inverses[...]).astype(bf16)
        put_dec(inner_rows(att[...], back), 0, up_count, proj_row)
        for i in range(MID_PIECES):
            pair_copy(i).start()

        ready(load.mixed, load.other)
        head_size = narrow // HD
        per_group = 128 // head_size
        scale = 1.0 / math.sqrt(head_size)
        masks, wide_masks = lane_masks(head_size, bf16), lane_masks(head_size, f32)

        def group_back(group, last):
            def cols(offset):
                return pl.ds(pl.multiple_of(offset * narrow + group * 128, 128), 128)

            query = mixed[:, cols(0)]
            small_key, small_value = mixed[:SMALL_PAD, cols(1)], mixed[:SMALL_PAD, cols(2)]
            keys = jnp.concatenate([mixed[SMALL_PAD:, cols(1)], other_kv[:, cols(0)]], axis=0)
            values = jnp.concatenate([mixed[SMALL_PAD:, cols(2)], other_kv[:, cols(1)]], axis=0)
            grads = grad_att[:, cols(0)]
            overlap = grads.astype(f32) * att[:, cols(0)].astype(f32)
            def turned(values):
                return values.astype(f32).T.astype(bf16)

            big_query, small_query = turned(query[SMALL_PAD:]), turned(query[:SMALL_PAD])
            big_grad, small_grad = turned(grads[SMALL_PAD:]), turned(grads[:SMALL_PAD])
            big_q = jnp.zeros((BIG_PAD, 128), f32)
            small_q = jnp.zeros((SMALL_PAD, 128), f32)
            big_k, big_v, small_k, small_v = [], [], [], []
            for head, mask in enumerate(masks):
                slot = head % 2
                number = group * per_group + head
                for copy in chance_copies(number, slot):
                    copy.wait()
                if head < per_group - 1:
                    for copy in chance_copies(number + 1, 1 - slot):
                        copy.start()
                else:

                    @pl.when(group < last)
                    def _():
                        for copy in chance_copies(number + 1, 1 - slot):
                            copy.start()

                delta = jnp.sum(overlap * wide_masks[head], axis=1, keepdims=True)
                one_grad = grads * mask
                own = slice(head * head_size, (head + 1) * head_size)
                probs = chances[slot, :, : 2 * BIG_PAD]
                one = head_back(probs, one_grad[SMALL_PAD:], values, delta[SMALL_PAD:])
                big_q += product(one, keys * mask)
                big_k.append(product(big_query[own], one))
                big_v.append(product(big_grad[own], probs))
                probs = small_chances[slot, :, :SMALL_PAD]
                one = head_back(probs, one_grad[:SMALL_PAD], small_value, delta[:SMALL_PAD])
                small_q += product(one, small_key * mask)
                small_k.append(product(small_query[own], one))
                small_v.append(product(small_grad[own], probs))
            big_k, big_v, small_k, small_v = (
                jnp.concatenate(parts, axis=0).T for parts in (big_k, big_v, small_k, small_v)
            )
            grad_mixed[:SMALL_PAD, cols(0)] = (small_q * scale).astype(bf16)
            grad_mixed[SMALL_PAD:, cols(0)] = (big_q * scale).astype(bf16)
            grad_mixed[:SMALL_PAD, cols(1)] = (small_k * scale).astype(bf16)
            grad_mixed[:SMALL_PAD, cols(2)] = small_v.astype(bf16)
            grad_kv[:, cols(0)] = big_k[:BIG_PAD] * scale
            grad_kv[:, cols(1)] = big_v[:BIG_PAD]
            kv_leaving[:, cols(0)] = (big_k[BIG_PAD:] * scale).astype(bf16)
            kv_leaving[:, cols(1)] = big_v[BIG_PAD:].astype(bf16)

        def kv_copies(group):
            for which in range(2):
                cols = slice(which * narrow + group * 128, which * narrow + (group + 1) * 128)
                yield remote(
                    kv_leaving.at[:, cols], r.dec_kv_in.at[:, cols], r.kv_sem.at[group, which],
                    partner,
                )

        groups = narrow // 128
        for group in range(groups):
            lax.fori_loop(
                group, group + 1, lambda g, c: (group_back(g, groups - 1), c)[1], 0
            )
            for copy in kv_copies(group):
                copy.start()
            if group == 0:
                stage_pair(0)
                far_start(0)
                stage_pair(1)
                pump(1)
            if group == 1:
                stage_pair(2)
                pump(2)
            if group == 2:
                pump(None)
        pump(None)

        normed, inverse = norm_parts(dec_input[...])
        attn_in = (normed * vecs[0:1] + vecs[1:2]).astype(bf16)
        chosen = chosen_rows(core, r.row_ids[...])
        seen = jnp.sum(chosen, axis=1, keepdims=True)
        ready(load.qkv)
        for group in range(groups):
            for copy in kv_copies(group):
                copy.wait()
        grad_mixed[SMALL_PAD:, narrow:] = (grad_kv[...] + r.dec_kv_in[...].astype(f32)).astype(bf16)
        grad_values, gain, shift = norm_backward(
            inner_cols(grad_mixed[...], w_qkv[...]), normed, inverse, vecs[0:1]
        )
        r.vec_own[8:9, :narrow] = gain
        r.vec_own[9:10, :narrow] = shift
        back = grad_middle[...] + grad_values
        spread = inner_rows(chosen.astype(bf16), back.astype(bf16)).astype(bf16)
        r.spread_own[...] = spread[:rows]
        r.spread_leaving[...] = spread[rows:]
        spread_copy.start()
        pump(0)
        r.vec_own[12:13, :narrow] = jnp.sum(
            jnp.where(seen > 0.0, 0.0, back), axis=0, keepdims=True
        )
        put_dec(inner_rows(attn_in, grad_mixed[...]), 0, up_count, MID_PIECES * SUB_ROWS)
        pair_copy(MID_PIECES).start()
        pump(None)
        p.send_home(wait_copy, decoded_parts, r.rows_sem)

    def early_loads():
        return [
            pltpu.make_async_copy(source, dest, r.load_sem.at[10 + index])
            for index, (source, dest) in enumerate(
                (
                    (r.w_embed, r.v_embed), (r.out, r.v_out),
                )
            )
        ]

    spread_copy = remote(r.spread_leaving, r.spread_in, r.swap_sem.at[2], partner)
    dec_rows, big = DEC_PAD, BIG_PAD
    pl.run_scoped(
        decoder,
        pltpu.VMEM((dec_rows, narrow), f32),
        pltpu.VMEM((dec_rows, narrow), bf16),
        pltpu.VMEM((dec_rows, narrow), f32),
        pltpu.VMEM((dec_rows, narrow), bf16),
        pltpu.VMEM(r.dec_proj.shape, bf16),
        pltpu.VMEM(r.dec_up.shape, bf16),
        pltpu.VMEM(r.dec_down.shape, bf16),
        pltpu.VMEM(r.dec_qkv.shape, bf16),
        pltpu.VMEM((dec_rows, 3 * narrow), bf16),
        pltpu.VMEM((big, 2 * narrow), bf16),
        pltpu.VMEM((2, big, BIG_LANES), bf16),
        pltpu.VMEM((2, SMALL_PAD, SMALL_LANES), bf16),
        pltpu.VMEM((2, dec_rows // 2, narrow), bf16),
        pltpu.VMEM((dec_rows, narrow), f32),
        pltpu.VMEM((dec_rows, narrow), bf16),
        pltpu.VMEM((dec_rows, 3 * narrow), bf16),
        pltpu.VMEM((big, 2 * narrow), f32),
        pltpu.VMEM((big, 2 * narrow), bf16),
    )

    def encoder(
        v_down, v_slope, v_up, v_proj, v_middle, v_att, v_probs, v_query,
        v_own_kv, v_other_kv, v_x, v_lefts, v_lefts_other, right_own, kv_own, kv_leaving, grad_rows,
    ):
        load = loader(
        r.load_sem.at[12:],
        down=(r.w_down, v_down),
        slope=(r.slope, v_slope),
        lefts=(r.lefts_own, v_lefts),
        lefts_other=(r.lefts_other, v_lefts_other),
        up=(r.w_up, v_up),
        middle=(r.middle, v_middle),
        proj=(r.w_proj, v_proj),
        att=(r.att, v_att),
        probs=(r.probs, v_probs),
        query=(r.query, v_query),
        own_kv=(r.own_kv, v_own_kv),
        other_kv=(r.other_kv, v_other_kv),
        x=(r.x, v_x),
    )
        early = early_loads()
        vecs = r.enc_vecs
        starts = [0]
        for columns in (width, wide, narrow, width, 3 * width):
            starts.append(starts[-1] + columns)
        out_at, hidden_at, embedded_at, middle_at, all_mixed_at = (
            slice(*pair) for pair in zip(starts, starts[1:])
        )

        def give(cols, value, index):
            if value is not None:
                right_own[:, cols] = value
            copy = remote(
                right_own.at[:, cols], r.right_other.at[:, cols], r.swap_sem.at[index], partner
            )
            copy.start()
            return copy

        def weight_grad(cols, left, count, row, first_block=0, blocks=None):
            last_block = (
                (cols.stop - cols.start) // LANES if blocks is None else first_block + blocks
            )
            own = v_lefts[:, left : left + count, :rows].reshape(chips * count, rows)
            other = v_lefts_other[:, left : left + count, :rows].reshape(chips * count, rows)
            for block in range(first_block, last_block):
                columns = slice(cols.start + block * LANES, cols.start + (block + 1) * LANES)
                grad = product(own, right_own[:, columns]) + product(
                    other, r.right_other[:, columns]
                )
                grad = grad.astype(bf16)
                for piece, half, up, across, begin, end, at in sub_rows(
                    row + block * count, count
                ):
                    for image in range(chips):
                        held[piece, image, half, up, across, begin:end] = grad[
                            image * count + at : image * count + at + end - begin
                        ]

        left_hidden, left_mid = wide // (2 * chips), width // (2 * chips)
        left_mlp = left_hidden
        left_att, left_final, left_attn = (left_hidden + place * left_mid for place in (1, 2, 3))

        spread_copy.wait()
        grad_embedded = r.spread_own[...] + r.spread_in[...]
        embedded_copy = give(embedded_at, grad_embedded, 3)
        stage_pair(MID_PIECES)
        far_start(MID_PIECES)
        ready(*early)
        normed, inverse = norm_parts(r.v_out[...])
        grad_out, gain, shift = norm_backward(
            inner_cols(grad_embedded, r.v_embed[...]), normed, inverse, vecs[4:5]
        )
        r.vec_own[4:5] = gain
        r.vec_own[5:6] = shift
        grad_low = grad_out.astype(bf16)
        out_copy = give(out_at, grad_low, 4)
        ready(load.down, load.slope)
        grad_hidden = (v_slope[...].astype(f32) * inner_cols(grad_low, v_down[...])).astype(bf16)
        qkv_copies = [
            pltpu.make_async_copy(
                r.w_qkv.at[:, part * width : (part + 1) * width],
                v_down.at[part * width : (part + 1) * width],
                r.load_sem.at[25 + part],
            )
            for part in range(3)
        ]
        for copy in qkv_copies:
            copy.start()
        hidden_copy = give(hidden_at, grad_hidden, 5)
        ready(load.lefts, load.lefts_other)
        out_copy.wait()
        weight_grad(out_at, 0, left_hidden, DOWN_AT * SUB_ROWS, 0, 1)
        pump(DOWN_AT)
        weight_grad(out_at, 0, left_hidden, DOWN_AT * SUB_ROWS, 1, 2)
        ready(load.up, load.middle, load.proj)
        normed, inverse = norm_parts(v_middle[...])
        grad_values, gain, shift = norm_backward(
            inner_cols(grad_hidden, v_up[...]), normed, inverse, vecs[2:3]
        )
        r.vec_own[2:3] = gain
        r.vec_own[3:4] = shift
        grad_middle = grad_out + grad_values
        grad_low = grad_middle.astype(bf16)
        middle_copy = give(middle_at, grad_low, 6)
        grads = inner_cols(grad_low, v_proj[...]).astype(bf16)
        pump(DOWN_AT + 2)

        ready(load.att, load.probs, load.query, load.own_kv, load.other_kv)
        head_size = width // HE
        scale = 1.0 / math.sqrt(head_size)
        overlap = grads.astype(f32) * v_att[...].astype(f32)
        masks = lane_masks(head_size, bf16)
        wide_masks = lane_masks(head_size, f32)
        mixed_at = all_mixed_at.start
        for pair in range(width // 128):
            cols = slice(128 * pair, 128 * pair + 128)
            value_cols = slice(width + 128 * pair, width + 128 * pair + 128)
            keys = jnp.concatenate([v_own_kv[:, cols], v_other_kv[:, cols]], axis=0)
            values = jnp.concatenate([v_own_kv[:, value_cols], v_other_kv[:, value_cols]], axis=0)
            total_q = jnp.zeros((rows, 128), f32)
            total_k = jnp.zeros((2 * rows, 128), f32)
            total_v = jnp.zeros((2 * rows, 128), f32)
            for head, mask in enumerate(masks):
                delta = jnp.sum(overlap[:, cols] * wide_masks[head], axis=1, keepdims=True)
                one_grad = grads[:, cols] * mask
                chances = v_probs[len(masks) * pair + head, :, : 2 * rows]
                one_back = head_back(chances, one_grad, values, delta)
                total_q += product(one_back, keys * mask)
                total_k += inner_rows(one_back, v_query[:, cols] * mask)
                total_v += inner_rows(chances, one_grad)
            right_own[:, mixed_at + 128 * pair : mixed_at + 128 * pair + 128] = (
                total_q * scale
            ).astype(bf16)
            kv_own[:, cols] = total_k[:rows] * scale
            kv_own[:, value_cols] = total_v[:rows]
            kv_leaving[:, cols] = (total_k[rows:] * scale).astype(bf16)
            kv_leaving[:, value_cols] = total_v[rows:].astype(bf16)
        kv_copy = remote(kv_leaving, r.kv_in, r.swap_sem.at[7], partner)
        kv_copy.start()
        pump(MID_PIECES)
        hidden_copy.wait()
        weight_grad(hidden_at, left_mlp, left_mid, UP_AT * SUB_ROWS)
        late = DOWN_AT + 1
        pump(UP_AT)
        far_start(late, 0, 2)

        kv_copy.wait()
        right_own[:, mixed_at + width : mixed_at + 3 * width] = (
            kv_own[...] + r.kv_in[...].astype(f32)
        ).astype(bf16)
        mixed_copy = give(all_mixed_at, None, 8)
        ready(load.x)
        normed, inverse = norm_parts(v_x[...].reshape(rows, width).astype(f32))
        grad_norm = jnp.zeros((rows, width), f32)
        for part, copy in enumerate(qkv_copies):
            copy.wait()
            place = mixed_at + part * width
            grad_norm += inner_cols(
                right_own[:, place : place + width], v_down[part * width : (part + 1) * width]
            )
        grad_values, gain, shift = norm_backward(grad_norm, normed, inverse, vecs[0:1])
        r.vec_own[0:1] = gain
        r.vec_own[1:2] = shift
        vec_copy = remote(r.vec_own, r.vec_in, r.swap_sem.at[9], partner)
        vec_copy.start()
        grad_values = grad_middle + grad_values
        grad_rows[0] = grad_values[: rows // 2]
        grad_rows[1] = grad_values[rows // 2 :]

        def grad_parts(segment):
            return [(grad_rows.at[segment], r.home_grad.at[low])]

        p.send_home(start_copy, grad_parts, r.grad_sem)
        pump(UP_AT + 1)
        far_start(late, 2, 4)
        middle_copy.wait()
        embedded_copy.wait()
        embed_row = ATT_AT * SUB_ROWS + left_mid * width // LANES
        weight_grad(middle_at, left_att, left_mid, ATT_AT * SUB_ROWS)
        weight_grad(embedded_at, left_final, left_mid, embed_row)
        pump(UP_AT + 2)
        far_start(late, 4, 6)
        mixed_copy.wait()
        qkv_row = embed_row + left_mid * narrow // LANES
        weight_grad(all_mixed_at, left_attn, left_mid, qkv_row)
        pump(ATT_AT)
        far_start(late, 6, 8)
        vec_copy.wait()
        vectors = (r.vec_own[...] + r.vec_in[...]).astype(bf16)
        vec_row = qkv_row + left_mid * 3 * width // LANES
        piece, half, up, across, begin, end, _ = next(iter(sub_rows(vec_row, 16)))
        entry = lax.broadcasted_iota(jnp.int32, (width, LANES), 0)
        lane = lax.broadcasted_iota(jnp.int32, (width, LANES), 1)
        row_index = lax.broadcasted_iota(jnp.int32, (16, LANES), 0)
        narrow_left = narrow // (2 * chips)
        for image in range(chips):
            number = 2 * image + core
            enc_pick = (entry == lane + number * left_mid) & (lane < left_mid)
            dec_pick = (entry == lane + number * narrow_left) & (lane < narrow_left)
            enc_part = product(vectors, enc_pick.astype(f32).astype(bf16))
            dec_part = product(vectors, dec_pick.astype(f32).astype(bf16))
            held[piece, image, half, up, across, begin:end] = jnp.where(
                row_index < 8, enc_part, dec_part
            ).astype(bf16)
        pump(ATT_AT + 1)
        far_start(late, 8, 9)
        for piece in (ATT_AT + 2, PIECES - 1, late):
            pump(piece)
        p.send_home(wait_copy, grad_parts, r.grad_sem)

    pl.run_scoped(
        encoder,
        pltpu.VMEM(r.w_down.shape, bf16),
        pltpu.VMEM(r.slope.shape, bf16),
        pltpu.VMEM(r.w_up.shape, bf16),
        pltpu.VMEM(r.w_proj.shape, bf16),
        pltpu.VMEM(r.middle.shape, f32),
        pltpu.VMEM(r.att.shape, bf16),
        pltpu.VMEM(r.probs.shape, bf16),
        pltpu.VMEM(r.query.shape, bf16),
        pltpu.VMEM(r.own_kv.shape, bf16),
        pltpu.VMEM(r.other_kv.shape, bf16),
        pltpu.VMEM(r.x.shape, bf16),
        pltpu.VMEM(r.lefts_own.shape, bf16),
        pltpu.VMEM(r.lefts_own.shape, bf16),
        pltpu.VMEM(r.right_other.shape, bf16),
        pltpu.VMEM((rows, 2 * width), f32),
        pltpu.VMEM((rows, 2 * width), bf16),
        pltpu.VMEM((2, ENC_SEG, width), f32),
    )
    for _ in range(len(stages) - 1):
        pump(None)
    lax.fori_loop(0, PIECES, lambda i, c: (share_copy(i).wait(), c)[1], 0)


def back(chips, args):
    anywhere = pl.BlockSpec(memory_space=pl.ANY)
    vmem = pl.BlockSpec(memory_space=pltpu.VMEM)
    block = (EIGHTH, LANES)
    dma = pltpu.SemaphoreType.DMA
    width, narrow = by_name(args).w_embed.shape
    wide = by_name(args).w_up.shape[1]
    rights = width + wide + narrow + width + 3 * width
    outs = dict(
        shares=((PIECES, 2, 2, 2) + block, bf16),
        home_rows=((2, DEC_PAD // 2, narrow), bf16),
        home_grad=((2, ENC_SEG, width), f32),
    )
    scratch = dict(
        held=pltpu.VMEM((PIECES, chips, 2, 2, 2) + block, bf16),
        v_embed=pltpu.VMEM(by_name(args).w_embed.shape, bf16),
        v_out=pltpu.VMEM(by_name(args).out.shape, f32),
        leaving=pltpu.VMEM((DEC_PIECES, chips, 2, 2, 2) + block, bf16),
        from_pair=pltpu.VMEM((DEC_PIECES, chips, 2, 2, 2) + block, bf16),
        first=pltpu.VMEM((PIECES, 2, chips, 2) + block, bf16),
        second=pltpu.VMEM((PIECES, 2, chips) + block, bf16),
        from_chips=pltpu.VMEM((PIECES, chips - 1, 2) + block, bf16),
        gathered=pltpu.VMEM((PIECES, 2, 2, 2) + block, bf16),
        dec_kv_in=pltpu.VMEM((BIG_PAD, 2 * narrow), bf16),
        spread_own=pltpu.VMEM((ENC_PAD, narrow), bf16),
        spread_leaving=pltpu.VMEM((ENC_PAD, narrow), bf16),
        spread_in=pltpu.VMEM((ENC_PAD, narrow), bf16),
        right_other=pltpu.VMEM((ENC_PAD, rights), bf16),
        kv_in=pltpu.VMEM((ENC_PAD, 2 * width), bf16),
        vec_own=pltpu.VMEM((16, width), f32),
        vec_in=pltpu.VMEM((16, width), f32),
        load_sem=dma((28,)),
        chance_sem=dma((2, 2)),
        pair_sem=dma((DEC_PIECES, 2)),
        first_sem=dma((PIECES, 2, 2)),
        second_sem=dma((PIECES, 2, 2)),
        chip_sem=dma((PIECES, chips - 1, 2)),
        gather_sem=dma((PIECES, 4, 2)),
        share_sem=dma((PIECES,)),
        far_sem=dma((len(FAR), chips - 1, 3, 2)),
        swap_sem=dma((10, 2)),
        kv_sem=dma((4, 2, 2)),
        rows_sem=dma((2, 1, 2)),
        grad_sem=dma((2, 1, 2)),
    )
    names = list(args) + list(outs) + list(scratch)
    in_vmem = ("row_ids", "dec_vecs", "enc_vecs")
    return pl.pallas_call(
        functools.partial(back_kernel, chips, names),
        out_shape=[jax.ShapeDtypeStruct(shape, kind) for shape, kind in outs.values()],
        in_specs=[vmem if name in in_vmem else anywhere for name in args],
        out_specs=[anywhere] * len(outs),
        scratch_shapes=list(scratch.values()),
        compiler_params=pltpu.CompilerParams(
            collective_id=1, has_side_effects=True, vmem_limit_bytes=63 << 20
        ),
    )(*args.values())


def unstack_kernel(counts, enc_count, dec_count, flat, *outs):
    def runs(row, count):
        for piece, half, up, across, begin, end, at in sub_rows(row, count):
            start = piece * SUB_ROWS + (4 * half + 2 * up + across) * EIGHTH + begin
            yield flat[start : start + end - begin].astype(f32), at

    row = 0
    for out, count in zip(outs, counts):
        for block in range(out.shape[1] // LANES):
            for values, at in runs(row, count):
                out[at : at + values.shape[0], block * LANES : (block + 1) * LANES] = values
            row += count
    ((rows, _),) = runs(row, 16)
    outs[-2][...] = rows[:6, :enc_count]
    outs[-1][...] = rows[8:13, :dec_count]


def reduce_rest(chunk, seq):
    chips, rows, width = chunk.shape
    high, low = seq // 2, seq % 2
    eighth = rows // 8
    parts = chunk.reshape(chips, 2, 2, 2, eighth, width)

    def along_x(array):
        return permute(array, lambda s, i: (s ^ 1, i))

    def along_y(array):
        return permute(array, lambda s, i: (s ^ 2, i))

    def add(one, two):
        return (one.astype(f32) + two.astype(f32)).astype(bf16)

    one, two = parts[:, 0], parts[:, 1]
    one = add(pick(one, low, 2), along_x(pick(one, 1 - low, 2)))
    two = add(pick(two, high, 1), along_y(pick(two, 1 - high, 1)))
    one = add(pick(one, high, 1), along_y(pick(one, 1 - high, 1)))
    two = add(pick(two, low, 1), along_x(pick(two, 1 - low, 1)))
    mine = jnp.stack([one, two], axis=1)
    chip = lax.axis_index("img") // 2
    total = pick(mine, chip, 0).astype(f32)
    for step in range(1, chips):
        leaving = pick(mine, (chip + step) % chips, 0)
        arrived = permute(
            leaving,
            lambda s, i, step=step: (s, ((i // 2 + step) % chips) * 2 + (i & 1)),
        )
        total = total + arrived.astype(f32)
    own = total.astype(bf16)
    others = [permute(own, lambda s, i, step=step: (s ^ step, i)) for step in (1, 2, 3)]
    by_xor = jnp.stack([own] + others)
    ordered = jnp.stack([pick(by_xor, seq ^ place, 0) for place in range(4)], axis=1)
    return ordered.reshape(rows, width)


def shards(
    enc_input,
    cotangent,
    enc_image,
    visible_rows,
    enc_norms,
    enc_qkv,
    enc_proj,
    enc_up,
    enc_down,
    embed,
    dec_vecs,
    dec_qkv,
    dec_proj,
    dec_up,
    dec_down,
):
    seq = lax.axis_index("seq")
    img = lax.axis_index("img")
    images = lax.axis_size("img")
    core = img % 2
    odd = seq % 2 == 1
    enc_width = enc_input.shape[3]
    dec_width = dec_vecs.shape[0]
    enc_half = 2 * enc_input.shape[2]
    dec_quarter = cotangent.shape[2]

    enc_vecs = jnp.pad(enc_norms.T, ((0, 2), (0, 0)))
    dec_rows_vecs = jnp.pad(dec_vecs.T, ((0, 3), (0, 0)))
    table = position_table(dec_width)
    codes = np.zeros((2, DEC_PAD, dec_width), np.float32)
    for which in range(2):
        codes[which, :SMALL] = table[:SMALL]
        codes[which, SMALL_PAD : SMALL_PAD + HALF] = table[which * HALF : (which + 1) * HALF]
    chips = images // 2
    tables = jnp.stack([enc_image[0], visible_rows[0]])
    if images == 8:
        segments = tables.reshape(2, 2, 2, 2, enc_half // 2)
        segments = jnp.pad(
            segments, ((0, 0),) * 4 + ((0, ENC_SEG - enc_half // 2),), constant_values=-2
        )
        segments = segments.reshape(2, 2, 2, ENC_PAD)
        straight = segments.reshape(2, 2, 1, 2 * ENC_PAD)
        crossed = segments[:, :, ::-1].reshape(2, 2, 1, 2 * ENC_PAD)
        ordered = jnp.stack(
            [jnp.where(core == 0, straight, crossed), jnp.where(core == 0, crossed, straight)]
        )
        weights = dict(
            w_embed=embed, w_down=enc_down, w_up=enc_up, w_proj=enc_proj,
            w_qkv=enc_qkv, dec_qkv=dec_qkv, enc_vecs=enc_norms.T, dec_vecs=dec_vecs.T,
        )
        kept = front(
            dict(
                enc_input=enc_input[0], cotangent=cotangent[0], tables=ordered,
                codes=jnp.asarray(codes), **weights,
            ),
            chips,
        )
        shares, home_rows, home_grad = back(
            chips,
            dict(
                **kept, **weights, dec_proj=dec_proj, dec_up=dec_up, dec_down=dec_down
            ),
        )
        shapes = (
            dec_down.shape, dec_up.shape, dec_proj.shape, dec_qkv.shape, enc_down.shape,
            enc_up.shape, enc_proj.shape, embed.shape, enc_qkv.shape,
        )
        counts = [shape[0] // images for shape in shapes]
        (
            dec_down_share, dec_up_share, dec_proj_share, dec_qkv_share, enc_down_share,
            enc_up_share, enc_proj_share, embed_share, enc_qkv_share, enc_norm_share,
            dec_vec_share,
        ) = call(
            functools.partial(
                unstack_kernel, counts, enc_width // images, dec_width // images
            ),
            0,
            [((count, shape[1]), f32) for count, shape in zip(counts, shapes)]
            + [((6, enc_width // images), f32), ((5, dec_width // images), f32)],
            (shares.reshape(-1, LANES),),
            40,
        )
        enc_norm_share, dec_vec_share = enc_norm_share.T, dec_vec_share.T
        grad_input = home_grad[None, :, : enc_half // 2]
        decoded = home_rows[None, :, :dec_quarter]
        return (
            decoded,
            grad_input,
            enc_norm_share,
            enc_qkv_share,
            enc_proj_share,
            enc_up_share,
            enc_down_share,
            embed_share,
            dec_vec_share,
            dec_qkv_share,
            dec_proj_share,
            dec_up_share,
            dec_down_share,
        )

    other_tables = swap(tables)
    tables = jnp.where(seq // 2 == core, tables, other_tables)
    tables = jnp.where(odd, tables[:, 1], tables[:, 0])
    segments = tables.reshape(2, 2, 2, enc_half // 2)
    segments = jnp.pad(
        segments, ((0, 0),) * 3 + ((0, ENC_SEG - enc_half // 2),), constant_values=-2
    )
    halves = segments.reshape(2, 2, ENC_PAD)
    own = pick(halves, core, 1)
    ids = jnp.concatenate([own, pick(halves, 1 - core, 1)], axis=1)
    row_ids = ids[1:2]
    core_arg = core.reshape(1)

    blocks = jnp.pad(enc_input[0], ((0, 0), (0, ENC_SEG - enc_half // 2), (0, 0)))
    x = jnp.concatenate(exchange_packs(blocks, odd), axis=0)
    cot = jnp.concatenate(exchange_packs(cotangent[0], odd), axis=0)
    cot = jnp.concatenate(
        [
            pad_rows(lax.dynamic_slice_in_dim(cot, core * HALF, SMALL, 0), SMALL_PAD),
            pad_rows(lax.dynamic_slice_in_dim(cot, (1 - core) * SMALL, HALF, 0), BIG_PAD),
        ],
        axis=0,
    )
    enc_hidden_width = enc_up.shape[1]

    enc_query, enc_kv = call(
        enc_pre_kernel,
        0,
        [((ENC_PAD, enc_width), bf16), ((ENC_PAD, 2 * enc_width), bf16)],
        (x, enc_vecs, enc_qkv),
        40,
    )
    enc_other = swap(enc_kv)
    embedded, enc_att, enc_probs, enc_middle, enc_active, enc_slope, enc_out = call(
        enc_main_kernel,
        0,
        [
            ((ENC_PAD, dec_width), bf16),
            ((ENC_PAD, enc_width), bf16),
            ((HE, ENC_PAD, 2 * ENC_PAD), bf16),
            ((ENC_PAD, enc_width), f32),
            ((ENC_PAD, enc_hidden_width), bf16),
            ((ENC_PAD, enc_hidden_width), bf16),
            ((ENC_PAD, enc_width), f32),
        ],
        (
            x, enc_query, enc_kv, enc_other, own[0][:, None], ids[0:1], enc_vecs,
            enc_proj, enc_up, enc_down, embed,
        ),
        48,
    )

    code = pick(jnp.asarray(codes), core, 0)
    dec_input, dec_mixed, big_kv = call(
        dec_pre_kernel,
        1,
        [
            ((DEC_PAD, dec_width), f32),
            ((DEC_PAD, 3 * dec_width), bf16),
            ((BIG_PAD, 2 * dec_width), bf16),
        ],
        (core_arg, embedded, swap(embedded), row_ids, code, dec_rows_vecs, dec_qkv),
        40,
    )
    other_kv = swap(big_kv)
    groups = dec_width // 128

    def columns(rows, offset=0):
        return pl.BlockSpec((rows, 128), lambda group: (0, offset + group))

    def heads(rows, cols):
        return pl.BlockSpec((HD // groups, rows, cols), lambda group: (group, 0, 0))

    qkv_specs = [
        columns(DEC_PAD),
        columns(DEC_PAD, groups),
        columns(DEC_PAD, 2 * groups),
        columns(BIG_PAD),
        columns(BIG_PAD, groups),
    ]
    qkv_args = (dec_mixed, dec_mixed, dec_mixed, other_kv, other_kv)
    prob_specs = [heads(BIG_PAD, 2 * BIG_PAD), heads(SMALL_PAD, SMALL_PAD)]
    dec_att, big_probs, small_probs = pl.pallas_call(
        dec_att_kernel,
        grid=(groups,),
        in_specs=qkv_specs,
        out_specs=[columns(DEC_PAD)] + prob_specs,
        out_shape=[
            jax.ShapeDtypeStruct((DEC_PAD, dec_width), bf16),
            jax.ShapeDtypeStruct((HD, BIG_PAD, 2 * BIG_PAD), bf16),
            jax.ShapeDtypeStruct((HD, SMALL_PAD, SMALL_PAD), bf16),
        ],
        compiler_params=pltpu.CompilerParams(vmem_limit_bytes=48 << 20),
    )(*qkv_args)
    chunk_mid = Chunk(images, [dec_down.shape, dec_up.shape, dec_proj.shape])
    decoded, grad_dec_middle, dec_grad_att, vectors_two, *mid_grads = call(
        functools.partial(dec_mid_kernel, chunk_mid),
        1,
        [
            ((DEC_PAD, dec_width), bf16),
            ((DEC_PAD, dec_width), f32),
            ((DEC_PAD, dec_width), bf16),
            ((2, dec_width), f32),
        ]
        + chunk_mid.outs(),
        (core_arg, dec_input, dec_att, cot, dec_rows_vecs, dec_proj, dec_up, dec_down),
        48,
    )
    grad_specs = [columns(DEC_PAD)] * 3 + [columns(BIG_PAD)] * 2
    grad_query, grad_key, grad_value, leaving_key, leaving_value = pl.pallas_call(
        dec_att_back_kernel,
        grid=(groups,),
        in_specs=qkv_specs + [columns(DEC_PAD)] * 2 + prob_specs,
        out_specs=grad_specs,
        out_shape=[
            jax.ShapeDtypeStruct((DEC_PAD, dec_width), bf16),
            jax.ShapeDtypeStruct((DEC_PAD, dec_width), f32),
            jax.ShapeDtypeStruct((DEC_PAD, dec_width), f32),
            jax.ShapeDtypeStruct((BIG_PAD, dec_width), bf16),
            jax.ShapeDtypeStruct((BIG_PAD, dec_width), bf16),
        ],
        compiler_params=pltpu.CompilerParams(vmem_limit_bytes=48 << 20),
    )(*qkv_args, dec_grad_att, dec_att, big_probs, small_probs)
    chunk_post = Chunk(images, [dec_qkv.shape])
    own_spread, other_spread, vectors_one, *post_grads = call(
        functools.partial(dec_post_kernel, chunk_post),
        1,
        [
            ((ENC_PAD, dec_width), bf16),
            ((ENC_PAD, dec_width), bf16),
            ((3, dec_width), f32),
        ]
        + chunk_post.outs(),
        (
            core_arg, dec_input, grad_dec_middle, grad_query, grad_key, grad_value,
            swap(leaving_key), swap(leaving_value), row_ids, dec_rows_vecs, dec_qkv,
        ),
        48,
    )
    arrived_spread = swap(other_spread)
    chunk_down = Chunk(images, [enc_down.shape])
    chunk_up = Chunk(images, [enc_up.shape])
    grad_enc_middle, enc_grad_att, enc_vectors_two, *mlp_grads = call(
        functools.partial(enc_mlp_back_kernel, chunk_down, chunk_up),
        1,
        [
            ((ENC_PAD, enc_width), f32),
            ((ENC_PAD, enc_width), bf16),
            ((4, enc_width), f32),
        ]
        + chunk_down.outs()
        + chunk_up.outs(),
        (
            core_arg, own_spread, arrived_spread, enc_out, enc_middle, enc_active, enc_slope,
            enc_vecs, embed, enc_down, enc_up, enc_proj,
        ),
        56,
    )
    down_grads, up_grads = mlp_grads[: len(chunk_down.outs())], mlp_grads[len(chunk_down.outs()) :]
    enc_grad_query, enc_grad_kv, enc_leaving = call(
        enc_att_back_kernel,
        0,
        [
            ((ENC_PAD, enc_width), bf16),
            ((ENC_PAD, 2 * enc_width), f32),
            ((ENC_PAD, 2 * enc_width), bf16),
        ],
        (enc_grad_att, enc_att, enc_probs, enc_query, enc_kv, enc_other),
        48,
    )
    chunk_att = Chunk(images, [enc_qkv.shape, enc_proj.shape, embed.shape], 16)
    grad_input, enc_vectors_one, *att_grads = call(
        functools.partial(enc_post_kernel, chunk_att),
        1,
        [((ENC_PAD, enc_width), f32), ((2, enc_width), f32)] + chunk_att.outs(),
        (
            core_arg, x, enc_att, grad_enc_middle, enc_grad_query, enc_grad_kv,
            swap(enc_leaving), enc_out, own_spread, arrived_spread, enc_vecs, enc_qkv,
        ),
        48,
    )

    def by_image(rows):
        flat = rows.reshape(rows.shape[0], images, rows.shape[1] // images)
        return flat.transpose(1, 0, 2).reshape(images, -1)

    vectors = jnp.concatenate(
        [
            by_image(jnp.concatenate([enc_vectors_one, enc_vectors_two])),
            by_image(jnp.concatenate([vectors_one[:2], vectors_two, vectors_one[2:]])),
        ],
        axis=1,
    ).astype(bf16)
    vectors = jnp.pad(vectors, ((0, 0), (0, 16 * LANES - vectors.shape[1])))
    vectors = vectors.reshape(images // 2, 2, 16, LANES)
    vectors = (pick(vectors, core, 1), pick(vectors, 1 - core, 1))
    chunk_pairs = [
        chunk.pair(grads, core)
        for chunk, grads in (
            (chunk_mid, mid_grads),
            (chunk_post, post_grads),
            (chunk_down, down_grads),
            (chunk_up, up_grads),
            (chunk_att, att_grads),
        )
    ]
    place = slice(chunk_att.used, chunk_att.used + 16)
    chunk_pairs[-1] = tuple(
        array.at[:, place].set(rows) for array, rows in zip(chunk_pairs[-1], vectors)
    )
    shares = [reduce_rest(reduce_pair(*pair), seq) for pair in chunk_pairs]
    mid_share, post_share, down_share, up_share, att_share = shares
    dec_down_share, dec_up_share, dec_proj_share = chunk_mid.split(mid_share)
    (dec_qkv_share,) = chunk_post.split(post_share)
    (enc_down_share,) = chunk_down.split(down_share)
    (enc_up_share,) = chunk_up.split(up_share)
    enc_qkv_share, enc_proj_share, embed_share = chunk_att.split(att_share)
    vectors = att_share[chunk_att.used : chunk_att.used + 16].reshape(-1).astype(f32)
    enc_count, dec_count = enc_width // images, dec_width // images
    enc_norm_share = vectors[: 6 * enc_count].reshape(6, enc_count).T
    dec_vec_share = vectors[6 * enc_count : 6 * enc_count + 5 * dec_count].reshape(5, dec_count).T

    start = jnp.concatenate([decoded[:SMALL], decoded[SMALL_PAD : SMALL_PAD + HALF]])
    end = jnp.concatenate([decoded[SMALL_PAD : SMALL_PAD + HALF], decoded[:SMALL]])
    natural = jnp.where(core == 0, start, end)
    decoded = jnp.stack(exchange_packs(natural.reshape(2, dec_quarter, dec_width), odd))[None]
    grad_input = jnp.stack(
        exchange_packs(grad_input.reshape(2, ENC_SEG, enc_width)[:, : enc_half // 2], odd)
    )[None]
    return (
        decoded,
        grad_input,
        enc_norm_share,
        enc_qkv_share,
        enc_proj_share,
        enc_up_share,
        enc_down_share,
        embed_share,
        dec_vec_share,
        dec_qkv_share,
        dec_proj_share,
        dec_up_share,
        dec_down_share,
    )


def solution(mesh):
    rows = P("img", None, "seq", None)
    tables = P("img", None, None)
    shares = P("img", None)
    return jax.shard_map(
        shards,
        mesh=mesh,
        in_specs=(rows, rows, tables, tables) + (P(),) * 11,
        out_specs=(rows, rows) + (shares,) * 11,
        check_vma=False,
    )
```
